32 devices in a mesh: lon: 16 (over z, y, core), head: 2 (over x).
Axes of the slice: x: 2, y: 2, z: 4, core: 2. Of those that a mesh axis runs over, the one named last changes fastest.
Arguments:
- pixels: bfloat16 [48, 32, 4096], P(None, None, 'lon'), may hold values from -6 to 6
- crop_starts: int32 [4, 8], replicated, may hold values from 0 to 30
- crop_shifts: int32 [4, 8], replicated, may hold values from -1 to 1, as said below
- slot_crops: int32 [4, 2048], P(None, 'lon'), may hold values from 0 to 7, as said below
- occupied: int32 [4, 2048], P(None, 'lon'), may hold values from 0 to 1, as said below
- lead_hours: int32 [4, 8], replicated, may hold values from 6 to 168
- patch_weight: bfloat16 [48, 4, 1024], P(None, None, ('lon', 'head')), may hold values from -3 to 3
- variable_embed: bfloat16 [48, 1024], P(None, ('lon', 'head')), may hold values from -3 to 3
- mixer_query: bfloat16 [16, 64], P('head', 'lon'), may hold values from -9 to 9
- mixer_keys: bfloat16 [1024, 1024], P('lon', 'head'), may hold values from -0.1875 to 0.1875
- mixer_values: bfloat16 [1024, 1024], P('lon', 'head'), may hold values from -0.1875 to 0.1875
- mixer_output: bfloat16 [1024, 1024], P('head', 'lon'), may hold values from -0.5 to 0.5
- lead_embed: bfloat16 [2, 1024], P(None, ('lon', 'head')), may hold values from -6 to 6
- first_gain: bfloat16 [1024], P(('lon', 'head')), may hold values from 0.5 to 1.5
- first_bias: bfloat16 [1024], P(('lon', 'head')), may hold values from -3 to 3
- attention_in: bfloat16 [3, 1024, 1024], P(None, 'lon', 'head'), may hold values from -0.25 to 0.25
- attention_out: bfloat16 [1024, 1024], P('head', 'lon'), may hold values from -0.75 to 0.75
- second_gain: bfloat16 [1024], P(('lon', 'head')), may hold values from 0.5 to 1.5
- second_bias: bfloat16 [1024], P(('lon', 'head')), may hold values from -3 to 3
- expand_weight: bfloat16 [1024, 4096], P('lon', 'head'), may hold values from -0.1875 to 0.1875
- expand_bias: bfloat16 [64, 64], P('head', 'lon'), may hold values from -3 to 3
- reduce_weight: bfloat16 [4096, 1024], P('head', 'lon'), may hold values from -0.125 to 0.125
- output_weight: bfloat16 [1024, 192], P('lon', 'head'), may hold values from -0.1875 to 0.1875
- cotangent: bfloat16 [4, 2048, 192], P(None, 'lon', 'head'), may hold values from -6 to 6
Outputs:
- predicted: bfloat16 [4, 2048, 192], P(None, 'lon', 'head')
- pixel_grad: float32 [48, 32, 4096], P(None, None, 'lon')
- grad_patch_weight: float32 [48, 4, 1024], P(None, None, ('lon', 'head'))
- grad_variable_embed: float32 [48, 1024], P(None, ('lon', 'head'))
- grad_mixer_query: float32 [16, 64], P('head', 'lon')
- grad_mixer_keys: float32 [1024, 1024], P('lon', 'head')
- grad_mixer_values: float32 [1024, 1024], P('lon', 'head')
- grad_mixer_output: float32 [1024, 1024], P('head', 'lon')
- grad_lead_embed: float32 [2, 1024], P(None, ('lon', 'head'))
- grad_first_gain: float32 [1024], P(('lon', 'head'))
- grad_first_bias: float32 [1024], P(('lon', 'head'))
- grad_attention_in: float32 [3, 1024, 1024], P(None, 'lon', 'head')
- grad_attention_out: float32 [1024, 1024], P('head', 'lon')
- grad_second_gain: float32 [1024], P(('lon', 'head'))
- grad_second_bias: float32 [1024], P(('lon', 'head'))
- grad_expand_weight: float32 [1024, 4096], P('lon', 'head')
- grad_expand_bias: float32 [64, 64], P('head', 'lon')
- grad_reduce_weight: float32 [4096, 1024], P('head', 'lon')
- grad_output_weight: float32 [1024, 192], P('lon', 'head')
The draws below stay inside these ranges and needn't reach their ends.
Inputs may be any that keep to these rules, and one draw needn't show every extreme that they name: `crop_shifts`: each is -1 or +1. `slot_crops`: crop numbers start at 0 and never fall along a row; a row's padded slots lie in its last crop. `occupied`: the padded slots of a row form its tail.
All inputs are finite; a program needn't handle non-finite values.
Results may differ from the reference program's by a relative error of at most 0.035.
Values may be sent and summed in bfloat16 or wider, within the bound.
A program may use at most 192 MiB of HBM per device.

```python
import jax
import jax.numpy as jnp
from jax import lax

D = 1024
HEADS = 16
HEAD_DIM = 64
FF = 4096
VARS = 48
SEGS = 8
LATP = 32
ROWS = 4
SLOTS_DEV = 128
SLOTS = 2048
LONPIX = 4096
OUT_WIDTH = 192


def row_layout(key):
    first_row = jax.random.randint(jax.random.fold_in(key, 11), (), 0, ROWS)
    second_row = (first_row + 1) % ROWS
    row_index = jnp.arange(ROWS)
    whole_rows = (row_index == first_row) | (row_index == second_row)
    tail_lengths = jax.random.randint(jax.random.fold_in(key, 12), (ROWS,), 1, 2 * SLOTS_DEV + 1)
    tail_lengths = jnp.where(whole_rows, 0, tail_lengths)
    return (first_row, second_row, whole_rows, tail_lengths)


def draw_slot_crops(key, part):
    first_row, second_row, whole_rows, tail_lengths = row_layout(key)
    key = jax.random.fold_in(key, 3)
    cut_range = SLOTS - 2 * SLOTS_DEV - 1
    positions = jnp.arange(SLOTS)

    def one_row(row_key):
        cut_points = jax.random.permutation(row_key, cut_range)[:SEGS - 1] + 1
        return jnp.sum((positions[:, None] >= cut_points[None, :]).astype(jnp.int32), axis=1)
    crop_numbers = jax.vmap(one_row)(jax.random.split(key, ROWS))
    return jnp.where(whole_rows[:, None], 0, crop_numbers).astype(jnp.int32)


def draw_occupied(key, part):
    first_row, second_row, whole_rows, tail_lengths = row_layout(key)
    return (jnp.arange(SLOTS)[None, :] < (SLOTS - tail_lengths)[:, None]).astype(jnp.int32)


def draw_crop_shifts(key, part):
    first_row, second_row, whole_rows, tail_lengths = row_layout(key)
    key = jax.random.fold_in(key, 5)
    offsets = 2 * jax.random.randint(key, (ROWS, SEGS), 0, 2) - 1
    row_index = jnp.arange(ROWS)[:, None]
    column = jnp.arange(SEGS)[None, :]
    offsets = jnp.where((row_index == first_row) & (column == 0), -1, offsets)
    offsets = jnp.where((row_index == second_row) & (column == 0), 1, offsets)
    return offsets.astype(jnp.int32)


def set_ends(entries, key, least, high):
    index_at = [jax.random.randint(jax.random.fold_in(key, axis), (), 0, length) for axis, length in enumerate(entries.shape)]
    widest = entries.shape.index(max(entries.shape))
    next_to = index_at[:widest] + [(index_at[widest] + 1) % entries.shape[widest]] + index_at[widest + 1:]
    return entries.at[tuple(index_at)].set(least).at[tuple(next_to)].set(high)


def steps_of(own_key, dims, shards, least, high):
    level = 1.0
    for dim, blocks in shards:
        steps = jax.random.uniform(jax.random.fold_in(jax.random.fold_in(own_key, 6), dim), (blocks,), jnp.float32, least / len(shards), high / len(shards))
        level = level * jnp.repeat(jnp.exp(steps), dims[dim] // blocks).reshape((-1,) + (1,) * (len(dims) - 1 - dim))
    return level


def bell_draw(key, shape, scale, reach, shards=(), kind=jnp.bfloat16):
    entries = scale * jax.random.normal(key, shape, jnp.float32)
    if shards:
        entries = entries * steps_of(key, shape, shards, -0.22, 0.18)
    return jnp.clip(entries, -reach, reach).astype(kind)


def setup_inputs(seed: int = 0) -> dict:
    keys = jax.random.split(jax.random.key(seed), 25)
    return {
        "pixels": bell_draw(keys[0], (VARS, LATP, LONPIX), 1.0, 6.0, ((2, 16),)),
        "crop_starts": set_ends(jax.random.randint(keys[1], (ROWS, SEGS), 0, LATP - 1), jax.random.fold_in(keys[1], 1), 0, (LATP - 1) - 1).astype(jnp.int32),
        "crop_shifts": draw_crop_shifts(jax.random.fold_in(keys[24], 71), 0),
        "slot_crops": draw_slot_crops(jax.random.fold_in(keys[24], 71), 0),
        "occupied": draw_occupied(jax.random.fold_in(keys[24], 71), 0),
        "lead_hours": set_ends(jax.random.randint(keys[5], (ROWS, SEGS), 6, 169), jax.random.fold_in(keys[5], 1), 6, 168).astype(jnp.int32),
        "patch_weight": bell_draw(keys[6], (VARS, 4, D), 4 ** -0.5, 3.0, ((2, 32),)),
        "variable_embed": bell_draw(keys[7], (VARS, D), 0.5, 3.0, ((1, 32),)),
        "mixer_query": bell_draw(keys[8], (HEADS, HEAD_DIM), 1.5, 9.0, ((0, 2), (1, 16))),
        "mixer_keys": bell_draw(keys[9], (D, D), D ** -0.5, 0.1875, ((0, 16), (1, 2))),
        "mixer_values": bell_draw(keys[10], (D, D), D ** -0.5, 0.1875, ((0, 16), (1, 2))),
        "mixer_output": bell_draw(keys[11], (D, D), (D // 8) ** -0.5, 0.5, ((0, 2), (1, 16))),
        "lead_embed": bell_draw(keys[12], (2, D), 1.0, 6.0, ((1, 32),)),
        "first_gain": jnp.clip(1.0 + 0.1 * jax.random.normal(keys[13], (D,), jnp.float32), 0.5, 1.5).astype(jnp.bfloat16),
        "first_bias": bell_draw(keys[14], (D,), 0.5, 3.0, ((0, 32),)),
        "attention_in": bell_draw(keys[15], (3, D, D), (D // 2) ** -0.5, 0.25, ((1, 16), (2, 2))),
        "attention_out": bell_draw(keys[16], (D, D), (D // 16) ** -0.5, 0.75, ((0, 2), (1, 16))),
        "second_gain": jnp.clip(1.0 + 0.1 * jax.random.normal(keys[17], (D,), jnp.float32), 0.5, 1.5).astype(jnp.bfloat16),
        "second_bias": bell_draw(keys[18], (D,), 0.5, 3.0, ((0, 32),)),
        "expand_weight": bell_draw(keys[19], (D, FF), D ** -0.5, 0.1875, ((0, 16), (1, 2))),
        "expand_bias": bell_draw(keys[20], (FF // 64, 64), 0.5, 3.0, ((0, 2), (1, 16))),
        "reduce_weight": bell_draw(keys[21], (FF, D), (FF // 2) ** -0.5, 0.125, ((0, 2), (1, 16))),
        "output_weight": bell_draw(keys[22], (D, OUT_WIDTH), D ** -0.5, 0.1875, ((0, 16), (1, 2))),
        "cotangent": bell_draw(keys[23], (ROWS, SLOTS, OUT_WIDTH), 1.0, 6.0, ((1, 16), (2, 2))),
    }


highest = lax.Precision.HIGHEST
epsilon = 1e-05
masked_score = -1e+30

@jax.custom_vjp
def low(v):
    return lax.optimization_barrier(v.astype(jnp.bfloat16)).astype(jnp.float32)

@jax.custom_vjp
def low_back(v):
    return v

def low_keep(v):
    return (low(v), None)

def low_pass(kept, grad):
    return (grad,)

def back_keep(v):
    return (v, None)

def back_low(kept, grad):
    return (low(grad),)
low.defvjp(low_keep, low_pass)
low_back.defvjp(back_keep, back_low)

def rounded_both(value):
    return low(low_back(value))

def layer_norm(values, gain_vector, shift_vector):
    center = values - lax.optimization_barrier(jnp.mean(values, axis=-1, keepdims=True))
    spread = lax.optimization_barrier(jnp.mean(center * center, axis=-1, keepdims=True))
    return center * lax.rsqrt(spread + epsilon) * gain_vector + shift_vector

def mixer_block(patch_block, patch_weight, variable_embed, mixer_query, mixer_keys, mixer_values, mixer_output):
    slot_count = patch_block.shape[0]
    embedded = low(jnp.einsum('svk,vkd->svd', patch_block, patch_weight, precision=highest) + variable_embed)
    key_rows = rounded_both(jnp.einsum('svd,de->sve', embedded, mixer_keys, precision=highest))
    value_rows = rounded_both(jnp.einsum('svd,de->sve', embedded, mixer_values, precision=highest))
    key_rows = key_rows.reshape(slot_count, VARS, HEADS, HEAD_DIM)
    value_rows = value_rows.reshape(slot_count, VARS, HEADS, HEAD_DIM)
    scores = jnp.einsum('svhd,hd->shv', key_rows, mixer_query, precision=highest) * HEAD_DIM ** (-0.5)
    weights = jax.nn.softmax(scores, axis=-1)
    mixed_rows = rounded_both(jnp.einsum('shv,svhd->shd', weights, value_rows, precision=highest).reshape(slot_count, D))
    return low_back(jnp.dot(mixed_rows, mixer_output, precision=highest))

def attention_block(queries, query_crops, key_rows, value_rows, key_tags):
    scores = low_back(jnp.einsum('qhd,khd->hqk', queries, key_rows, precision=highest) * HEAD_DIM ** (-0.5))
    matched = query_crops[:, None] == key_tags[None, :]
    scores = jnp.where(matched[None], scores, masked_score)
    weights = low(jax.nn.softmax(scores, axis=-1))
    return jnp.einsum('hqk,khd->qhd', weights, value_rows, precision=highest)

def one_row(field, params, row_inputs):
    patch_weight, variable_embed, mixer_query, mixer_keys, mixer_values, mixer_output, lead_embed, first_gain, first_bias, attention_in, attention_out, second_gain, second_bias, expand_weight, expand_bias, reduce_weight, output_weight = params
    slot_crops, occupied, crop_starts, crop_shifts, lead_hours = row_inputs
    starts = crop_starts[slot_crops]
    shifts = crop_shifts[slot_crops]
    lead_slot = lead_hours[slot_crops].astype(jnp.float32) / 100.0
    columns = (2 * jnp.arange(SLOTS, dtype=jnp.int32) + shifts)[:, None] + jnp.arange(2, dtype=jnp.int32)[None, :]
    columns = columns % LONPIX
    lat_rows = starts[:, None] + jnp.arange(2, dtype=jnp.int32)[None, :]
    picked = field[:, lat_rows[:, :, None], columns[:, None, :]]
    patches = jnp.transpose(picked, (1, 0, 2, 3)).reshape(SLOTS, VARS, 4)
    block_width = min(512, SLOTS)
    block_count = SLOTS // block_width

    def mixer_piece(patch_block):
        return mixer_block(patch_block, patch_weight, variable_embed, mixer_query, mixer_keys, mixer_values, mixer_output)
    mixed_sum = lax.map(jax.checkpoint(mixer_piece), patches.reshape(block_count, block_width, VARS, 4)).reshape(SLOTS, D)
    start_sum = mixed_sum + lead_slot[:, None] * lead_embed[0] + lead_embed[1]
    first_low = low(layer_norm(start_sum, first_gain, first_bias))
    projected = rounded_both(jnp.einsum('td,kde->kte', first_low, attention_in, precision=highest))
    projected = projected.reshape(3, SLOTS, HEADS, HEAD_DIM)
    key_tags = jnp.where(occupied == 1, slot_crops, -1)

    def attend_piece(pieces):
        return attention_block(pieces[0], pieces[1], projected[1], projected[2], key_tags)
    attended = lax.map(jax.checkpoint(attend_piece), (projected[0].reshape(block_count, block_width, HEADS, HEAD_DIM), slot_crops.reshape(block_count, block_width)))
    attended = rounded_both(attended.reshape(SLOTS, D))
    middle = start_sum + low_back(jnp.dot(attended, attention_out, precision=highest))
    second_low = low(layer_norm(middle, second_gain, second_bias))
    hidden = low_back(jnp.dot(second_low, expand_weight, precision=highest) + expand_bias.reshape(-1))
    active = low(jax.nn.gelu(hidden, approximate=False))
    final_sum = middle + low_back(jnp.dot(active, reduce_weight, precision=highest))
    return occupied[:, None].astype(jnp.float32) * jnp.dot(low(final_sum), output_weight, precision=highest)

def reference(pixels, crop_starts, crop_shifts, slot_crops, occupied, lead_hours, patch_weight, variable_embed, mixer_query, mixer_keys, mixer_values, mixer_output, lead_embed, first_gain, first_bias, attention_in, attention_out, second_gain, second_bias, expand_weight, expand_bias, reduce_weight, output_weight, cotangent):
    params = tuple((weight.astype(jnp.float32) for weight in (patch_weight, variable_embed, mixer_query, mixer_keys, mixer_values, mixer_output, lead_embed, first_gain, first_bias, attention_in, attention_out, second_gain, second_bias, expand_weight, expand_bias, reduce_weight, output_weight)))

    def forward(field, weights):
        return lax.map(lambda row_inputs: one_row(field, weights, row_inputs), (slot_crops, occupied, crop_starts, crop_shifts, lead_hours))
    predicted, backward = jax.vjp(forward, pixels.astype(jnp.float32), params)
    pixel_grad, grads = backward(cotangent.astype(jnp.float32))
    return (predicted.astype(jnp.bfloat16), pixel_grad, grads[0], grads[1], grads[2], grads[3], grads[4], grads[5], grads[6], grads[7], grads[8], grads[9], grads[10], grads[11], grads[12], grads[13], grads[14], grads[15], grads[16])
```

```python
from functools import partial

import jax
import jax.numpy as jnp
from jax import lax
from jax.experimental import pallas as pl
from jax.experimental.pallas import tpu as pltpu
from jax.sharding import PartitionSpec as P

HEAD_DIM = 64
LON, HEAD = "lon", "head"


epsilon = 1e-05
masked_score = -1e30
highest = lax.Precision.HIGHEST


def extended(array, sides, width):
    for axis, dim in sides:
        count, length = (lax.axis_size(axis), array.shape[dim])
        up = [(i, (i + 1) % count) for i in range(count)]
        down = [(j, i) for i, j in up]
        last = lax.slice_in_dim(array, length - width, length, axis=dim)
        leading = lax.slice_in_dim(array, 0, width, axis=dim)
        before = lax.ppermute(last, axis, up)
        after = lax.ppermute(leading, axis, down)
        array = jnp.concatenate([before, array, after], axis=dim)
    return array


def layer_norm(values, gain_vector, shift_vector):
    center = values - jnp.mean(values, axis=-1, keepdims=True)
    spread = jnp.mean(center * center, axis=-1, keepdims=True)
    return center * lax.rsqrt(spread + epsilon) * gain_vector + shift_vector


def head_total(partial_sum):
    return lax.psum(partial_sum.astype(jnp.bfloat16), HEAD).astype(jnp.float32)


def head_share(partial_sum):
    return lax.psum_scatter(
        partial_sum.astype(jnp.bfloat16), HEAD, scatter_dimension=0, tiled=True
    ).astype(jnp.float32)


def head_rows(values):
    return lax.all_gather(values, HEAD, axis=0, tiled=True)


def reduce_rows(partial_sum):
    return head_share(partial_sum)


def spread_rows(values):
    return head_rows(values)


def crop_lookup(crop_table, slot_numbers):
    numbers = jnp.arange(crop_table.shape[1], dtype=jnp.int32)
    picked = slot_numbers[:, :, None] == numbers[None, None, :]
    return jnp.sum(jnp.where(picked, crop_table[:, None, :], 0), axis=2)


def outer_sum(left_rows, right_rows):
    return jnp.einsum("ti,tj->ij", left_rows, right_rows, preferred_element_type=jnp.float32)


def block_slice(values, block_index, block_width, axis_number):
    return lax.dynamic_slice_in_dim(values, block_index * block_width, block_width, axis_number)


def block_scores(queries, query_crops, key_block, key_tags):
    scores = jnp.einsum(
        "rqhd,rkhd->rhqk", queries, key_block, preferred_element_type=jnp.float32
    ) * HEAD_DIM ** (-0.5)
    matched = query_crops[:, None, :, None] == key_tags[:, None, None, :]
    return (jnp.where(matched, scores, masked_score), matched)


def key_stats(queries, query_crops, key_rows, key_tags, block_width):
    row_count, slot_count, head_count, head_size = queries.shape

    def key_step(carried, block_index):
        largest, totals = carried
        scores, matched = block_scores(
            queries,
            query_crops,
            block_slice(key_rows, block_index, block_width, 1),
            block_slice(key_tags, block_index, block_width, 1),
        )
        raised = jnp.maximum(largest, jnp.max(scores, axis=-1))
        totals = totals * jnp.exp(largest - raised) + jnp.sum(
            jnp.where(matched, jnp.exp(scores - raised[..., None]), 0.0), axis=-1
        )
        return ((raised, totals), None)

    initial = (
        jnp.full((row_count, head_count, slot_count), masked_score, jnp.float32),
        jnp.zeros((row_count, head_count, slot_count), jnp.float32),
    )
    (largest, totals), _ = lax.scan(key_step, initial, jnp.arange(key_rows.shape[1] // block_width))
    return largest + jnp.log(totals)


def attend(queries, query_crops, key_rows, value_rows, key_tags, log_totals, block_width):

    def attend_step(running, block_index):
        scores, matched = block_scores(
            queries,
            query_crops,
            block_slice(key_rows, block_index, block_width, 1),
            block_slice(key_tags, block_index, block_width, 1),
        )
        weights = jnp.where(matched, jnp.exp(scores - log_totals[..., None]), 0.0).astype(
            jnp.bfloat16
        )
        value_block = block_slice(value_rows, block_index, block_width, 1)
        return (
            running
            + jnp.einsum(
                "rhqk,rkhd->rqhd", weights, value_block, preferred_element_type=jnp.float32
            ),
            None,
        )

    outputs, _ = lax.scan(
        attend_step,
        jnp.zeros(queries.shape, jnp.float32),
        jnp.arange(key_rows.shape[1] // block_width),
    )
    return outputs


def score_grads(
    queries, query_crops, out_grads, log_totals, deltas, key_block, value_block, key_tags
):
    scores, matched = block_scores(queries, query_crops, key_block, key_tags)
    weights = jnp.where(matched, jnp.exp(scores - log_totals[..., None]), 0.0)
    weight_grads = jnp.einsum(
        "rqhd,rkhd->rhqk", out_grads, value_block, preferred_element_type=jnp.float32
    )
    score_delta = (weights * (weight_grads - deltas[..., None])).astype(jnp.bfloat16)
    return (score_delta, weights.astype(jnp.bfloat16))


def mixer_row(patch_row, full_patch, full_variable, pair_weight, head_query):
    embedded = jnp.einsum(
        "svk,vkd->svd", patch_row, full_patch, preferred_element_type=jnp.float32
    ) + full_variable.astype(jnp.float32)
    embedded = embedded.astype(jnp.bfloat16)
    slot_count, var_count, model_width = embedded.shape
    head_count, head_size = head_query.shape
    local_width = head_count * head_size
    paired = jnp.dot(
        embedded.reshape(slot_count * var_count, model_width),
        pair_weight,
        preferred_element_type=jnp.float32,
    ).astype(jnp.bfloat16)
    key_rows = paired[:, :local_width].reshape(slot_count, var_count, head_count, head_size)
    value_rows = paired[:, local_width:].reshape(slot_count, var_count, head_count, head_size)
    scores = jnp.einsum(
        "svhd,hd->shv", key_rows, head_query, preferred_element_type=jnp.float32
    ) * HEAD_DIM ** (-0.5)
    weights = jax.nn.softmax(scores, axis=-1)
    return (embedded, key_rows, value_rows, weights)


def mixer_back(carried, inputs, full_patch, full_variable, pair_weight, head_query):
    patch_row, mixed_grad = inputs
    embedded, key_rows, value_rows, weights = mixer_row(
        patch_row, full_patch, full_variable, pair_weight, head_query
    )
    slot_count, var_count, model_width = embedded.shape
    local_width = key_rows.shape[2] * key_rows.shape[3]
    mixed_wide = mixed_grad.astype(jnp.float32)
    value_grads = jnp.einsum("shv,shd->svhd", weights, mixed_wide, precision=highest).astype(
        jnp.bfloat16
    )
    weight_grads = jnp.einsum(
        "shd,svhd->shv", mixed_wide, value_rows.astype(jnp.float32), precision=highest
    )
    score_delta = (
        weights
        * (weight_grads - jnp.sum(weights * weight_grads, axis=-1, keepdims=True))
        * HEAD_DIM ** (-0.5)
    )
    key_grads = jnp.einsum(
        "shv,hd->svhd", score_delta, head_query.astype(jnp.float32), precision=highest
    ).astype(jnp.bfloat16)
    query_grad = jnp.einsum(
        "shv,svhd->hd", score_delta, key_rows.astype(jnp.float32), precision=highest
    )
    pair_grads = jnp.concatenate(
        [
            key_grads.reshape(slot_count * var_count, local_width),
            value_grads.reshape(slot_count * var_count, local_width),
        ],
        axis=1,
    )
    embed_grad = jnp.einsum(
        "ne,de->nd", pair_grads, pair_weight, preferred_element_type=jnp.float32
    )
    pair_weight_grad = outer_sum(embedded.reshape(slot_count * var_count, model_width), pair_grads)
    embed_grad = embed_grad.reshape(slot_count, var_count, model_width)
    patch_grad = jnp.einsum(
        "svk,svd->vkd", patch_row.astype(jnp.float32), embed_grad, precision=highest
    )
    variable_grad = jnp.sum(embed_grad, axis=0)
    slot_grad = jnp.einsum(
        "svd,vkd->svk", embed_grad, full_patch.astype(jnp.float32), precision=highest
    )
    patch_acc, variable_acc, query_acc, pair_acc = carried
    return (
        (
            patch_acc + patch_grad,
            variable_acc + variable_grad,
            query_acc + query_grad,
            pair_acc + pair_weight_grad,
        ),
        slot_grad,
    )


def local(
    pixels,
    crop_starts,
    crop_shifts,
    slot_crops,
    occupied,
    lead_hours,
    patch_weight,
    variable_embed,
    mixer_query,
    mixer_keys,
    mixer_values,
    mixer_output,
    lead_embed,
    first_gain,
    first_bias,
    attention_in,
    attention_out,
    second_gain,
    second_bias,
    expand_weight,
    expand_bias,
    reduce_weight,
    output_weight,
    cotangent,
):
    shared = (
        lax.all_gather(patch_weight, (LON, HEAD), axis=2, tiled=True),
        lax.all_gather(variable_embed, (LON, HEAD), axis=1, tiled=True),
        lax.all_gather(lead_embed, (LON, HEAD), axis=1, tiled=True),
        lax.all_gather(first_gain, (LON, HEAD), axis=0, tiled=True),
        lax.all_gather(first_bias, (LON, HEAD), axis=0, tiled=True),
        lax.all_gather(second_gain, (LON, HEAD), axis=0, tiled=True),
        lax.all_gather(second_bias, (LON, HEAD), axis=0, tiled=True),
    )
    full_patch, full_variable, full_lead, gain_first, shift_first, gain_second, shift_second = (
        shared
    )
    sector = (
        lax.all_gather(mixer_query, LON, axis=1, tiled=True),
        lax.all_gather(mixer_keys, LON, axis=0, tiled=True),
        lax.all_gather(mixer_values, LON, axis=0, tiled=True),
        lax.all_gather(mixer_output, LON, axis=1, tiled=True),
        lax.all_gather(attention_in, LON, axis=1, tiled=True),
        lax.all_gather(attention_out, LON, axis=1, tiled=True),
        lax.all_gather(expand_weight, LON, axis=0, tiled=True),
        lax.all_gather(expand_bias, LON, axis=1, tiled=True),
        lax.all_gather(reduce_weight, LON, axis=1, tiled=True),
        lax.all_gather(output_weight, LON, axis=0, tiled=True),
    )
    (
        head_query,
        key_weight,
        value_weight,
        mixer_weight,
        input_weight,
        output_proj,
        up_weight,
        up_bias,
        down_weight,
        final_weight,
    ) = sector
    row_count, slot_width = slot_crops.shape
    token_count = row_count * slot_width
    local_width = key_weight.shape[1]
    head_count = local_width // HEAD_DIM
    pair_weight = jnp.concatenate([key_weight, value_weight], axis=1)
    gain_one = gain_first.astype(jnp.float32)
    shift_one = shift_first.astype(jnp.float32)
    gain_two = gain_second.astype(jnp.float32)
    shift_two = shift_second.astype(jnp.float32)
    lat_slot = crop_lookup(crop_starts, slot_crops)
    shift_slot = crop_lookup(crop_shifts, slot_crops)
    lead_slot = crop_lookup(lead_hours, slot_crops).astype(jnp.float32).reshape(token_count) / 100.0
    share_count = token_count // lax.axis_size(HEAD)
    lead_rows = lax.dynamic_slice_in_dim(
        lead_slot, lax.axis_index(HEAD) * share_count, share_count
    )
    padded = extended(pixels, ((LON, 2),), 1)
    var_count, lat_count = (pixels.shape[0], pixels.shape[1])
    west_pairs = padded[:, :, : 2 * slot_width].reshape(var_count, lat_count, slot_width, 2)
    east_pairs = padded[:, :, 2:].reshape(var_count, lat_count, slot_width, 2)
    side_pairs = jnp.stack([west_pairs, east_pairs])
    tables = jnp.stack([side_pairs[:, :, :-1], side_pairs[:, :, 1:]], axis=3)
    lat_index = jnp.arange(lat_count - 1, dtype=jnp.int32)
    side_shift = 2 * jnp.arange(2, dtype=jnp.int32) - 1
    chosen = (lat_slot[:, :, None, None] == lat_index[None, None, None, :]) & (
        shift_slot[:, :, None, None] == side_shift[None, None, :, None]
    )
    patches = jnp.einsum(
        "rjsa,svapjx->rjvpx",
        chosen.astype(jnp.bfloat16),
        tables,
        preferred_element_type=jnp.float32,
    )
    patches = patches.astype(jnp.bfloat16).reshape(row_count, slot_width, var_count, 4)

    def mixer_forward(patch_row):
        embedded, key_rows, value_rows, weights = mixer_row(
            patch_row, full_patch, full_variable, pair_weight, head_query
        )
        return jnp.einsum(
            "shv,svhd->shd", weights, value_rows.astype(jnp.float32), precision=highest
        ).astype(jnp.bfloat16)

    mixed_low = lax.map(mixer_forward, patches).reshape(token_count, local_width)
    start_sum = reduce_rows(jnp.dot(mixed_low, mixer_weight, preferred_element_type=jnp.float32))
    start_sum = (
        start_sum
        + lead_rows[:, None] * full_lead[0].astype(jnp.float32)
        + full_lead[1].astype(jnp.float32)
    )
    first_low = spread_rows(layer_norm(start_sum, gain_one, shift_one).astype(jnp.bfloat16))
    projected = jnp.einsum(
        "td,kde->kte", first_low, input_weight, preferred_element_type=jnp.float32
    ).astype(jnp.bfloat16)
    projected = projected.reshape(3, row_count, slot_width, head_count, HEAD_DIM)
    queries, key_local, value_local = (projected[0], projected[1], projected[2])
    query_crops = slot_crops.astype(jnp.float32)
    key_tags = jnp.where(occupied == 1, slot_crops, -1).astype(jnp.bfloat16)
    key_all, value_all, tag_all = (
        lax.all_gather(key_local, LON, axis=1, tiled=True),
        lax.all_gather(value_local, LON, axis=1, tiled=True),
        lax.all_gather(key_tags, LON, axis=1, tiled=True),
    )
    block_width = min(512, key_all.shape[1])
    tag_wide = tag_all.astype(jnp.float32)
    log_totals = key_stats(queries, query_crops, key_all, tag_wide, block_width)
    attended = attend(queries, query_crops, key_all, value_all, tag_wide, log_totals, block_width)
    attended_low = attended.astype(jnp.bfloat16).reshape(token_count, local_width)
    middle = start_sum + reduce_rows(
        jnp.dot(attended_low, output_proj, preferred_element_type=jnp.float32)
    )
    second_low = spread_rows(layer_norm(middle, gain_two, shift_two).astype(jnp.bfloat16))
    hidden = jnp.dot(second_low, up_weight, preferred_element_type=jnp.float32) + up_bias.reshape(
        -1
    ).astype(jnp.float32)
    active = jax.nn.gelu(hidden, approximate=False).astype(jnp.bfloat16)
    final_sum = middle + reduce_rows(
        jnp.dot(active, down_weight, preferred_element_type=jnp.float32)
    )
    final_low = spread_rows(final_sum.astype(jnp.bfloat16))
    keep_mask = occupied.reshape(token_count, 1)
    predicted = (
        jnp.dot(final_low, final_weight, preferred_element_type=jnp.float32)
        * keep_mask.astype(jnp.float32)
    ).astype(jnp.bfloat16)
    predicted = predicted.reshape(row_count, slot_width, -1)
    masked_grad = (cotangent * occupied[:, :, None].astype(jnp.bfloat16)).reshape(token_count, -1)
    grad_final_weight = outer_sum(final_low, masked_grad)
    part_top = jnp.einsum(
        "to,do->td", masked_grad, final_weight, preferred_element_type=jnp.float32
    )
    final_grad = reduce_rows(part_top)
    final_grad_low = spread_rows(final_grad.astype(jnp.bfloat16))
    grad_down = outer_sum(active, final_grad_low)
    active_grad = jnp.einsum(
        "td,fd->tf", final_grad_low, down_weight, preferred_element_type=jnp.float32
    )
    _, gelu_back = jax.vjp(partial(jax.nn.gelu, approximate=False), hidden)
    hidden_grad = gelu_back(active_grad)[0].astype(jnp.bfloat16)
    grad_up = outer_sum(second_low, hidden_grad)
    grad_up_bias = jnp.sum(hidden_grad.astype(jnp.float32), axis=0).reshape(up_bias.shape)
    second_grad = jnp.einsum(
        "tf,df->td", hidden_grad, up_weight, preferred_element_type=jnp.float32
    )
    second_in = head_share(second_grad)
    _, second_back = jax.vjp(layer_norm, middle, gain_two, shift_two)
    part_mid, grad_gain_two, grad_shift_two = second_back(second_in)
    middle_grad = final_grad + part_mid
    middle_low = spread_rows(middle_grad.astype(jnp.bfloat16))
    grad_proj = outer_sum(attended_low, middle_low)
    out_grads = jnp.einsum(
        "td,ed->te", middle_low, output_proj, preferred_element_type=jnp.float32
    ).astype(jnp.bfloat16)
    out_grads = out_grads.reshape(row_count, slot_width, head_count, HEAD_DIM)
    deltas = jnp.transpose(jnp.sum(out_grads.astype(jnp.float32) * attended, axis=-1), (0, 2, 1))
    back_keys, back_values, back_raw = (
        lax.all_gather(key_local, LON, axis=1, tiled=True),
        lax.all_gather(value_local, LON, axis=1, tiled=True),
        lax.all_gather(key_tags, LON, axis=1, tiled=True),
    )
    back_tags = back_raw.astype(jnp.float32)
    scale = HEAD_DIM ** (-0.5)
    key_count = back_keys.shape[1] // block_width
    local_zeros = jnp.zeros(queries.shape, jnp.float32)
    whole_zeros = jnp.zeros(back_keys.shape, jnp.float32)

    def both_step(running, block_index):
        query_acc, key_acc, value_acc = running
        key_block = block_slice(back_keys, block_index, block_width, 1)
        score_delta, weights_low = score_grads(
            queries,
            query_crops,
            out_grads,
            log_totals,
            deltas,
            key_block,
            block_slice(back_values, block_index, block_width, 1),
            block_slice(back_tags, block_index, block_width, 1),
        )
        query_acc = (
            query_acc
            + jnp.einsum(
                "rhqk,rkhd->rqhd", score_delta, key_block, preferred_element_type=jnp.float32
            )
            * scale
        )
        key_piece = (
            jnp.einsum("rhqk,rqhd->rkhd", score_delta, queries, preferred_element_type=jnp.float32)
            * scale
        )
        value_piece = jnp.einsum(
            "rhqk,rqhd->rkhd", weights_low, out_grads, preferred_element_type=jnp.float32
        )
        key_acc = lax.dynamic_update_slice_in_dim(key_acc, key_piece, block_index * block_width, 1)
        value_acc = lax.dynamic_update_slice_in_dim(
            value_acc, value_piece, block_index * block_width, 1
        )
        return ((query_acc, key_acc, value_acc), None)

    (query_grad, key_part, value_part), _ = lax.scan(
        both_step, (local_zeros, whole_zeros, whole_zeros), jnp.arange(key_count)
    )
    key_grad, value_grad = (
        lax.psum_scatter(
            key_part.astype(jnp.bfloat16), LON, scatter_dimension=1, tiled=True
        ).astype(jnp.float32),
        lax.psum_scatter(
            value_part.astype(jnp.bfloat16), LON, scatter_dimension=1, tiled=True
        ).astype(jnp.float32),
    )
    stacked = (
        jnp.stack([query_grad, key_grad, value_grad])
        .astype(jnp.bfloat16)
        .reshape(3, token_count, local_width)
    )
    first_grad = jnp.einsum(
        "kte,kde->td", stacked, input_weight, preferred_element_type=jnp.float32
    )
    grad_input = jnp.einsum("td,kte->kde", first_low, stacked, preferred_element_type=jnp.float32)
    first_in = head_share(first_grad)
    _, first_back = jax.vjp(layer_norm, start_sum, gain_one, shift_one)
    part_low, grad_gain_one, grad_shift_one = first_back(first_in)
    start_grad = middle_grad + part_low
    grad_lead = jnp.stack(
        [jnp.sum(start_grad * lead_rows[:, None], axis=0), jnp.sum(start_grad, axis=0)]
    )
    start_low = spread_rows(start_grad.astype(jnp.bfloat16))
    grad_mixer = outer_sum(mixed_low, start_low)
    mixed_grad = jnp.einsum(
        "td,ed->te", start_low, mixer_weight, preferred_element_type=jnp.float32
    ).astype(jnp.bfloat16)
    mixed_grad = mixed_grad.reshape(row_count, slot_width, head_count, HEAD_DIM)
    initial = (
        jnp.zeros(full_patch.shape, jnp.float32),
        jnp.zeros(full_variable.shape, jnp.float32),
        jnp.zeros(head_query.shape, jnp.float32),
        jnp.zeros(pair_weight.shape, jnp.float32),
    )
    mixer_step = partial(
        mixer_back,
        full_patch=full_patch,
        full_variable=full_variable,
        pair_weight=pair_weight,
        head_query=head_query,
    )
    (grad_patch, grad_variable, grad_query, grad_pair), slot_grads = lax.scan(
        mixer_step, initial, (patches, mixed_grad)
    )
    slot_total = head_total(slot_grads).reshape(row_count, slot_width, var_count, 2, 2)
    table_grads = jnp.einsum(
        "rjsa,rjvpx->svapjx", chosen.astype(jnp.float32), slot_total, precision=highest
    )
    side_grads = jnp.pad(
        table_grads[:, :, :, 0], ((0, 0), (0, 0), (0, 1), (0, 0), (0, 0))
    ) + jnp.pad(table_grads[:, :, :, 1], ((0, 0), (0, 0), (1, 0), (0, 0), (0, 0)))
    west_grad = side_grads[0].reshape(var_count, lat_count, 2 * slot_width)
    east_grad = side_grads[1].reshape(var_count, lat_count, 2 * slot_width)
    padded_grad = jnp.pad(west_grad, ((0, 0), (0, 0), (0, 2))) + jnp.pad(
        east_grad, ((0, 0), (0, 0), (2, 0))
    )
    rim_values = jnp.stack([padded_grad[:, :, 0], padded_grad[:, :, -1]], axis=2)
    returned = extended(rim_values, ((LON, 2),), 1)
    pixel_grad = (
        padded_grad[:, :, 1:-1]
        + jnp.pad(returned[:, :, 0:1], ((0, 0), (0, 0), (0, 2 * slot_width - 1)))
        + jnp.pad(returned[:, :, 3:4], ((0, 0), (0, 0), (2 * slot_width - 1, 0)))
    )
    sector_out = (
        lax.psum_scatter(
            grad_query.astype(jnp.bfloat16), LON, scatter_dimension=1, tiled=True
        ).astype(jnp.float32),
        lax.psum_scatter(
            grad_pair[:, :local_width].astype(jnp.bfloat16), LON, scatter_dimension=0, tiled=True
        ).astype(jnp.float32),
        lax.psum_scatter(
            grad_pair[:, local_width:].astype(jnp.bfloat16), LON, scatter_dimension=0, tiled=True
        ).astype(jnp.float32),
        lax.psum_scatter(
            grad_mixer.astype(jnp.bfloat16), LON, scatter_dimension=1, tiled=True
        ).astype(jnp.float32),
        lax.psum_scatter(
            grad_input.astype(jnp.bfloat16), LON, scatter_dimension=1, tiled=True
        ).astype(jnp.float32),
        lax.psum_scatter(
            grad_proj.astype(jnp.bfloat16), LON, scatter_dimension=1, tiled=True
        ).astype(jnp.float32),
        lax.psum_scatter(
            grad_up.astype(jnp.bfloat16), LON, scatter_dimension=0, tiled=True
        ).astype(jnp.float32),
        lax.psum_scatter(
            grad_up_bias.astype(jnp.bfloat16), LON, scatter_dimension=1, tiled=True
        ).astype(jnp.float32),
        lax.psum_scatter(
            grad_down.astype(jnp.bfloat16), LON, scatter_dimension=1, tiled=True
        ).astype(jnp.float32),
        lax.psum_scatter(
            grad_final_weight.astype(jnp.bfloat16), LON, scatter_dimension=0, tiled=True
        ).astype(jnp.float32),
    )
    shared_out = (
        lax.psum_scatter(grad_patch, (LON, HEAD), scatter_dimension=2, tiled=True),
        lax.psum_scatter(grad_variable, (LON, HEAD), scatter_dimension=1, tiled=True),
        lax.psum_scatter(grad_lead, (LON, HEAD), scatter_dimension=1, tiled=True),
        lax.psum_scatter(grad_gain_one, (LON, HEAD), scatter_dimension=0, tiled=True),
        lax.psum_scatter(grad_shift_one, (LON, HEAD), scatter_dimension=0, tiled=True),
        lax.psum_scatter(grad_gain_two, (LON, HEAD), scatter_dimension=0, tiled=True),
        lax.psum_scatter(grad_shift_two, (LON, HEAD), scatter_dimension=0, tiled=True),
    )
    return (
        predicted,
        pixel_grad,
        shared_out[0],
        shared_out[1],
        sector_out[0],
        sector_out[1],
        sector_out[2],
        sector_out[3],
        shared_out[2],
        shared_out[3],
        shared_out[4],
        sector_out[4],
        sector_out[5],
        shared_out[5],
        shared_out[6],
        sector_out[6],
        sector_out[7],
        sector_out[8],
        sector_out[9],
    )


MESH = pl.DeviceIdType.MESH
BOTH = (LON, HEAD)
LON_SIZE = 16
HEAD_SIZE = 2
CHUNK = 256
low = jnp.bfloat16
wide = jnp.float32


def planned(mesh):
    return mesh.shape[LON] == LON_SIZE and mesh.shape[HEAD] == HEAD_SIZE


def dot(left, right, left_dim=1, right_dim=0):
    return lax.dot_general(
        left, right, (((left_dim,), (right_dim,)), ((), ())), preferred_element_type=wide
    )


def position():
    lon = lax.axis_index(LON)
    x = lax.axis_index(HEAD)
    z = lax.div(lon, 4)
    y = lax.rem(lax.div(lon, 2), 2)
    c = lax.rem(lon, 2)
    return x, z, y, c


def partners(x, z, y, c):
    here = z * 4 + y * 2 + c
    across = {
        "x": (here, 1 - x),
        "y": (z * 4 + (1 - y) * 2 + c, x),
        "c": (z * 4 + y * 2 + 1 - c, x),
    }
    line = [(lax.rem(z + step, 4) * 4 + y * 2 + c, x) for step in (1, 2, 3)]
    return across, line


def sector_of(z, y, c, x, part, side):
    return (y * 2 + c) * 4 + x * 2 + part, side


def block_of(z, y, row):
    return row * 4 + z, y


def meet(peers, others=(), own=None):
    barrier = pltpu.get_barrier_semaphore()
    for device in peers:
        pl.semaphore_signal(barrier, inc=1, device_id=device, device_id_type=MESH)
    for device in others:

        @pl.when(jnp.logical_not(same(device, own)))
        def _():
            pl.semaphore_signal(barrier, inc=1, device_id=device, device_id_type=MESH)

    expected = len(peers)
    for device in others:
        expected = expected + 1 - same(device, own).astype(jnp.int32)
    pl.semaphore_wait(barrier, expected)


def same(device, own):
    return jnp.logical_and(device[0] == own[0], device[1] == own[1])


def post(source, target, send_sem, recv_sem, device, own):
    here = same(device, own)

    @pl.when(here)
    def _():
        pltpu.make_async_copy(source, target, recv_sem).start()

    @pl.when(jnp.logical_not(here))
    def _():
        remote(source, target, send_sem, recv_sem, device).start()


def settle(source, target, send_sem, recv_sem, device, own):
    @pl.when(jnp.logical_not(same(device, own)))
    def _():
        remote(source, target, send_sem, recv_sem, device).wait_send()


def remote(source, target, send_sem, recv_sem, device):
    return pltpu.make_async_remote_copy(
        src_ref=source,
        dst_ref=target,
        send_sem=send_sem,
        recv_sem=recv_sem,
        device_id=device,
        device_id_type=MESH,
    )


def gather_kernel(items, count, *refs):
    ins, outs = refs[:count], refs[count + 2 : 2 * count + 2]
    patch_in, grad_in = refs[count : count + 2]
    patch_out, grad_out = refs[2 * count + 2 : 2 * count + 4]
    own_sem, line_send, line_recv, hop_send, hop_recv, post_send, post_recv = refs[
        2 * count + 4 :
    ]
    x, z, y, c = position()
    across, line = partners(x, z, y, c)
    own = (z * 4 + y * 2 + c, x)
    sources = [sector_of(z, y, c, x, part, side) for part in range(2) for side in range(2)]
    meet(list(across.values()) + line, sources, own)
    letters = []
    for part in range(2):
        row = 2 * x + part
        letters.append(
            (patch_in.at[part], patch_out.at[c], post_send.at[part], post_recv.at[c])
            + (block_of(z, y, row), own)
        )
    for row in range(4):
        letters.append(
            (grad_in.at[row], grad_out.at[x, c], post_send.at[2 + row])
            + (post_recv.at[2 + 2 * x + c], block_of(z, y, row), own)
        )
    for letter in letters:
        post(*letter)

    def views(item):
        index, lead, first, rows, _ = item
        source, target = ins[index], outs[index]
        if lead is not None:
            source, target = source.at[lead], target.at[lead]
        return source.at[pl.ds(first, rows)], target, pl.ds(first, rows)

    def copies(number):
        item = items[number]
        source, target, span = views(item)
        own = target.at[x, z, y, c, span]
        keep = pltpu.make_async_copy(source, own, own_sem.at[number])
        along = [
            remote(source, own, line_send.at[number, d], line_recv.at[number, d], line[d])
            for d in range(3)
        ]
        quarter = target.at[x, :, y, c, span]
        if item[4] == 0:
            half, order = target.at[x, :, :, c, span], ("y", "x")
        else:
            half, order = target.at[:, :, y, c, span], ("x", "y")
        full = target.at[:, :, :, c, span]
        hops = [
            remote(part, part, hop_send.at[number, k], hop_recv.at[number, k], across[axis])
            for k, (part, axis) in enumerate(
                ((quarter, order[0]), (half, order[1]), (full, "c"))
            )
        ]
        return keep, along, hops

    plan = [copies(number) for number in range(len(items))]
    total = len(items)
    for step in range(total + 8):
        if step < total:
            keep, along, _ = plan[step]
            keep.start()
            for one in along:
                one.start()
        if 0 <= step - 2 < total:
            keep, along, hops = plan[step - 2]
            keep.wait()
            for one in along:
                one.wait_recv()
            hops[0].start()
        if 0 <= step - 4 < total:
            hops = plan[step - 4][2]
            hops[0].wait_recv()
            hops[1].start()
        if 0 <= step - 6 < total:
            hops = plan[step - 6][2]
            hops[1].wait_recv()
            hops[2].start()
        if 0 <= step - 8 < total:
            plan[step - 8][2][2].wait_recv()
    for _, along, hops in plan:
        for one in along + hops:
            one.wait_send()
    for letter in letters:
        settle(*letter)
    for part in range(2):
        pltpu.make_async_copy(patch_in.at[part], patch_out.at[part], post_recv.at[part]).wait()
    for side in range(2):
        for part in range(2):
            pltpu.make_async_copy(
                grad_in.at[0], grad_out.at[side, part], post_recv.at[2 + 2 * side + part]
            ).wait()


def gather_all(arrays, patches, grads, number):
    items = []
    for index, array in enumerate(arrays):
        leads = range(array.shape[0]) if array.ndim == 3 else (None,)
        rows = array.shape[-2]
        for lead in leads:
            if rows >= 64:
                half = rows // 2
                items.append((index, lead, 0, half, 0))
                items.append((index, lead, half, half, 1))
            else:
                items.append((index, lead, 0, rows, 0))
    count = len(arrays)
    shapes = [
        jax.ShapeDtypeStruct(a.shape[:-2] + (2, 4, 2, 2) + a.shape[-2:], a.dtype) for a in arrays
    ] + [
        jax.ShapeDtypeStruct(patches.shape, low),
        jax.ShapeDtypeStruct((2, 2) + grads.shape[1:], low),
    ]
    sem = pltpu.SemaphoreType.DMA
    gathered = pl.pallas_call(
        partial(gather_kernel, items, count),
        out_shape=shapes,
        in_specs=[pl.BlockSpec(memory_space=pl.ANY)] * (count + 2),
        out_specs=[pl.BlockSpec(memory_space=pl.ANY)] * (count + 2),
        scratch_shapes=[
            sem((len(items),)),
            sem((len(items), 3)),
            sem((len(items), 3)),
            sem((len(items), 3)),
            sem((len(items), 3)),
            sem((6,)),
            sem((6,)),
        ],
        compiler_params=pltpu.CompilerParams(collective_id=number, has_side_effects=True),
    )(*arrays, patches, grads)
    return [
        g.reshape(a.shape[:-2] + (2, 16 * a.shape[-2], a.shape[-1]))
        for g, a in zip(gathered, arrays)
    ] + list(gathered[count:])


def plane_kernel(source, target, own_sem, send_sem, recv_sem):
    x, z, y, c = position()
    here = y * 4 + c * 2 + x
    copies = []
    for flip in range(1, 8):
        there_y = 1 - y if flip & 4 else y
        there_c = 1 - c if flip & 2 else c
        there_x = 1 - x if flip & 1 else x
        there = there_y * 4 + there_c * 2 + there_x
        copies.append(
            remote(
                source.at[there],
                target.at[here],
                send_sem.at[flip],
                recv_sem.at[flip],
                (z * 4 + there_y * 2 + there_c, there_x),
            )
        )
    keep = pltpu.make_async_copy(source.at[here], target.at[here], own_sem)
    keep.start()
    barrier = pltpu.get_barrier_semaphore()
    for flip in range(1, 8):
        there_y = 1 - y if flip & 4 else y
        there_c = 1 - c if flip & 2 else c
        there_x = 1 - x if flip & 1 else x
        pl.semaphore_signal(
            barrier,
            inc=1,
            device_id=(z * 4 + there_y * 2 + there_c, there_x),
            device_id_type=MESH,
        )
    pl.semaphore_wait(barrier, 7)
    for copy in copies:
        copy.start()
    keep.wait()
    for copy in copies:
        copy.wait()


def exchange(values, number):
    sem = pltpu.SemaphoreType.DMA
    return pl.pallas_call(
        plane_kernel,
        out_shape=jax.ShapeDtypeStruct(values.shape, values.dtype),
        in_specs=[pl.BlockSpec(memory_space=pl.ANY)],
        out_specs=pl.BlockSpec(memory_space=pl.ANY),
        scratch_shapes=[sem, sem((8,)), sem((8,))],
        compiler_params=pltpu.CompilerParams(collective_id=number, has_side_effects=True),
    )(values)


def reduce_kernel(chunks, count, *refs):
    ins, value_in, grad_in = refs[:count], refs[count], refs[count + 1]
    out, value_out, grad_out = refs[count + 2 : count + 5]
    mine, other, first_a, first_b, second, third = refs[count + 5 : count + 11]
    own_sem, core_send, core_recv, hop_send, hop_recv, line_send, line_recv = refs[
        count + 11 : count + 18
    ]
    value_send, value_recv, grad_send, grad_recv = refs[count + 18 :]
    x, z, y, c = position()
    across, line = partners(x, z, y, c)
    own = (z * 4 + y * 2 + c, x)
    sources = [block_of(z, y, row) for row in range(4)]
    meet(list(across.values()) + line, sources, own)
    letters = []
    for part in range(2):
        for side in range(2):
            device = sector_of(z, y, c, x, part, side)
            at = 2 * part + side
            letters.append(
                (value_in.at[side, part], value_out.at[z], value_send.at[at], value_recv.at[z])
                + (device, own)
            )
            letters.append(
                (grad_in.at[part], grad_out.at[z], grad_send.at[at], grad_recv.at[z])
                + (device, own)
            )
    for letter in letters:
        post(*letter)
    total = len(chunks)

    def plan(k):
        keep, core = [], []
        for side in range(2):
            index, lead, offset = chunks[k][side]
            source = ins[index] if lead is None else ins[index].at[lead]
            span = pl.ds(offset, CHUNK)
            keep.append(
                pltpu.make_async_copy(
                    source.at[:, :, c, :, span], mine.at[2 * k + side], own_sem.at[k, side]
                )
            )
            core.append(
                remote(
                    source.at[:, :, 1 - c, :, span],
                    other.at[2 * k + side],
                    core_send.at[k, side],
                    core_recv.at[k, side],
                    across["c"],
                )
            )
        if k % 2 == 0:
            one, axis_one = (mine.at[2 * k + 1 - x], first_a.at[k // 2]), "x"
            two, axis_two = mine.at[2 * k + x, :, 1 - y], "y"
        else:
            one, axis_one = (mine.at[pl.ds(2 * k, 2), :, 1 - y], first_b.at[k // 2]), "y"
            two, axis_two = mine.at[2 * k + 1 - x, :, y], "x"
        hops = [
            remote(one[0], one[1], hop_send.at[k, 0], hop_recv.at[k, 0], across[axis_one]),
            remote(two, second.at[k], hop_send.at[k, 1], hop_recv.at[k, 1], across[axis_two]),
        ]
        along = [
            remote(
                mine.at[2 * k + x, lax.rem(z + d + 1, 4), y],
                third.at[k, d],
                line_send.at[k, d],
                line_recv.at[k, d],
                line[d],
            )
            for d in range(3)
        ]
        return keep, core, hops, along

    plans = [plan(k) for k in range(total)]

    def joined(left, right):
        return (left.astype(wide) + right.astype(wide)).astype(low)

    def add_core(k):
        def body(step, carry):
            side, row = lax.div(step, 4), lax.rem(step, 4)
            for line_y in range(2):
                mine[2 * k + side, row, line_y] = joined(
                    mine[2 * k + side, row, line_y], other[2 * k + side, row, line_y]
                )
            return carry

        lax.fori_loop(0, 8, body, 0)

    def add_first(k):
        def body(row, carry):
            for part in range(2):
                if k % 2 == 0:
                    mine[2 * k + x, row, part] = joined(
                        mine[2 * k + x, row, part], first_a[k // 2, row, part]
                    )
                else:
                    mine[2 * k + part, row, y] = joined(
                        mine[2 * k + part, row, y], first_b[k // 2, part, row]
                    )
            return carry

        lax.fori_loop(0, 4, body, 0)

    def add_second(k):
        def body(row, carry):
            mine[2 * k + x, row, y] = joined(mine[2 * k + x, row, y], second[k, row])
            return carry

        lax.fori_loop(0, 4, body, 0)

    def add_third(k):
        result = mine[2 * k + x, z, y].astype(wide)
        for d in range(3):
            result = result + third[k, d].astype(wide)
        out[:, pl.ds(k * CHUNK, CHUNK)] = result

    for step in range(total + 8):
        if step < total:
            keep, core, _, _ = plans[step]
            for copy in core + keep:
                copy.start()
        if 0 <= step - 2 < total:
            k = step - 2
            keep, core, hops, _ = plans[k]
            for copy in keep:
                copy.wait()
            for copy in core:
                copy.wait_recv()
            add_core(k)
            hops[0].start()
        if 0 <= step - 4 < total:
            k = step - 4
            hops = plans[k][2]
            hops[0].wait_recv()
            add_first(k)
            hops[1].start()
        if 0 <= step - 6 < total:
            k = step - 6
            plans[k][2][1].wait_recv()
            add_second(k)
            for copy in plans[k][3]:
                copy.start()
        if 0 <= step - 8 < total:
            k = step - 8
            for copy in plans[k][3]:
                copy.wait_recv()
            add_third(k)
    for _, core, hops, along in plans:
        for copy in core + hops + along:
            copy.wait_send()
    for letter in letters:
        settle(*letter)
    for row in range(4):
        pltpu.make_async_copy(value_in.at[0, 0], value_out.at[row], value_recv.at[row]).wait()
        pltpu.make_async_copy(grad_in.at[0], grad_out.at[row], grad_recv.at[row]).wait()


def reduce_all(items, values, grads, number):
    chunks, views = [], []
    for index, item in enumerate(items):
        rows, columns = item.shape[-2:]
        lead = item.shape[:-2]
        item = item.reshape((-1, 4, 2, 2, rows // 16, columns))
        if not lead:
            views.append(item[0])
            for offset in range(0, columns // 2, CHUNK):
                chunks.append(((index, None, offset), (index, None, columns // 2 + offset)))
            continue
        views.append(item)
        for first in range(0, item.shape[0], 2):
            for offset in range(0, columns, CHUNK):
                chunks.append(((index, first, offset), (index, first + 1, offset)))
    rows = views[0].shape[-2]
    count, total = len(views), len(chunks)
    sem = pltpu.SemaphoreType.DMA
    return pl.pallas_call(
        partial(reduce_kernel, chunks, count),
        out_shape=[
            jax.ShapeDtypeStruct((rows, total * CHUNK), wide),
            jax.ShapeDtypeStruct((4,) + values.shape[2:], values.dtype),
            jax.ShapeDtypeStruct((4,) + grads.shape[1:], grads.dtype),
        ],
        in_specs=[pl.BlockSpec(memory_space=pl.ANY)] * (count + 2),
        out_specs=[pl.BlockSpec(memory_space=pltpu.VMEM)]
        + [pl.BlockSpec(memory_space=pl.ANY)] * 2,
        scratch_shapes=[
            pltpu.VMEM((2 * total, 4, 2, rows, CHUNK), low),
            pltpu.VMEM((2 * total, 4, 2, rows, CHUNK), low),
            pltpu.VMEM(((total + 1) // 2, 4, 2, rows, CHUNK), low),
            pltpu.VMEM(((total + 1) // 2, 2, 4, rows, CHUNK), low),
            pltpu.VMEM((total, 4, rows, CHUNK), low),
            pltpu.VMEM((total, 3, rows, CHUNK), low),
            sem((total, 2)),
            sem((total, 2)),
            sem((total, 2)),
            sem((total, 2)),
            sem((total, 2)),
            sem((total, 3)),
            sem((total, 3)),
            sem((4,)),
            sem((4,)),
            sem((4,)),
            sem((4,)),
        ],
        compiler_params=pltpu.CompilerParams(
            collective_id=number, has_side_effects=True, vmem_limit_bytes=60 * 2**20
        ),
    )(*views, values, grads)


def diagonal(var_count, columns):
    column = lax.broadcasted_iota(jnp.int32, (var_count, columns), 1)
    row = lax.broadcasted_iota(jnp.int32, (var_count, columns), 0)
    return (lax.rem(column, var_count) == row) & (column < 5 * var_count)


def patch_kernel(field_ref, lat_ref, shift_ref, patch_ref):
    lat_count, var_count, _ = field_ref.shape
    row_count, lanes = lat_ref.shape
    slots = lanes // 2
    for r in range(row_count):
        lat = lat_ref[r : r + 1, :]
        west = shift_ref[r : r + 1, :] < 0

        def body(b, carry):
            top, bottom = carry
            wide_row = field_ref[b].astype(wide)
            chosen = jnp.where(west, wide_row[:, :lanes], wide_row[:, lanes:])
            return (jnp.where(lat == b, chosen, top), jnp.where(lat == b - 1, chosen, bottom))

        zero = jnp.zeros((var_count, lanes), wide)
        rows = lax.fori_loop(0, lat_count, body, (zero, zero), unroll=4)
        for py in range(2):
            for px in range(2):
                k = 2 * py + px
                patch_ref[r, k * var_count : (k + 1) * var_count, :] = rows[py][
                    :, px * slots : (px + 1) * slots
                ].astype(low)


def cut_patches(field, lat_lanes, shift_lanes):
    row_count, lanes = lat_lanes.shape
    return pl.pallas_call(
        patch_kernel,
        out_shape=jax.ShapeDtypeStruct((row_count, 4 * field.shape[1], lanes // 2), low),
    )(field, lat_lanes, shift_lanes)


def paste_kernel(grad_ref, lat_ref, shift_ref, field_ref):
    lat_count, var_count, _ = field_ref.shape
    row_count, lanes = lat_ref.shape
    field_ref[...] = jnp.zeros_like(field_ref)
    for r in range(row_count):
        lat = lat_ref[r : r + 1, :]
        west = shift_ref[r : r + 1, :] < 0
        lat_both = jnp.concatenate([lat, lat], axis=1)
        both = []
        for py in range(2):
            k = 2 * py
            grads = jnp.concatenate(
                [
                    grad_ref[r, k * var_count : (k + 1) * var_count, :],
                    grad_ref[r, (k + 1) * var_count : (k + 2) * var_count, :],
                ],
                axis=1,
            )
            left = jnp.where(west, grads, 0.0)
            both.append(jnp.concatenate([left, grads - left], axis=1))

        def body(b, carry):
            field_ref[b] += jnp.where(lat_both == b, both[0], 0.0) + jnp.where(
                lat_both == b - 1, both[1], 0.0
            )
            return carry

        lax.fori_loop(0, lat_count, body, 0)


def paste_patches(grads, lat_lanes, shift_lanes, lat_count):
    return pl.pallas_call(
        paste_kernel,
        out_shape=jax.ShapeDtypeStruct(
            (lat_count, grads.shape[1] // 4, 2 * lat_lanes.shape[1]), wide
        ),
    )(grads, lat_lanes, shift_lanes)


def mixer_forward_kernel(cut_ref, score_ref, value_ref, patch_ref, prob_ref, mixed_ref):
    head_count, var_count, tokens = prob_ref.shape
    parts, taps, width = cut_ref.shape
    for part in range(parts):
        patch_ref[:taps, part * width : (part + 1) * width] = cut_ref[part]
    patch_ref[taps : taps + var_count, :] = jnp.ones((var_count, tokens), low)
    rest = patch_ref.shape[0] - 5 * var_count
    patch_ref[5 * var_count :, :] = jnp.zeros((rest, tokens), low)
    mask = diagonal(var_count, patch_ref.shape[0])

    def head_step(h, carry):
        spread = jnp.where(mask, score_ref[pl.ds(h, 1), :], 0.0)
        upper = spread.astype(low)
        lower = (spread - upper.astype(wide)).astype(low)
        patch = patch_ref[...]
        scores = dot(upper, patch) + dot(lower, patch)
        raised = jnp.exp(scores - jnp.max(scores, axis=0, keepdims=True))
        prob = raised / jnp.sum(raised, axis=0, keepdims=True)
        prob_ref[h] = prob
        pooled = jnp.concatenate(
            [
                (prob * patch_ref[k * var_count : (k + 1) * var_count, :].astype(wide)).astype(low)
                for k in range(5)
            ]
            + [jnp.zeros((rest, tokens), low)],
            axis=0,
        )
        start = pl.multiple_of(h * HEAD_DIM, HEAD_DIM)
        mixed_ref[pl.ds(start, HEAD_DIM), :] = dot(
            value_ref[pl.ds(start, HEAD_DIM), :], pooled
        ).astype(low)
        return carry

    lax.fori_loop(0, head_count, head_step, 0)


def mixer_forward(cut, score_table, value_table):
    head_count, padded = score_table.shape
    var_count = cut.shape[1] // 4
    tokens = cut.shape[0] * cut.shape[2]
    return pl.pallas_call(
        mixer_forward_kernel,
        out_shape=[
            jax.ShapeDtypeStruct((padded, tokens), low),
            jax.ShapeDtypeStruct((head_count, var_count, tokens), wide),
            jax.ShapeDtypeStruct((head_count * HEAD_DIM, tokens), low),
        ],
        compiler_params=pltpu.CompilerParams(vmem_limit_bytes=40 * 2**20),
    )(cut, score_table, value_table)


def mixer_backward_kernel(
    patch_ref,
    prob_ref,
    score_ref,
    value_ref,
    grad_ref,
    pooled_ref,
    count_ref,
    cut_ref,
    patch_grad_ref,
):
    head_count, var_count, _ = prob_ref.shape
    padded, tokens = patch_ref.shape
    rest = padded - 5 * var_count
    mask = diagonal(var_count, padded)
    patch_grad_ref[...] = jnp.zeros_like(patch_grad_ref)

    def head_step(h, carry):
        start = pl.multiple_of(h * HEAD_DIM, HEAD_DIM)
        grads = grad_ref[pl.ds(start, HEAD_DIM), :]
        prob = prob_ref[h]
        back = dot(value_ref[pl.ds(start, HEAD_DIM), :], grads, 0, 0)
        pieces = [patch_ref[k * var_count : (k + 1) * var_count, :].astype(wide) for k in range(5)]
        backs = [back[k * var_count : (k + 1) * var_count, :] for k in range(5)]
        prob_grad = pieces[0] * backs[0]
        for k in range(1, 5):
            prob_grad = prob_grad + pieces[k] * backs[k]
        mean = jnp.sum(prob * prob_grad, axis=0, keepdims=True)
        delta = prob * (prob_grad - mean)
        upper = delta.astype(low)
        lower = (delta - upper.astype(wide)).astype(low)
        spread = jnp.where(mask, score_ref[pl.ds(h, 1), :], 0.0).astype(low)
        patch_grad_ref[...] += dot(spread, upper, 0, 0)
        for k in range(4):
            patch_grad_ref[k * var_count : (k + 1) * var_count, :] += prob * backs[k]
        patch = patch_ref[...]
        counts = dot(upper, patch, 1, 1) + dot(lower, patch, 1, 1)
        count_ref[pl.ds(h, 1), :] = jnp.sum(jnp.where(mask, counts, 0.0), axis=0, keepdims=True)
        pooled = jnp.concatenate(
            [(prob * piece).astype(low) for piece in pieces] + [jnp.zeros((rest, tokens), low)],
            axis=0,
        )
        pooled_ref[pl.ds(start, HEAD_DIM), :] = dot(grads, pooled, 1, 1)
        return carry

    lax.fori_loop(0, head_count, head_step, 0)
    parts, taps, width = cut_ref.shape
    for part in range(parts):
        cut_ref[part] = patch_grad_ref[:taps, part * width : (part + 1) * width]


def mixer_backward(patches, probs, score_table, value_table, mixed_grads):
    head_count, padded = score_table.shape
    var_count = probs.shape[1]
    tokens = patches.shape[1]
    return pl.pallas_call(
        mixer_backward_kernel,
        out_shape=[
            jax.ShapeDtypeStruct((head_count * HEAD_DIM, padded), wide),
            jax.ShapeDtypeStruct((head_count, padded), wide),
            jax.ShapeDtypeStruct((2, 4 * var_count, tokens // 2), wide),
        ],
        scratch_shapes=[pltpu.VMEM((padded, tokens), wide)],
        compiler_params=pltpu.CompilerParams(vmem_limit_bytes=40 * 2**20),
    )(patches, probs, score_table, value_table, mixed_grads)


def head_lanes(values, h):
    lane = lax.broadcasted_iota(jnp.int32, values.shape, values.ndim - 1)
    inside = lane < HEAD_DIM if h == 0 else lane >= HEAD_DIM
    return jnp.where(inside, values, jnp.zeros_like(values))


def attention_forward_kernel(joint_ref, tag_ref, crop_ref, low_ref, wide_ref, total_ref):
    blocks, _, share, lanes = joint_ref.shape
    count = low_ref.shape[0]
    step = pl.program_id(0)
    queries = joint_ref[pl.ds(step * count, count), 0].reshape(count * share, lanes)
    keys = joint_ref[:, 1].reshape(blocks * share, lanes)
    values = joint_ref[:, 2].reshape(blocks * share, lanes)
    allowed = crop_ref[...] == tag_ref[...]
    result = None
    for h in range(2):
        scores = dot(head_lanes(queries, h), keys, 1, 1)
        scores = jnp.where(allowed, scores, masked_score)
        largest = jnp.max(scores, axis=1, keepdims=True)
        weights = jnp.exp(scores - largest)
        total = jnp.sum(weights, axis=1, keepdims=True)
        weights = (weights * (1.0 / total)).astype(low)
        part = head_lanes(dot(weights, values), h)
        result = part if result is None else result + part
        total_ref[h] = largest + jnp.log(total)
    wide_ref[...] = result
    low_ref[...] = result.astype(low).reshape(low_ref.shape)


def attention_forward(joint, tags, crops, steps):
    blocks, _, share, lanes = joint.shape
    slots = blocks * share
    width = slots // steps
    return pl.pallas_call(
        attention_forward_kernel,
        grid=(steps,),
        out_shape=[
            jax.ShapeDtypeStruct((blocks, share, lanes), low),
            jax.ShapeDtypeStruct((slots, lanes), wide),
            jax.ShapeDtypeStruct((2, slots, 1), wide),
        ],
        in_specs=[
            pl.BlockSpec(joint.shape, lambda i: (0, 0, 0, 0)),
            pl.BlockSpec((1, slots), lambda i: (0, 0)),
            pl.BlockSpec((width, 1), lambda i: (i, 0)),
        ],
        out_specs=[
            pl.BlockSpec((blocks // steps, share, lanes), lambda i: (i, 0, 0)),
            pl.BlockSpec((width, lanes), lambda i: (i, 0)),
            pl.BlockSpec((2, width, 1), lambda i: (0, i, 0)),
        ],
        compiler_params=pltpu.CompilerParams(vmem_limit_bytes=50 * 2**20),
    )(joint, tags, crops)


def attention_backward_kernel(
    joint_ref, tag_ref, crop_ref, grad_ref, out_ref, total_ref, result_ref, key_acc, value_acc
):
    blocks, _, share, lanes = joint_ref.shape
    count = grad_ref.shape[0]
    step = pl.program_id(0)
    queries = joint_ref[pl.ds(step * count, count), 0].reshape(count * share, lanes)
    keys = joint_ref[:, 1].reshape(blocks * share, lanes)
    values = joint_ref[:, 2].reshape(blocks * share, lanes)
    grads = grad_ref[...].reshape(count * share, lanes)
    product = grads.astype(wide) * out_ref[...]
    allowed = crop_ref[...] == tag_ref[...]
    scale = HEAD_DIM ** (-0.5)

    @pl.when(step == 0)
    def _():
        key_acc[...] = jnp.zeros_like(key_acc)
        value_acc[...] = jnp.zeros_like(value_acc)

    query_grad = None
    for h in range(2):
        query_part, grad_part = head_lanes(queries, h), head_lanes(grads, h)
        scores = jnp.where(allowed, dot(query_part, keys, 1, 1), masked_score)
        weights = jnp.exp(scores - total_ref[h])
        weight_grads = dot(grad_part, values, 1, 1)
        delta = jnp.sum(head_lanes(product, h), axis=1, keepdims=True)
        score_grads = (weights * (weight_grads - delta)).astype(low)
        weights = weights.astype(low)
        value_acc[...] += dot(grad_part, weights, 0, 0)
        key_acc[...] += dot(query_part, score_grads, 0, 0)
        part = head_lanes(dot(score_grads, keys), h)
        query_grad = part if query_grad is None else query_grad + part
    result_ref[pl.ds(step * count, count), 0] = (
        (query_grad * scale).astype(low).reshape(count, share, lanes)
    )

    @pl.when(step == pl.num_programs(0) - 1)
    def _():
        shape = (blocks, share, lanes)
        result_ref[:, 1] = key_acc[...].T.astype(low).reshape(shape)
        result_ref[:, 2] = value_acc[...].T.astype(low).reshape(shape)


def attention_backward(joint, tags, crops, grads, outputs, totals, steps):
    blocks, _, share, lanes = joint.shape
    slots = blocks * share
    width = slots // steps
    return pl.pallas_call(
        attention_backward_kernel,
        grid=(steps,),
        out_shape=jax.ShapeDtypeStruct(joint.shape, low),
        in_specs=[
            pl.BlockSpec(joint.shape, lambda i: (0, 0, 0, 0)),
            pl.BlockSpec((1, slots), lambda i: (0, 0)),
            pl.BlockSpec((width, 1), lambda i: (i, 0)),
            pl.BlockSpec((blocks // steps, share, lanes), lambda i: (i, 0, 0)),
            pl.BlockSpec((width, lanes), lambda i: (i, 0)),
            pl.BlockSpec((2, width, 1), lambda i: (0, i, 0)),
        ],
        out_specs=pl.BlockSpec(joint.shape, lambda i: (0, 0, 0, 0)),
        scratch_shapes=[pltpu.VMEM((lanes, slots), wide), pltpu.VMEM((lanes, slots), wide)],
        compiler_params=pltpu.CompilerParams(vmem_limit_bytes=56 * 2**20),
    )(joint, tags, crops, grads, outputs, totals)


def whole(array):
    rank = len(array.shape)
    return pl.BlockSpec(array.shape, lambda *_: (0,) * rank)


def norm_parts(values):
    center = values - jnp.mean(values, axis=-1, keepdims=True)
    inverse = lax.rsqrt(jnp.mean(center * center, axis=-1, keepdims=True) + epsilon)
    return center * inverse, inverse


def norm_back(values, gain, grads):
    normed, inverse = norm_parts(values)
    scaled = grads * gain
    inner = (
        scaled
        - jnp.mean(scaled, axis=-1, keepdims=True)
        - normed * jnp.mean(scaled * normed, axis=-1, keepdims=True)
    )
    return (
        inner * inverse,
        jnp.sum(grads * normed, axis=0, keepdims=True),
        jnp.sum(grads, axis=0, keepdims=True),
    )


def project_kernel(mixed_ref, back_ref, lead_ref, vector_ref, weight_ref, start_ref, low_ref, out_ref):
    step = pl.program_id(0)
    halves, _, half_width = back_ref.shape
    row_count, _, _, share, lanes = out_ref.shape

    @pl.when(step == 0)
    def _():
        total = lead_ref[...] * vector_ref[0:1] + vector_ref[1:2]
        mixed = mixed_ref[...].T
        for side in range(halves):
            total = total + dot(
                mixed[:, side * half_width : (side + 1) * half_width], back_ref[side], 1, 1
            )
        start_ref[...] = total
        normed, _ = norm_parts(total)
        low_ref[...] = (normed * vector_ref[2:3] + vector_ref[3:4]).astype(low)

    kind, side = lax.div(step, halves), lax.rem(step, halves)
    result = dot(low_ref[...], weight_ref[...].reshape(weight_ref.shape[2:])).astype(low)
    result = result * jnp.where(kind == 0, HEAD_DIM ** (-0.5), 1.0).astype(low)
    pairs = half_width // lanes
    for pair in range(pairs):
        out_ref[:, side * pairs + pair, kind] = result[
            :, pair * lanes : (pair + 1) * lanes
        ].reshape(row_count, share, lanes)


def project(mixed, back_weight, lead_column, vectors, weights, row_count):
    model, tokens = mixed.shape
    kinds, halves, _, half_width = weights.shape
    return pl.pallas_call(
        project_kernel,
        grid=(kinds * halves,),
        out_shape=[
            jax.ShapeDtypeStruct((tokens, model), wide),
            jax.ShapeDtypeStruct((tokens, model), low),
            jax.ShapeDtypeStruct(
                (row_count, halves * half_width // 128, kinds, tokens // row_count, 128), low
            ),
        ],
        in_specs=[
            whole(mixed),
            whole(back_weight),
            whole(lead_column),
            whole(vectors),
            pl.BlockSpec((1, 1, model, half_width), lambda i: (i // halves, i % halves, 0, 0)),
        ],
        out_specs=[
            pl.BlockSpec((tokens, model), lambda i: (0, 0)),
            pl.BlockSpec((tokens, model), lambda i: (0, 0)),
            pl.BlockSpec(
                (row_count, halves * half_width // 128, kinds, tokens // row_count, 128),
                lambda i: (0, 0, 0, 0, 0),
            ),
        ],
        compiler_params=pltpu.CompilerParams(vmem_limit_bytes=40 * 2**20),
    )(mixed, back_weight, lead_column, vectors, weights)


def feed_kernel(
    attended_ref,
    proj_ref,
    start_ref,
    vector_ref,
    up_ref,
    down_ref,
    bias_ref,
    final_ref,
    masked_ref,
    keep_ref,
    predicted_ref,
    middle_grad_ref,
    unit_ref,
    grad_up_ref,
    grad_down_ref,
    grad_proj_ref,
    grad_final_ref,
    grad_bias_ref,
    grad_vector_ref,
    flat,
    middle,
    second,
    second_turned,
    active,
    slope,
    total,
    grad_low,
    grad_turned,
    grad_final,
):
    step = pl.program_id(0)
    count = active.shape[0]
    row_count, units, share, lanes = attended_ref.shape
    halves, _, half_width = proj_ref.shape
    tokens = row_count * share

    @pl.when(step == 0)
    def _():
        for unit in range(units):
            flat[:, unit * lanes : (unit + 1) * lanes] = attended_ref[:, unit].reshape(
                tokens, lanes
            )
        result = start_ref[...]
        for side in range(halves):
            result = result + dot(
                flat[:, side * half_width : (side + 1) * half_width], proj_ref[side], 1, 1
            )
        middle[...] = result
        normed, _ = norm_parts(result)
        normed = (normed * vector_ref[4:5] + vector_ref[5:6]).astype(low)
        second[...] = normed
        second_turned[...] = normed.T
        total[...] = result

    @pl.when(step < count)
    def _():
        hidden = dot(second[...], up_ref[0]) + bias_ref[...]
        share_of = 0.5 * (1.0 + lax.erf(hidden * (0.5**0.5)))
        fired = (hidden * share_of).astype(low)
        active[step] = fired
        slope[step] = share_of + hidden * jnp.exp(-0.5 * hidden * hidden) * (
            0.5 / 1.2533141373155003
        )
        total[...] += dot(fired, down_ref[0], 1, 1)

    @pl.when(step == count - 1)
    def _():
        final_low = total[...].astype(low)
        final_turned = final_low.T
        grads = None
        for side in range(halves):
            predicted_ref[side] = (dot(final_low, final_ref[side]) * keep_ref[...]).astype(low)
            part = dot(masked_ref[side], final_ref[side], 1, 1)
            grads = part if grads is None else grads + part
            grad_final_ref[side] = dot(final_turned, masked_ref[side]).astype(low)
        grad_final[...] = grads
        grad_low[...] = grads.astype(low)
        grad_turned[...] = grads.astype(low).T
        total[...] = jnp.zeros_like(total)

    @pl.when(step >= count)
    def _():
        block = step - count
        hidden_grad = dot(grad_low[...], down_ref[0]) * slope[block]
        hidden_low = hidden_grad.astype(low)
        grad_bias_ref[...] = jnp.sum(hidden_low.astype(wide), axis=0, keepdims=True)
        total[...] += dot(hidden_low, up_ref[0], 1, 1)
        grad_down_ref[0] = dot(grad_turned[...], active[block]).astype(low)
        grad_up_ref[0] = dot(second_turned[...], hidden_low).astype(low)

    @pl.when(step == 2 * count - 1)
    def _():
        part, grad_gain, grad_shift = norm_back(middle[...], vector_ref[4:5], total[...])
        result = grad_final[...] + part
        middle_grad_ref[...] = result
        grad_vector_ref[0:1] = grad_gain
        grad_vector_ref[1:2] = grad_shift
        result_low = result.astype(low)
        result_turned = result_low.T
        pairs = half_width // lanes
        for side in range(halves):
            span = slice(side * half_width, (side + 1) * half_width)
            grad_proj_ref[side] = dot(result_turned, flat[:, span]).astype(low)
            out = dot(result_low, proj_ref[side]).astype(low)
            for pair in range(pairs):
                unit_ref[:, side * pairs + pair] = out[
                    :, pair * lanes : (pair + 1) * lanes
                ].reshape(row_count, share, lanes)


def feed(attended, proj, start, vectors, up_weight, down_weight, up_bias, final_weight, masked, keep):
    halves, model, full = up_weight.shape
    half_width = proj.shape[2]
    tokens = start.shape[0]
    block = 512
    each = full // block
    count = halves * each

    def block_at(i):
        j = lax.rem(i, count)
        return (lax.div(j, each), 0, lax.rem(j, each))

    def late_block(i):
        j = lax.max(i - count, 0)
        return (lax.div(j, each), 0, lax.rem(j, each))

    def fixed(shape, dtype):
        rank = len(shape)
        return jax.ShapeDtypeStruct(shape, dtype), pl.BlockSpec(shape, lambda i: (0,) * rank)

    outs = [
        fixed((halves, tokens, 128), low),
        fixed((tokens, model), wide),
        fixed(attended.shape, low),
        (
            jax.ShapeDtypeStruct(up_weight.shape, low),
            pl.BlockSpec((1, model, block), late_block),
        ),
        (
            jax.ShapeDtypeStruct(up_weight.shape, low),
            pl.BlockSpec((1, model, block), late_block),
        ),
        fixed((halves, model, half_width), low),
        fixed((halves, model, 128), low),
        (
            jax.ShapeDtypeStruct((1, halves * full), wide),
            pl.BlockSpec((1, block), lambda i: (0, lax.max(i - count, 0))),
        ),
        fixed((2, model), wide),
    ]
    return pl.pallas_call(
        feed_kernel,
        grid=(2 * count,),
        out_shape=[shape for shape, _ in outs],
        in_specs=[
            whole(attended),
            whole(proj),
            whole(start),
            whole(vectors),
            pl.BlockSpec((1, model, block), block_at),
            pl.BlockSpec((1, model, block), block_at),
            pl.BlockSpec((1, block), lambda i: (0, lax.rem(i, count))),
            whole(final_weight),
            whole(masked),
            whole(keep),
        ],
        out_specs=[spec for _, spec in outs],
        scratch_shapes=[
            pltpu.VMEM((tokens, model), low),
            pltpu.VMEM((tokens, model), wide),
            pltpu.VMEM((tokens, model), low),
            pltpu.VMEM((model, tokens), low),
            pltpu.VMEM((count, tokens, block), low),
            pltpu.VMEM((count, tokens, block), wide),
            pltpu.VMEM((tokens, model), wide),
            pltpu.VMEM((tokens, model), low),
            pltpu.VMEM((model, tokens), low),
            pltpu.VMEM((tokens, model), wide),
        ],
        compiler_params=pltpu.CompilerParams(vmem_limit_bytes=56 * 2**20),
    )(attended, proj, start, vectors, up_weight, down_weight, up_bias, final_weight, masked, keep)


def return_kernel(
    grads_ref,
    weight_ref,
    low_ref,
    start_ref,
    middle_grad_ref,
    vector_ref,
    lead_ref,
    back_ref,
    mixed_ref,
    grad_input_ref,
    grad_mixer_ref,
    mixed_grad_ref,
    grad_vector_ref,
    turned,
    total,
):
    step = pl.program_id(0)
    halves, _, half_width = back_ref.shape
    row_count, _, _, share, lanes = grads_ref.shape
    tokens = row_count * share
    pairs = half_width // lanes

    @pl.when(step == 0)
    def _():
        turned[...] = low_ref[...].T
        total[...] = jnp.zeros_like(total)

    kind, side = lax.div(step, halves), lax.rem(step, halves)
    piece = jnp.concatenate(
        [grads_ref[:, side * pairs + pair, kind].reshape(tokens, lanes) for pair in range(pairs)],
        axis=1,
    )
    total[...] += dot(piece, weight_ref[0, 0], 1, 1)
    grad_input_ref[0, 0] = dot(turned[...], piece).astype(low)

    @pl.when(step == pl.num_programs(0) - 1)
    def _():
        part, grad_gain, grad_shift = norm_back(start_ref[...], vector_ref[2:3], total[...])
        result = middle_grad_ref[...] + part
        grad_vector_ref[0:1] = jnp.sum(result * lead_ref[...], axis=0, keepdims=True)
        grad_vector_ref[1:2] = jnp.sum(result, axis=0, keepdims=True)
        grad_vector_ref[2:3] = grad_gain
        grad_vector_ref[3:4] = grad_shift
        result_low = result.astype(low)
        result_turned = result_low.T
        for half in range(halves):
            span = slice(half * half_width, (half + 1) * half_width)
            grad_mixer_ref[half] = dot(result_turned, mixed_ref[span, :], 1, 1).astype(low)
            mixed_grad_ref[span, :] = dot(result_low, back_ref[half]).astype(low).T


def go_back(grads, weights, first_low, start, middle_grad, vectors, lead_column, back_weight, mixed):
    kinds, halves, model, half_width = weights.shape
    tokens = start.shape[0]
    block = pl.BlockSpec((1, 1, model, half_width), lambda i: (i // halves, i % halves, 0, 0))
    return pl.pallas_call(
        return_kernel,
        grid=(kinds * halves,),
        out_shape=[
            jax.ShapeDtypeStruct(weights.shape, low),
            jax.ShapeDtypeStruct((halves, model, half_width), low),
            jax.ShapeDtypeStruct((model, tokens), low),
            jax.ShapeDtypeStruct((4, model), wide),
        ],
        in_specs=[
            whole(grads),
            block,
            whole(first_low),
            whole(start),
            whole(middle_grad),
            whole(vectors),
            whole(lead_column),
            whole(back_weight),
            whole(mixed),
        ],
        out_specs=[
            block,
            pl.BlockSpec((halves, model, half_width), lambda i: (0, 0, 0)),
            pl.BlockSpec((model, tokens), lambda i: (0, 0)),
            pl.BlockSpec((4, model), lambda i: (0, 0)),
        ],
        scratch_shapes=[pltpu.VMEM((model, tokens), low), pltpu.VMEM((tokens, model), wide)],
        compiler_params=pltpu.CompilerParams(vmem_limit_bytes=50 * 2**20),
    )(grads, weights, first_low, start, middle_grad, vectors, lead_column, back_weight, mixed)


def einsum(spec, left, right):
    return jnp.einsum(spec, left, right, preferred_element_type=wide)


def fast_local(
    pixels,
    crop_starts,
    crop_shifts,
    slot_crops,
    occupied,
    lead_hours,
    patch_weight,
    variable_embed,
    mixer_query,
    mixer_keys,
    mixer_values,
    mixer_output,
    lead_embed,
    first_gain,
    first_bias,
    attention_in,
    attention_out,
    second_gain,
    second_bias,
    expand_weight,
    expand_bias,
    reduce_weight,
    output_weight,
    cotangent,
):
    lon, head = lax.axis_index(LON), lax.axis_index(HEAD)
    row_count, slot_width = slot_crops.shape
    share = slot_width // HEAD_SIZE
    tokens = row_count * share
    var_count, lat_count, column_count = pixels.shape
    head_half, query_width = mixer_query.shape
    head_count = HEAD_SIZE * head_half
    half_width = head_half * HEAD_DIM
    out_half = output_weight.shape[1]
    slice_width = patch_weight.shape[2]
    model = slice_width * LON_SIZE * HEAD_SIZE
    block_rows = model // LON_SIZE
    taps = 4 * var_count
    pairs = half_width // 128
    scale = HEAD_DIM ** (-0.5)

    last = lax.slice_in_dim(pixels, column_count - 1, column_count, axis=2)
    up = [(i, (i + 1) % LON_SIZE) for i in range(LON_SIZE)]
    down = [(j, i) for i, j in up]
    before = lax.ppermute(last, LON, up)
    after = lax.ppermute(pixels[:, :, :1], LON, down)
    lat_slot = crop_lookup(crop_starts, slot_crops)
    shift_slot = crop_lookup(crop_shifts, slot_crops)
    lat_lanes = jnp.tile(lat_slot, (1, 2))
    shift_lanes = jnp.tile(shift_slot, (1, 2))
    wanted = jnp.arange(2 * 2 * slot_width)
    side, wanted = wanted // (2 * slot_width), wanted % (2 * slot_width)
    wanted = 2 * (wanted % slot_width) + 2 * side + wanted // slot_width - 1
    select = (jnp.arange(column_count)[:, None] == wanted[None, :]).astype(low)
    field = einsum("vac,cn->avn", pixels, select)
    field = field + jnp.where(wanted == -1, jnp.transpose(before, (1, 0, 2)).astype(wide), 0.0)
    field = field + jnp.where(
        wanted == column_count, jnp.transpose(after, (1, 0, 2)).astype(wide), 0.0
    )
    field = field.astype(low)
    pair_rows = row_count // HEAD_SIZE
    cut = cut_patches(
        field,
        block_slice(lat_lanes, head, pair_rows, 0),
        block_slice(shift_lanes, head, pair_rows, 0),
    )
    masked = cotangent * occupied[:, :, None].astype(low)
    masked = jnp.pad(masked, ((0, 0), (0, 0), (0, 128 - out_half)))
    my_crops = block_slice(slot_crops, head, share, 1)
    my_occupied = block_slice(occupied, head, share, 1)

    around = (HEAD, LON)
    up_weight = lax.all_gather(expand_weight, around, axis=0, tiled=True)
    up_weight = up_weight.reshape(HEAD_SIZE, model, -1)
    down_weight = lax.all_gather(reduce_weight.T, around, axis=0, tiled=True)
    down_weight = down_weight.reshape(HEAD_SIZE, model, -1)
    padded = 256
    small = jnp.concatenate(
        [
            jnp.transpose(patch_weight, (1, 0, 2)).reshape(taps, slice_width),
            variable_embed,
            lead_embed,
            first_gain[None],
            first_bias[None],
            second_gain[None],
            second_bias[None],
            jnp.zeros((padded - taps - var_count - 6, slice_width), low),
        ]
    ).T
    small = jnp.concatenate([small[:, :128], small[:, 128:]])
    pieces = [
        jnp.where(my_occupied == 1, my_crops, -1).astype(low).reshape(-1),
        my_crops.astype(low).reshape(-1),
        jnp.pad(mixer_query.reshape(-1), (0, 128 - head_half * query_width)),
        expand_bias.reshape(-1),
    ]
    used = sum(piece.shape[0] for piece in pieces)
    misc = jnp.concatenate(pieces + [jnp.zeros((2048 - used,), low)]).reshape(16, 128)
    out_block = jnp.pad(output_weight, ((0, 0), (0, 128 - out_half)))
    (
        misc_all,
        small_all,
        key_weight,
        value_weight,
        mixer_weight,
        input_weight,
        output_proj,
        final_weight,
        cut,
        masked,
    ) = gather_all(
        [
            misc,
            small,
            mixer_keys,
            mixer_values,
            mixer_output.T,
            attention_in,
            attention_out.T,
            out_block,
        ],
        cut,
        masked,
        1,
    )
    masked = masked.reshape(HEAD_SIZE, tokens, 128)
    misc_all = misc_all.reshape(HEAD_SIZE, LON_SIZE, 2048)
    slots_all = jnp.transpose(
        misc_all[:, :, : 2 * row_count * share].reshape(
            HEAD_SIZE, LON_SIZE, 2, row_count, share
        ),
        (2, 3, 1, 0, 4),
    ).reshape(2, row_count, -1)
    my_row = lax.div(lon, LON_SIZE // row_count)
    my_block = lax.rem(lon, LON_SIZE // row_count) * HEAD_SIZE + head
    slots_row = lax.dynamic_index_in_dim(slots_all, my_row, 1, keepdims=False).astype(wide)
    tag_row, crop_column = slots_row[0:1], slots_row[1][:, None]
    my_slots = block_slice(slots_row, my_block, tokens, 1)
    keep_mask = jnp.where(my_slots[0] >= 0.0, 1.0, 0.0)[:, None]
    my_hours = lax.dynamic_index_in_dim(lead_hours, my_row, 0)
    lead_column = crop_lookup(my_hours, my_slots[1:2].astype(jnp.int32)).astype(wide)
    lead_column = lead_column.reshape(tokens, 1) / 100.0
    at = 2 * row_count * share
    query = jnp.transpose(
        misc_all[:, :, at : at + head_half * query_width].reshape(
            HEAD_SIZE, LON_SIZE, head_half, query_width
        ),
        (0, 2, 1, 3),
    ).reshape(head_count, HEAD_DIM)
    query = query.astype(wide)
    at += 128
    bias_rows = expand_bias.shape[0]
    up_bias = jnp.transpose(
        misc_all[:, :, at : at + expand_bias.size].reshape(HEAD_SIZE, LON_SIZE, bias_rows, -1),
        (0, 2, 1, 3),
    ).reshape(HEAD_SIZE, -1)
    up_bias = up_bias.astype(wide)
    patch_full = jnp.transpose(
        small_all.reshape(HEAD_SIZE, LON_SIZE, 2, slice_width, 128), (1, 0, 3, 2, 4)
    ).reshape(model, padded)
    vectors = patch_full[:, taps + var_count : taps + var_count + 6].T.astype(wide)
    patch_full = jnp.where(jnp.arange(padded)[None, :] < taps + var_count, patch_full, 0)

    key_table = einsum("xde,dm->xem", key_weight, patch_full).reshape(model, padded)
    value_table = einsum("xde,dm->xem", value_weight, patch_full).astype(low).reshape(model, padded)
    score_table = (
        jnp.sum(key_table.reshape(head_count, HEAD_DIM, padded) * query[:, :, None], axis=1) * scale
    )

    patches, probs, mixed = mixer_forward(cut, score_table, value_table)
    start_sum, first_low, projected = project(
        mixed, mixer_weight, lead_column, vectors, input_weight, 1
    )
    units = HEAD_SIZE * pairs
    joint = exchange(projected.reshape(units, 3, tokens, 128), 3)
    steps = 8
    attended_unit, attended_wide, totals = attention_forward(joint, tag_row, crop_column, steps)
    attended = exchange(attended_unit, 4)[None]
    (
        predicted,
        middle_grad,
        out_grads,
        grad_up,
        grad_down,
        grad_proj,
        grad_out,
        grad_up_bias,
        second_vectors,
    ) = feed(
        attended,
        output_proj,
        start_sum,
        vectors,
        up_weight,
        down_weight,
        up_bias.reshape(1, -1),
        final_weight,
        masked,
        keep_mask,
    )
    unit_grads = exchange(out_grads.reshape(units, tokens, 128), 5)
    joint_grads = attention_backward(
        joint, tag_row, crop_column, unit_grads, attended_wide, totals, steps
    )
    stacked = exchange(joint_grads, 6)[None]
    grad_input, grad_mixer, mixed_grads, first_vectors = go_back(
        stacked,
        input_weight,
        first_low,
        start_sum,
        middle_grad,
        vectors,
        lead_column,
        mixer_weight,
        mixed,
    )
    pooled_grads, counts, cut_grads = mixer_backward(
        patches, probs, score_table, value_table, mixed_grads
    )
    counts = counts * scale
    pooled_low = pooled_grads.astype(low)
    grad_values = dot(patch_full, pooled_low, 1, 1).astype(low)
    key_low = (query[:, :, None] * counts[:, None, :]).astype(low).reshape(model, padded)
    grad_small = einsum(
        "xde,xem->dm", key_weight, key_low.reshape(HEAD_SIZE, half_width, padded)
    ) + einsum("xde,xem->dm", value_weight, pooled_low.reshape(HEAD_SIZE, half_width, padded))
    head_sums = einsum("dm,hm->dh", patch_full.astype(wide), counts)
    grad_query = jnp.sum(
        key_table.reshape(head_count, HEAD_DIM, padded) * counts[:, None, :], axis=2
    )

    vector_grads = jnp.concatenate([first_vectors, second_vectors]).T
    spot = taps + var_count
    grad_small = jnp.concatenate(
        [grad_small[:, :spot], vector_grads, jnp.zeros((model, padded - spot - 6), wide)], axis=1
    )
    grad_small = jnp.transpose(
        grad_small.reshape(LON_SIZE, HEAD_SIZE, slice_width, 2, 128), (0, 3, 2, 1, 4)
    ).reshape(model, HEAD_SIZE, 128)
    head_block = head_sums.reshape(model, HEAD_SIZE, head_half)
    bias_cols = expand_bias.shape[1]
    bias_block = jnp.transpose(
        grad_up_bias.reshape(HEAD_SIZE, bias_rows, LON_SIZE, bias_cols), (2, 1, 0, 3)
    )
    bias_block = jnp.pad(
        bias_block, ((0, 0), (0, block_rows - bias_rows), (0, 0), (0, 0))
    ).reshape(model, HEAD_SIZE, bias_cols)
    query_block = jnp.transpose(
        grad_query.reshape(HEAD_SIZE, head_half, LON_SIZE, query_width), (2, 1, 0, 3)
    )
    query_block = jnp.pad(
        query_block, ((0, 0), (0, block_rows - head_half), (0, 0), (0, 0))
    ).reshape(model, HEAD_SIZE, query_width)
    extra = head_half + bias_cols + query_width
    filler = jnp.zeros((model, 128 - out_half - extra), wide)
    tail = jnp.stack(
        [
            jnp.concatenate(
                [
                    grad_small[:, side],
                    grad_out[side, :, :out_half].astype(wide),
                    head_block[:, side],
                    bias_block[:, side],
                    query_block[:, side],
                    filler,
                ],
                axis=1,
            )
            for side in range(2)
        ]
    ).astype(low)
    sums, predicted, cut_grads = reduce_all(
        [grad_up, grad_down, grad_proj, grad_input, grad_mixer, grad_values, tail],
        predicted.reshape(HEAD_SIZE, 2, slot_width, 128),
        cut_grads,
        2,
    )
    predicted = predicted[:, :, :out_half]
    full_half = up_weight.shape[2]
    place = [0]

    def take(width):
        begin = place[0]
        place[0] = begin + width
        return sums[:, begin : begin + width]

    out_up = take(full_half)
    out_down = take(full_half).T
    out_proj = take(half_width).T
    out_input = jnp.stack([take(half_width) for _ in range(3)])
    out_mixer = take(half_width).T
    out_values = take(half_width)
    tail_small = take(128)
    tail_rest = take(128)
    tail_small = jnp.concatenate([tail_small[:slice_width], tail_small[slice_width:]], axis=1).T
    out_patch = jnp.transpose(tail_small[:taps].reshape(4, var_count, slice_width), (1, 0, 2))
    out_variable = tail_small[taps:spot]
    out_lead = tail_small[spot : spot + 2]
    out_final = tail_rest[:, :out_half]
    at = out_half
    my_heads = tail_rest[:, at : at + head_half]
    at += head_half
    out_bias = tail_rest[:bias_rows, at : at + bias_cols]
    at += bias_cols
    out_query = tail_rest[:head_half, at : at + query_width]
    my_query = block_slice(query, head, head_half, 0)
    out_keys = (my_heads[:, :, None] * my_query[None]).reshape(block_rows, half_width)

    field_grads = paste_patches(cut_grads, lat_lanes, shift_lanes, lat_count)
    choose = (jnp.arange(column_count + 2)[:, None] - 1 == wanted[None, :]).astype(wide)
    columns = jnp.einsum("avn,cn->vac", field_grads, choose, precision=highest)
    from_west = lax.ppermute(columns[:, :, -1:], LON, up)
    from_east = lax.ppermute(columns[:, :, :1], LON, down)
    spot_at = jnp.arange(column_count)
    pixel_grad = columns[:, :, 1:-1] + jnp.where(spot_at == 0, from_west, 0.0)
    pixel_grad = pixel_grad + jnp.where(spot_at == column_count - 1, from_east, 0.0)
    return (
        predicted,
        pixel_grad,
        out_patch,
        out_variable,
        out_query,
        out_keys,
        out_values,
        out_mixer,
        out_lead,
        tail_small[spot + 2],
        tail_small[spot + 3],
        out_input,
        out_proj,
        tail_small[spot + 4],
        tail_small[spot + 5],
        out_up,
        out_bias,
        out_down,
        out_final,
    )


def solution(mesh):
    body = fast_local if planned(mesh) else local
    placed = (
        P(None, None, LON),
        P(),
        P(),
        P(None, LON),
        P(None, LON),
        P(),
        P(None, None, (LON, HEAD)),
        P(None, (LON, HEAD)),
        P(HEAD, LON),
        P(LON, HEAD),
        P(LON, HEAD),
        P(HEAD, LON),
        P(None, (LON, HEAD)),
        P((LON, HEAD)),
        P((LON, HEAD)),
        P(None, LON, HEAD),
        P(HEAD, LON),
        P((LON, HEAD)),
        P((LON, HEAD)),
        P(LON, HEAD),
        P(HEAD, LON),
        P(HEAD, LON),
        P(LON, HEAD),
        P(None, LON, HEAD),
    )
    return jax.shard_map(
        body,
        mesh=mesh,
        in_specs=placed,
        out_specs=(
            P(None, LON, HEAD),
            P(None, None, LON),
            P(None, None, (LON, HEAD)),
            P(None, (LON, HEAD)),
            P(HEAD, LON),
            P(LON, HEAD),
            P(LON, HEAD),
            P(HEAD, LON),
            P(None, (LON, HEAD)),
            P((LON, HEAD)),
            P((LON, HEAD)),
            P(None, LON, HEAD),
            P(HEAD, LON),
            P((LON, HEAD)),
            P((LON, HEAD)),
            P(LON, HEAD),
            P(HEAD, LON),
            P(HEAD, LON),
            P(LON, HEAD),
        ),
        check_vma=False,
    )
```

```python
from functools import partial

import jax
import jax.numpy as jnp
from jax import lax
from jax.experimental import pallas as pl
from jax.experimental.pallas import tpu as pltpu
from jax.sharding import PartitionSpec as P

HEAD_DIM = 64
LON, HEAD = "lon", "head"


epsilon = 1e-05
masked_score = -1e30
highest = lax.Precision.HIGHEST


def extended(array, sides, width):
    for axis, dim in sides:
        count, length = (lax.axis_size(axis), array.shape[dim])
        up = [(i, (i + 1) % count) for i in range(count)]
        down = [(j, i) for i, j in up]
        last = lax.slice_in_dim(array, length - width, length, axis=dim)
        leading = lax.slice_in_dim(array, 0, width, axis=dim)
        before = lax.ppermute(last, axis, up)
        after = lax.ppermute(leading, axis, down)
        array = jnp.concatenate([before, array, after], axis=dim)
    return array


def layer_norm(values, gain_vector, shift_vector):
    center = values - jnp.mean(values, axis=-1, keepdims=True)
    spread = jnp.mean(center * center, axis=-1, keepdims=True)
    return center * lax.rsqrt(spread + epsilon) * gain_vector + shift_vector


def head_total(partial_sum):
    return lax.psum(partial_sum.astype(jnp.bfloat16), HEAD).astype(jnp.float32)


def head_share(partial_sum):
    return lax.psum_scatter(
        partial_sum.astype(jnp.bfloat16), HEAD, scatter_dimension=0, tiled=True
    ).astype(jnp.float32)


def head_rows(values):
    return lax.all_gather(values, HEAD, axis=0, tiled=True)


def reduce_rows(partial_sum):
    return head_share(partial_sum)


def spread_rows(values):
    return head_rows(values)


def crop_lookup(crop_table, slot_numbers):
    numbers = jnp.arange(crop_table.shape[1], dtype=jnp.int32)
    picked = slot_numbers[:, :, None] == numbers[None, None, :]
    return jnp.sum(jnp.where(picked, crop_table[:, None, :], 0), axis=2)


def outer_sum(left_rows, right_rows):
    return jnp.einsum("ti,tj->ij", left_rows, right_rows, preferred_element_type=jnp.float32)


def block_slice(values, block_index, block_width, axis_number):
    return lax.dynamic_slice_in_dim(values, block_index * block_width, block_width, axis_number)


def block_scores(queries, query_crops, key_block, key_tags):
    scores = jnp.einsum(
        "rqhd,rkhd->rhqk", queries, key_block, preferred_element_type=jnp.float32
    ) * HEAD_DIM ** (-0.5)
    matched = query_crops[:, None, :, None] == key_tags[:, None, None, :]
    return (jnp.where(matched, scores, masked_score), matched)


def key_stats(queries, query_crops, key_rows, key_tags, block_width):
    row_count, slot_count, head_count, head_size = queries.shape

    def key_step(carried, block_index):
        largest, totals = carried
        scores, matched = block_scores(
            queries,
            query_crops,
            block_slice(key_rows, block_index, block_width, 1),
            block_slice(key_tags, block_index, block_width, 1),
        )
        raised = jnp.maximum(largest, jnp.max(scores, axis=-1))
        totals = totals * jnp.exp(largest - raised) + jnp.sum(
            jnp.where(matched, jnp.exp(scores - raised[..., None]), 0.0), axis=-1
        )
        return ((raised, totals), None)

    initial = (
        jnp.full((row_count, head_count, slot_count), masked_score, jnp.float32),
        jnp.zeros((row_count, head_count, slot_count), jnp.float32),
    )
    (largest, totals), _ = lax.scan(key_step, initial, jnp.arange(key_rows.shape[1] // block_width))
    return largest + jnp.log(totals)


def attend(queries, query_crops, key_rows, value_rows, key_tags, log_totals, block_width):

    def attend_step(running, block_index):
        scores, matched = block_scores(
            queries,
            query_crops,
            block_slice(key_rows, block_index, block_width, 1),
            block_slice(key_tags, block_index, block_width, 1),
        )
        weights = jnp.where(matched, jnp.exp(scores - log_totals[..., None]), 0.0).astype(
            jnp.bfloat16
        )
        value_block = block_slice(value_rows, block_index, block_width, 1)
        return (
            running
            + jnp.einsum(
                "rhqk,rkhd->rqhd", weights, value_block, preferred_element_type=jnp.float32
            ),
            None,
        )

    outputs, _ = lax.scan(
        attend_step,
        jnp.zeros(queries.shape, jnp.float32),
        jnp.arange(key_rows.shape[1] // block_width),
    )
    return outputs


def score_grads(
    queries, query_crops, out_grads, log_totals, deltas, key_block, value_block, key_tags
):
    scores, matched = block_scores(queries, query_crops, key_block, key_tags)
    weights = jnp.where(matched, jnp.exp(scores - log_totals[..., None]), 0.0)
    weight_grads = jnp.einsum(
        "rqhd,rkhd->rhqk", out_grads, value_block, preferred_element_type=jnp.float32
    )
    score_delta = (weights * (weight_grads - deltas[..., None])).astype(jnp.bfloat16)
    return (score_delta, weights.astype(jnp.bfloat16))


def mixer_row(patch_row, full_patch, full_variable, pair_weight, head_query):
    embedded = jnp.einsum(
        "svk,vkd->svd", patch_row, full_patch, preferred_element_type=jnp.float32
    ) + full_variable.astype(jnp.float32)
    embedded = embedded.astype(jnp.bfloat16)
    slot_count, var_count, model_width = embedded.shape
    head_count, head_size = head_query.shape
    local_width = head_count * head_size
    paired = jnp.dot(
        embedded.reshape(slot_count * var_count, model_width),
        pair_weight,
        preferred_element_type=jnp.float32,
    ).astype(jnp.bfloat16)
    key_rows = paired[:, :local_width].reshape(slot_count, var_count, head_count, head_size)
    value_rows = paired[:, local_width:].reshape(slot_count, var_count, head_count, head_size)
    scores = jnp.einsum(
        "svhd,hd->shv", key_rows, head_query, preferred_element_type=jnp.float32
    ) * HEAD_DIM ** (-0.5)
    weights = jax.nn.softmax(scores, axis=-1)
    return (embedded, key_rows, value_rows, weights)


def mixer_back(carried, inputs, full_patch, full_variable, pair_weight, head_query):
    patch_row, mixed_grad = inputs
    embedded, key_rows, value_rows, weights = mixer_row(
        patch_row, full_patch, full_variable, pair_weight, head_query
    )
    slot_count, var_count, model_width = embedded.shape
    local_width = key_rows.shape[2] * key_rows.shape[3]
    mixed_wide = mixed_grad.astype(jnp.float32)
    value_grads = jnp.einsum("shv,shd->svhd", weights, mixed_wide, precision=highest).astype(
        jnp.bfloat16
    )
    weight_grads = jnp.einsum(
        "shd,svhd->shv", mixed_wide, value_rows.astype(jnp.float32), precision=highest
    )
    score_delta = (
        weights
        * (weight_grads - jnp.sum(weights * weight_grads, axis=-1, keepdims=True))
        * HEAD_DIM ** (-0.5)
    )
    key_grads = jnp.einsum(
        "shv,hd->svhd", score_delta, head_query.astype(jnp.float32), precision=highest
    ).astype(jnp.bfloat16)
    query_grad = jnp.einsum(
        "shv,svhd->hd", score_delta, key_rows.astype(jnp.float32), precision=highest
    )
    pair_grads = jnp.concatenate(
        [
            key_grads.reshape(slot_count * var_count, local_width),
            value_grads.reshape(slot_count * var_count, local_width),
        ],
        axis=1,
    )
    embed_grad = jnp.einsum(
        "ne,de->nd", pair_grads, pair_weight, preferred_element_type=jnp.float32
    )
    pair_weight_grad = outer_sum(embedded.reshape(slot_count * var_count, model_width), pair_grads)
    embed_grad = embed_grad.reshape(slot_count, var_count, model_width)
    patch_grad = jnp.einsum(
        "svk,svd->vkd", patch_row.astype(jnp.float32), embed_grad, precision=highest
    )
    variable_grad = jnp.sum(embed_grad, axis=0)
    slot_grad = jnp.einsum(
        "svd,vkd->svk", embed_grad, full_patch.astype(jnp.float32), precision=highest
    )
    patch_acc, variable_acc, query_acc, pair_acc = carried
    return (
        (
            patch_acc + patch_grad,
            variable_acc + variable_grad,
            query_acc + query_grad,
            pair_acc + pair_weight_grad,
        ),
        slot_grad,
    )


def local(
    pixels,
    crop_starts,
    crop_shifts,
    slot_crops,
    occupied,
    lead_hours,
    patch_weight,
    variable_embed,
    mixer_query,
    mixer_keys,
    mixer_values,
    mixer_output,
    lead_embed,
    first_gain,
    first_bias,
    attention_in,
    attention_out,
    second_gain,
    second_bias,
    expand_weight,
    expand_bias,
    reduce_weight,
    output_weight,
    cotangent,
):
    shared = (
        lax.all_gather(patch_weight, (LON, HEAD), axis=2, tiled=True),
        lax.all_gather(variable_embed, (LON, HEAD), axis=1, tiled=True),
        lax.all_gather(lead_embed, (LON, HEAD), axis=1, tiled=True),
        lax.all_gather(first_gain, (LON, HEAD), axis=0, tiled=True),
        lax.all_gather(first_bias, (LON, HEAD), axis=0, tiled=True),
        lax.all_gather(second_gain, (LON, HEAD), axis=0, tiled=True),
        lax.all_gather(second_bias, (LON, HEAD), axis=0, tiled=True),
    )
    full_patch, full_variable, full_lead, gain_first, shift_first, gain_second, shift_second = (
        shared
    )
    sector = (
        lax.all_gather(mixer_query, LON, axis=1, tiled=True),
        lax.all_gather(mixer_keys, LON, axis=0, tiled=True),
        lax.all_gather(mixer_values, LON, axis=0, tiled=True),
        lax.all_gather(mixer_output, LON, axis=1, tiled=True),
        lax.all_gather(attention_in, LON, axis=1, tiled=True),
        lax.all_gather(attention_out, LON, axis=1, tiled=True),
        lax.all_gather(expand_weight, LON, axis=0, tiled=True),
        lax.all_gather(expand_bias, LON, axis=1, tiled=True),
        lax.all_gather(reduce_weight, LON, axis=1, tiled=True),
        lax.all_gather(output_weight, LON, axis=0, tiled=True),
    )
    (
        head_query,
        key_weight,
        value_weight,
        mixer_weight,
        input_weight,
        output_proj,
        up_weight,
        up_bias,
        down_weight,
        final_weight,
    ) = sector
    row_count, slot_width = slot_crops.shape
    token_count = row_count * slot_width
    local_width = key_weight.shape[1]
    head_count = local_width // HEAD_DIM
    pair_weight = jnp.concatenate([key_weight, value_weight], axis=1)
    gain_one = gain_first.astype(jnp.float32)
    shift_one = shift_first.astype(jnp.float32)
    gain_two = gain_second.astype(jnp.float32)
    shift_two = shift_second.astype(jnp.float32)
    lat_slot = crop_lookup(crop_starts, slot_crops)
    shift_slot = crop_lookup(crop_shifts, slot_crops)
    lead_slot = crop_lookup(lead_hours, slot_crops).astype(jnp.float32).reshape(token_count) / 100.0
    share_count = token_count // lax.axis_size(HEAD)
    lead_rows = lax.dynamic_slice_in_dim(
        lead_slot, lax.axis_index(HEAD) * share_count, share_count
    )
    padded = extended(pixels, ((LON, 2),), 1)
    var_count, lat_count = (pixels.shape[0], pixels.shape[1])
    west_pairs = padded[:, :, : 2 * slot_width].reshape(var_count, lat_count, slot_width, 2)
    east_pairs = padded[:, :, 2:].reshape(var_count, lat_count, slot_width, 2)
    side_pairs = jnp.stack([west_pairs, east_pairs])
    tables = jnp.stack([side_pairs[:, :, :-1], side_pairs[:, :, 1:]], axis=3)
    lat_index = jnp.arange(lat_count - 1, dtype=jnp.int32)
    side_shift = 2 * jnp.arange(2, dtype=jnp.int32) - 1
    chosen = (lat_slot[:, :, None, None] == lat_index[None, None, None, :]) & (
        shift_slot[:, :, None, None] == side_shift[None, None, :, None]
    )
    patches = jnp.einsum(
        "rjsa,svapjx->rjvpx",
        chosen.astype(jnp.bfloat16),
        tables,
        preferred_element_type=jnp.float32,
    )
    patches = patches.astype(jnp.bfloat16).reshape(row_count, slot_width, var_count, 4)

    def mixer_forward(patch_row):
        embedded, key_rows, value_rows, weights = mixer_row(
            patch_row, full_patch, full_variable, pair_weight, head_query
        )
        return jnp.einsum(
            "shv,svhd->shd", weights, value_rows.astype(jnp.float32), precision=highest
        ).astype(jnp.bfloat16)

    mixed_low = lax.map(mixer_forward, patches).reshape(token_count, local_width)
    start_sum = reduce_rows(jnp.dot(mixed_low, mixer_weight, preferred_element_type=jnp.float32))
    start_sum = (
        start_sum
        + lead_rows[:, None] * full_lead[0].astype(jnp.float32)
        + full_lead[1].astype(jnp.float32)
    )
    first_low = spread_rows(layer_norm(start_sum, gain_one, shift_one).astype(jnp.bfloat16))
    projected = jnp.einsum(
        "td,kde->kte", first_low, input_weight, preferred_element_type=jnp.float32
    ).astype(jnp.bfloat16)
    projected = projected.reshape(3, row_count, slot_width, head_count, HEAD_DIM)
    queries, key_local, value_local = (projected[0], projected[1], projected[2])
    query_crops = slot_crops.astype(jnp.float32)
    key_tags = jnp.where(occupied == 1, slot_crops, -1).astype(jnp.bfloat16)
    key_all, value_all, tag_all = (
        lax.all_gather(key_local, LON, axis=1, tiled=True),
        lax.all_gather(value_local, LON, axis=1, tiled=True),
        lax.all_gather(key_tags, LON, axis=1, tiled=True),
    )
    block_width = min(512, key_all.shape[1])
    tag_wide = tag_all.astype(jnp.float32)
    log_totals = key_stats(queries, query_crops, key_all, tag_wide, block_width)
    attended = attend(queries, query_crops, key_all, value_all, tag_wide, log_totals, block_width)
    attended_low = attended.astype(jnp.bfloat16).reshape(token_count, local_width)
    middle = start_sum + reduce_rows(
        jnp.dot(attended_low, output_proj, preferred_element_type=jnp.float32)
    )
    second_low = spread_rows(layer_norm(middle, gain_two, shift_two).astype(jnp.bfloat16))
    hidden = jnp.dot(second_low, up_weight, preferred_element_type=jnp.float32) + up_bias.reshape(
        -1
    ).astype(jnp.float32)
    active = jax.nn.gelu(hidden, approximate=False).astype(jnp.bfloat16)
    final_sum = middle + reduce_rows(
        jnp.dot(active, down_weight, preferred_element_type=jnp.float32)
    )
    final_low = spread_rows(final_sum.astype(jnp.bfloat16))
    keep_mask = occupied.reshape(token_count, 1)
    predicted = (
        jnp.dot(final_low, final_weight, preferred_element_type=jnp.float32)
        * keep_mask.astype(jnp.float32)
    ).astype(jnp.bfloat16)
    predicted = predicted.reshape(row_count, slot_width, -1)
    masked_grad = (cotangent * occupied[:, :, None].astype(jnp.bfloat16)).reshape(token_count, -1)
    grad_final_weight = outer_sum(final_low, masked_grad)
    part_top = jnp.einsum(
        "to,do->td", masked_grad, final_weight, preferred_element_type=jnp.float32
    )
    final_grad = reduce_rows(part_top)
    final_grad_low = spread_rows(final_grad.astype(jnp.bfloat16))
    grad_down = outer_sum(active, final_grad_low)
    active_grad = jnp.einsum(
        "td,fd->tf", final_grad_low, down_weight, preferred_element_type=jnp.float32
    )
    _, gelu_back = jax.vjp(partial(jax.nn.gelu, approximate=False), hidden)
    hidden_grad = gelu_back(active_grad)[0].astype(jnp.bfloat16)
    grad_up = outer_sum(second_low, hidden_grad)
    grad_up_bias = jnp.sum(hidden_grad.astype(jnp.float32), axis=0).reshape(up_bias.shape)
    second_grad = jnp.einsum(
        "tf,df->td", hidden_grad, up_weight, preferred_element_type=jnp.float32
    )
    second_in = head_share(second_grad)
    _, second_back = jax.vjp(layer_norm, middle, gain_two, shift_two)
    part_mid, grad_gain_two, grad_shift_two = second_back(second_in)
    middle_grad = final_grad + part_mid
    middle_low = spread_rows(middle_grad.astype(jnp.bfloat16))
    grad_proj = outer_sum(attended_low, middle_low)
    out_grads = jnp.einsum(
        "td,ed->te", middle_low, output_proj, preferred_element_type=jnp.float32
    ).astype(jnp.bfloat16)
    out_grads = out_grads.reshape(row_count, slot_width, head_count, HEAD_DIM)
    deltas = jnp.transpose(jnp.sum(out_grads.astype(jnp.float32) * attended, axis=-1), (0, 2, 1))
    back_keys, back_values, back_raw = (
        lax.all_gather(key_local, LON, axis=1, tiled=True),
        lax.all_gather(value_local, LON, axis=1, tiled=True),
        lax.all_gather(key_tags, LON, axis=1, tiled=True),
    )
    back_tags = back_raw.astype(jnp.float32)
    scale = HEAD_DIM ** (-0.5)
    key_count = back_keys.shape[1] // block_width
    local_zeros = jnp.zeros(queries.shape, jnp.float32)
    whole_zeros = jnp.zeros(back_keys.shape, jnp.float32)

    def both_step(running, block_index):
        query_acc, key_acc, value_acc = running
        key_block = block_slice(back_keys, block_index, block_width, 1)
        score_delta, weights_low = score_grads(
            queries,
            query_crops,
            out_grads,
            log_totals,
            deltas,
            key_block,
            block_slice(back_values, block_index, block_width, 1),
            block_slice(back_tags, block_index, block_width, 1),
        )
        query_acc = (
            query_acc
            + jnp.einsum(
                "rhqk,rkhd->rqhd", score_delta, key_block, preferred_element_type=jnp.float32
            )
            * scale
        )
        key_piece = (
            jnp.einsum("rhqk,rqhd->rkhd", score_delta, queries, preferred_element_type=jnp.float32)
            * scale
        )
        value_piece = jnp.einsum(
            "rhqk,rqhd->rkhd", weights_low, out_grads, preferred_element_type=jnp.float32
        )
        key_acc = lax.dynamic_update_slice_in_dim(key_acc, key_piece, block_index * block_width, 1)
        value_acc = lax.dynamic_update_slice_in_dim(
            value_acc, value_piece, block_index * block_width, 1
        )
        return ((query_acc, key_acc, value_acc), None)

    (query_grad, key_part, value_part), _ = lax.scan(
        both_step, (local_zeros, whole_zeros, whole_zeros), jnp.arange(key_count)
    )
    key_grad, value_grad = (
        lax.psum_scatter(
            key_part.astype(jnp.bfloat16), LON, scatter_dimension=1, tiled=True
        ).astype(jnp.float32),
        lax.psum_scatter(
            value_part.astype(jnp.bfloat16), LON, scatter_dimension=1, tiled=True
        ).astype(jnp.float32),
    )
    stacked = (
        jnp.stack([query_grad, key_grad, value_grad])
        .astype(jnp.bfloat16)
        .reshape(3, token_count, local_width)
    )
    first_grad = jnp.einsum(
        "kte,kde->td", stacked, input_weight, preferred_element_type=jnp.float32
    )
    grad_input = jnp.einsum("td,kte->kde", first_low, stacked, preferred_element_type=jnp.float32)
    first_in = head_share(first_grad)
    _, first_back = jax.vjp(layer_norm, start_sum, gain_one, shift_one)
    part_low, grad_gain_one, grad_shift_one = first_back(first_in)
    start_grad = middle_grad + part_low
    grad_lead = jnp.stack(
        [jnp.sum(start_grad * lead_rows[:, None], axis=0), jnp.sum(start_grad, axis=0)]
    )
    start_low = spread_rows(start_grad.astype(jnp.bfloat16))
    grad_mixer = outer_sum(mixed_low, start_low)
    mixed_grad = jnp.einsum(
        "td,ed->te", start_low, mixer_weight, preferred_element_type=jnp.float32
    ).astype(jnp.bfloat16)
    mixed_grad = mixed_grad.reshape(row_count, slot_width, head_count, HEAD_DIM)
    initial = (
        jnp.zeros(full_patch.shape, jnp.float32),
        jnp.zeros(full_variable.shape, jnp.float32),
        jnp.zeros(head_query.shape, jnp.float32),
        jnp.zeros(pair_weight.shape, jnp.float32),
    )
    mixer_step = partial(
        mixer_back,
        full_patch=full_patch,
        full_variable=full_variable,
        pair_weight=pair_weight,
        head_query=head_query,
    )
    (grad_patch, grad_variable, grad_query, grad_pair), slot_grads = lax.scan(
        mixer_step, initial, (patches, mixed_grad)
    )
    slot_total = head_total(slot_grads).reshape(row_count, slot_width, var_count, 2, 2)
    table_grads = jnp.einsum(
        "rjsa,rjvpx->svapjx", chosen.astype(jnp.float32), slot_total, precision=highest
    )
    side_grads = jnp.pad(
        table_grads[:, :, :, 0], ((0, 0), (0, 0), (0, 1), (0, 0), (0, 0))
    ) + jnp.pad(table_grads[:, :, :, 1], ((0, 0), (0, 0), (1, 0), (0, 0), (0, 0)))
    west_grad = side_grads[0].reshape(var_count, lat_count, 2 * slot_width)
    east_grad = side_grads[1].reshape(var_count, lat_count, 2 * slot_width)
    padded_grad = jnp.pad(west_grad, ((0, 0), (0, 0), (0, 2))) + jnp.pad(
        east_grad, ((0, 0), (0, 0), (2, 0))
    )
    rim_values = jnp.stack([padded_grad[:, :, 0], padded_grad[:, :, -1]], axis=2)
    returned = extended(rim_values, ((LON, 2),), 1)
    pixel_grad = (
        padded_grad[:, :, 1:-1]
        + jnp.pad(returned[:, :, 0:1], ((0, 0), (0, 0), (0, 2 * slot_width - 1)))
        + jnp.pad(returned[:, :, 3:4], ((0, 0), (0, 0), (2 * slot_width - 1, 0)))
    )
    sector_out = (
        lax.psum_scatter(
            grad_query.astype(jnp.bfloat16), LON, scatter_dimension=1, tiled=True
        ).astype(jnp.float32),
        lax.psum_scatter(
            grad_pair[:, :local_width].astype(jnp.bfloat16), LON, scatter_dimension=0, tiled=True
        ).astype(jnp.float32),
        lax.psum_scatter(
            grad_pair[:, local_width:].astype(jnp.bfloat16), LON, scatter_dimension=0, tiled=True
        ).astype(jnp.float32),
        lax.psum_scatter(
            grad_mixer.astype(jnp.bfloat16), LON, scatter_dimension=1, tiled=True
        ).astype(jnp.float32),
        lax.psum_scatter(
            grad_input.astype(jnp.bfloat16), LON, scatter_dimension=1, tiled=True
        ).astype(jnp.float32),
        lax.psum_scatter(
            grad_proj.astype(jnp.bfloat16), LON, scatter_dimension=1, tiled=True
        ).astype(jnp.float32),
        lax.psum_scatter(
            grad_up.astype(jnp.bfloat16), LON, scatter_dimension=0, tiled=True
        ).astype(jnp.float32),
        lax.psum_scatter(
            grad_up_bias.astype(jnp.bfloat16), LON, scatter_dimension=1, tiled=True
        ).astype(jnp.float32),
        lax.psum_scatter(
            grad_down.astype(jnp.bfloat16), LON, scatter_dimension=1, tiled=True
        ).astype(jnp.float32),
        lax.psum_scatter(
            grad_final_weight.astype(jnp.bfloat16), LON, scatter_dimension=0, tiled=True
        ).astype(jnp.float32),
    )
    shared_out = (
        lax.psum_scatter(grad_patch, (LON, HEAD), scatter_dimension=2, tiled=True),
        lax.psum_scatter(grad_variable, (LON, HEAD), scatter_dimension=1, tiled=True),
        lax.psum_scatter(grad_lead, (LON, HEAD), scatter_dimension=1, tiled=True),
        lax.psum_scatter(grad_gain_one, (LON, HEAD), scatter_dimension=0, tiled=True),
        lax.psum_scatter(grad_shift_one, (LON, HEAD), scatter_dimension=0, tiled=True),
        lax.psum_scatter(grad_gain_two, (LON, HEAD), scatter_dimension=0, tiled=True),
        lax.psum_scatter(grad_shift_two, (LON, HEAD), scatter_dimension=0, tiled=True),
    )
    return (
        predicted,
        pixel_grad,
        shared_out[0],
        shared_out[1],
        sector_out[0],
        sector_out[1],
        sector_out[2],
        sector_out[3],
        shared_out[2],
        shared_out[3],
        shared_out[4],
        sector_out[4],
        sector_out[5],
        shared_out[5],
        shared_out[6],
        sector_out[6],
        sector_out[7],
        sector_out[8],
        sector_out[9],
    )


MESH = pl.DeviceIdType.MESH
BOTH = (LON, HEAD)
LON_SIZE = 16
HEAD_SIZE = 2
CHUNK = 256
low = jnp.bfloat16
wide = jnp.float32


def planned(mesh):
    return mesh.shape[LON] == LON_SIZE and mesh.shape[HEAD] == HEAD_SIZE


def dot(left, right, left_dim=1, right_dim=0):
    return lax.dot_general(
        left, right, (((left_dim,), (right_dim,)), ((), ())), preferred_element_type=wide
    )


def position():
    lon = lax.axis_index(LON)
    x = lax.axis_index(HEAD)
    z = lax.div(lon, 4)
    y = lax.rem(lax.div(lon, 2), 2)
    c = lax.rem(lon, 2)
    return x, z, y, c


def partners(x, z, y, c):
    here = z * 4 + y * 2 + c
    across = {
        "x": (here, 1 - x),
        "y": (z * 4 + (1 - y) * 2 + c, x),
        "c": (z * 4 + y * 2 + 1 - c, x),
    }
    line = [(lax.rem(z + step, 4) * 4 + y * 2 + c, x) for step in (1, 2, 3)]
    return across, line


def sector_of(z, y, c, x, part, side):
    return (y * 2 + c) * 4 + x * 2 + part, side


def block_of(z, y, row):
    return row * 4 + z, y


def meet(peers, others=(), own=None):
    barrier = pltpu.get_barrier_semaphore()
    for device in peers:
        pl.semaphore_signal(barrier, inc=1, device_id=device, device_id_type=MESH)
    for device in others:

        @pl.when(jnp.logical_not(same(device, own)))
        def _():
            pl.semaphore_signal(barrier, inc=1, device_id=device, device_id_type=MESH)

    expected = len(peers)
    for device in others:
        expected = expected + 1 - same(device, own).astype(jnp.int32)
    pl.semaphore_wait(barrier, expected)


def same(device, own):
    return jnp.logical_and(device[0] == own[0], device[1] == own[1])


def post(source, target, send_sem, recv_sem, device, own):
    here = same(device, own)

    @pl.when(here)
    def _():
        pltpu.make_async_copy(source, target, recv_sem).start()

    @pl.when(jnp.logical_not(here))
    def _():
        remote(source, target, send_sem, recv_sem, device).start()


def settle(source, target, send_sem, recv_sem, device, own):
    @pl.when(jnp.logical_not(same(device, own)))
    def _():
        remote(source, target, send_sem, recv_sem, device).wait_send()


def remote(source, target, send_sem, recv_sem, device):
    return pltpu.make_async_remote_copy(
        src_ref=source,
        dst_ref=target,
        send_sem=send_sem,
        recv_sem=recv_sem,
        device_id=device,
        device_id_type=MESH,
    )


def gather_kernel(items, count, *refs):
    ins, outs = refs[:count], refs[count + 2 : 2 * count + 2]
    patch_in, grad_in = refs[count : count + 2]
    patch_out, grad_out = refs[2 * count + 2 : 2 * count + 4]
    own_sem, line_send, line_recv, hop_send, hop_recv, post_send, post_recv = refs[
        2 * count + 4 :
    ]
    x, z, y, c = position()
    across, line = partners(x, z, y, c)
    own = (z * 4 + y * 2 + c, x)
    sources = [sector_of(z, y, c, x, part, side) for part in range(2) for side in range(2)]
    meet(list(across.values()) + line, sources, own)
    letters = []
    for part in range(2):
        row = 2 * x + part
        letters.append(
            (patch_in.at[part], patch_out.at[c], post_send.at[part], post_recv.at[c])
            + (block_of(z, y, row), own)
        )
    for row in range(4):
        letters.append(
            (grad_in.at[row], grad_out.at[x, c], post_send.at[2 + row])
            + (post_recv.at[2 + 2 * x + c], block_of(z, y, row), own)
        )
    for letter in letters:
        post(*letter)

    def views(item):
        index, lead, first, rows, _ = item
        source, target = ins[index], outs[index]
        if lead is not None:
            source, target = source.at[lead], target.at[lead]
        return source.at[pl.ds(first, rows)], target, pl.ds(first, rows)

    def copies(number):
        item = items[number]
        source, target, span = views(item)
        own = target.at[x, z, y, c, span]
        keep = pltpu.make_async_copy(source, own, own_sem.at[number])
        along = [
            remote(source, own, line_send.at[number, d], line_recv.at[number, d], line[d])
            for d in range(3)
        ]
        quarter = target.at[x, :, y, c, span]
        if item[4] == 0:
            half, order = target.at[x, :, :, c, span], ("y", "x")
        else:
            half, order = target.at[:, :, y, c, span], ("x", "y")
        full = target.at[:, :, :, c, span]
        hops = [
            remote(part, part, hop_send.at[number, k], hop_recv.at[number, k], across[axis])
            for k, (part, axis) in enumerate(
                ((quarter, order[0]), (half, order[1]), (full, "c"))
            )
        ]
        return keep, along, hops

    plan = [copies(number) for number in range(len(items))]
    total = len(items)
    for step in range(total + 8):
        if step < total:
            keep, along, _ = plan[step]
            keep.start()
            for one in along:
                one.start()
        if 0 <= step - 2 < total:
            keep, along, hops = plan[step - 2]
            keep.wait()
            for one in along:
                one.wait_recv()
            hops[0].start()
        if 0 <= step - 4 < total:
            hops = plan[step - 4][2]
            hops[0].wait_recv()
            hops[1].start()
        if 0 <= step - 6 < total:
            hops = plan[step - 6][2]
            hops[1].wait_recv()
            hops[2].start()
        if 0 <= step - 8 < total:
            plan[step - 8][2][2].wait_recv()
    for _, along, hops in plan:
        for one in along + hops:
            one.wait_send()
    for letter in letters:
        settle(*letter)
    for part in range(2):
        pltpu.make_async_copy(patch_in.at[part], patch_out.at[part], post_recv.at[part]).wait()
    for side in range(2):
        for part in range(2):
            pltpu.make_async_copy(
                grad_in.at[0], grad_out.at[side, part], post_recv.at[2 + 2 * side + part]
            ).wait()


def gather_all(arrays, patches, grads, number):
    items = []
    for index, array in enumerate(arrays):
        leads = range(array.shape[0]) if array.ndim == 3 else (None,)
        rows = array.shape[-2]
        for lead in leads:
            if rows >= 64:
                half = rows // 2
                items.append((index, lead, 0, half, 0))
                items.append((index, lead, half, half, 1))
            else:
                items.append((index, lead, 0, rows, 0))
    count = len(arrays)
    shapes = [
        jax.ShapeDtypeStruct(a.shape[:-2] + (2, 4, 2, 2) + a.shape[-2:], a.dtype) for a in arrays
    ] + [
        jax.ShapeDtypeStruct(patches.shape, low),
        jax.ShapeDtypeStruct((2, 2) + grads.shape[1:], low),
    ]
    sem = pltpu.SemaphoreType.DMA
    gathered = pl.pallas_call(
        partial(gather_kernel, items, count),
        out_shape=shapes,
        in_specs=[pl.BlockSpec(memory_space=pl.ANY)] * (count + 2),
        out_specs=[pl.BlockSpec(memory_space=pl.ANY)] * (count + 2),
        scratch_shapes=[
            sem((len(items),)),
            sem((len(items), 3)),
            sem((len(items), 3)),
            sem((len(items), 3)),
            sem((len(items), 3)),
            sem((6,)),
            sem((6,)),
        ],
        compiler_params=pltpu.CompilerParams(collective_id=number, has_side_effects=True),
    )(*arrays, patches, grads)
    return [
        g.reshape(a.shape[:-2] + (2, 16 * a.shape[-2], a.shape[-1]))
        for g, a in zip(gathered, arrays)
    ] + list(gathered[count:])


def reduce_kernel(chunks, count, *refs):
    ins, value_in, grad_in = refs[:count], refs[count], refs[count + 1]
    out, value_out, grad_out = refs[count + 2 : count + 5]
    buffers, sems = refs[count + 5 : count + 11], refs[count + 11 : count + 18]
    value_send, value_recv, grad_send, grad_recv = refs[count + 18 :]
    x, z, y, c = position()
    across, line = partners(x, z, y, c)
    own = (z * 4 + y * 2 + c, x)
    sources = [block_of(z, y, row) for row in range(4)]
    meet(list(across.values()) + line, sources, own)
    letters = []
    for part in range(2):
        for side in range(2):
            device = sector_of(z, y, c, x, part, side)
            at = 2 * part + side
            letters.append(
                (value_in.at[side, part], value_out.at[z], value_send.at[at], value_recv.at[z])
                + (device, own)
            )
            letters.append(
                (grad_in.at[part], grad_out.at[z], grad_send.at[at], grad_recv.at[z])
                + (device, own)
            )
    for letter in letters:
        post(*letter)
    total = len(chunks)

    def source_of(pair, color, side, core):
        index, lead, offset = chunks[2 * pair + color][side]
        source = ins[index] if lead is None else ins[index].at[lead]
        return source.at[:, :, core, :, pl.ds(offset, CHUNK)]

    begin, stage_core, stage_first, stage_second, stage_third, finish = reducer(
        source_of, buffers, sems, out
    )
    plan = ((0, begin), (2, stage_core), (4, stage_first), (6, stage_second), (8, stage_third))
    for step in range(total + 8):
        for back, stage in plan:
            if 0 <= step - back < total:
                stage((step - back) // 2, (step - back) % 2)
    for k in range(total):
        finish(k // 2, k % 2)
    for letter in letters:
        settle(*letter)
    for row in range(4):
        pltpu.make_async_copy(value_in.at[0, 0], value_out.at[row], value_recv.at[row]).wait()
        pltpu.make_async_copy(grad_in.at[0], grad_out.at[row], grad_recv.at[row]).wait()


def reduce_all(items, values, grads, number):
    chunks, views = [], []
    for index, item in enumerate(items):
        rows, columns = item.shape[-2:]
        lead = item.shape[:-2]
        item = item.reshape((-1, 4, 2, 2, rows // 16, columns))
        if not lead:
            views.append(item[0])
            for offset in range(0, columns // 2, CHUNK):
                chunks.append(((index, None, offset), (index, None, columns // 2 + offset)))
            continue
        views.append(item)
        for first in range(0, item.shape[0], 2):
            for offset in range(0, columns, CHUNK):
                chunks.append(((index, first, offset), (index, first + 1, offset)))
    rows = views[0].shape[-2]
    count, total = len(views), len(chunks)
    sem = pltpu.SemaphoreType.DMA
    return pl.pallas_call(
        partial(reduce_kernel, chunks, count),
        out_shape=[
            jax.ShapeDtypeStruct((rows, total * CHUNK), wide),
            jax.ShapeDtypeStruct((4,) + values.shape[2:], values.dtype),
            jax.ShapeDtypeStruct((4,) + grads.shape[1:], grads.dtype),
        ],
        in_specs=[pl.BlockSpec(memory_space=pl.ANY)] * (count + 2),
        out_specs=[pl.BlockSpec(memory_space=pltpu.VMEM)]
        + [pl.BlockSpec(memory_space=pl.ANY)] * 2,
        scratch_shapes=reducer_scratch(total, rows)
        + [
            sem((4,)),
            sem((4,)),
            sem((4,)),
            sem((4,)),
        ],
        compiler_params=pltpu.CompilerParams(
            collective_id=number, has_side_effects=True, vmem_limit_bytes=60 * 2**20
        ),
    )(*views, values, grads)


def diagonal(var_count, columns):
    column = lax.broadcasted_iota(jnp.int32, (var_count, columns), 1)
    row = lax.broadcasted_iota(jnp.int32, (var_count, columns), 0)
    return (lax.rem(column, var_count) == row) & (column < 5 * var_count)


def patch_kernel(field_ref, lat_ref, shift_ref, patch_ref):
    lat_count, var_count, _ = field_ref.shape
    row_count, lanes = lat_ref.shape
    slots = lanes // 2
    for r in range(row_count):
        lat = lat_ref[r : r + 1, :]
        west = shift_ref[r : r + 1, :] < 0

        def body(b, carry):
            top, bottom = carry
            wide_row = field_ref[b].astype(wide)
            chosen = jnp.where(west, wide_row[:, :lanes], wide_row[:, lanes:])
            return (jnp.where(lat == b, chosen, top), jnp.where(lat == b - 1, chosen, bottom))

        zero = jnp.zeros((var_count, lanes), wide)
        rows = lax.fori_loop(0, lat_count, body, (zero, zero), unroll=4)
        for py in range(2):
            for px in range(2):
                k = 2 * py + px
                patch_ref[r, k * var_count : (k + 1) * var_count, :] = rows[py][
                    :, px * slots : (px + 1) * slots
                ].astype(low)


def cut_patches(field, lat_lanes, shift_lanes):
    row_count, lanes = lat_lanes.shape
    return pl.pallas_call(
        patch_kernel,
        out_shape=jax.ShapeDtypeStruct((row_count, 4 * field.shape[1], lanes // 2), low),
    )(field, lat_lanes, shift_lanes)


def paste_kernel(grad_ref, lat_ref, shift_ref, field_ref):
    lat_count, var_count, _ = field_ref.shape
    row_count, lanes = lat_ref.shape
    field_ref[...] = jnp.zeros_like(field_ref)
    for r in range(row_count):
        lat = lat_ref[r : r + 1, :]
        west = shift_ref[r : r + 1, :] < 0
        lat_both = jnp.concatenate([lat, lat], axis=1)
        both = []
        for py in range(2):
            k = 2 * py
            grads = jnp.concatenate(
                [
                    grad_ref[r, k * var_count : (k + 1) * var_count, :],
                    grad_ref[r, (k + 1) * var_count : (k + 2) * var_count, :],
                ],
                axis=1,
            )
            left = jnp.where(west, grads, 0.0)
            both.append(jnp.concatenate([left, grads - left], axis=1))

        def body(b, carry):
            field_ref[b] += jnp.where(lat_both == b, both[0], 0.0) + jnp.where(
                lat_both == b - 1, both[1], 0.0
            )
            return carry

        lax.fori_loop(0, lat_count, body, 0)


def paste_patches(grads, lat_lanes, shift_lanes, lat_count):
    return pl.pallas_call(
        paste_kernel,
        out_shape=jax.ShapeDtypeStruct(
            (lat_count, grads.shape[1] // 4, 2 * lat_lanes.shape[1]), wide
        ),
    )(grads, lat_lanes, shift_lanes)


def mixer_forward_kernel(cut_ref, score_ref, value_ref, patch_ref, prob_ref, mixed_ref):
    head_count, var_count, tokens = prob_ref.shape
    parts, taps, width = cut_ref.shape
    for part in range(parts):
        patch_ref[:taps, part * width : (part + 1) * width] = cut_ref[part]
    patch_ref[taps : taps + var_count, :] = jnp.ones((var_count, tokens), low)
    rest = patch_ref.shape[0] - 5 * var_count
    patch_ref[5 * var_count :, :] = jnp.zeros((rest, tokens), low)
    mask = diagonal(var_count, patch_ref.shape[0])

    def head_step(h, carry):
        spread = jnp.where(mask, score_ref[pl.ds(h, 1), :], 0.0)
        upper = spread.astype(low)
        lower = (spread - upper.astype(wide)).astype(low)
        patch = patch_ref[...]
        scores = dot(upper, patch) + dot(lower, patch)
        raised = jnp.exp(scores - jnp.max(scores, axis=0, keepdims=True))
        prob = raised / jnp.sum(raised, axis=0, keepdims=True)
        prob_ref[h] = prob
        pooled = jnp.concatenate(
            [
                (prob * patch_ref[k * var_count : (k + 1) * var_count, :].astype(wide)).astype(low)
                for k in range(5)
            ]
            + [jnp.zeros((rest, tokens), low)],
            axis=0,
        )
        start = pl.multiple_of(h * HEAD_DIM, HEAD_DIM)
        mixed_ref[pl.ds(start, HEAD_DIM), :] = dot(
            value_ref[pl.ds(start, HEAD_DIM), :], pooled
        ).astype(low)
        return carry

    lax.fori_loop(0, head_count, head_step, 0)


def mixer_forward(cut, score_table, value_table):
    head_count, padded = score_table.shape
    var_count = cut.shape[1] // 4
    tokens = cut.shape[0] * cut.shape[2]
    return pl.pallas_call(
        mixer_forward_kernel,
        out_shape=[
            jax.ShapeDtypeStruct((padded, tokens), low),
            jax.ShapeDtypeStruct((head_count, var_count, tokens), wide),
            jax.ShapeDtypeStruct((head_count * HEAD_DIM, tokens), low),
        ],
        compiler_params=pltpu.CompilerParams(vmem_limit_bytes=40 * 2**20),
    )(cut, score_table, value_table)


def mixer_backward_kernel(
    patch_ref,
    prob_ref,
    score_ref,
    value_ref,
    grad_ref,
    pooled_ref,
    count_ref,
    cut_ref,
    patch_grad_ref,
):
    head_count, var_count, _ = prob_ref.shape
    padded, tokens = patch_ref.shape
    rest = padded - 5 * var_count
    mask = diagonal(var_count, padded)
    patch_grad_ref[...] = jnp.zeros_like(patch_grad_ref)

    def head_step(h, carry):
        start = pl.multiple_of(h * HEAD_DIM, HEAD_DIM)
        grads = grad_ref[pl.ds(start, HEAD_DIM), :]
        prob = prob_ref[h]
        back = dot(value_ref[pl.ds(start, HEAD_DIM), :], grads, 0, 0)
        pieces = [patch_ref[k * var_count : (k + 1) * var_count, :].astype(wide) for k in range(5)]
        backs = [back[k * var_count : (k + 1) * var_count, :] for k in range(5)]
        prob_grad = pieces[0] * backs[0]
        for k in range(1, 5):
            prob_grad = prob_grad + pieces[k] * backs[k]
        mean = jnp.sum(prob * prob_grad, axis=0, keepdims=True)
        delta = prob * (prob_grad - mean)
        upper = delta.astype(low)
        lower = (delta - upper.astype(wide)).astype(low)
        spread = jnp.where(mask, score_ref[pl.ds(h, 1), :], 0.0).astype(low)
        patch_grad_ref[...] += dot(spread, upper, 0, 0)
        for k in range(4):
            patch_grad_ref[k * var_count : (k + 1) * var_count, :] += prob * backs[k]
        patch = patch_ref[...]
        counts = dot(upper, patch, 1, 1) + dot(lower, patch, 1, 1)
        count_ref[pl.ds(h, 1), :] = jnp.sum(jnp.where(mask, counts, 0.0), axis=0, keepdims=True)
        pooled = jnp.concatenate(
            [(prob * piece).astype(low) for piece in pieces] + [jnp.zeros((rest, tokens), low)],
            axis=0,
        )
        pooled_ref[pl.ds(start, HEAD_DIM), :] = dot(grads, pooled, 1, 1)
        return carry

    lax.fori_loop(0, head_count, head_step, 0)
    parts, taps, width = cut_ref.shape
    for part in range(parts):
        cut_ref[part] = patch_grad_ref[:taps, part * width : (part + 1) * width]


def mixer_backward(patches, probs, score_table, value_table, mixed_grads):
    head_count, padded = score_table.shape
    var_count = probs.shape[1]
    tokens = patches.shape[1]
    return pl.pallas_call(
        mixer_backward_kernel,
        out_shape=[
            jax.ShapeDtypeStruct((head_count * HEAD_DIM, padded), wide),
            jax.ShapeDtypeStruct((head_count, padded), wide),
            jax.ShapeDtypeStruct((2, 4 * var_count, tokens // 2), wide),
        ],
        scratch_shapes=[pltpu.VMEM((padded, tokens), wide)],
        compiler_params=pltpu.CompilerParams(vmem_limit_bytes=40 * 2**20),
    )(patches, probs, score_table, value_table, mixed_grads)


def head_lanes(values, h):
    lane = lax.broadcasted_iota(jnp.int32, values.shape, values.ndim - 1)
    inside = lane < HEAD_DIM if h == 0 else lane >= HEAD_DIM
    return jnp.where(inside, values, jnp.zeros_like(values))


def plane_device(z, index):
    return z * 4 + lax.div(index, 2), lax.rem(index, 2)


def plane_meet(x, z, y, c):
    barrier = pltpu.get_barrier_semaphore()
    for flip in range(1, 8):
        there_y = 1 - y if flip & 4 else y
        there_c = 1 - c if flip & 2 else c
        there_x = 1 - x if flip & 1 else x
        device = (z * 4 + there_y * 2 + there_c, there_x)
        pl.semaphore_signal(barrier, inc=1, device_id=device, device_id_type=MESH)
    return barrier


def attend_kernel(
    source,
    tag_ref,
    crop_ref,
    joint,
    received,
    wide_ref,
    total_ref,
    sending,
    own_sem,
    send_sem,
    recv_sem,
    out_own,
    out_send,
    out_recv,
):
    x, z, y, c = position()
    me = y * 4 + c * 2 + x
    peers, kinds, share, lanes = joint.shape
    slots = peers * share
    keep = pltpu.make_async_copy(source.at[me], joint.at[me], own_sem)
    keep.start()
    barrier = plane_meet(x, z, y, c)
    pl.semaphore_wait(barrier, peers - 1)

    def inward(step):
        there = lax.rem(me + step, peers)
        return remote(
            source.at[there],
            joint.at[me],
            send_sem.at[there],
            recv_sem.at[me],
            plane_device(z, there),
        )

    def arrived(index):
        return pltpu.make_async_copy(joint.at[index], joint.at[index], recv_sem.at[index])

    for step in range(1, peers):
        inward(step).start()
    keep.wait()
    for step in range(1, peers):
        arrived(lax.rem(me + step, peers)).wait()

    def block(step, carry):
        index = lax.rem(me + 1 + step, peers)
        span = pl.ds(pl.multiple_of(index * share, share), share)
        queries = joint[index, 0]
        keys = joint[:, 1].reshape(slots, lanes)
        values = joint[:, 2].reshape(slots, lanes)
        allowed = crop_ref[span, :] == tag_ref[...]
        result = None
        for h in range(2):
            scores = dot(head_lanes(queries, h), keys, 1, 1)
            scores = jnp.where(allowed, scores, masked_score)
            largest = jnp.max(scores, axis=1, keepdims=True)
            weights = jnp.exp(scores - largest)
            total = jnp.sum(weights, axis=1, keepdims=True)
            weights = (weights * (1.0 / total)).astype(low)
            part = head_lanes(dot(weights, values), h)
            result = part if result is None else result + part
            total_ref[h, span, :] = largest + jnp.log(total)
        wide_ref[span, :] = result
        sending[index] = result.astype(low)

        @pl.when(step < peers - 1)
        def _():
            outward(index).start()

        return carry

    def outward(index):
        return remote(
            sending.at[index],
            received.at[me],
            out_send.at[index],
            out_recv.at[me],
            plane_device(z, index),
        )

    lax.fori_loop(0, peers, block, 0)
    last = pltpu.make_async_copy(sending.at[me], received.at[me], out_own)
    last.start()
    for step in range(1, peers):
        inward(step).wait_send()
        outward(lax.rem(me + step, peers)).wait_send()
        there = lax.rem(me + step, peers)
        pltpu.make_async_copy(
            sending.at[there], received.at[there], out_recv.at[there]
        ).wait()
    last.wait()


def attend_all(source, tags, crops, number):
    peers, kinds, share, lanes = source.shape
    slots = peers * share
    sem = pltpu.SemaphoreType.DMA
    vmem = pl.BlockSpec(memory_space=pltpu.VMEM)
    hbm = pl.BlockSpec(memory_space=pl.ANY)
    return pl.pallas_call(
        attend_kernel,
        out_shape=[
            jax.ShapeDtypeStruct(source.shape, low),
            jax.ShapeDtypeStruct((peers, share, lanes), low),
            jax.ShapeDtypeStruct((slots, lanes), wide),
            jax.ShapeDtypeStruct((2, slots, 1), wide),
        ],
        in_specs=[hbm, vmem, vmem],
        out_specs=[vmem, hbm, vmem, vmem],
        scratch_shapes=[
            pltpu.VMEM((peers, share, lanes), low),
            sem,
            sem((peers,)),
            sem((peers,)),
            sem,
            sem((peers,)),
            sem((peers,)),
        ],
        compiler_params=pltpu.CompilerParams(
            collective_id=number, has_side_effects=True, vmem_limit_bytes=50 * 2**20
        ),
    )(source, tags, crops)


def joined(left, right):
    return (left.astype(wide) + right.astype(wide)).astype(low)


def reducer(source_of, buffers, sems, out):
    mine, other, first_a, first_b, second, third = buffers
    own_sem, core_send, core_recv, hop_send, hop_recv, line_send, line_recv = sems
    x, z, y, c = position()
    across, line = partners(x, z, y, c)

    def keeps(pair, color):
        k = 2 * pair + color
        return [
            pltpu.make_async_copy(
                source_of(pair, color, side, c), mine.at[2 * k + side], own_sem.at[k, side]
            )
            for side in range(2)
        ]

    def swaps(pair, color):
        k = 2 * pair + color
        return [
            remote(
                source_of(pair, color, side, 1 - c),
                other.at[2 * k + side],
                core_send.at[k, side],
                core_recv.at[k, side],
                across["c"],
            )
            for side in range(2)
        ]

    def hop_one(pair, color):
        k = 2 * pair + color
        if color == 0:
            source, target, axis = mine.at[2 * k + 1 - x], first_a.at[pair], "x"
        else:
            source = mine.at[pl.ds(2 * k, 2), :, 1 - y]
            target, axis = first_b.at[pair], "y"
        return remote(source, target, hop_send.at[k, 0], hop_recv.at[k, 0], across[axis])

    def hop_two(pair, color):
        k = 2 * pair + color
        if color == 0:
            source, axis = mine.at[2 * k + x, :, 1 - y], "y"
        else:
            source, axis = mine.at[2 * k + 1 - x, :, y], "x"
        return remote(source, second.at[k], hop_send.at[k, 1], hop_recv.at[k, 1], across[axis])

    def along(pair, color):
        k = 2 * pair + color
        return [
            remote(
                mine.at[2 * k + x, lax.rem(z + d + 1, 4), y],
                third.at[k, d],
                line_send.at[k, d],
                line_recv.at[k, d],
                line[d],
            )
            for d in range(3)
        ]

    def begin(pair, color):
        for copy in swaps(pair, color) + keeps(pair, color):
            copy.start()

    def stage_core(pair, color):
        k = 2 * pair + color
        for copy in keeps(pair, color):
            copy.wait()
        for copy in swaps(pair, color):
            copy.wait_recv()

        def body(step, carry):
            side, row = lax.div(step, 4), lax.rem(step, 4)
            for part in range(2):
                mine[2 * k + side, row, part] = joined(
                    mine[2 * k + side, row, part], other[2 * k + side, row, part]
                )
            return carry

        lax.fori_loop(0, 8, body, 0)
        hop_one(pair, color).start()

    def stage_first(pair, color):
        k = 2 * pair + color
        hop_one(pair, color).wait_recv()

        def body(row, carry):
            for part in range(2):
                if color == 0:
                    mine[2 * k + x, row, part] = joined(
                        mine[2 * k + x, row, part], first_a[pair, row, part]
                    )
                else:
                    mine[2 * k + part, row, y] = joined(
                        mine[2 * k + part, row, y], first_b[pair, part, row]
                    )
            return carry

        lax.fori_loop(0, 4, body, 0)
        hop_two(pair, color).start()

    def stage_second(pair, color):
        k = 2 * pair + color
        hop_two(pair, color).wait_recv()

        def body(row, carry):
            mine[2 * k + x, row, y] = joined(mine[2 * k + x, row, y], second[k, row])
            return carry

        lax.fori_loop(0, 4, body, 0)
        for copy in along(pair, color):
            copy.start()

    def stage_third(pair, color):
        k = 2 * pair + color
        for copy in along(pair, color):
            copy.wait_recv()
        result = mine[2 * k + x, z, y].astype(wide)
        for d in range(3):
            result = result + third[k, d].astype(wide)
        start = k * CHUNK
        if not isinstance(k, int):
            start = pl.multiple_of(start, CHUNK)
        out[:, pl.ds(start, CHUNK)] = result

    def finish(pair, color):
        hop_one(pair, color).wait_send()
        hop_two(pair, color).wait_send()
        for copy in swaps(pair, color) + along(pair, color):
            copy.wait_send()

    return begin, stage_core, stage_first, stage_second, stage_third, finish


def reducer_scratch(total, rows):
    sem = pltpu.SemaphoreType.DMA
    pairs = (total + 1) // 2
    return [
        pltpu.VMEM((2 * total, 4, 2, rows, CHUNK), low),
        pltpu.VMEM((2 * total, 4, 2, rows, CHUNK), low),
        pltpu.VMEM((pairs, 4, 2, rows, CHUNK), low),
        pltpu.VMEM((pairs, 2, 4, rows, CHUNK), low),
        pltpu.VMEM((total, 4, rows, CHUNK), low),
        pltpu.VMEM((total, 3, rows, CHUNK), low),
    ] + [
        sem((total, 2)),
        sem((total, 2)),
        sem((total, 2)),
        sem((total, 2)),
        sem((total, 2)),
        sem((total, 3)),
        sem((total, 3)),
    ]


def attend_back_kernel(
    joint,
    tag_ref,
    crop_ref,
    out_ref,
    total_ref,
    source,
    feed_ref,
    stacked,
    sums,
    grads,
    result,
    key_acc,
    value_acc,
    *rest
):
    buffers, sems = rest[:6], rest[6:13]
    in_own, in_send, in_recv, back_own, back_send, back_recv = rest[13:]
    x, z, y, c = position()
    across, line = partners(x, z, y, c)
    me = y * 4 + c * 2 + x
    peers, kinds, share, lanes = joint.shape
    slots = peers * share
    scale = HEAD_DIM ** (-0.5)
    each = feed_ref.shape[-1] // CHUNK

    def source_of(pair, color, side, core):
        k = 2 * pair + color
        offset = pl.multiple_of(lax.rem(k, each) * CHUNK, CHUNK)
        return feed_ref.at[lax.div(k, each), side, :, :, core, :, pl.ds(offset, CHUNK)]

    begin, stage_core, stage_first, stage_second, stage_third, finish = reducer(
        source_of, buffers, sems, sums
    )
    keep = pltpu.make_async_copy(source.at[me], grads.at[me], in_own)
    keep.start()
    barrier = plane_meet(x, z, y, c)
    for device in line:
        pl.semaphore_signal(barrier, inc=1, device_id=device, device_id_type=MESH)
    pl.semaphore_wait(barrier, peers - 1 + len(line))

    def inward(there):
        return remote(
            source.at[there],
            grads.at[me],
            in_send.at[there],
            in_recv.at[me],
            plane_device(z, there),
        )

    def outward(there, part):
        span = pl.ds(0, 1) if part == 0 else pl.ds(1, 2)
        return remote(
            result.at[there, span],
            stacked.at[me, span],
            back_send.at[there, part],
            back_recv.at[me, part],
            plane_device(z, there),
        )

    for step in range(1, peers):
        inward(lax.rem(me + step, peers)).start()
    key_acc[...] = jnp.zeros_like(key_acc)
    value_acc[...] = jnp.zeros_like(value_acc)
    pairs = feed_ref.shape[0] * each // 2

    def attention(index):
        span = pl.ds(pl.multiple_of(index * share, share), share)
        queries = joint[index, 0]
        keys = joint[:, 1].reshape(slots, lanes)
        values = joint[:, 2].reshape(slots, lanes)
        grad = grads[index]
        product = grad.astype(wide) * out_ref[span, :]
        allowed = crop_ref[span, :] == tag_ref[...]
        query_grad = None
        for h in range(2):
            query_part, grad_part = head_lanes(queries, h), head_lanes(grad, h)
            scores = jnp.where(allowed, dot(query_part, keys, 1, 1), masked_score)
            weights = jnp.exp(scores - total_ref[h, span, :])
            weight_grads = dot(grad_part, values, 1, 1)
            delta = jnp.sum(head_lanes(product, h), axis=1, keepdims=True)
            score_grads = (weights * (weight_grads - delta)).astype(low)
            weights = weights.astype(low)
            value_acc[...] += dot(grad_part, weights, 0, 0)
            key_acc[...] += dot(query_part, score_grads, 0, 0)
            part = head_lanes(dot(score_grads, keys), h)
            query_grad = part if query_grad is None else query_grad + part
        result[index, 0] = (query_grad * scale).astype(low)

    def step_body(step, carry):
        @pl.when(step < pairs)
        def _():
            begin(step, 0)
            begin(step, 1)

        for back, stage in ((1, stage_core), (2, stage_first), (3, stage_second), (4, stage_third)):

            @pl.when(jnp.logical_and(step >= back, step < pairs + back))
            def _():
                stage(step - back, 0)
                stage(step - back, 1)

        @pl.when(step < peers)
        def _():
            index = lax.rem(me + step, peers)

            @pl.when(step == 0)
            def _():
                keep.wait()

            @pl.when(step > 0)
            def _():
                pltpu.make_async_copy(
                    grads.at[index], grads.at[index], in_recv.at[index]
                ).wait()

            attention(index)

            @pl.when(step > 0)
            def _():
                outward(index, 0).start()

        @pl.when(step == peers - 1)
        def _():
            for index in range(peers):
                span = slice(index * share, (index + 1) * share)
                result[index, 1] = key_acc[:, span].T.astype(low)
                result[index, 2] = value_acc[:, span].T.astype(low)
            for other in range(1, peers):
                outward(lax.rem(me + other, peers), 1).start()
            pltpu.make_async_copy(result.at[me], stacked.at[me], back_own).start()

        return carry

    lax.fori_loop(0, pairs + 4, step_body, 0)

    def finish_body(pair, carry):
        finish(pair, 0)
        finish(pair, 1)
        return carry

    lax.fori_loop(0, pairs, finish_body, 0)
    for step in range(1, peers):
        there = lax.rem(me + step, peers)
        inward(there).wait_send()
        for part in range(2):
            outward(there, part).wait_send()
            span = pl.ds(0, 1) if part == 0 else pl.ds(1, 2)
            pltpu.make_async_copy(
                result.at[there, span], stacked.at[there, span], back_recv.at[there, part]
            ).wait()
    pltpu.make_async_copy(result.at[me], stacked.at[me], back_own).wait()


def attend_back(joint, tags, crops, outputs, totals, source, feed_grads, number):
    peers, kinds, share, lanes = joint.shape
    slots = peers * share
    sides, halves, rows, columns = feed_grads.shape
    total = sides * columns // CHUNK
    sem = pltpu.SemaphoreType.DMA
    vmem = pl.BlockSpec(memory_space=pltpu.VMEM)
    hbm = pl.BlockSpec(memory_space=pl.ANY)
    return pl.pallas_call(
        attend_back_kernel,
        out_shape=[
            jax.ShapeDtypeStruct(joint.shape, low),
            jax.ShapeDtypeStruct((rows // 16, total * CHUNK), wide),
        ],
        in_specs=[vmem] * 5 + [hbm] * 2,
        out_specs=[hbm, vmem],
        scratch_shapes=[
            pltpu.VMEM((peers, share, lanes), low),
            pltpu.VMEM(joint.shape, low),
            pltpu.VMEM((lanes, slots), wide),
            pltpu.VMEM((lanes, slots), wide),
        ]
        + reducer_scratch(total, rows // 16)
        + [
            sem,
            sem((peers,)),
            sem((peers,)),
            sem,
            sem((peers, 2)),
            sem((peers, 2)),
        ],
        compiler_params=pltpu.CompilerParams(
            collective_id=number, has_side_effects=True, vmem_limit_bytes=60 * 2**20
        ),
    )(
        joint,
        tags,
        crops,
        outputs,
        totals,
        source,
        feed_grads.reshape(sides, halves, 4, 2, 2, rows // 16, columns),
    )


def whole(array):
    rank = len(array.shape)
    return pl.BlockSpec(array.shape, lambda *_: (0,) * rank)


def norm_parts(values):
    center = values - jnp.mean(values, axis=-1, keepdims=True)
    inverse = lax.rsqrt(jnp.mean(center * center, axis=-1, keepdims=True) + epsilon)
    return center * inverse, inverse


def norm_back(values, gain, grads):
    normed, inverse = norm_parts(values)
    scaled = grads * gain
    inner = (
        scaled
        - jnp.mean(scaled, axis=-1, keepdims=True)
        - normed * jnp.mean(scaled * normed, axis=-1, keepdims=True)
    )
    return (
        inner * inverse,
        jnp.sum(grads * normed, axis=0, keepdims=True),
        jnp.sum(grads, axis=0, keepdims=True),
    )


def project_kernel(mixed_ref, back_ref, lead_ref, vector_ref, weight_ref, start_ref, low_ref, out_ref):
    step = pl.program_id(0)
    halves, _, half_width = back_ref.shape
    row_count, _, _, share, lanes = out_ref.shape

    @pl.when(step == 0)
    def _():
        total = lead_ref[...] * vector_ref[0:1] + vector_ref[1:2]
        mixed = mixed_ref[...].T
        for side in range(halves):
            total = total + dot(
                mixed[:, side * half_width : (side + 1) * half_width], back_ref[side], 1, 1
            )
        start_ref[...] = total
        normed, _ = norm_parts(total)
        low_ref[...] = (normed * vector_ref[2:3] + vector_ref[3:4]).astype(low)

    kind, side = lax.div(step, halves), lax.rem(step, halves)
    result = dot(low_ref[...], weight_ref[...].reshape(weight_ref.shape[2:])).astype(low)
    result = result * jnp.where(kind == 0, HEAD_DIM ** (-0.5), 1.0).astype(low)
    pairs = half_width // lanes
    for pair in range(pairs):
        out_ref[:, side * pairs + pair, kind] = result[
            :, pair * lanes : (pair + 1) * lanes
        ].reshape(row_count, share, lanes)


def project(mixed, back_weight, lead_column, vectors, weights, row_count):
    model, tokens = mixed.shape
    kinds, halves, _, half_width = weights.shape
    return pl.pallas_call(
        project_kernel,
        grid=(kinds * halves,),
        out_shape=[
            jax.ShapeDtypeStruct((tokens, model), wide),
            jax.ShapeDtypeStruct((tokens, model), low),
            jax.ShapeDtypeStruct(
                (row_count, halves * half_width // 128, kinds, tokens // row_count, 128), low
            ),
        ],
        in_specs=[
            whole(mixed),
            whole(back_weight),
            whole(lead_column),
            whole(vectors),
            pl.BlockSpec((1, 1, model, half_width), lambda i: (i // halves, i % halves, 0, 0)),
        ],
        out_specs=[
            pl.BlockSpec((tokens, model), lambda i: (0, 0)),
            pl.BlockSpec((tokens, model), lambda i: (0, 0)),
            pl.BlockSpec(
                (row_count, halves * half_width // 128, kinds, tokens // row_count, 128),
                lambda i: (0, 0, 0, 0, 0),
            ),
        ],
        compiler_params=pltpu.CompilerParams(vmem_limit_bytes=40 * 2**20),
    )(mixed, back_weight, lead_column, vectors, weights)


def feed_kernel(
    attended_ref,
    proj_ref,
    start_ref,
    vector_ref,
    up_ref,
    down_ref,
    bias_ref,
    final_ref,
    masked_ref,
    keep_ref,
    predicted_ref,
    middle_grad_ref,
    unit_ref,
    grad_feed_ref,
    grad_proj_ref,
    grad_final_ref,
    grad_bias_ref,
    grad_vector_ref,
    flat,
    middle,
    second,
    second_turned,
    active,
    slope,
    total,
    grad_low,
    grad_turned,
    grad_final,
):
    step = pl.program_id(0)
    count = active.shape[0]
    row_count, units, share, lanes = attended_ref.shape
    halves, _, half_width = proj_ref.shape
    tokens = row_count * share

    @pl.when(step == 0)
    def _():
        for unit in range(units):
            flat[:, unit * lanes : (unit + 1) * lanes] = attended_ref[:, unit].reshape(
                tokens, lanes
            )
        result = start_ref[...]
        for side in range(halves):
            result = result + dot(
                flat[:, side * half_width : (side + 1) * half_width], proj_ref[side], 1, 1
            )
        middle[...] = result
        normed, _ = norm_parts(result)
        normed = (normed * vector_ref[4:5] + vector_ref[5:6]).astype(low)
        second[...] = normed
        second_turned[...] = normed.T
        total[...] = result

    @pl.when(step < count)
    def _():
        hidden = dot(second[...], up_ref[0]) + bias_ref[...]
        share_of = 0.5 * (1.0 + lax.erf(hidden * (0.5**0.5)))
        fired = (hidden * share_of).astype(low)
        active[step] = fired
        slope[step] = share_of + hidden * jnp.exp(-0.5 * hidden * hidden) * (
            0.5 / 1.2533141373155003
        )
        total[...] += dot(fired, down_ref[0], 1, 1)

    @pl.when(step == count - 1)
    def _():
        final_low = total[...].astype(low)
        final_turned = final_low.T
        grads = None
        for side in range(halves):
            predicted_ref[side] = (dot(final_low, final_ref[side]) * keep_ref[...]).astype(low)
            part = dot(masked_ref[side], final_ref[side], 1, 1)
            grads = part if grads is None else grads + part
            grad_final_ref[side] = dot(final_turned, masked_ref[side]).astype(low)
        grad_final[...] = grads
        grad_low[...] = grads.astype(low)
        grad_turned[...] = grads.astype(low).T
        total[...] = jnp.zeros_like(total)

    @pl.when(step >= count)
    def _():
        block = step - count
        hidden_grad = dot(grad_low[...], down_ref[0]) * slope[block]
        hidden_low = hidden_grad.astype(low)
        grad_bias_ref[...] = jnp.sum(hidden_low.astype(wide), axis=0, keepdims=True)
        total[...] += dot(hidden_low, up_ref[0], 1, 1)
        grad_feed_ref[0, 0] = dot(second_turned[...], hidden_low).astype(low)
        grad_feed_ref[1, 0] = dot(grad_turned[...], active[block]).astype(low)

    @pl.when(step == 2 * count - 1)
    def _():
        part, grad_gain, grad_shift = norm_back(middle[...], vector_ref[4:5], total[...])
        result = grad_final[...] + part
        middle_grad_ref[...] = result
        grad_vector_ref[0:1] = grad_gain
        grad_vector_ref[1:2] = grad_shift
        result_low = result.astype(low)
        result_turned = result_low.T
        pairs = half_width // lanes
        for side in range(halves):
            span = slice(side * half_width, (side + 1) * half_width)
            grad_proj_ref[side] = dot(result_turned, flat[:, span]).astype(low)
            out = dot(result_low, proj_ref[side]).astype(low)
            for pair in range(pairs):
                unit_ref[:, side * pairs + pair] = out[
                    :, pair * lanes : (pair + 1) * lanes
                ].reshape(row_count, share, lanes)


def feed(attended, proj, start, vectors, up_weight, down_weight, up_bias, final_weight, masked, keep):
    halves, model, full = up_weight.shape
    half_width = proj.shape[2]
    tokens = start.shape[0]
    block = 512
    each = full // block
    count = halves * each

    def block_at(i):
        j = lax.rem(i, count)
        return (lax.div(j, each), 0, lax.rem(j, each))

    def late_block(i):
        j = lax.max(i - count, 0)
        return (0, lax.div(j, each), 0, lax.rem(j, each))

    def fixed(shape, dtype):
        rank = len(shape)
        return jax.ShapeDtypeStruct(shape, dtype), pl.BlockSpec(shape, lambda i: (0,) * rank)

    outs = [
        fixed((halves, tokens, 128), low),
        fixed((tokens, model), wide),
        fixed(attended.shape, low),
        (
            jax.ShapeDtypeStruct((2,) + up_weight.shape, low),
            pl.BlockSpec((2, 1, model, block), late_block),
        ),
        fixed((halves, model, half_width), low),
        fixed((halves, model, 128), low),
        (
            jax.ShapeDtypeStruct((1, halves * full), wide),
            pl.BlockSpec((1, block), lambda i: (0, lax.max(i - count, 0))),
        ),
        fixed((2, model), wide),
    ]
    return pl.pallas_call(
        feed_kernel,
        grid=(2 * count,),
        out_shape=[shape for shape, _ in outs],
        in_specs=[
            whole(attended),
            whole(proj),
            whole(start),
            whole(vectors),
            pl.BlockSpec((1, model, block), block_at),
            pl.BlockSpec((1, model, block), block_at),
            pl.BlockSpec((1, block), lambda i: (0, lax.rem(i, count))),
            whole(final_weight),
            whole(masked),
            whole(keep),
        ],
        out_specs=[spec for _, spec in outs],
        scratch_shapes=[
            pltpu.VMEM((tokens, model), low),
            pltpu.VMEM((tokens, model), wide),
            pltpu.VMEM((tokens, model), low),
            pltpu.VMEM((model, tokens), low),
            pltpu.VMEM((count, tokens, block), low),
            pltpu.VMEM((count, tokens, block), wide),
            pltpu.VMEM((tokens, model), wide),
            pltpu.VMEM((tokens, model), low),
            pltpu.VMEM((model, tokens), low),
            pltpu.VMEM((tokens, model), wide),
        ],
        compiler_params=pltpu.CompilerParams(vmem_limit_bytes=56 * 2**20),
    )(attended, proj, start, vectors, up_weight, down_weight, up_bias, final_weight, masked, keep)


def return_kernel(
    grads_ref,
    weight_ref,
    low_ref,
    start_ref,
    middle_grad_ref,
    vector_ref,
    lead_ref,
    back_ref,
    mixed_ref,
    grad_input_ref,
    grad_mixer_ref,
    mixed_grad_ref,
    grad_vector_ref,
    turned,
    total,
):
    step = pl.program_id(0)
    halves, _, half_width = back_ref.shape
    row_count, _, _, share, lanes = grads_ref.shape
    tokens = row_count * share
    pairs = half_width // lanes

    @pl.when(step == 0)
    def _():
        turned[...] = low_ref[...].T
        total[...] = jnp.zeros_like(total)

    kind, side = lax.div(step, halves), lax.rem(step, halves)
    piece = jnp.concatenate(
        [grads_ref[:, side * pairs + pair, kind].reshape(tokens, lanes) for pair in range(pairs)],
        axis=1,
    )
    total[...] += dot(piece, weight_ref[0, 0], 1, 1)
    grad_input_ref[0, 0] = dot(turned[...], piece).astype(low)

    @pl.when(step == pl.num_programs(0) - 1)
    def _():
        part, grad_gain, grad_shift = norm_back(start_ref[...], vector_ref[2:3], total[...])
        result = middle_grad_ref[...] + part
        grad_vector_ref[0:1] = jnp.sum(result * lead_ref[...], axis=0, keepdims=True)
        grad_vector_ref[1:2] = jnp.sum(result, axis=0, keepdims=True)
        grad_vector_ref[2:3] = grad_gain
        grad_vector_ref[3:4] = grad_shift
        result_low = result.astype(low)
        result_turned = result_low.T
        for half in range(halves):
            span = slice(half * half_width, (half + 1) * half_width)
            grad_mixer_ref[half] = dot(result_turned, mixed_ref[span, :], 1, 1).astype(low)
            mixed_grad_ref[span, :] = dot(result_low, back_ref[half]).astype(low).T


def go_back(grads, weights, first_low, start, middle_grad, vectors, lead_column, back_weight, mixed):
    kinds, halves, model, half_width = weights.shape
    tokens = start.shape[0]
    block = pl.BlockSpec((1, 1, model, half_width), lambda i: (i // halves, i % halves, 0, 0))
    return pl.pallas_call(
        return_kernel,
        grid=(kinds * halves,),
        out_shape=[
            jax.ShapeDtypeStruct(weights.shape, low),
            jax.ShapeDtypeStruct((halves, model, half_width), low),
            jax.ShapeDtypeStruct((model, tokens), low),
            jax.ShapeDtypeStruct((4, model), wide),
        ],
        in_specs=[
            whole(grads),
            block,
            whole(first_low),
            whole(start),
            whole(middle_grad),
            whole(vectors),
            whole(lead_column),
            whole(back_weight),
            whole(mixed),
        ],
        out_specs=[
            block,
            pl.BlockSpec((halves, model, half_width), lambda i: (0, 0, 0)),
            pl.BlockSpec((model, tokens), lambda i: (0, 0)),
            pl.BlockSpec((4, model), lambda i: (0, 0)),
        ],
        scratch_shapes=[pltpu.VMEM((model, tokens), low), pltpu.VMEM((tokens, model), wide)],
        compiler_params=pltpu.CompilerParams(vmem_limit_bytes=50 * 2**20),
    )(grads, weights, first_low, start, middle_grad, vectors, lead_column, back_weight, mixed)


def einsum(spec, left, right):
    return jnp.einsum(spec, left, right, preferred_element_type=wide)


def fast_local(
    pixels,
    crop_starts,
    crop_shifts,
    slot_crops,
    occupied,
    lead_hours,
    patch_weight,
    variable_embed,
    mixer_query,
    mixer_keys,
    mixer_values,
    mixer_output,
    lead_embed,
    first_gain,
    first_bias,
    attention_in,
    attention_out,
    second_gain,
    second_bias,
    expand_weight,
    expand_bias,
    reduce_weight,
    output_weight,
    cotangent,
):
    lon, head = lax.axis_index(LON), lax.axis_index(HEAD)
    row_count, slot_width = slot_crops.shape
    share = slot_width // HEAD_SIZE
    tokens = row_count * share
    var_count, lat_count, column_count = pixels.shape
    head_half, query_width = mixer_query.shape
    head_count = HEAD_SIZE * head_half
    half_width = head_half * HEAD_DIM
    out_half = output_weight.shape[1]
    slice_width = patch_weight.shape[2]
    model = slice_width * LON_SIZE * HEAD_SIZE
    block_rows = model // LON_SIZE
    taps = 4 * var_count
    pairs = half_width // 128
    scale = HEAD_DIM ** (-0.5)

    last = lax.slice_in_dim(pixels, column_count - 1, column_count, axis=2)
    up = [(i, (i + 1) % LON_SIZE) for i in range(LON_SIZE)]
    down = [(j, i) for i, j in up]
    before = lax.ppermute(last, LON, up)
    after = lax.ppermute(pixels[:, :, :1], LON, down)
    lat_slot = crop_lookup(crop_starts, slot_crops)
    shift_slot = crop_lookup(crop_shifts, slot_crops)
    lat_lanes = jnp.tile(lat_slot, (1, 2))
    shift_lanes = jnp.tile(shift_slot, (1, 2))
    wanted = jnp.arange(2 * 2 * slot_width)
    side, wanted = wanted // (2 * slot_width), wanted % (2 * slot_width)
    wanted = 2 * (wanted % slot_width) + 2 * side + wanted // slot_width - 1
    select = (jnp.arange(column_count)[:, None] == wanted[None, :]).astype(low)
    field = einsum("vac,cn->avn", pixels, select)
    field = field + jnp.where(wanted == -1, jnp.transpose(before, (1, 0, 2)).astype(wide), 0.0)
    field = field + jnp.where(
        wanted == column_count, jnp.transpose(after, (1, 0, 2)).astype(wide), 0.0
    )
    field = field.astype(low)
    pair_rows = row_count // HEAD_SIZE
    cut = cut_patches(
        field,
        block_slice(lat_lanes, head, pair_rows, 0),
        block_slice(shift_lanes, head, pair_rows, 0),
    )
    masked = cotangent * occupied[:, :, None].astype(low)
    masked = jnp.pad(masked, ((0, 0), (0, 0), (0, 128 - out_half)))
    my_crops = block_slice(slot_crops, head, share, 1)
    my_occupied = block_slice(occupied, head, share, 1)

    around = (HEAD, LON)
    up_weight = lax.all_gather(expand_weight, around, axis=0, tiled=True)
    up_weight = up_weight.reshape(HEAD_SIZE, model, -1)
    down_weight = lax.all_gather(reduce_weight.T, around, axis=0, tiled=True)
    down_weight = down_weight.reshape(HEAD_SIZE, model, -1)
    padded = 256
    small = jnp.concatenate(
        [
            jnp.transpose(patch_weight, (1, 0, 2)).reshape(taps, slice_width),
            variable_embed,
            lead_embed,
            first_gain[None],
            first_bias[None],
            second_gain[None],
            second_bias[None],
            jnp.zeros((padded - taps - var_count - 6, slice_width), low),
        ]
    ).T
    small = jnp.concatenate([small[:, :128], small[:, 128:]])
    pieces = [
        jnp.where(my_occupied == 1, my_crops, -1).astype(low).reshape(-1),
        my_crops.astype(low).reshape(-1),
        jnp.pad(mixer_query.reshape(-1), (0, 128 - head_half * query_width)),
        expand_bias.reshape(-1),
    ]
    used = sum(piece.shape[0] for piece in pieces)
    misc = jnp.concatenate(pieces + [jnp.zeros((2048 - used,), low)]).reshape(16, 128)
    out_block = jnp.pad(output_weight, ((0, 0), (0, 128 - out_half)))
    (
        misc_all,
        small_all,
        key_weight,
        value_weight,
        mixer_weight,
        input_weight,
        output_proj,
        final_weight,
        cut,
        masked,
    ) = gather_all(
        [
            misc,
            small,
            mixer_keys,
            mixer_values,
            mixer_output.T,
            attention_in,
            attention_out.T,
            out_block,
        ],
        cut,
        masked,
        1,
    )
    masked = masked.reshape(HEAD_SIZE, tokens, 128)
    misc_all = misc_all.reshape(HEAD_SIZE, LON_SIZE, 2048)
    slots_all = jnp.transpose(
        misc_all[:, :, : 2 * row_count * share].reshape(
            HEAD_SIZE, LON_SIZE, 2, row_count, share
        ),
        (2, 3, 1, 0, 4),
    ).reshape(2, row_count, -1)
    my_row = lax.div(lon, LON_SIZE // row_count)
    my_block = lax.rem(lon, LON_SIZE // row_count) * HEAD_SIZE + head
    slots_row = lax.dynamic_index_in_dim(slots_all, my_row, 1, keepdims=False).astype(wide)
    tag_row, crop_column = slots_row[0:1], slots_row[1][:, None]
    my_slots = block_slice(slots_row, my_block, tokens, 1)
    keep_mask = jnp.where(my_slots[0] >= 0.0, 1.0, 0.0)[:, None]
    my_hours = lax.dynamic_index_in_dim(lead_hours, my_row, 0)
    lead_column = crop_lookup(my_hours, my_slots[1:2].astype(jnp.int32)).astype(wide)
    lead_column = lead_column.reshape(tokens, 1) / 100.0
    at = 2 * row_count * share
    query = jnp.transpose(
        misc_all[:, :, at : at + head_half * query_width].reshape(
            HEAD_SIZE, LON_SIZE, head_half, query_width
        ),
        (0, 2, 1, 3),
    ).reshape(head_count, HEAD_DIM)
    query = query.astype(wide)
    at += 128
    bias_rows = expand_bias.shape[0]
    up_bias = jnp.transpose(
        misc_all[:, :, at : at + expand_bias.size].reshape(HEAD_SIZE, LON_SIZE, bias_rows, -1),
        (0, 2, 1, 3),
    ).reshape(HEAD_SIZE, -1)
    up_bias = up_bias.astype(wide)
    patch_full = jnp.transpose(
        small_all.reshape(HEAD_SIZE, LON_SIZE, 2, slice_width, 128), (1, 0, 3, 2, 4)
    ).reshape(model, padded)
    vectors = patch_full[:, taps + var_count : taps + var_count + 6].T.astype(wide)
    patch_full = jnp.where(jnp.arange(padded)[None, :] < taps + var_count, patch_full, 0)

    key_table = einsum("xde,dm->xem", key_weight, patch_full).reshape(model, padded)
    value_table = einsum("xde,dm->xem", value_weight, patch_full).astype(low).reshape(model, padded)
    score_table = (
        jnp.sum(key_table.reshape(head_count, HEAD_DIM, padded) * query[:, :, None], axis=1) * scale
    )

    patches, probs, mixed = mixer_forward(cut, score_table, value_table)
    start_sum, first_low, projected = project(
        mixed, mixer_weight, lead_column, vectors, input_weight, 1
    )
    units = HEAD_SIZE * pairs
    joint, attended, attended_wide, totals = attend_all(
        projected.reshape(units, 3, tokens, 128), tag_row, crop_column, 3
    )
    attended = attended[None]
    (
        predicted,
        middle_grad,
        out_grads,
        grad_feed,
        grad_proj,
        grad_out,
        grad_up_bias,
        second_vectors,
    ) = feed(
        attended,
        output_proj,
        start_sum,
        vectors,
        up_weight,
        down_weight,
        up_bias.reshape(1, -1),
        final_weight,
        masked,
        keep_mask,
    )
    stacked, feed_sums = attend_back(
        joint,
        tag_row,
        crop_column,
        attended_wide,
        totals,
        out_grads.reshape(units, tokens, 128),
        grad_feed,
        4,
    )
    stacked = stacked[None]
    grad_input, grad_mixer, mixed_grads, first_vectors = go_back(
        stacked,
        input_weight,
        first_low,
        start_sum,
        middle_grad,
        vectors,
        lead_column,
        mixer_weight,
        mixed,
    )
    pooled_grads, counts, cut_grads = mixer_backward(
        patches, probs, score_table, value_table, mixed_grads
    )
    counts = counts * scale
    pooled_low = pooled_grads.astype(low)
    grad_values = dot(patch_full, pooled_low, 1, 1).astype(low)
    key_low = (query[:, :, None] * counts[:, None, :]).astype(low).reshape(model, padded)
    grad_small = einsum(
        "xde,xem->dm", key_weight, key_low.reshape(HEAD_SIZE, half_width, padded)
    ) + einsum("xde,xem->dm", value_weight, pooled_low.reshape(HEAD_SIZE, half_width, padded))
    head_sums = einsum("dm,hm->dh", patch_full.astype(wide), counts)
    grad_query = jnp.sum(
        key_table.reshape(head_count, HEAD_DIM, padded) * counts[:, None, :], axis=2
    )

    vector_grads = jnp.concatenate([first_vectors, second_vectors]).T
    spot = taps + var_count
    grad_small = jnp.concatenate(
        [grad_small[:, :spot], vector_grads, jnp.zeros((model, padded - spot - 6), wide)], axis=1
    )
    grad_small = jnp.transpose(
        grad_small.reshape(LON_SIZE, HEAD_SIZE, slice_width, 2, 128), (0, 3, 2, 1, 4)
    ).reshape(model, HEAD_SIZE, 128)
    head_block = head_sums.reshape(model, HEAD_SIZE, head_half)
    bias_cols = expand_bias.shape[1]
    bias_block = jnp.transpose(
        grad_up_bias.reshape(HEAD_SIZE, bias_rows, LON_SIZE, bias_cols), (2, 1, 0, 3)
    )
    bias_block = jnp.pad(
        bias_block, ((0, 0), (0, block_rows - bias_rows), (0, 0), (0, 0))
    ).reshape(model, HEAD_SIZE, bias_cols)
    query_block = jnp.transpose(
        grad_query.reshape(HEAD_SIZE, head_half, LON_SIZE, query_width), (2, 1, 0, 3)
    )
    query_block = jnp.pad(
        query_block, ((0, 0), (0, block_rows - head_half), (0, 0), (0, 0))
    ).reshape(model, HEAD_SIZE, query_width)
    extra = head_half + bias_cols + query_width
    filler = jnp.zeros((model, 128 - out_half - extra), wide)
    tail = jnp.stack(
        [
            jnp.concatenate(
                [
                    grad_small[:, side],
                    grad_out[side, :, :out_half].astype(wide),
                    head_block[:, side],
                    bias_block[:, side],
                    query_block[:, side],
                    filler,
                ],
                axis=1,
            )
            for side in range(2)
        ]
    ).astype(low)
    sums, predicted, cut_grads = reduce_all(
        [grad_proj, grad_input, grad_mixer, grad_values, tail],
        predicted.reshape(HEAD_SIZE, 2, slot_width, 128),
        cut_grads,
        2,
    )
    predicted = predicted[:, :, :out_half]
    full_half = up_weight.shape[2]
    place = [0]

    def take(width):
        begin = place[0]
        place[0] = begin + width
        return sums[:, begin : begin + width]

    out_up = feed_sums[:, :full_half]
    out_down = feed_sums[:, full_half:].T
    out_proj = take(half_width).T
    out_input = jnp.stack([take(half_width) for _ in range(3)])
    out_mixer = take(half_width).T
    out_values = take(half_width)
    tail_small = take(128)
    tail_rest = take(128)
    tail_small = jnp.concatenate([tail_small[:slice_width], tail_small[slice_width:]], axis=1).T
    out_patch = jnp.transpose(tail_small[:taps].reshape(4, var_count, slice_width), (1, 0, 2))
    out_variable = tail_small[taps:spot]
    out_lead = tail_small[spot : spot + 2]
    out_final = tail_rest[:, :out_half]
    at = out_half
    my_heads = tail_rest[:, at : at + head_half]
    at += head_half
    out_bias = tail_rest[:bias_rows, at : at + bias_cols]
    at += bias_cols
    out_query = tail_rest[:head_half, at : at + query_width]
    my_query = block_slice(query, head, head_half, 0)
    out_keys = (my_heads[:, :, None] * my_query[None]).reshape(block_rows, half_width)

    field_grads = paste_patches(cut_grads, lat_lanes, shift_lanes, lat_count)
    choose = (jnp.arange(column_count + 2)[:, None] - 1 == wanted[None, :]).astype(wide)
    columns = jnp.einsum("avn,cn->vac", field_grads, choose, precision=highest)
    from_west = lax.ppermute(columns[:, :, -1:], LON, up)
    from_east = lax.ppermute(columns[:, :, :1], LON, down)
    spot_at = jnp.arange(column_count)
    pixel_grad = columns[:, :, 1:-1] + jnp.where(spot_at == 0, from_west, 0.0)
    pixel_grad = pixel_grad + jnp.where(spot_at == column_count - 1, from_east, 0.0)
    return (
        predicted,
        pixel_grad,
        out_patch,
        out_variable,
        out_query,
        out_keys,
        out_values,
        out_mixer,
        out_lead,
        tail_small[spot + 2],
        tail_small[spot + 3],
        out_input,
        out_proj,
        tail_small[spot + 4],
        tail_small[spot + 5],
        out_up,
        out_bias,
        out_down,
        out_final,
    )


def solution(mesh):
    body = fast_local if planned(mesh) else local
    placed = (
        P(None, None, LON),
        P(),
        P(),
        P(None, LON),
        P(None, LON),
        P(),
        P(None, None, (LON, HEAD)),
        P(None, (LON, HEAD)),
        P(HEAD, LON),
        P(LON, HEAD),
        P(LON, HEAD),
        P(HEAD, LON),
        P(None, (LON, HEAD)),
        P((LON, HEAD)),
        P((LON, HEAD)),
        P(None, LON, HEAD),
        P(HEAD, LON),
        P((LON, HEAD)),
        P((LON, HEAD)),
        P(LON, HEAD),
        P(HEAD, LON),
        P(HEAD, LON),
        P(LON, HEAD),
        P(None, LON, HEAD),
    )
    return jax.shard_map(
        body,
        mesh=mesh,
        in_specs=placed,
        out_specs=(
            P(None, LON, HEAD),
            P(None, None, LON),
            P(None, None, (LON, HEAD)),
            P(None, (LON, HEAD)),
            P(HEAD, LON),
            P(LON, HEAD),
            P(LON, HEAD),
            P(HEAD, LON),
            P(None, (LON, HEAD)),
            P((LON, HEAD)),
            P((LON, HEAD)),
            P(None, LON, HEAD),
            P(HEAD, LON),
            P((LON, HEAD)),
            P((LON, HEAD)),
            P(LON, HEAD),
            P(HEAD, LON),
            P(HEAD, LON),
            P(LON, HEAD),
        ),
        check_vma=False,
    )
```

```python
from functools import partial

import jax
import jax.numpy as jnp
from jax import lax
from jax.experimental import pallas as pl
from jax.experimental.pallas import tpu as pltpu
from jax.sharding import PartitionSpec as P

HEAD_DIM = 64
LON, HEAD = "lon", "head"


epsilon = 1e-05
masked_score = -1e30
highest = lax.Precision.HIGHEST


def extended(array, sides, width):
    for axis, dim in sides:
        count, length = (lax.axis_size(axis), array.shape[dim])
        up = [(i, (i + 1) % count) for i in range(count)]
        down = [(j, i) for i, j in up]
        last = lax.slice_in_dim(array, length - width, length, axis=dim)
        leading = lax.slice_in_dim(array, 0, width, axis=dim)
        before = lax.ppermute(last, axis, up)
        after = lax.ppermute(leading, axis, down)
        array = jnp.concatenate([before, array, after], axis=dim)
    return array


def layer_norm(values, gain_vector, shift_vector):
    center = values - jnp.mean(values, axis=-1, keepdims=True)
    spread = jnp.mean(center * center, axis=-1, keepdims=True)
    return center * lax.rsqrt(spread + epsilon) * gain_vector + shift_vector


def head_total(partial_sum):
    return lax.psum(partial_sum.astype(jnp.bfloat16), HEAD).astype(jnp.float32)


def head_share(partial_sum):
    return lax.psum_scatter(
        partial_sum.astype(jnp.bfloat16), HEAD, scatter_dimension=0, tiled=True
    ).astype(jnp.float32)


def head_rows(values):
    return lax.all_gather(values, HEAD, axis=0, tiled=True)


def reduce_rows(partial_sum):
    return head_share(partial_sum)


def spread_rows(values):
    return head_rows(values)


def crop_lookup(crop_table, slot_numbers):
    numbers = jnp.arange(crop_table.shape[1], dtype=jnp.int32)
    picked = slot_numbers[:, :, None] == numbers[None, None, :]
    return jnp.sum(jnp.where(picked, crop_table[:, None, :], 0), axis=2)


def outer_sum(left_rows, right_rows):
    return jnp.einsum("ti,tj->ij", left_rows, right_rows, preferred_element_type=jnp.float32)


def block_slice(values, block_index, block_width, axis_number):
    return lax.dynamic_slice_in_dim(values, block_index * block_width, block_width, axis_number)


def block_scores(queries, query_crops, key_block, key_tags):
    scores = jnp.einsum(
        "rqhd,rkhd->rhqk", queries, key_block, preferred_element_type=jnp.float32
    ) * HEAD_DIM ** (-0.5)
    matched = query_crops[:, None, :, None] == key_tags[:, None, None, :]
    return (jnp.where(matched, scores, masked_score), matched)


def key_stats(queries, query_crops, key_rows, key_tags, block_width):
    row_count, slot_count, head_count, head_size = queries.shape

    def key_step(carried, block_index):
        largest, totals = carried
        scores, matched = block_scores(
            queries,
            query_crops,
            block_slice(key_rows, block_index, block_width, 1),
            block_slice(key_tags, block_index, block_width, 1),
        )
        raised = jnp.maximum(largest, jnp.max(scores, axis=-1))
        totals = totals * jnp.exp(largest - raised) + jnp.sum(
            jnp.where(matched, jnp.exp(scores - raised[..., None]), 0.0), axis=-1
        )
        return ((raised, totals), None)

    initial = (
        jnp.full((row_count, head_count, slot_count), masked_score, jnp.float32),
        jnp.zeros((row_count, head_count, slot_count), jnp.float32),
    )
    (largest, totals), _ = lax.scan(key_step, initial, jnp.arange(key_rows.shape[1] // block_width))
    return largest + jnp.log(totals)


def attend(queries, query_crops, key_rows, value_rows, key_tags, log_totals, block_width):

    def attend_step(running, block_index):
        scores, matched = block_scores(
            queries,
            query_crops,
            block_slice(key_rows, block_index, block_width, 1),
            block_slice(key_tags, block_index, block_width, 1),
        )
        weights = jnp.where(matched, jnp.exp(scores - log_totals[..., None]), 0.0).astype(
            jnp.bfloat16
        )
        value_block = block_slice(value_rows, block_index, block_width, 1)
        return (
            running
            + jnp.einsum(
                "rhqk,rkhd->rqhd", weights, value_block, preferred_element_type=jnp.float32
            ),
            None,
        )

    outputs, _ = lax.scan(
        attend_step,
        jnp.zeros(queries.shape, jnp.float32),
        jnp.arange(key_rows.shape[1] // block_width),
    )
    return outputs


def score_grads(
    queries, query_crops, out_grads, log_totals, deltas, key_block, value_block, key_tags
):
    scores, matched = block_scores(queries, query_crops, key_block, key_tags)
    weights = jnp.where(matched, jnp.exp(scores - log_totals[..., None]), 0.0)
    weight_grads = jnp.einsum(
        "rqhd,rkhd->rhqk", out_grads, value_block, preferred_element_type=jnp.float32
    )
    score_delta = (weights * (weight_grads - deltas[..., None])).astype(jnp.bfloat16)
    return (score_delta, weights.astype(jnp.bfloat16))


def mixer_row(patch_row, full_patch, full_variable, pair_weight, head_query):
    embedded = jnp.einsum(
        "svk,vkd->svd", patch_row, full_patch, preferred_element_type=jnp.float32
    ) + full_variable.astype(jnp.float32)
    embedded = embedded.astype(jnp.bfloat16)
    slot_count, var_count, model_width = embedded.shape
    head_count, head_size = head_query.shape
    local_width = head_count * head_size
    paired = jnp.dot(
        embedded.reshape(slot_count * var_count, model_width),
        pair_weight,
        preferred_element_type=jnp.float32,
    ).astype(jnp.bfloat16)
    key_rows = paired[:, :local_width].reshape(slot_count, var_count, head_count, head_size)
    value_rows = paired[:, local_width:].reshape(slot_count, var_count, head_count, head_size)
    scores = jnp.einsum(
        "svhd,hd->shv", key_rows, head_query, preferred_element_type=jnp.float32
    ) * HEAD_DIM ** (-0.5)
    weights = jax.nn.softmax(scores, axis=-1)
    return (embedded, key_rows, value_rows, weights)


def mixer_back(carried, inputs, full_patch, full_variable, pair_weight, head_query):
    patch_row, mixed_grad = inputs
    embedded, key_rows, value_rows, weights = mixer_row(
        patch_row, full_patch, full_variable, pair_weight, head_query
    )
    slot_count, var_count, model_width = embedded.shape
    local_width = key_rows.shape[2] * key_rows.shape[3]
    mixed_wide = mixed_grad.astype(jnp.float32)
    value_grads = jnp.einsum("shv,shd->svhd", weights, mixed_wide, precision=highest).astype(
        jnp.bfloat16
    )
    weight_grads = jnp.einsum(
        "shd,svhd->shv", mixed_wide, value_rows.astype(jnp.float32), precision=highest
    )
    score_delta = (
        weights
        * (weight_grads - jnp.sum(weights * weight_grads, axis=-1, keepdims=True))
        * HEAD_DIM ** (-0.5)
    )
    key_grads = jnp.einsum(
        "shv,hd->svhd", score_delta, head_query.astype(jnp.float32), precision=highest
    ).astype(jnp.bfloat16)
    query_grad = jnp.einsum(
        "shv,svhd->hd", score_delta, key_rows.astype(jnp.float32), precision=highest
    )
    pair_grads = jnp.concatenate(
        [
            key_grads.reshape(slot_count * var_count, local_width),
            value_grads.reshape(slot_count * var_count, local_width),
        ],
        axis=1,
    )
    embed_grad = jnp.einsum(
        "ne,de->nd", pair_grads, pair_weight, preferred_element_type=jnp.float32
    )
    pair_weight_grad = outer_sum(embedded.reshape(slot_count * var_count, model_width), pair_grads)
    embed_grad = embed_grad.reshape(slot_count, var_count, model_width)
    patch_grad = jnp.einsum(
        "svk,svd->vkd", patch_row.astype(jnp.float32), embed_grad, precision=highest
    )
    variable_grad = jnp.sum(embed_grad, axis=0)
    slot_grad = jnp.einsum(
        "svd,vkd->svk", embed_grad, full_patch.astype(jnp.float32), precision=highest
    )
    patch_acc, variable_acc, query_acc, pair_acc = carried
    return (
        (
            patch_acc + patch_grad,
            variable_acc + variable_grad,
            query_acc + query_grad,
            pair_acc + pair_weight_grad,
        ),
        slot_grad,
    )


def local(
    pixels,
    crop_starts,
    crop_shifts,
    slot_crops,
    occupied,
    lead_hours,
    patch_weight,
    variable_embed,
    mixer_query,
    mixer_keys,
    mixer_values,
    mixer_output,
    lead_embed,
    first_gain,
    first_bias,
    attention_in,
    attention_out,
    second_gain,
    second_bias,
    expand_weight,
    expand_bias,
    reduce_weight,
    output_weight,
    cotangent,
):
    shared = (
        lax.all_gather(patch_weight, (LON, HEAD), axis=2, tiled=True),
        lax.all_gather(variable_embed, (LON, HEAD), axis=1, tiled=True),
        lax.all_gather(lead_embed, (LON, HEAD), axis=1, tiled=True),
        lax.all_gather(first_gain, (LON, HEAD), axis=0, tiled=True),
        lax.all_gather(first_bias, (LON, HEAD), axis=0, tiled=True),
        lax.all_gather(second_gain, (LON, HEAD), axis=0, tiled=True),
        lax.all_gather(second_bias, (LON, HEAD), axis=0, tiled=True),
    )
    full_patch, full_variable, full_lead, gain_first, shift_first, gain_second, shift_second = (
        shared
    )
    sector = (
        lax.all_gather(mixer_query, LON, axis=1, tiled=True),
        lax.all_gather(mixer_keys, LON, axis=0, tiled=True),
        lax.all_gather(mixer_values, LON, axis=0, tiled=True),
        lax.all_gather(mixer_output, LON, axis=1, tiled=True),
        lax.all_gather(attention_in, LON, axis=1, tiled=True),
        lax.all_gather(attention_out, LON, axis=1, tiled=True),
        lax.all_gather(expand_weight, LON, axis=0, tiled=True),
        lax.all_gather(expand_bias, LON, axis=1, tiled=True),
        lax.all_gather(reduce_weight, LON, axis=1, tiled=True),
        lax.all_gather(output_weight, LON, axis=0, tiled=True),
    )
    (
        head_query,
        key_weight,
        value_weight,
        mixer_weight,
        input_weight,
        output_proj,
        up_weight,
        up_bias,
        down_weight,
        final_weight,
    ) = sector
    row_count, slot_width = slot_crops.shape
    token_count = row_count * slot_width
    local_width = key_weight.shape[1]
    head_count = local_width // HEAD_DIM
    pair_weight = jnp.concatenate([key_weight, value_weight], axis=1)
    gain_one = gain_first.astype(jnp.float32)
    shift_one = shift_first.astype(jnp.float32)
    gain_two = gain_second.astype(jnp.float32)
    shift_two = shift_second.astype(jnp.float32)
    lat_slot = crop_lookup(crop_starts, slot_crops)
    shift_slot = crop_lookup(crop_shifts, slot_crops)
    lead_slot = crop_lookup(lead_hours, slot_crops).astype(jnp.float32).reshape(token_count) / 100.0
    share_count = token_count // lax.axis_size(HEAD)
    lead_rows = lax.dynamic_slice_in_dim(
        lead_slot, lax.axis_index(HEAD) * share_count, share_count
    )
    padded = extended(pixels, ((LON, 2),), 1)
    var_count, lat_count = (pixels.shape[0], pixels.shape[1])
    west_pairs = padded[:, :, : 2 * slot_width].reshape(var_count, lat_count, slot_width, 2)
    east_pairs = padded[:, :, 2:].reshape(var_count, lat_count, slot_width, 2)
    side_pairs = jnp.stack([west_pairs, east_pairs])
    tables = jnp.stack([side_pairs[:, :, :-1], side_pairs[:, :, 1:]], axis=3)
    lat_index = jnp.arange(lat_count - 1, dtype=jnp.int32)
    side_shift = 2 * jnp.arange(2, dtype=jnp.int32) - 1
    chosen = (lat_slot[:, :, None, None] == lat_index[None, None, None, :]) & (
        shift_slot[:, :, None, None] == side_shift[None, None, :, None]
    )
    patches = jnp.einsum(
        "rjsa,svapjx->rjvpx",
        chosen.astype(jnp.bfloat16),
        tables,
        preferred_element_type=jnp.float32,
    )
    patches = patches.astype(jnp.bfloat16).reshape(row_count, slot_width, var_count, 4)

    def mixer_forward(patch_row):
        embedded, key_rows, value_rows, weights = mixer_row(
            patch_row, full_patch, full_variable, pair_weight, head_query
        )
        return jnp.einsum(
            "shv,svhd->shd", weights, value_rows.astype(jnp.float32), precision=highest
        ).astype(jnp.bfloat16)

    mixed_low = lax.map(mixer_forward, patches).reshape(token_count, local_width)
    start_sum = reduce_rows(jnp.dot(mixed_low, mixer_weight, preferred_element_type=jnp.float32))
    start_sum = (
        start_sum
        + lead_rows[:, None] * full_lead[0].astype(jnp.float32)
        + full_lead[1].astype(jnp.float32)
    )
    first_low = spread_rows(layer_norm(start_sum, gain_one, shift_one).astype(jnp.bfloat16))
    projected = jnp.einsum(
        "td,kde->kte", first_low, input_weight, preferred_element_type=jnp.float32
    ).astype(jnp.bfloat16)
    projected = projected.reshape(3, row_count, slot_width, head_count, HEAD_DIM)
    queries, key_local, value_local = (projected[0], projected[1], projected[2])
    query_crops = slot_crops.astype(jnp.float32)
    key_tags = jnp.where(occupied == 1, slot_crops, -1).astype(jnp.bfloat16)
    key_all, value_all, tag_all = (
        lax.all_gather(key_local, LON, axis=1, tiled=True),
        lax.all_gather(value_local, LON, axis=1, tiled=True),
        lax.all_gather(key_tags, LON, axis=1, tiled=True),
    )
    block_width = min(512, key_all.shape[1])
    tag_wide = tag_all.astype(jnp.float32)
    log_totals = key_stats(queries, query_crops, key_all, tag_wide, block_width)
    attended = attend(queries, query_crops, key_all, value_all, tag_wide, log_totals, block_width)
    attended_low = attended.astype(jnp.bfloat16).reshape(token_count, local_width)
    middle = start_sum + reduce_rows(
        jnp.dot(attended_low, output_proj, preferred_element_type=jnp.float32)
    )
    second_low = spread_rows(layer_norm(middle, gain_two, shift_two).astype(jnp.bfloat16))
    hidden = jnp.dot(second_low, up_weight, preferred_element_type=jnp.float32) + up_bias.reshape(
        -1
    ).astype(jnp.float32)
    active = jax.nn.gelu(hidden, approximate=False).astype(jnp.bfloat16)
    final_sum = middle + reduce_rows(
        jnp.dot(active, down_weight, preferred_element_type=jnp.float32)
    )
    final_low = spread_rows(final_sum.astype(jnp.bfloat16))
    keep_mask = occupied.reshape(token_count, 1)
    predicted = (
        jnp.dot(final_low, final_weight, preferred_element_type=jnp.float32)
        * keep_mask.astype(jnp.float32)
    ).astype(jnp.bfloat16)
    predicted = predicted.reshape(row_count, slot_width, -1)
    masked_grad = (cotangent * occupied[:, :, None].astype(jnp.bfloat16)).reshape(token_count, -1)
    grad_final_weight = outer_sum(final_low, masked_grad)
    part_top = jnp.einsum(
        "to,do->td", masked_grad, final_weight, preferred_element_type=jnp.float32
    )
    final_grad = reduce_rows(part_top)
    final_grad_low = spread_rows(final_grad.astype(jnp.bfloat16))
    grad_down = outer_sum(active, final_grad_low)
    active_grad = jnp.einsum(
        "td,fd->tf", final_grad_low, down_weight, preferred_element_type=jnp.float32
    )
    _, gelu_back = jax.vjp(partial(jax.nn.gelu, approximate=False), hidden)
    hidden_grad = gelu_back(active_grad)[0].astype(jnp.bfloat16)
    grad_up = outer_sum(second_low, hidden_grad)
    grad_up_bias = jnp.sum(hidden_grad.astype(jnp.float32), axis=0).reshape(up_bias.shape)
    second_grad = jnp.einsum(
        "tf,df->td", hidden_grad, up_weight, preferred_element_type=jnp.float32
    )
    second_in = head_share(second_grad)
    _, second_back = jax.vjp(layer_norm, middle, gain_two, shift_two)
    part_mid, grad_gain_two, grad_shift_two = second_back(second_in)
    middle_grad = final_grad + part_mid
    middle_low = spread_rows(middle_grad.astype(jnp.bfloat16))
    grad_proj = outer_sum(attended_low, middle_low)
    out_grads = jnp.einsum(
        "td,ed->te", middle_low, output_proj, preferred_element_type=jnp.float32
    ).astype(jnp.bfloat16)
    out_grads = out_grads.reshape(row_count, slot_width, head_count, HEAD_DIM)
    deltas = jnp.transpose(jnp.sum(out_grads.astype(jnp.float32) * attended, axis=-1), (0, 2, 1))
    back_keys, back_values, back_raw = (
        lax.all_gather(key_local, LON, axis=1, tiled=True),
        lax.all_gather(value_local, LON, axis=1, tiled=True),
        lax.all_gather(key_tags, LON, axis=1, tiled=True),
    )
    back_tags = back_raw.astype(jnp.float32)
    scale = HEAD_DIM ** (-0.5)
    key_count = back_keys.shape[1] // block_width
    local_zeros = jnp.zeros(queries.shape, jnp.float32)
    whole_zeros = jnp.zeros(back_keys.shape, jnp.float32)

    def both_step(running, block_index):
        query_acc, key_acc, value_acc = running
        key_block = block_slice(back_keys, block_index, block_width, 1)
        score_delta, weights_low = score_grads(
            queries,
            query_crops,
            out_grads,
            log_totals,
            deltas,
            key_block,
            block_slice(back_values, block_index, block_width, 1),
            block_slice(back_tags, block_index, block_width, 1),
        )
        query_acc = (
            query_acc
            + jnp.einsum(
                "rhqk,rkhd->rqhd", score_delta, key_block, preferred_element_type=jnp.float32
            )
            * scale
        )
        key_piece = (
            jnp.einsum("rhqk,rqhd->rkhd", score_delta, queries, preferred_element_type=jnp.float32)
            * scale
        )
        value_piece = jnp.einsum(
            "rhqk,rqhd->rkhd", weights_low, out_grads, preferred_element_type=jnp.float32
        )
        key_acc = lax.dynamic_update_slice_in_dim(key_acc, key_piece, block_index * block_width, 1)
        value_acc = lax.dynamic_update_slice_in_dim(
            value_acc, value_piece, block_index * block_width, 1
        )
        return ((query_acc, key_acc, value_acc), None)

    (query_grad, key_part, value_part), _ = lax.scan(
        both_step, (local_zeros, whole_zeros, whole_zeros), jnp.arange(key_count)
    )
    key_grad, value_grad = (
        lax.psum_scatter(
            key_part.astype(jnp.bfloat16), LON, scatter_dimension=1, tiled=True
        ).astype(jnp.float32),
        lax.psum_scatter(
            value_part.astype(jnp.bfloat16), LON, scatter_dimension=1, tiled=True
        ).astype(jnp.float32),
    )
    stacked = (
        jnp.stack([query_grad, key_grad, value_grad])
        .astype(jnp.bfloat16)
        .reshape(3, token_count, local_width)
    )
    first_grad = jnp.einsum(
        "kte,kde->td", stacked, input_weight, preferred_element_type=jnp.float32
    )
    grad_input = jnp.einsum("td,kte->kde", first_low, stacked, preferred_element_type=jnp.float32)
    first_in = head_share(first_grad)
    _, first_back = jax.vjp(layer_norm, start_sum, gain_one, shift_one)
    part_low, grad_gain_one, grad_shift_one = first_back(first_in)
    start_grad = middle_grad + part_low
    grad_lead = jnp.stack(
        [jnp.sum(start_grad * lead_rows[:, None], axis=0), jnp.sum(start_grad, axis=0)]
    )
    start_low = spread_rows(start_grad.astype(jnp.bfloat16))
    grad_mixer = outer_sum(mixed_low, start_low)
    mixed_grad = jnp.einsum(
        "td,ed->te", start_low, mixer_weight, preferred_element_type=jnp.float32
    ).astype(jnp.bfloat16)
    mixed_grad = mixed_grad.reshape(row_count, slot_width, head_count, HEAD_DIM)
    initial = (
        jnp.zeros(full_patch.shape, jnp.float32),
        jnp.zeros(full_variable.shape, jnp.float32),
        jnp.zeros(head_query.shape, jnp.float32),
        jnp.zeros(pair_weight.shape, jnp.float32),
    )
    mixer_step = partial(
        mixer_back,
        full_patch=full_patch,
        full_variable=full_variable,
        pair_weight=pair_weight,
        head_query=head_query,
    )
    (grad_patch, grad_variable, grad_query, grad_pair), slot_grads = lax.scan(
        mixer_step, initial, (patches, mixed_grad)
    )
    slot_total = head_total(slot_grads).reshape(row_count, slot_width, var_count, 2, 2)
    table_grads = jnp.einsum(
        "rjsa,rjvpx->svapjx", chosen.astype(jnp.float32), slot_total, precision=highest
    )
    side_grads = jnp.pad(
        table_grads[:, :, :, 0], ((0, 0), (0, 0), (0, 1), (0, 0), (0, 0))
    ) + jnp.pad(table_grads[:, :, :, 1], ((0, 0), (0, 0), (1, 0), (0, 0), (0, 0)))
    west_grad = side_grads[0].reshape(var_count, lat_count, 2 * slot_width)
    east_grad = side_grads[1].reshape(var_count, lat_count, 2 * slot_width)
    padded_grad = jnp.pad(west_grad, ((0, 0), (0, 0), (0, 2))) + jnp.pad(
        east_grad, ((0, 0), (0, 0), (2, 0))
    )
    rim_values = jnp.stack([padded_grad[:, :, 0], padded_grad[:, :, -1]], axis=2)
    returned = extended(rim_values, ((LON, 2),), 1)
    pixel_grad = (
        padded_grad[:, :, 1:-1]
        + jnp.pad(returned[:, :, 0:1], ((0, 0), (0, 0), (0, 2 * slot_width - 1)))
        + jnp.pad(returned[:, :, 3:4], ((0, 0), (0, 0), (2 * slot_width - 1, 0)))
    )
    sector_out = (
        lax.psum_scatter(
            grad_query.astype(jnp.bfloat16), LON, scatter_dimension=1, tiled=True
        ).astype(jnp.float32),
        lax.psum_scatter(
            grad_pair[:, :local_width].astype(jnp.bfloat16), LON, scatter_dimension=0, tiled=True
        ).astype(jnp.float32),
        lax.psum_scatter(
            grad_pair[:, local_width:].astype(jnp.bfloat16), LON, scatter_dimension=0, tiled=True
        ).astype(jnp.float32),
        lax.psum_scatter(
            grad_mixer.astype(jnp.bfloat16), LON, scatter_dimension=1, tiled=True
        ).astype(jnp.float32),
        lax.psum_scatter(
            grad_input.astype(jnp.bfloat16), LON, scatter_dimension=1, tiled=True
        ).astype(jnp.float32),
        lax.psum_scatter(
            grad_proj.astype(jnp.bfloat16), LON, scatter_dimension=1, tiled=True
        ).astype(jnp.float32),
        lax.psum_scatter(
            grad_up.astype(jnp.bfloat16), LON, scatter_dimension=0, tiled=True
        ).astype(jnp.float32),
        lax.psum_scatter(
            grad_up_bias.astype(jnp.bfloat16), LON, scatter_dimension=1, tiled=True
        ).astype(jnp.float32),
        lax.psum_scatter(
            grad_down.astype(jnp.bfloat16), LON, scatter_dimension=1, tiled=True
        ).astype(jnp.float32),
        lax.psum_scatter(
            grad_final_weight.astype(jnp.bfloat16), LON, scatter_dimension=0, tiled=True
        ).astype(jnp.float32),
    )
    shared_out = (
        lax.psum_scatter(grad_patch, (LON, HEAD), scatter_dimension=2, tiled=True),
        lax.psum_scatter(grad_variable, (LON, HEAD), scatter_dimension=1, tiled=True),
        lax.psum_scatter(grad_lead, (LON, HEAD), scatter_dimension=1, tiled=True),
        lax.psum_scatter(grad_gain_one, (LON, HEAD), scatter_dimension=0, tiled=True),
        lax.psum_scatter(grad_shift_one, (LON, HEAD), scatter_dimension=0, tiled=True),
        lax.psum_scatter(grad_gain_two, (LON, HEAD), scatter_dimension=0, tiled=True),
        lax.psum_scatter(grad_shift_two, (LON, HEAD), scatter_dimension=0, tiled=True),
    )
    return (
        predicted,
        pixel_grad,
        shared_out[0],
        shared_out[1],
        sector_out[0],
        sector_out[1],
        sector_out[2],
        sector_out[3],
        shared_out[2],
        shared_out[3],
        shared_out[4],
        sector_out[4],
        sector_out[5],
        shared_out[5],
        shared_out[6],
        sector_out[6],
        sector_out[7],
        sector_out[8],
        sector_out[9],
    )


MESH = pl.DeviceIdType.MESH
BOTH = (LON, HEAD)
LON_SIZE = 16
HEAD_SIZE = 2
CHUNK = 256
low = jnp.bfloat16
wide = jnp.float32


def planned(mesh):
    return mesh.shape[LON] == LON_SIZE and mesh.shape[HEAD] == HEAD_SIZE


def dot(left, right, left_dim=1, right_dim=0):
    return lax.dot_general(
        left, right, (((left_dim,), (right_dim,)), ((), ())), preferred_element_type=wide
    )


def position():
    lon = lax.axis_index(LON)
    x = lax.axis_index(HEAD)
    z = lax.div(lon, 4)
    y = lax.rem(lax.div(lon, 2), 2)
    c = lax.rem(lon, 2)
    return x, z, y, c


def partners(x, z, y, c):
    here = z * 4 + y * 2 + c
    across = {
        "x": (here, 1 - x),
        "y": (z * 4 + (1 - y) * 2 + c, x),
        "c": (z * 4 + y * 2 + 1 - c, x),
    }
    line = [(lax.rem(z + step, 4) * 4 + y * 2 + c, x) for step in (1, 2, 3)]
    return across, line


def sector_of(z, y, c, x, part, side):
    return (y * 2 + c) * 4 + x * 2 + part, side


def block_of(z, y, row):
    return row * 4 + z, y


def meet(peers, others=(), own=None):
    barrier = pltpu.get_barrier_semaphore()
    for device in peers:
        pl.semaphore_signal(barrier, inc=1, device_id=device, device_id_type=MESH)
    for device in others:

        @pl.when(jnp.logical_not(same(device, own)))
        def _():
            pl.semaphore_signal(barrier, inc=1, device_id=device, device_id_type=MESH)

    expected = len(peers)
    for device in others:
        expected = expected + 1 - same(device, own).astype(jnp.int32)
    pl.semaphore_wait(barrier, expected)


def same(device, own):
    return jnp.logical_and(device[0] == own[0], device[1] == own[1])


def post(source, target, send_sem, recv_sem, device, own):
    here = same(device, own)

    @pl.when(here)
    def _():
        pltpu.make_async_copy(source, target, recv_sem).start()

    @pl.when(jnp.logical_not(here))
    def _():
        remote(source, target, send_sem, recv_sem, device).start()


def settle(source, target, send_sem, recv_sem, device, own):
    @pl.when(jnp.logical_not(same(device, own)))
    def _():
        remote(source, target, send_sem, recv_sem, device).wait_send()


def remote(source, target, send_sem, recv_sem, device):
    return pltpu.make_async_remote_copy(
        src_ref=source,
        dst_ref=target,
        send_sem=send_sem,
        recv_sem=recv_sem,
        device_id=device,
        device_id_type=MESH,
    )


def gather_kernel(items, count, *refs):
    ins, outs = refs[:count], refs[count + 2 : 2 * count + 2]
    patch_in, grad_in = refs[count : count + 2]
    patch_out, grad_out = refs[2 * count + 2 : 2 * count + 4]
    own_sem, line_send, line_recv, hop_send, hop_recv, post_send, post_recv = refs[
        2 * count + 4 :
    ]
    x, z, y, c = position()
    across, line = partners(x, z, y, c)
    own = (z * 4 + y * 2 + c, x)
    sources = [sector_of(z, y, c, x, part, side) for part in range(2) for side in range(2)]
    meet(list(across.values()) + line, sources, own)
    letters = []
    for part in range(2):
        row = 2 * x + part
        letters.append(
            (patch_in.at[part], patch_out.at[c], post_send.at[part], post_recv.at[c])
            + (block_of(z, y, row), own)
        )
    for row in range(4):
        letters.append(
            (grad_in.at[row], grad_out.at[x, c], post_send.at[2 + row])
            + (post_recv.at[2 + 2 * x + c], block_of(z, y, row), own)
        )
    for letter in letters:
        post(*letter)

    def views(item):
        index, lead, first, rows, _ = item
        source, target = ins[index], outs[index]
        if lead is not None:
            source, target = source.at[lead], target.at[lead]
        return source.at[pl.ds(first, rows)], target, pl.ds(first, rows)

    def copies(number):
        item = items[number]
        source, target, span = views(item)
        own = target.at[x, z, y, c, span]
        keep = pltpu.make_async_copy(source, own, own_sem.at[number])
        along = [
            remote(source, own, line_send.at[number, d], line_recv.at[number, d], line[d])
            for d in range(3)
        ]
        quarter = target.at[x, :, y, c, span]
        if item[4] == 0:
            half, order = target.at[x, :, :, c, span], ("y", "x")
        else:
            half, order = target.at[:, :, y, c, span], ("x", "y")
        full = target.at[:, :, :, c, span]
        hops = [
            remote(part, part, hop_send.at[number, k], hop_recv.at[number, k], across[axis])
            for k, (part, axis) in enumerate(
                ((quarter, order[0]), (half, order[1]), (full, "c"))
            )
        ]
        return keep, along, hops

    plan = [copies(number) for number in range(len(items))]
    total = len(items)
    for step in range(total + 8):
        if step < total:
            keep, along, _ = plan[step]
            keep.start()
            for one in along:
                one.start()
        if 0 <= step - 2 < total:
            keep, along, hops = plan[step - 2]
            keep.wait()
            for one in along:
                one.wait_recv()
            hops[0].start()
        if 0 <= step - 4 < total:
            hops = plan[step - 4][2]
            hops[0].wait_recv()
            hops[1].start()
        if 0 <= step - 6 < total:
            hops = plan[step - 6][2]
            hops[1].wait_recv()
            hops[2].start()
        if 0 <= step - 8 < total:
            plan[step - 8][2][2].wait_recv()
    for _, along, hops in plan:
        for one in along + hops:
            one.wait_send()
    for letter in letters:
        settle(*letter)
    for part in range(2):
        pltpu.make_async_copy(patch_in.at[part], patch_out.at[part], post_recv.at[part]).wait()
    for side in range(2):
        for part in range(2):
            pltpu.make_async_copy(
                grad_in.at[0], grad_out.at[side, part], post_recv.at[2 + 2 * side + part]
            ).wait()


def gather_all(arrays, patches, grads, number):
    items = []
    for index, array in enumerate(arrays):
        leads = range(array.shape[0]) if array.ndim == 3 else (None,)
        rows = array.shape[-2]
        for lead in leads:
            if rows >= 64:
                half = rows // 2
                items.append((index, lead, 0, half, 0))
                items.append((index, lead, half, half, 1))
            else:
                items.append((index, lead, 0, rows, 0))
    count = len(arrays)
    shapes = [
        jax.ShapeDtypeStruct(a.shape[:-2] + (2, 4, 2, 2) + a.shape[-2:], a.dtype) for a in arrays
    ] + [
        jax.ShapeDtypeStruct(patches.shape, low),
        jax.ShapeDtypeStruct((2, 2) + grads.shape[1:], low),
    ]
    sem = pltpu.SemaphoreType.DMA
    gathered = pl.pallas_call(
        partial(gather_kernel, items, count),
        out_shape=shapes,
        in_specs=[pl.BlockSpec(memory_space=pl.ANY)] * (count + 2),
        out_specs=[pl.BlockSpec(memory_space=pl.ANY)] * (count + 2),
        scratch_shapes=[
            sem((len(items),)),
            sem((len(items), 3)),
            sem((len(items), 3)),
            sem((len(items), 3)),
            sem((len(items), 3)),
            sem((6,)),
            sem((6,)),
        ],
        compiler_params=pltpu.CompilerParams(collective_id=number, has_side_effects=True),
    )(*arrays, patches, grads)
    return [
        g.reshape(a.shape[:-2] + (2, 16 * a.shape[-2], a.shape[-1]))
        for g, a in zip(gathered, arrays)
    ] + list(gathered[count:])


def reduce_kernel(chunks, count, *refs):
    ins = refs[:count]
    value_in, grad_in, lat_ref, shift_ref = refs[count : count + 4]
    out, value_out, pixel_out = refs[count + 4 : count + 7]
    buffers, sems = refs[count + 7 : count + 13], refs[count + 13 : count + 20]
    grad_out, field, edge, west_edge, east_edge = refs[count + 20 : count + 25]
    value_send, value_recv, grad_send, grad_recv, edge_send, edge_recv = refs[count + 25 :]
    x, z, y, c = position()
    across, line = partners(x, z, y, c)
    lon = z * 4 + y * 2 + c
    own = (lon, x)
    east, west = (lax.rem(lon + 1, 16), x), (lax.rem(lon + 15, 16), x)
    sources = [block_of(z, y, row) for row in range(4)]
    meet(list(across.values()) + line + [east, west], sources, own)
    letters = []
    for part in range(2):
        for side in range(2):
            device = sector_of(z, y, c, x, part, side)
            at = 2 * part + side
            letters.append(
                (value_in.at[side, part], value_out.at[z], value_send.at[at], value_recv.at[z])
                + (device, own)
            )
            letters.append(
                (grad_in.at[part], grad_out.at[z], grad_send.at[at], grad_recv.at[z])
                + (device, own)
            )
    for letter in letters:
        post(*letter)
    total = len(chunks)

    lat_count, var_count, lanes = field.shape
    half = lanes // 2
    column_count = pixel_out.shape[2]

    def paste(row):
        pltpu.make_async_copy(grad_in.at[0], grad_out.at[row], grad_recv.at[row]).wait()
        lat = lat_ref[row : row + 1, :]
        going_west = shift_ref[row : row + 1, :] < 0
        lat_both = jnp.concatenate([lat, lat], axis=1)
        both = []
        for py in range(2):
            k = 2 * py
            grads = jnp.concatenate(
                [
                    grad_out[row, k * var_count : (k + 1) * var_count, :],
                    grad_out[row, (k + 1) * var_count : (k + 2) * var_count, :],
                ],
                axis=1,
            )
            left = jnp.where(going_west, grads, 0.0)
            both.append(jnp.concatenate([left, grads - left], axis=1))

        def body(b, carry):
            piece = jnp.where(lat_both == b, both[0], 0.0) + jnp.where(
                lat_both == b - 1, both[1], 0.0
            )
            if row == 0:
                field[b] = piece
            else:
                field[b] += piece
            return carry

        lax.fori_loop(0, lat_count, body, 0)

    def thirds(values):
        one = values.astype(low)
        rest = values - one.astype(wide)
        two = rest.astype(low)
        return one, two, (rest - two.astype(wide)).astype(low)

    def columns_of(shape, axis):
        spot = lax.broadcasted_iota(jnp.int32, shape, axis)
        side, spot = lax.div(spot, half), lax.rem(spot, half)
        slots = half // 2
        return 2 * lax.rem(spot, slots) + 2 * side + lax.div(spot, slots) - 1

    def edges():
        kind = lax.broadcasted_iota(jnp.int32, (8, lanes), 0)
        wanted = columns_of((8, lanes), 1)
        pick = jnp.where(
            jnp.logical_or(
                jnp.logical_and(kind == 0, wanted == -1),
                jnp.logical_and(kind == 1, wanted == column_count),
            ),
            1.0,
            0.0,
        ).astype(low)
        flat = field[...].reshape(lat_count * var_count, lanes)
        one, two, three = thirds(flat)
        edge[...] = dot(pick, one, 1, 1) + dot(pick, two, 1, 1) + dot(pick, three, 1, 1)
        remote(edge, west_edge, edge_send.at[0], edge_recv.at[0], east).start()
        remote(edge, east_edge, edge_send.at[1], edge_recv.at[1], west).start()

    def pixels():
        remote(edge, west_edge, edge_send.at[0], edge_recv.at[0], east).wait()
        remote(edge, east_edge, edge_send.at[1], edge_recv.at[1], west).wait()
        wanted = columns_of((lanes, column_count), 0)
        column = lax.broadcasted_iota(jnp.int32, (lanes, column_count), 1)
        place = jnp.where(wanted == column, 1.0, 0.0).astype(low)
        kind = lax.broadcasted_iota(jnp.int32, (8, column_count), 0)
        column = lax.broadcasted_iota(jnp.int32, (8, column_count), 1)
        from_west = jnp.logical_and(kind == 1, column == 0)
        from_east = jnp.logical_and(kind == 0, column == column_count - 1)
        west_place = jnp.where(from_west, 1.0, 0.0).astype(low)
        east_place = jnp.where(from_east, 1.0, 0.0).astype(low)
        borders = None
        for values, target in ((west_edge[...], west_place), (east_edge[...], east_place)):
            for part in thirds(values):
                piece = dot(part, target, 0, 0)
                borders = piece if borders is None else borders + piece
        pixel_out[...] = borders.reshape(pixel_out.shape)

        def body(b, carry):
            result = pixel_out[b]
            for part in thirds(field[b]):
                result = result + dot(part, place)
            pixel_out[b] = result
            return carry

        lax.fori_loop(0, lat_count, body, 0)

    extra = {3: lambda: paste(0), 4: lambda: paste(1), 5: lambda: paste(2), 6: lambda: paste(3)}
    extra.update({7: edges, 10: pixels})

    def source_of(pair, color, side, core):
        index, lead, offset = chunks[2 * pair + color][side]
        source = ins[index] if lead is None else ins[index].at[lead]
        return source.at[:, :, core, :, pl.ds(offset, CHUNK)]

    begin, stage_core, stage_first, stage_second, stage_third, finish = reducer(
        source_of, buffers, sems, out
    )
    plan = ((0, begin), (2, stage_core), (4, stage_first), (6, stage_second), (8, stage_third))
    for step in range(total + 8):
        for back, stage in plan:
            if 0 <= step - back < total:
                stage((step - back) // 2, (step - back) % 2)
        if step in extra:
            extra[step]()
    for k in range(total):
        finish(k // 2, k % 2)
    for letter in letters:
        settle(*letter)
    for row in range(4):
        pltpu.make_async_copy(value_in.at[0, 0], value_out.at[row], value_recv.at[row]).wait()


def reduce_all(items, values, grads, lat_lanes, shift_lanes, lat_count, number):
    chunks, views = [], []
    for index, item in enumerate(items):
        rows, columns = item.shape[-2:]
        lead = item.shape[:-2]
        item = item.reshape((-1, 4, 2, 2, rows // 16, columns))
        if not lead:
            views.append(item[0])
            for offset in range(0, columns // 2, CHUNK):
                chunks.append(((index, None, offset), (index, None, columns // 2 + offset)))
            continue
        views.append(item)
        for first in range(0, item.shape[0], 2):
            for offset in range(0, columns, CHUNK):
                chunks.append(((index, first, offset), (index, first + 1, offset)))
    rows = views[0].shape[-2]
    var_count = grads.shape[1] // 4
    lanes = 2 * lat_lanes.shape[1]
    columns = lat_lanes.shape[1]
    vmem = pl.BlockSpec(memory_space=pltpu.VMEM)
    hbm = pl.BlockSpec(memory_space=pl.ANY)
    count, total = len(views), len(chunks)
    sem = pltpu.SemaphoreType.DMA
    return pl.pallas_call(
        partial(reduce_kernel, chunks, count),
        out_shape=[
            jax.ShapeDtypeStruct((rows, total * CHUNK), wide),
            jax.ShapeDtypeStruct((4,) + values.shape[2:], values.dtype),
            jax.ShapeDtypeStruct((lat_count, var_count, columns), wide),
        ],
        in_specs=[hbm] * (count + 2) + [vmem] * 2,
        out_specs=[vmem, hbm, vmem],
        scratch_shapes=reducer_scratch(total, rows)
        + [
            pltpu.VMEM((4,) + grads.shape[1:], wide),
            pltpu.VMEM((lat_count, var_count, lanes), wide),
            pltpu.VMEM((8, lat_count * var_count), wide),
            pltpu.VMEM((8, lat_count * var_count), wide),
            pltpu.VMEM((8, lat_count * var_count), wide),
            sem((4,)),
            sem((4,)),
            sem((4,)),
            sem((4,)),
            sem((2,)),
            sem((2,)),
        ],
        compiler_params=pltpu.CompilerParams(
            collective_id=number, has_side_effects=True, vmem_limit_bytes=60 * 2**20
        ),
    )(*views, values, grads, lat_lanes, shift_lanes)


def diagonal(var_count, columns):
    column = lax.broadcasted_iota(jnp.int32, (var_count, columns), 1)
    row = lax.broadcasted_iota(jnp.int32, (var_count, columns), 0)
    return (lax.rem(column, var_count) == row) & (column < 5 * var_count)


def patch_kernel(field_ref, lat_ref, shift_ref, patch_ref):
    lat_count, var_count, _ = field_ref.shape
    row_count, lanes = lat_ref.shape
    slots = lanes // 2
    for r in range(row_count):
        lat = lat_ref[r : r + 1, :]
        west = shift_ref[r : r + 1, :] < 0

        def body(b, carry):
            top, bottom = carry
            wide_row = field_ref[b].astype(wide)
            chosen = jnp.where(west, wide_row[:, :lanes], wide_row[:, lanes:])
            return (jnp.where(lat == b, chosen, top), jnp.where(lat == b - 1, chosen, bottom))

        zero = jnp.zeros((var_count, lanes), wide)
        rows = lax.fori_loop(0, lat_count, body, (zero, zero), unroll=4)
        for py in range(2):
            for px in range(2):
                k = 2 * py + px
                patch_ref[r, k * var_count : (k + 1) * var_count, :] = rows[py][
                    :, px * slots : (px + 1) * slots
                ].astype(low)


def cut_patches(field, lat_lanes, shift_lanes):
    row_count, lanes = lat_lanes.shape
    return pl.pallas_call(
        patch_kernel,
        out_shape=jax.ShapeDtypeStruct((row_count, 4 * field.shape[1], lanes // 2), low),
    )(field, lat_lanes, shift_lanes)


def mixer_forward_kernel(cut_ref, score_ref, value_ref, patch_ref, prob_ref, mixed_ref):
    head_count, var_count, tokens = prob_ref.shape
    parts, taps, width = cut_ref.shape
    for part in range(parts):
        patch_ref[:taps, part * width : (part + 1) * width] = cut_ref[part]
    patch_ref[taps : taps + var_count, :] = jnp.ones((var_count, tokens), low)
    rest = patch_ref.shape[0] - 5 * var_count
    patch_ref[5 * var_count :, :] = jnp.zeros((rest, tokens), low)
    mask = diagonal(var_count, patch_ref.shape[0])

    def head_step(h, carry):
        spread = jnp.where(mask, score_ref[pl.ds(h, 1), :], 0.0)
        upper = spread.astype(low)
        lower = (spread - upper.astype(wide)).astype(low)
        patch = patch_ref[...]
        scores = dot(upper, patch) + dot(lower, patch)
        raised = jnp.exp(scores - jnp.max(scores, axis=0, keepdims=True))
        prob = raised / jnp.sum(raised, axis=0, keepdims=True)
        prob_ref[h] = prob
        pooled = jnp.concatenate(
            [
                (prob * patch_ref[k * var_count : (k + 1) * var_count, :].astype(wide)).astype(low)
                for k in range(5)
            ]
            + [jnp.zeros((rest, tokens), low)],
            axis=0,
        )
        start = pl.multiple_of(h * HEAD_DIM, HEAD_DIM)
        mixed_ref[pl.ds(start, HEAD_DIM), :] = dot(
            value_ref[pl.ds(start, HEAD_DIM), :], pooled
        ).astype(low)
        return carry

    lax.fori_loop(0, head_count, head_step, 0)


def mixer_forward(cut, score_table, value_table):
    head_count, padded = score_table.shape
    var_count = cut.shape[1] // 4
    tokens = cut.shape[0] * cut.shape[2]
    return pl.pallas_call(
        mixer_forward_kernel,
        out_shape=[
            jax.ShapeDtypeStruct((padded, tokens), low),
            jax.ShapeDtypeStruct((head_count, var_count, tokens), wide),
            jax.ShapeDtypeStruct((head_count * HEAD_DIM, tokens), low),
        ],
        compiler_params=pltpu.CompilerParams(vmem_limit_bytes=40 * 2**20),
    )(cut, score_table, value_table)


def mixer_backward_kernel(
    patch_ref,
    prob_ref,
    score_ref,
    value_ref,
    grad_ref,
    pooled_ref,
    count_ref,
    cut_ref,
    patch_grad_ref,
):
    head_count, var_count, _ = prob_ref.shape
    padded, tokens = patch_ref.shape
    rest = padded - 5 * var_count
    mask = diagonal(var_count, padded)
    patch_grad_ref[...] = jnp.zeros_like(patch_grad_ref)

    def head_step(h, carry):
        start = pl.multiple_of(h * HEAD_DIM, HEAD_DIM)
        grads = grad_ref[pl.ds(start, HEAD_DIM), :]
        prob = prob_ref[h]
        back = dot(value_ref[pl.ds(start, HEAD_DIM), :], grads, 0, 0)
        pieces = [patch_ref[k * var_count : (k + 1) * var_count, :].astype(wide) for k in range(5)]
        backs = [back[k * var_count : (k + 1) * var_count, :] for k in range(5)]
        prob_grad = pieces[0] * backs[0]
        for k in range(1, 5):
            prob_grad = prob_grad + pieces[k] * backs[k]
        mean = jnp.sum(prob * prob_grad, axis=0, keepdims=True)
        delta = prob * (prob_grad - mean)
        upper = delta.astype(low)
        lower = (delta - upper.astype(wide)).astype(low)
        spread = jnp.where(mask, score_ref[pl.ds(h, 1), :], 0.0).astype(low)
        patch_grad_ref[...] += dot(spread, upper, 0, 0)
        for k in range(4):
            patch_grad_ref[k * var_count : (k + 1) * var_count, :] += prob * backs[k]
        patch = patch_ref[...]
        counts = dot(upper, patch, 1, 1) + dot(lower, patch, 1, 1)
        count_ref[pl.ds(h, 1), :] = jnp.sum(jnp.where(mask, counts, 0.0), axis=0, keepdims=True)
        pooled = jnp.concatenate(
            [(prob * piece).astype(low) for piece in pieces] + [jnp.zeros((rest, tokens), low)],
            axis=0,
        )
        pooled_ref[pl.ds(start, HEAD_DIM), :] = dot(grads, pooled, 1, 1)
        return carry

    lax.fori_loop(0, head_count, head_step, 0)
    parts, taps, width = cut_ref.shape
    for part in range(parts):
        cut_ref[part] = patch_grad_ref[:taps, part * width : (part + 1) * width]


def mixer_backward(patches, probs, score_table, value_table, mixed_grads):
    head_count, padded = score_table.shape
    var_count = probs.shape[1]
    tokens = patches.shape[1]
    return pl.pallas_call(
        mixer_backward_kernel,
        out_shape=[
            jax.ShapeDtypeStruct((head_count * HEAD_DIM, padded), wide),
            jax.ShapeDtypeStruct((head_count, padded), wide),
            jax.ShapeDtypeStruct((2, 4 * var_count, tokens // 2), wide),
        ],
        scratch_shapes=[pltpu.VMEM((padded, tokens), wide)],
        compiler_params=pltpu.CompilerParams(vmem_limit_bytes=40 * 2**20),
    )(patches, probs, score_table, value_table, mixed_grads)


def head_lanes(values, h):
    lane = lax.broadcasted_iota(jnp.int32, values.shape, values.ndim - 1)
    inside = lane < HEAD_DIM if h == 0 else lane >= HEAD_DIM
    return jnp.where(inside, values, jnp.zeros_like(values))


def plane_device(z, index):
    return z * 4 + lax.div(index, 2), lax.rem(index, 2)


def plane_meet(x, z, y, c):
    barrier = pltpu.get_barrier_semaphore()
    for flip in range(1, 8):
        there_y = 1 - y if flip & 4 else y
        there_c = 1 - c if flip & 2 else c
        there_x = 1 - x if flip & 1 else x
        device = (z * 4 + there_y * 2 + there_c, there_x)
        pl.semaphore_signal(barrier, inc=1, device_id=device, device_id_type=MESH)
    return barrier


def attend_kernel(
    source,
    tag_ref,
    crop_ref,
    joint,
    received,
    wide_ref,
    total_ref,
    sending,
    own_sem,
    send_sem,
    recv_sem,
    out_own,
    out_send,
    out_recv,
):
    x, z, y, c = position()
    me = y * 4 + c * 2 + x
    peers, kinds, share, lanes = joint.shape
    slots = peers * share
    keep = pltpu.make_async_copy(source.at[me], joint.at[me], own_sem)
    keep.start()
    barrier = plane_meet(x, z, y, c)
    pl.semaphore_wait(barrier, peers - 1)

    def inward(step):
        there = lax.rem(me + step, peers)
        return remote(
            source.at[there],
            joint.at[me],
            send_sem.at[there],
            recv_sem.at[me],
            plane_device(z, there),
        )

    def arrived(index):
        return pltpu.make_async_copy(joint.at[index], joint.at[index], recv_sem.at[index])

    for step in range(1, peers):
        inward(step).start()
    keep.wait()
    for step in range(1, peers):
        arrived(lax.rem(me + step, peers)).wait()

    def block(step, carry):
        index = lax.rem(me + 1 + step, peers)
        span = pl.ds(pl.multiple_of(index * share, share), share)
        queries = joint[index, 0]
        keys = joint[:, 1].reshape(slots, lanes)
        values = joint[:, 2].reshape(slots, lanes)
        allowed = crop_ref[span, :] == tag_ref[...]
        result = None
        for h in range(2):
            scores = dot(head_lanes(queries, h), keys, 1, 1)
            scores = jnp.where(allowed, scores, masked_score)
            largest = jnp.max(scores, axis=1, keepdims=True)
            weights = jnp.exp(scores - largest)
            total = jnp.sum(weights, axis=1, keepdims=True)
            weights = (weights * (1.0 / total)).astype(low)
            part = head_lanes(dot(weights, values), h)
            result = part if result is None else result + part
            total_ref[h, span, :] = largest + jnp.log(total)
        wide_ref[span, :] = result
        sending[index] = result.astype(low)

        @pl.when(step < peers - 1)
        def _():
            outward(index).start()

        return carry

    def outward(index):
        return remote(
            sending.at[index],
            received.at[me],
            out_send.at[index],
            out_recv.at[me],
            plane_device(z, index),
        )

    lax.fori_loop(0, peers, block, 0)
    last = pltpu.make_async_copy(sending.at[me], received.at[me], out_own)
    last.start()
    for step in range(1, peers):
        inward(step).wait_send()
        outward(lax.rem(me + step, peers)).wait_send()
        there = lax.rem(me + step, peers)
        pltpu.make_async_copy(
            sending.at[there], received.at[there], out_recv.at[there]
        ).wait()
    last.wait()


def attend_all(source, tags, crops, number):
    peers, kinds, share, lanes = source.shape
    slots = peers * share
    sem = pltpu.SemaphoreType.DMA
    vmem = pl.BlockSpec(memory_space=pltpu.VMEM)
    hbm = pl.BlockSpec(memory_space=pl.ANY)
    return pl.pallas_call(
        attend_kernel,
        out_shape=[
            jax.ShapeDtypeStruct(source.shape, low),
            jax.ShapeDtypeStruct((peers, share, lanes), low),
            jax.ShapeDtypeStruct((slots, lanes), wide),
            jax.ShapeDtypeStruct((2, slots, 1), wide),
        ],
        in_specs=[hbm, vmem, vmem],
        out_specs=[vmem, hbm, vmem, vmem],
        scratch_shapes=[
            pltpu.VMEM((peers, share, lanes), low),
            sem,
            sem((peers,)),
            sem((peers,)),
            sem,
            sem((peers,)),
            sem((peers,)),
        ],
        compiler_params=pltpu.CompilerParams(
            collective_id=number, has_side_effects=True, vmem_limit_bytes=50 * 2**20
        ),
    )(source, tags, crops)


def joined(left, right):
    return (left.astype(wide) + right.astype(wide)).astype(low)


def reducer(source_of, buffers, sems, out):
    mine, other, first_a, first_b, second, third = buffers
    own_sem, core_send, core_recv, hop_send, hop_recv, line_send, line_recv = sems
    x, z, y, c = position()
    across, line = partners(x, z, y, c)

    def keeps(pair, color):
        k = 2 * pair + color
        return [
            pltpu.make_async_copy(
                source_of(pair, color, side, c), mine.at[2 * k + side], own_sem.at[k, side]
            )
            for side in range(2)
        ]

    def swaps(pair, color):
        k = 2 * pair + color
        return [
            remote(
                source_of(pair, color, side, 1 - c),
                other.at[2 * k + side],
                core_send.at[k, side],
                core_recv.at[k, side],
                across["c"],
            )
            for side in range(2)
        ]

    def hop_one(pair, color):
        k = 2 * pair + color
        if color == 0:
            source, target, axis = mine.at[2 * k + 1 - x], first_a.at[pair], "x"
        else:
            source = mine.at[pl.ds(2 * k, 2), :, 1 - y]
            target, axis = first_b.at[pair], "y"
        return remote(source, target, hop_send.at[k, 0], hop_recv.at[k, 0], across[axis])

    def hop_two(pair, color):
        k = 2 * pair + color
        if color == 0:
            source, axis = mine.at[2 * k + x, :, 1 - y], "y"
        else:
            source, axis = mine.at[2 * k + 1 - x, :, y], "x"
        return remote(source, second.at[k], hop_send.at[k, 1], hop_recv.at[k, 1], across[axis])

    def along(pair, color):
        k = 2 * pair + color
        return [
            remote(
                mine.at[2 * k + x, lax.rem(z + d + 1, 4), y],
                third.at[k, d],
                line_send.at[k, d],
                line_recv.at[k, d],
                line[d],
            )
            for d in range(3)
        ]

    def begin(pair, color):
        for copy in swaps(pair, color) + keeps(pair, color):
            copy.start()

    def stage_core(pair, color):
        k = 2 * pair + color
        for copy in keeps(pair, color):
            copy.wait()
        for copy in swaps(pair, color):
            copy.wait_recv()

        def body(step, carry):
            side, row = lax.div(step, 4), lax.rem(step, 4)
            for part in range(2):
                mine[2 * k + side, row, part] = joined(
                    mine[2 * k + side, row, part], other[2 * k + side, row, part]
                )
            return carry

        lax.fori_loop(0, 8, body, 0)
        hop_one(pair, color).start()

    def stage_first(pair, color):
        k = 2 * pair + color
        hop_one(pair, color).wait_recv()

        def body(row, carry):
            for part in range(2):
                if color == 0:
                    mine[2 * k + x, row, part] = joined(
                        mine[2 * k + x, row, part], first_a[pair, row, part]
                    )
                else:
                    mine[2 * k + part, row, y] = joined(
                        mine[2 * k + part, row, y], first_b[pair, part, row]
                    )
            return carry

        lax.fori_loop(0, 4, body, 0)
        hop_two(pair, color).start()

    def stage_second(pair, color):
        k = 2 * pair + color
        hop_two(pair, color).wait_recv()

        def body(row, carry):
            mine[2 * k + x, row, y] = joined(mine[2 * k + x, row, y], second[k, row])
            return carry

        lax.fori_loop(0, 4, body, 0)
        for copy in along(pair, color):
            copy.start()

    def stage_third(pair, color):
        k = 2 * pair + color
        for copy in along(pair, color):
            copy.wait_recv()
        result = mine[2 * k + x, z, y].astype(wide)
        for d in range(3):
            result = result + third[k, d].astype(wide)
        start = k * CHUNK
        if not isinstance(k, int):
            start = pl.multiple_of(start, CHUNK)
        out[:, pl.ds(start, CHUNK)] = result

    def finish(pair, color):
        hop_one(pair, color).wait_send()
        hop_two(pair, color).wait_send()
        for copy in swaps(pair, color) + along(pair, color):
            copy.wait_send()

    return begin, stage_core, stage_first, stage_second, stage_third, finish


def reducer_scratch(total, rows):
    sem = pltpu.SemaphoreType.DMA
    pairs = (total + 1) // 2
    return [
        pltpu.VMEM((2 * total, 4, 2, rows, CHUNK), low),
        pltpu.VMEM((2 * total, 4, 2, rows, CHUNK), low),
        pltpu.VMEM((pairs, 4, 2, rows, CHUNK), low),
        pltpu.VMEM((pairs, 2, 4, rows, CHUNK), low),
        pltpu.VMEM((total, 4, rows, CHUNK), low),
        pltpu.VMEM((total, 3, rows, CHUNK), low),
    ] + [
        sem((total, 2)),
        sem((total, 2)),
        sem((total, 2)),
        sem((total, 2)),
        sem((total, 2)),
        sem((total, 3)),
        sem((total, 3)),
    ]


def attend_back_kernel(
    joint,
    tag_ref,
    crop_ref,
    out_ref,
    total_ref,
    source,
    feed_ref,
    stacked,
    sums,
    grads,
    result,
    key_acc,
    value_acc,
    *rest
):
    buffers, sems = rest[:6], rest[6:13]
    in_own, in_send, in_recv, back_own, back_send, back_recv = rest[13:]
    x, z, y, c = position()
    across, line = partners(x, z, y, c)
    me = y * 4 + c * 2 + x
    peers, kinds, share, lanes = joint.shape
    slots = peers * share
    scale = HEAD_DIM ** (-0.5)
    each = feed_ref.shape[-1] // CHUNK

    def source_of(pair, color, side, core):
        k = 2 * pair + color
        offset = pl.multiple_of(lax.rem(k, each) * CHUNK, CHUNK)
        return feed_ref.at[lax.div(k, each), side, :, :, core, :, pl.ds(offset, CHUNK)]

    begin, stage_core, stage_first, stage_second, stage_third, finish = reducer(
        source_of, buffers, sems, sums
    )
    keep = pltpu.make_async_copy(source.at[me], grads.at[me], in_own)
    keep.start()
    barrier = plane_meet(x, z, y, c)
    for device in line:
        pl.semaphore_signal(barrier, inc=1, device_id=device, device_id_type=MESH)
    pl.semaphore_wait(barrier, peers - 1 + len(line))

    def inward(there):
        return remote(
            source.at[there],
            grads.at[me],
            in_send.at[there],
            in_recv.at[me],
            plane_device(z, there),
        )

    def outward(there, part):
        span = pl.ds(0, 1) if part == 0 else pl.ds(1, 2)
        return remote(
            result.at[there, span],
            stacked.at[me, span],
            back_send.at[there, part],
            back_recv.at[me, part],
            plane_device(z, there),
        )

    for step in range(1, peers):
        inward(lax.rem(me + step, peers)).start()
    key_acc[...] = jnp.zeros_like(key_acc)
    value_acc[...] = jnp.zeros_like(value_acc)
    pairs = feed_ref.shape[0] * each // 2

    def attention(index):
        span = pl.ds(pl.multiple_of(index * share, share), share)
        queries = joint[index, 0]
        keys = joint[:, 1].reshape(slots, lanes)
        values = joint[:, 2].reshape(slots, lanes)
        grad = grads[index]
        product = grad.astype(wide) * out_ref[span, :]
        allowed = crop_ref[span, :] == tag_ref[...]
        query_grad = None
        for h in range(2):
            query_part, grad_part = head_lanes(queries, h), head_lanes(grad, h)
            scores = jnp.where(allowed, dot(query_part, keys, 1, 1), masked_score)
            weights = jnp.exp(scores - total_ref[h, span, :])
            weight_grads = dot(grad_part, values, 1, 1)
            delta = jnp.sum(head_lanes(product, h), axis=1, keepdims=True)
            score_grads = (weights * (weight_grads - delta)).astype(low)
            weights = weights.astype(low)
            value_acc[...] += dot(grad_part, weights, 0, 0)
            key_acc[...] += dot(query_part, score_grads, 0, 0)
            part = head_lanes(dot(score_grads, keys), h)
            query_grad = part if query_grad is None else query_grad + part
        result[index, 0] = (query_grad * scale).astype(low)

    def step_body(step, carry):
        @pl.when(step < pairs)
        def _():
            begin(step, 0)
            begin(step, 1)

        for back, stage in ((1, stage_core), (2, stage_first), (3, stage_second), (4, stage_third)):

            @pl.when(jnp.logical_and(step >= back, step < pairs + back))
            def _():
                stage(step - back, 0)
                stage(step - back, 1)

        @pl.when(step < peers)
        def _():
            index = lax.rem(me + step, peers)

            @pl.when(step == 0)
            def _():
                keep.wait()

            @pl.when(step > 0)
            def _():
                pltpu.make_async_copy(
                    grads.at[index], grads.at[index], in_recv.at[index]
                ).wait()

            attention(index)

            @pl.when(step > 0)
            def _():
                outward(index, 0).start()

        @pl.when(step == peers - 1)
        def _():
            for index in range(peers):
                span = slice(index * share, (index + 1) * share)
                result[index, 1] = key_acc[:, span].T.astype(low)
                result[index, 2] = value_acc[:, span].T.astype(low)
            for other in range(1, peers):
                outward(lax.rem(me + other, peers), 1).start()
            pltpu.make_async_copy(result.at[me], stacked.at[me], back_own).start()

        return carry

    lax.fori_loop(0, pairs + 4, step_body, 0)

    def finish_body(pair, carry):
        finish(pair, 0)
        finish(pair, 1)
        return carry

    lax.fori_loop(0, pairs, finish_body, 0)
    for step in range(1, peers):
        there = lax.rem(me + step, peers)
        inward(there).wait_send()
        for part in range(2):
            outward(there, part).wait_send()
            span = pl.ds(0, 1) if part == 0 else pl.ds(1, 2)
            pltpu.make_async_copy(
                result.at[there, span], stacked.at[there, span], back_recv.at[there, part]
            ).wait()
    pltpu.make_async_copy(result.at[me], stacked.at[me], back_own).wait()


def attend_back(joint, tags, crops, outputs, totals, source, feed_grads, number):
    peers, kinds, share, lanes = joint.shape
    slots = peers * share
    sides, halves, rows, columns = feed_grads.shape
    total = sides * columns // CHUNK
    sem = pltpu.SemaphoreType.DMA
    vmem = pl.BlockSpec(memory_space=pltpu.VMEM)
    hbm = pl.BlockSpec(memory_space=pl.ANY)
    return pl.pallas_call(
        attend_back_kernel,
        out_shape=[
            jax.ShapeDtypeStruct(joint.shape, low),
            jax.ShapeDtypeStruct((rows // 16, total * CHUNK), wide),
        ],
        in_specs=[vmem] * 5 + [hbm] * 2,
        out_specs=[hbm, vmem],
        scratch_shapes=[
            pltpu.VMEM((peers, share, lanes), low),
            pltpu.VMEM(joint.shape, low),
            pltpu.VMEM((lanes, slots), wide),
            pltpu.VMEM((lanes, slots), wide),
        ]
        + reducer_scratch(total, rows // 16)
        + [
            sem,
            sem((peers,)),
            sem((peers,)),
            sem,
            sem((peers, 2)),
            sem((peers, 2)),
        ],
        compiler_params=pltpu.CompilerParams(
            collective_id=number, has_side_effects=True, vmem_limit_bytes=60 * 2**20
        ),
    )(
        joint,
        tags,
        crops,
        outputs,
        totals,
        source,
        feed_grads.reshape(sides, halves, 4, 2, 2, rows // 16, columns),
    )


def whole(array):
    rank = len(array.shape)
    return pl.BlockSpec(array.shape, lambda *_: (0,) * rank)


def norm_parts(values):
    center = values - jnp.mean(values, axis=-1, keepdims=True)
    inverse = lax.rsqrt(jnp.mean(center * center, axis=-1, keepdims=True) + epsilon)
    return center * inverse, inverse


def norm_back(values, gain, grads):
    normed, inverse = norm_parts(values)
    scaled = grads * gain
    inner = (
        scaled
        - jnp.mean(scaled, axis=-1, keepdims=True)
        - normed * jnp.mean(scaled * normed, axis=-1, keepdims=True)
    )
    return (
        inner * inverse,
        jnp.sum(grads * normed, axis=0, keepdims=True),
        jnp.sum(grads, axis=0, keepdims=True),
    )


def project_kernel(mixed_ref, back_ref, lead_ref, vector_ref, weight_ref, start_ref, low_ref, out_ref):
    step = pl.program_id(0)
    halves, _, half_width = back_ref.shape
    row_count, _, _, share, lanes = out_ref.shape

    @pl.when(step == 0)
    def _():
        total = lead_ref[...] * vector_ref[0:1] + vector_ref[1:2]
        mixed = mixed_ref[...].T
        for side in range(halves):
            total = total + dot(
                mixed[:, side * half_width : (side + 1) * half_width], back_ref[side], 1, 1
            )
        start_ref[...] = total
        normed, _ = norm_parts(total)
        low_ref[...] = (normed * vector_ref[2:3] + vector_ref[3:4]).astype(low)

    kind, side = lax.div(step, halves), lax.rem(step, halves)
    result = dot(low_ref[...], weight_ref[...].reshape(weight_ref.shape[2:])).astype(low)
    result = result * jnp.where(kind == 0, HEAD_DIM ** (-0.5), 1.0).astype(low)
    pairs = half_width // lanes
    for pair in range(pairs):
        out_ref[:, side * pairs + pair, kind] = result[
            :, pair * lanes : (pair + 1) * lanes
        ].reshape(row_count, share, lanes)


def project(mixed, back_weight, lead_column, vectors, weights, row_count):
    model, tokens = mixed.shape
    kinds, halves, _, half_width = weights.shape
    return pl.pallas_call(
        project_kernel,
        grid=(kinds * halves,),
        out_shape=[
            jax.ShapeDtypeStruct((tokens, model), wide),
            jax.ShapeDtypeStruct((tokens, model), low),
            jax.ShapeDtypeStruct(
                (row_count, halves * half_width // 128, kinds, tokens // row_count, 128), low
            ),
        ],
        in_specs=[
            whole(mixed),
            whole(back_weight),
            whole(lead_column),
            whole(vectors),
            pl.BlockSpec((1, 1, model, half_width), lambda i: (i // halves, i % halves, 0, 0)),
        ],
        out_specs=[
            pl.BlockSpec((tokens, model), lambda i: (0, 0)),
            pl.BlockSpec((tokens, model), lambda i: (0, 0)),
            pl.BlockSpec(
                (row_count, halves * half_width // 128, kinds, tokens // row_count, 128),
                lambda i: (0, 0, 0, 0, 0),
            ),
        ],
        compiler_params=pltpu.CompilerParams(vmem_limit_bytes=40 * 2**20),
    )(mixed, back_weight, lead_column, vectors, weights)


def feed_kernel(
    attended_ref,
    proj_ref,
    start_ref,
    vector_ref,
    up_ref,
    down_ref,
    bias_ref,
    final_ref,
    masked_ref,
    keep_ref,
    predicted_ref,
    middle_grad_ref,
    unit_ref,
    grad_feed_ref,
    grad_proj_ref,
    grad_final_ref,
    grad_bias_ref,
    grad_vector_ref,
    flat,
    middle,
    second,
    second_turned,
    active,
    slope,
    total,
    grad_low,
    grad_turned,
    grad_final,
):
    step = pl.program_id(0)
    count = active.shape[0]
    row_count, units, share, lanes = attended_ref.shape
    halves, _, half_width = proj_ref.shape
    tokens = row_count * share

    @pl.when(step == 0)
    def _():
        for unit in range(units):
            flat[:, unit * lanes : (unit + 1) * lanes] = attended_ref[:, unit].reshape(
                tokens, lanes
            )
        result = start_ref[...]
        for side in range(halves):
            result = result + dot(
                flat[:, side * half_width : (side + 1) * half_width], proj_ref[side], 1, 1
            )
        middle[...] = result
        normed, _ = norm_parts(result)
        normed = (normed * vector_ref[4:5] + vector_ref[5:6]).astype(low)
        second[...] = normed
        second_turned[...] = normed.T
        total[...] = result

    @pl.when(step < count)
    def _():
        hidden = dot(second[...], up_ref[0]) + bias_ref[...]
        share_of = 0.5 * (1.0 + lax.erf(hidden * (0.5**0.5)))
        fired = (hidden * share_of).astype(low)
        active[step] = fired
        slope[step] = share_of + hidden * jnp.exp(-0.5 * hidden * hidden) * (
            0.5 / 1.2533141373155003
        )
        total[...] += dot(fired, down_ref[0], 1, 1)

    @pl.when(step == count - 1)
    def _():
        final_low = total[...].astype(low)
        final_turned = final_low.T
        grads = None
        for side in range(halves):
            predicted_ref[side] = (dot(final_low, final_ref[side]) * keep_ref[...]).astype(low)
            part = dot(masked_ref[side], final_ref[side], 1, 1)
            grads = part if grads is None else grads + part
            grad_final_ref[side] = dot(final_turned, masked_ref[side]).astype(low)
        grad_final[...] = grads
        grad_low[...] = grads.astype(low)
        grad_turned[...] = grads.astype(low).T
        total[...] = jnp.zeros_like(total)

    @pl.when(step >= count)
    def _():
        block = step - count
        hidden_grad = dot(grad_low[...], down_ref[0]) * slope[block]
        hidden_low = hidden_grad.astype(low)
        grad_bias_ref[...] = jnp.sum(hidden_low.astype(wide), axis=0, keepdims=True)
        total[...] += dot(hidden_low, up_ref[0], 1, 1)
        grad_feed_ref[0, 0] = dot(second_turned[...], hidden_low).astype(low)
        grad_feed_ref[1, 0] = dot(grad_turned[...], active[block]).astype(low)

    @pl.when(step == 2 * count - 1)
    def _():
        part, grad_gain, grad_shift = norm_back(middle[...], vector_ref[4:5], total[...])
        result = grad_final[...] + part
        middle_grad_ref[...] = result
        grad_vector_ref[0:1] = grad_gain
        grad_vector_ref[1:2] = grad_shift
        result_low = result.astype(low)
        result_turned = result_low.T
        pairs = half_width // lanes
        for side in range(halves):
            span = slice(side * half_width, (side + 1) * half_width)
            grad_proj_ref[side] = dot(result_turned, flat[:, span]).astype(low)
            out = dot(result_low, proj_ref[side]).astype(low)
            for pair in range(pairs):
                unit_ref[:, side * pairs + pair] = out[
                    :, pair * lanes : (pair + 1) * lanes
                ].reshape(row_count, share, lanes)


def feed(attended, proj, start, vectors, up_weight, down_weight, up_bias, final_weight, masked, keep):
    halves, model, full = up_weight.shape
    half_width = proj.shape[2]
    tokens = start.shape[0]
    block = 512
    each = full // block
    count = halves * each

    def block_at(i):
        j = lax.rem(i, count)
        return (lax.div(j, each), 0, lax.rem(j, each))

    def late_block(i):
        j = lax.max(i - count, 0)
        return (0, lax.div(j, each), 0, lax.rem(j, each))

    def fixed(shape, dtype):
        rank = len(shape)
        return jax.ShapeDtypeStruct(shape, dtype), pl.BlockSpec(shape, lambda i: (0,) * rank)

    outs = [
        fixed((halves, tokens, 128), low),
        fixed((tokens, model), wide),
        fixed(attended.shape, low),
        (
            jax.ShapeDtypeStruct((2,) + up_weight.shape, low),
            pl.BlockSpec((2, 1, model, block), late_block),
        ),
        fixed((halves, model, half_width), low),
        fixed((halves, model, 128), low),
        (
            jax.ShapeDtypeStruct((1, halves * full), wide),
            pl.BlockSpec((1, block), lambda i: (0, lax.max(i - count, 0))),
        ),
        fixed((2, model), wide),
    ]
    return pl.pallas_call(
        feed_kernel,
        grid=(2 * count,),
        out_shape=[shape for shape, _ in outs],
        in_specs=[
            whole(attended),
            whole(proj),
            whole(start),
            whole(vectors),
            pl.BlockSpec((1, model, block), block_at),
            pl.BlockSpec((1, model, block), block_at),
            pl.BlockSpec((1, block), lambda i: (0, lax.rem(i, count))),
            whole(final_weight),
            whole(masked),
            whole(keep),
        ],
        out_specs=[spec for _, spec in outs],
        scratch_shapes=[
            pltpu.VMEM((tokens, model), low),
            pltpu.VMEM((tokens, model), wide),
            pltpu.VMEM((tokens, model), low),
            pltpu.VMEM((model, tokens), low),
            pltpu.VMEM((count, tokens, block), low),
            pltpu.VMEM((count, tokens, block), wide),
            pltpu.VMEM((tokens, model), wide),
            pltpu.VMEM((tokens, model), low),
            pltpu.VMEM((model, tokens), low),
            pltpu.VMEM((tokens, model), wide),
        ],
        compiler_params=pltpu.CompilerParams(vmem_limit_bytes=56 * 2**20),
    )(attended, proj, start, vectors, up_weight, down_weight, up_bias, final_weight, masked, keep)


def return_kernel(
    grads_ref,
    weight_ref,
    low_ref,
    start_ref,
    middle_grad_ref,
    vector_ref,
    lead_ref,
    back_ref,
    mixed_ref,
    grad_input_ref,
    grad_mixer_ref,
    mixed_grad_ref,
    grad_vector_ref,
    turned,
    total,
):
    step = pl.program_id(0)
    halves, _, half_width = back_ref.shape
    row_count, _, _, share, lanes = grads_ref.shape
    tokens = row_count * share
    pairs = half_width // lanes

    @pl.when(step == 0)
    def _():
        turned[...] = low_ref[...].T
        total[...] = jnp.zeros_like(total)

    kind, side = lax.div(step, halves), lax.rem(step, halves)
    piece = jnp.concatenate(
        [grads_ref[:, side * pairs + pair, kind].reshape(tokens, lanes) for pair in range(pairs)],
        axis=1,
    )
    total[...] += dot(piece, weight_ref[0, 0], 1, 1)
    grad_input_ref[0, 0] = dot(turned[...], piece).astype(low)

    @pl.when(step == pl.num_programs(0) - 1)
    def _():
        part, grad_gain, grad_shift = norm_back(start_ref[...], vector_ref[2:3], total[...])
        result = middle_grad_ref[...] + part
        grad_vector_ref[0:1] = jnp.sum(result * lead_ref[...], axis=0, keepdims=True)
        grad_vector_ref[1:2] = jnp.sum(result, axis=0, keepdims=True)
        grad_vector_ref[2:3] = grad_gain
        grad_vector_ref[3:4] = grad_shift
        result_low = result.astype(low)
        result_turned = result_low.T
        for half in range(halves):
            span = slice(half * half_width, (half + 1) * half_width)
            grad_mixer_ref[half] = dot(result_turned, mixed_ref[span, :], 1, 1).astype(low)
            mixed_grad_ref[span, :] = dot(result_low, back_ref[half]).astype(low).T


def go_back(grads, weights, first_low, start, middle_grad, vectors, lead_column, back_weight, mixed):
    kinds, halves, model, half_width = weights.shape
    tokens = start.shape[0]
    block = pl.BlockSpec((1, 1, model, half_width), lambda i: (i // halves, i % halves, 0, 0))
    return pl.pallas_call(
        return_kernel,
        grid=(kinds * halves,),
        out_shape=[
            jax.ShapeDtypeStruct(weights.shape, low),
            jax.ShapeDtypeStruct((halves, model, half_width), low),
            jax.ShapeDtypeStruct((model, tokens), low),
            jax.ShapeDtypeStruct((4, model), wide),
        ],
        in_specs=[
            whole(grads),
            block,
            whole(first_low),
            whole(start),
            whole(middle_grad),
            whole(vectors),
            whole(lead_column),
            whole(back_weight),
            whole(mixed),
        ],
        out_specs=[
            block,
            pl.BlockSpec((halves, model, half_width), lambda i: (0, 0, 0)),
            pl.BlockSpec((model, tokens), lambda i: (0, 0)),
            pl.BlockSpec((4, model), lambda i: (0, 0)),
        ],
        scratch_shapes=[pltpu.VMEM((model, tokens), low), pltpu.VMEM((tokens, model), wide)],
        compiler_params=pltpu.CompilerParams(vmem_limit_bytes=50 * 2**20),
    )(grads, weights, first_low, start, middle_grad, vectors, lead_column, back_weight, mixed)


def einsum(spec, left, right):
    return jnp.einsum(spec, left, right, preferred_element_type=wide)


def fast_local(
    pixels,
    crop_starts,
    crop_shifts,
    slot_crops,
    occupied,
    lead_hours,
    patch_weight,
    variable_embed,
    mixer_query,
    mixer_keys,
    mixer_values,
    mixer_output,
    lead_embed,
    first_gain,
    first_bias,
    attention_in,
    attention_out,
    second_gain,
    second_bias,
    expand_weight,
    expand_bias,
    reduce_weight,
    output_weight,
    cotangent,
):
    lon, head = lax.axis_index(LON), lax.axis_index(HEAD)
    row_count, slot_width = slot_crops.shape
    share = slot_width // HEAD_SIZE
    tokens = row_count * share
    var_count, lat_count, column_count = pixels.shape
    head_half, query_width = mixer_query.shape
    head_count = HEAD_SIZE * head_half
    half_width = head_half * HEAD_DIM
    out_half = output_weight.shape[1]
    slice_width = patch_weight.shape[2]
    model = slice_width * LON_SIZE * HEAD_SIZE
    block_rows = model // LON_SIZE
    taps = 4 * var_count
    pairs = half_width // 128
    scale = HEAD_DIM ** (-0.5)

    last = lax.slice_in_dim(pixels, column_count - 1, column_count, axis=2)
    up = [(i, (i + 1) % LON_SIZE) for i in range(LON_SIZE)]
    down = [(j, i) for i, j in up]
    before = lax.ppermute(last, LON, up)
    after = lax.ppermute(pixels[:, :, :1], LON, down)
    lat_slot = crop_lookup(crop_starts, slot_crops)
    shift_slot = crop_lookup(crop_shifts, slot_crops)
    lat_lanes = jnp.tile(lat_slot, (1, 2))
    shift_lanes = jnp.tile(shift_slot, (1, 2))
    wanted = jnp.arange(2 * 2 * slot_width)
    side, wanted = wanted // (2 * slot_width), wanted % (2 * slot_width)
    wanted = 2 * (wanted % slot_width) + 2 * side + wanted // slot_width - 1
    select = (jnp.arange(column_count)[:, None] == wanted[None, :]).astype(low)
    field = einsum("vac,cn->avn", pixels, select)
    field = field + jnp.where(wanted == -1, jnp.transpose(before, (1, 0, 2)).astype(wide), 0.0)
    field = field + jnp.where(
        wanted == column_count, jnp.transpose(after, (1, 0, 2)).astype(wide), 0.0
    )
    field = field.astype(low)
    pair_rows = row_count // HEAD_SIZE
    cut = cut_patches(
        field,
        block_slice(lat_lanes, head, pair_rows, 0),
        block_slice(shift_lanes, head, pair_rows, 0),
    )
    masked = cotangent * occupied[:, :, None].astype(low)
    masked = jnp.pad(masked, ((0, 0), (0, 0), (0, 128 - out_half)))
    my_crops = block_slice(slot_crops, head, share, 1)
    my_occupied = block_slice(occupied, head, share, 1)

    around = (HEAD, LON)
    up_weight = lax.all_gather(expand_weight, around, axis=0, tiled=True)
    up_weight = up_weight.reshape(HEAD_SIZE, model, -1)
    down_weight = lax.all_gather(reduce_weight.T, around, axis=0, tiled=True)
    down_weight = down_weight.reshape(HEAD_SIZE, model, -1)
    padded = 256
    small = jnp.concatenate(
        [
            jnp.transpose(patch_weight, (1, 0, 2)).reshape(taps, slice_width),
            variable_embed,
            lead_embed,
            first_gain[None],
            first_bias[None],
            second_gain[None],
            second_bias[None],
            jnp.zeros((padded - taps - var_count - 6, slice_width), low),
        ]
    ).T
    small = jnp.concatenate([small[:, :128], small[:, 128:]])
    pieces = [
        jnp.where(my_occupied == 1, my_crops, -1).astype(low).reshape(-1),
        my_crops.astype(low).reshape(-1),
        jnp.pad(mixer_query.reshape(-1), (0, 128 - head_half * query_width)),
        expand_bias.reshape(-1),
    ]
    used = sum(piece.shape[0] for piece in pieces)
    misc = jnp.concatenate(pieces + [jnp.zeros((2048 - used,), low)]).reshape(16, 128)
    out_block = jnp.pad(output_weight, ((0, 0), (0, 128 - out_half)))
    (
        misc_all,
        small_all,
        key_weight,
        value_weight,
        mixer_weight,
        input_weight,
        output_proj,
        final_weight,
        cut,
        masked,
    ) = gather_all(
        [
            misc,
            small,
            mixer_keys,
            mixer_values,
            mixer_output.T,
            attention_in,
            attention_out.T,
            out_block,
        ],
        cut,
        masked,
        1,
    )
    masked = masked.reshape(HEAD_SIZE, tokens, 128)
    misc_all = misc_all.reshape(HEAD_SIZE, LON_SIZE, 2048)
    slots_all = jnp.transpose(
        misc_all[:, :, : 2 * row_count * share].reshape(
            HEAD_SIZE, LON_SIZE, 2, row_count, share
        ),
        (2, 3, 1, 0, 4),
    ).reshape(2, row_count, -1)
    my_row = lax.div(lon, LON_SIZE // row_count)
    my_block = lax.rem(lon, LON_SIZE // row_count) * HEAD_SIZE + head
    slots_row = lax.dynamic_index_in_dim(slots_all, my_row, 1, keepdims=False).astype(wide)
    tag_row, crop_column = slots_row[0:1], slots_row[1][:, None]
    my_slots = block_slice(slots_row, my_block, tokens, 1)
    keep_mask = jnp.where(my_slots[0] >= 0.0, 1.0, 0.0)[:, None]
    my_hours = lax.dynamic_index_in_dim(lead_hours, my_row, 0)
    lead_column = crop_lookup(my_hours, my_slots[1:2].astype(jnp.int32)).astype(wide)
    lead_column = lead_column.reshape(tokens, 1) / 100.0
    at = 2 * row_count * share
    query = jnp.transpose(
        misc_all[:, :, at : at + head_half * query_width].reshape(
            HEAD_SIZE, LON_SIZE, head_half, query_width
        ),
        (0, 2, 1, 3),
    ).reshape(head_count, HEAD_DIM)
    query = query.astype(wide)
    at += 128
    bias_rows = expand_bias.shape[0]
    up_bias = jnp.transpose(
        misc_all[:, :, at : at + expand_bias.size].reshape(HEAD_SIZE, LON_SIZE, bias_rows, -1),
        (0, 2, 1, 3),
    ).reshape(HEAD_SIZE, -1)
    up_bias = up_bias.astype(wide)
    patch_full = jnp.transpose(
        small_all.reshape(HEAD_SIZE, LON_SIZE, 2, slice_width, 128), (1, 0, 3, 2, 4)
    ).reshape(model, padded)
    vectors = patch_full[:, taps + var_count : taps + var_count + 6].T.astype(wide)
    patch_full = jnp.where(jnp.arange(padded)[None, :] < taps + var_count, patch_full, 0)

    key_table = einsum("xde,dm->xem", key_weight, patch_full).reshape(model, padded)
    value_table = einsum("xde,dm->xem", value_weight, patch_full).astype(low).reshape(model, padded)
    score_table = (
        jnp.sum(key_table.reshape(head_count, HEAD_DIM, padded) * query[:, :, None], axis=1) * scale
    )

    patches, probs, mixed = mixer_forward(cut, score_table, value_table)
    start_sum, first_low, projected = project(
        mixed, mixer_weight, lead_column, vectors, input_weight, 1
    )
    units = HEAD_SIZE * pairs
    joint, attended, attended_wide, totals = attend_all(
        projected.reshape(units, 3, tokens, 128), tag_row, crop_column, 3
    )
    attended = attended[None]
    (
        predicted,
        middle_grad,
        out_grads,
        grad_feed,
        grad_proj,
        grad_out,
        grad_up_bias,
        second_vectors,
    ) = feed(
        attended,
        output_proj,
        start_sum,
        vectors,
        up_weight,
        down_weight,
        up_bias.reshape(1, -1),
        final_weight,
        masked,
        keep_mask,
    )
    stacked, feed_sums = attend_back(
        joint,
        tag_row,
        crop_column,
        attended_wide,
        totals,
        out_grads.reshape(units, tokens, 128),
        grad_feed,
        4,
    )
    stacked = stacked[None]
    grad_input, grad_mixer, mixed_grads, first_vectors = go_back(
        stacked,
        input_weight,
        first_low,
        start_sum,
        middle_grad,
        vectors,
        lead_column,
        mixer_weight,
        mixed,
    )
    pooled_grads, counts, cut_grads = mixer_backward(
        patches, probs, score_table, value_table, mixed_grads
    )
    counts = counts * scale
    pooled_low = pooled_grads.astype(low)
    grad_values = dot(patch_full, pooled_low, 1, 1).astype(low)
    key_low = (query[:, :, None] * counts[:, None, :]).astype(low).reshape(model, padded)
    grad_small = einsum(
        "xde,xem->dm", key_weight, key_low.reshape(HEAD_SIZE, half_width, padded)
    ) + einsum("xde,xem->dm", value_weight, pooled_low.reshape(HEAD_SIZE, half_width, padded))
    head_sums = einsum("dm,hm->dh", patch_full.astype(wide), counts)
    grad_query = jnp.sum(
        key_table.reshape(head_count, HEAD_DIM, padded) * counts[:, None, :], axis=2
    )

    vector_grads = jnp.concatenate([first_vectors, second_vectors]).T
    spot = taps + var_count
    grad_small = jnp.concatenate(
        [grad_small[:, :spot], vector_grads, jnp.zeros((model, padded - spot - 6), wide)], axis=1
    )
    grad_small = jnp.transpose(
        grad_small.reshape(LON_SIZE, HEAD_SIZE, slice_width, 2, 128), (0, 3, 2, 1, 4)
    ).reshape(model, HEAD_SIZE, 128)
    head_block = head_sums.reshape(model, HEAD_SIZE, head_half)
    bias_cols = expand_bias.shape[1]
    bias_block = jnp.transpose(
        grad_up_bias.reshape(HEAD_SIZE, bias_rows, LON_SIZE, bias_cols), (2, 1, 0, 3)
    )
    bias_block = jnp.pad(
        bias_block, ((0, 0), (0, block_rows - bias_rows), (0, 0), (0, 0))
    ).reshape(model, HEAD_SIZE, bias_cols)
    query_block = jnp.transpose(
        grad_query.reshape(HEAD_SIZE, head_half, LON_SIZE, query_width), (2, 1, 0, 3)
    )
    query_block = jnp.pad(
        query_block, ((0, 0), (0, block_rows - head_half), (0, 0), (0, 0))
    ).reshape(model, HEAD_SIZE, query_width)
    extra = head_half + bias_cols + query_width
    filler = jnp.zeros((model, 128 - out_half - extra), wide)
    tail = jnp.stack(
        [
            jnp.concatenate(
                [
                    grad_small[:, side],
                    grad_out[side, :, :out_half].astype(wide),
                    head_block[:, side],
                    bias_block[:, side],
                    query_block[:, side],
                    filler,
                ],
                axis=1,
            )
            for side in range(2)
        ]
    ).astype(low)
    sums, predicted, pixel_grad = reduce_all(
        [grad_proj, grad_input, grad_mixer, grad_values, tail],
        predicted.reshape(HEAD_SIZE, 2, slot_width, 128),
        cut_grads,
        lat_lanes,
        shift_lanes,
        lat_count,
        2,
    )
    predicted = predicted[:, :, :out_half]
    full_half = up_weight.shape[2]
    place = [0]

    def take(width):
        begin = place[0]
        place[0] = begin + width
        return sums[:, begin : begin + width]

    out_up = feed_sums[:, :full_half]
    out_down = feed_sums[:, full_half:].T
    out_proj = take(half_width).T
    out_input = jnp.stack([take(half_width) for _ in range(3)])
    out_mixer = take(half_width).T
    out_values = take(half_width)
    tail_small = take(128)
    tail_rest = take(128)
    tail_small = jnp.concatenate([tail_small[:slice_width], tail_small[slice_width:]], axis=1).T
    out_patch = jnp.transpose(tail_small[:taps].reshape(4, var_count, slice_width), (1, 0, 2))
    out_variable = tail_small[taps:spot]
    out_lead = tail_small[spot : spot + 2]
    out_final = tail_rest[:, :out_half]
    at = out_half
    my_heads = tail_rest[:, at : at + head_half]
    at += head_half
    out_bias = tail_rest[:bias_rows, at : at + bias_cols]
    at += bias_cols
    out_query = tail_rest[:head_half, at : at + query_width]
    my_query = block_slice(query, head, head_half, 0)
    out_keys = (my_heads[:, :, None] * my_query[None]).reshape(block_rows, half_width)

    pixel_grad = jnp.transpose(pixel_grad, (1, 0, 2))
    return (
        predicted,
        pixel_grad,
        out_patch,
        out_variable,
        out_query,
        out_keys,
        out_values,
        out_mixer,
        out_lead,
        tail_small[spot + 2],
        tail_small[spot + 3],
        out_input,
        out_proj,
        tail_small[spot + 4],
        tail_small[spot + 5],
        out_up,
        out_bias,
        out_down,
        out_final,
    )


def solution(mesh):
    body = fast_local if planned(mesh) else local
    placed = (
        P(None, None, LON),
        P(),
        P(),
        P(None, LON),
        P(None, LON),
        P(),
        P(None, None, (LON, HEAD)),
        P(None, (LON, HEAD)),
        P(HEAD, LON),
        P(LON, HEAD),
        P(LON, HEAD),
        P(HEAD, LON),
        P(None, (LON, HEAD)),
        P((LON, HEAD)),
        P((LON, HEAD)),
        P(None, LON, HEAD),
        P(HEAD, LON),
        P((LON, HEAD)),
        P((LON, HEAD)),
        P(LON, HEAD),
        P(HEAD, LON),
        P(HEAD, LON),
        P(LON, HEAD),
        P(None, LON, HEAD),
    )
    return jax.shard_map(
        body,
        mesh=mesh,
        in_specs=placed,
        out_specs=(
            P(None, LON, HEAD),
            P(None, None, LON),
            P(None, None, (LON, HEAD)),
            P(None, (LON, HEAD)),
            P(HEAD, LON),
            P(LON, HEAD),
            P(LON, HEAD),
            P(HEAD, LON),
            P(None, (LON, HEAD)),
            P((LON, HEAD)),
            P((LON, HEAD)),
            P(None, LON, HEAD),
            P(HEAD, LON),
            P((LON, HEAD)),
            P((LON, HEAD)),
            P(LON, HEAD),
            P(HEAD, LON),
            P(HEAD, LON),
            P(LON, HEAD),
        ),
        check_vma=False,
    )
```

```python
from functools import partial

import jax
import jax.numpy as jnp
from jax import lax
from jax.experimental import pallas as pl
from jax.experimental.pallas import tpu as pltpu
from jax.sharding import PartitionSpec as P

HEAD_DIM = 64
LON, HEAD = "lon", "head"


epsilon = 1e-05
masked_score = -1e30
highest = lax.Precision.HIGHEST


def extended(array, sides, width):
    for axis, dim in sides:
        count, length = (lax.axis_size(axis), array.shape[dim])
        up = [(i, (i + 1) % count) for i in range(count)]
        down = [(j, i) for i, j in up]
        last = lax.slice_in_dim(array, length - width, length, axis=dim)
        leading = lax.slice_in_dim(array, 0, width, axis=dim)
        before = lax.ppermute(last, axis, up)
        after = lax.ppermute(leading, axis, down)
        array = jnp.concatenate([before, array, after], axis=dim)
    return array


def layer_norm(values, gain_vector, shift_vector):
    center = values - jnp.mean(values, axis=-1, keepdims=True)
    spread = jnp.mean(center * center, axis=-1, keepdims=True)
    return center * lax.rsqrt(spread + epsilon) * gain_vector + shift_vector


def head_total(partial_sum):
    return lax.psum(partial_sum.astype(jnp.bfloat16), HEAD).astype(jnp.float32)


def head_share(partial_sum):
    return lax.psum_scatter(
        partial_sum.astype(jnp.bfloat16), HEAD, scatter_dimension=0, tiled=True
    ).astype(jnp.float32)


def head_rows(values):
    return lax.all_gather(values, HEAD, axis=0, tiled=True)


def reduce_rows(partial_sum):
    return head_share(partial_sum)


def spread_rows(values):
    return head_rows(values)


def crop_lookup(crop_table, slot_numbers):
    numbers = jnp.arange(crop_table.shape[1], dtype=jnp.int32)
    picked = slot_numbers[:, :, None] == numbers[None, None, :]
    return jnp.sum(jnp.where(picked, crop_table[:, None, :], 0), axis=2)


def outer_sum(left_rows, right_rows):
    return jnp.einsum("ti,tj->ij", left_rows, right_rows, preferred_element_type=jnp.float32)


def block_slice(values, block_index, block_width, axis_number):
    return lax.dynamic_slice_in_dim(values, block_index * block_width, block_width, axis_number)


def block_scores(queries, query_crops, key_block, key_tags):
    scores = jnp.einsum(
        "rqhd,rkhd->rhqk", queries, key_block, preferred_element_type=jnp.float32
    ) * HEAD_DIM ** (-0.5)
    matched = query_crops[:, None, :, None] == key_tags[:, None, None, :]
    return (jnp.where(matched, scores, masked_score), matched)


def key_stats(queries, query_crops, key_rows, key_tags, block_width):
    row_count, slot_count, head_count, head_size = queries.shape

    def key_step(carried, block_index):
        largest, totals = carried
        scores, matched = block_scores(
            queries,
            query_crops,
            block_slice(key_rows, block_index, block_width, 1),
            block_slice(key_tags, block_index, block_width, 1),
        )
        raised = jnp.maximum(largest, jnp.max(scores, axis=-1))
        totals = totals * jnp.exp(largest - raised) + jnp.sum(
            jnp.where(matched, jnp.exp(scores - raised[..., None]), 0.0), axis=-1
        )
        return ((raised, totals), None)

    initial = (
        jnp.full((row_count, head_count, slot_count), masked_score, jnp.float32),
        jnp.zeros((row_count, head_count, slot_count), jnp.float32),
    )
    (largest, totals), _ = lax.scan(key_step, initial, jnp.arange(key_rows.shape[1] // block_width))
    return largest + jnp.log(totals)


def attend(queries, query_crops, key_rows, value_rows, key_tags, log_totals, block_width):

    def attend_step(running, block_index):
        scores, matched = block_scores(
            queries,
            query_crops,
            block_slice(key_rows, block_index, block_width, 1),
            block_slice(key_tags, block_index, block_width, 1),
        )
        weights = jnp.where(matched, jnp.exp(scores - log_totals[..., None]), 0.0).astype(
            jnp.bfloat16
        )
        value_block = block_slice(value_rows, block_index, block_width, 1)
        return (
            running
            + jnp.einsum(
                "rhqk,rkhd->rqhd", weights, value_block, preferred_element_type=jnp.float32
            ),
            None,
        )

    outputs, _ = lax.scan(
        attend_step,
        jnp.zeros(queries.shape, jnp.float32),
        jnp.arange(key_rows.shape[1] // block_width),
    )
    return outputs


def score_grads(
    queries, query_crops, out_grads, log_totals, deltas, key_block, value_block, key_tags
):
    scores, matched = block_scores(queries, query_crops, key_block, key_tags)
    weights = jnp.where(matched, jnp.exp(scores - log_totals[..., None]), 0.0)
    weight_grads = jnp.einsum(
        "rqhd,rkhd->rhqk", out_grads, value_block, preferred_element_type=jnp.float32
    )
    score_delta = (weights * (weight_grads - deltas[..., None])).astype(jnp.bfloat16)
    return (score_delta, weights.astype(jnp.bfloat16))


def mixer_row(patch_row, full_patch, full_variable, pair_weight, head_query):
    embedded = jnp.einsum(
        "svk,vkd->svd", patch_row, full_patch, preferred_element_type=jnp.float32
    ) + full_variable.astype(jnp.float32)
    embedded = embedded.astype(jnp.bfloat16)
    slot_count, var_count, model_width = embedded.shape
    head_count, head_size = head_query.shape
    local_width = head_count * head_size
    paired = jnp.dot(
        embedded.reshape(slot_count * var_count, model_width),
        pair_weight,
        preferred_element_type=jnp.float32,
    ).astype(jnp.bfloat16)
    key_rows = paired[:, :local_width].reshape(slot_count, var_count, head_count, head_size)
    value_rows = paired[:, local_width:].reshape(slot_count, var_count, head_count, head_size)
    scores = jnp.einsum(
        "svhd,hd->shv", key_rows, head_query, preferred_element_type=jnp.float32
    ) * HEAD_DIM ** (-0.5)
    weights = jax.nn.softmax(scores, axis=-1)
    return (embedded, key_rows, value_rows, weights)


def mixer_back(carried, inputs, full_patch, full_variable, pair_weight, head_query):
    patch_row, mixed_grad = inputs
    embedded, key_rows, value_rows, weights = mixer_row(
        patch_row, full_patch, full_variable, pair_weight, head_query
    )
    slot_count, var_count, model_width = embedded.shape
    local_width = key_rows.shape[2] * key_rows.shape[3]
    mixed_wide = mixed_grad.astype(jnp.float32)
    value_grads = jnp.einsum("shv,shd->svhd", weights, mixed_wide, precision=highest).astype(
        jnp.bfloat16
    )
    weight_grads = jnp.einsum(
        "shd,svhd->shv", mixed_wide, value_rows.astype(jnp.float32), precision=highest
    )
    score_delta = (
        weights
        * (weight_grads - jnp.sum(weights * weight_grads, axis=-1, keepdims=True))
        * HEAD_DIM ** (-0.5)
    )
    key_grads = jnp.einsum(
        "shv,hd->svhd", score_delta, head_query.astype(jnp.float32), precision=highest
    ).astype(jnp.bfloat16)
    query_grad = jnp.einsum(
        "shv,svhd->hd", score_delta, key_rows.astype(jnp.float32), precision=highest
    )
    pair_grads = jnp.concatenate(
        [
            key_grads.reshape(slot_count * var_count, local_width),
            value_grads.reshape(slot_count * var_count, local_width),
        ],
        axis=1,
    )
    embed_grad = jnp.einsum(
        "ne,de->nd", pair_grads, pair_weight, preferred_element_type=jnp.float32
    )
    pair_weight_grad = outer_sum(embedded.reshape(slot_count * var_count, model_width), pair_grads)
    embed_grad = embed_grad.reshape(slot_count, var_count, model_width)
    patch_grad = jnp.einsum(
        "svk,svd->vkd", patch_row.astype(jnp.float32), embed_grad, precision=highest
    )
    variable_grad = jnp.sum(embed_grad, axis=0)
    slot_grad = jnp.einsum(
        "svd,vkd->svk", embed_grad, full_patch.astype(jnp.float32), precision=highest
    )
    patch_acc, variable_acc, query_acc, pair_acc = carried
    return (
        (
            patch_acc + patch_grad,
            variable_acc + variable_grad,
            query_acc + query_grad,
            pair_acc + pair_weight_grad,
        ),
        slot_grad,
    )


def local(
    pixels,
    crop_starts,
    crop_shifts,
    slot_crops,
    occupied,
    lead_hours,
    patch_weight,
    variable_embed,
    mixer_query,
    mixer_keys,
    mixer_values,
    mixer_output,
    lead_embed,
    first_gain,
    first_bias,
    attention_in,
    attention_out,
    second_gain,
    second_bias,
    expand_weight,
    expand_bias,
    reduce_weight,
    output_weight,
    cotangent,
):
    shared = (
        lax.all_gather(patch_weight, (LON, HEAD), axis=2, tiled=True),
        lax.all_gather(variable_embed, (LON, HEAD), axis=1, tiled=True),
        lax.all_gather(lead_embed, (LON, HEAD), axis=1, tiled=True),
        lax.all_gather(first_gain, (LON, HEAD), axis=0, tiled=True),
        lax.all_gather(first_bias, (LON, HEAD), axis=0, tiled=True),
        lax.all_gather(second_gain, (LON, HEAD), axis=0, tiled=True),
        lax.all_gather(second_bias, (LON, HEAD), axis=0, tiled=True),
    )
    full_patch, full_variable, full_lead, gain_first, shift_first, gain_second, shift_second = (
        shared
    )
    sector = (
        lax.all_gather(mixer_query, LON, axis=1, tiled=True),
        lax.all_gather(mixer_keys, LON, axis=0, tiled=True),
        lax.all_gather(mixer_values, LON, axis=0, tiled=True),
        lax.all_gather(mixer_output, LON, axis=1, tiled=True),
        lax.all_gather(attention_in, LON, axis=1, tiled=True),
        lax.all_gather(attention_out, LON, axis=1, tiled=True),
        lax.all_gather(expand_weight, LON, axis=0, tiled=True),
        lax.all_gather(expand_bias, LON, axis=1, tiled=True),
        lax.all_gather(reduce_weight, LON, axis=1, tiled=True),
        lax.all_gather(output_weight, LON, axis=0, tiled=True),
    )
    (
        head_query,
        key_weight,
        value_weight,
        mixer_weight,
        input_weight,
        output_proj,
        up_weight,
        up_bias,
        down_weight,
        final_weight,
    ) = sector
    row_count, slot_width = slot_crops.shape
    token_count = row_count * slot_width
    local_width = key_weight.shape[1]
    head_count = local_width // HEAD_DIM
    pair_weight = jnp.concatenate([key_weight, value_weight], axis=1)
    gain_one = gain_first.astype(jnp.float32)
    shift_one = shift_first.astype(jnp.float32)
    gain_two = gain_second.astype(jnp.float32)
    shift_two = shift_second.astype(jnp.float32)
    lat_slot = crop_lookup(crop_starts, slot_crops)
    shift_slot = crop_lookup(crop_shifts, slot_crops)
    lead_slot = crop_lookup(lead_hours, slot_crops).astype(jnp.float32).reshape(token_count) / 100.0
    share_count = token_count // lax.axis_size(HEAD)
    lead_rows = lax.dynamic_slice_in_dim(
        lead_slot, lax.axis_index(HEAD) * share_count, share_count
    )
    padded = extended(pixels, ((LON, 2),), 1)
    var_count, lat_count = (pixels.shape[0], pixels.shape[1])
    west_pairs = padded[:, :, : 2 * slot_width].reshape(var_count, lat_count, slot_width, 2)
    east_pairs = padded[:, :, 2:].reshape(var_count, lat_count, slot_width, 2)
    side_pairs = jnp.stack([west_pairs, east_pairs])
    tables = jnp.stack([side_pairs[:, :, :-1], side_pairs[:, :, 1:]], axis=3)
    lat_index = jnp.arange(lat_count - 1, dtype=jnp.int32)
    side_shift = 2 * jnp.arange(2, dtype=jnp.int32) - 1
    chosen = (lat_slot[:, :, None, None] == lat_index[None, None, None, :]) & (
        shift_slot[:, :, None, None] == side_shift[None, None, :, None]
    )
    patches = jnp.einsum(
        "rjsa,svapjx->rjvpx",
        chosen.astype(jnp.bfloat16),
        tables,
        preferred_element_type=jnp.float32,
    )
    patches = patches.astype(jnp.bfloat16).reshape(row_count, slot_width, var_count, 4)

    def mixer_forward(patch_row):
        embedded, key_rows, value_rows, weights = mixer_row(
            patch_row, full_patch, full_variable, pair_weight, head_query
        )
        return jnp.einsum(
            "shv,svhd->shd", weights, value_rows.astype(jnp.float32), precision=highest
        ).astype(jnp.bfloat16)

    mixed_low = lax.map(mixer_forward, patches).reshape(token_count, local_width)
    start_sum = reduce_rows(jnp.dot(mixed_low, mixer_weight, preferred_element_type=jnp.float32))
    start_sum = (
        start_sum
        + lead_rows[:, None] * full_lead[0].astype(jnp.float32)
        + full_lead[1].astype(jnp.float32)
    )
    first_low = spread_rows(layer_norm(start_sum, gain_one, shift_one).astype(jnp.bfloat16))
    projected = jnp.einsum(
        "td,kde->kte", first_low, input_weight, preferred_element_type=jnp.float32
    ).astype(jnp.bfloat16)
    projected = projected.reshape(3, row_count, slot_width, head_count, HEAD_DIM)
    queries, key_local, value_local = (projected[0], projected[1], projected[2])
    query_crops = slot_crops.astype(jnp.float32)
    key_tags = jnp.where(occupied == 1, slot_crops, -1).astype(jnp.bfloat16)
    key_all, value_all, tag_all = (
        lax.all_gather(key_local, LON, axis=1, tiled=True),
        lax.all_gather(value_local, LON, axis=1, tiled=True),
        lax.all_gather(key_tags, LON, axis=1, tiled=True),
    )
    block_width = min(512, key_all.shape[1])
    tag_wide = tag_all.astype(jnp.float32)
    log_totals = key_stats(queries, query_crops, key_all, tag_wide, block_width)
    attended = attend(queries, query_crops, key_all, value_all, tag_wide, log_totals, block_width)
    attended_low = attended.astype(jnp.bfloat16).reshape(token_count, local_width)
    middle = start_sum + reduce_rows(
        jnp.dot(attended_low, output_proj, preferred_element_type=jnp.float32)
    )
    second_low = spread_rows(layer_norm(middle, gain_two, shift_two).astype(jnp.bfloat16))
    hidden = jnp.dot(second_low, up_weight, preferred_element_type=jnp.float32) + up_bias.reshape(
        -1
    ).astype(jnp.float32)
    active = jax.nn.gelu(hidden, approximate=False).astype(jnp.bfloat16)
    final_sum = middle + reduce_rows(
        jnp.dot(active, down_weight, preferred_element_type=jnp.float32)
    )
    final_low = spread_rows(final_sum.astype(jnp.bfloat16))
    keep_mask = occupied.reshape(token_count, 1)
    predicted = (
        jnp.dot(final_low, final_weight, preferred_element_type=jnp.float32)
        * keep_mask.astype(jnp.float32)
    ).astype(jnp.bfloat16)
    predicted = predicted.reshape(row_count, slot_width, -1)
    masked_grad = (cotangent * occupied[:, :, None].astype(jnp.bfloat16)).reshape(token_count, -1)
    grad_final_weight = outer_sum(final_low, masked_grad)
    part_top = jnp.einsum(
        "to,do->td", masked_grad, final_weight, preferred_element_type=jnp.float32
    )
    final_grad = reduce_rows(part_top)
    final_grad_low = spread_rows(final_grad.astype(jnp.bfloat16))
    grad_down = outer_sum(active, final_grad_low)
    active_grad = jnp.einsum(
        "td,fd->tf", final_grad_low, down_weight, preferred_element_type=jnp.float32
    )
    _, gelu_back = jax.vjp(partial(jax.nn.gelu, approximate=False), hidden)
    hidden_grad = gelu_back(active_grad)[0].astype(jnp.bfloat16)
    grad_up = outer_sum(second_low, hidden_grad)
    grad_up_bias = jnp.sum(hidden_grad.astype(jnp.float32), axis=0).reshape(up_bias.shape)
    second_grad = jnp.einsum(
        "tf,df->td", hidden_grad, up_weight, preferred_element_type=jnp.float32
    )
    second_in = head_share(second_grad)
    _, second_back = jax.vjp(layer_norm, middle, gain_two, shift_two)
    part_mid, grad_gain_two, grad_shift_two = second_back(second_in)
    middle_grad = final_grad + part_mid
    middle_low = spread_rows(middle_grad.astype(jnp.bfloat16))
    grad_proj = outer_sum(attended_low, middle_low)
    out_grads = jnp.einsum(
        "td,ed->te", middle_low, output_proj, preferred_element_type=jnp.float32
    ).astype(jnp.bfloat16)
    out_grads = out_grads.reshape(row_count, slot_width, head_count, HEAD_DIM)
    deltas = jnp.transpose(jnp.sum(out_grads.astype(jnp.float32) * attended, axis=-1), (0, 2, 1))
    back_keys, back_values, back_raw = (
        lax.all_gather(key_local, LON, axis=1, tiled=True),
        lax.all_gather(value_local, LON, axis=1, tiled=True),
        lax.all_gather(key_tags, LON, axis=1, tiled=True),
    )
    back_tags = back_raw.astype(jnp.float32)
    scale = HEAD_DIM ** (-0.5)
    key_count = back_keys.shape[1] // block_width
    local_zeros = jnp.zeros(queries.shape, jnp.float32)
    whole_zeros = jnp.zeros(back_keys.shape, jnp.float32)

    def both_step(running, block_index):
        query_acc, key_acc, value_acc = running
        key_block = block_slice(back_keys, block_index, block_width, 1)
        score_delta, weights_low = score_grads(
            queries,
            query_crops,
            out_grads,
            log_totals,
            deltas,
            key_block,
            block_slice(back_values, block_index, block_width, 1),
            block_slice(back_tags, block_index, block_width, 1),
        )
        query_acc = (
            query_acc
            + jnp.einsum(
                "rhqk,rkhd->rqhd", score_delta, key_block, preferred_element_type=jnp.float32
            )
            * scale
        )
        key_piece = (
            jnp.einsum("rhqk,rqhd->rkhd", score_delta, queries, preferred_element_type=jnp.float32)
            * scale
        )
        value_piece = jnp.einsum(
            "rhqk,rqhd->rkhd", weights_low, out_grads, preferred_element_type=jnp.float32
        )
        key_acc = lax.dynamic_update_slice_in_dim(key_acc, key_piece, block_index * block_width, 1)
        value_acc = lax.dynamic_update_slice_in_dim(
            value_acc, value_piece, block_index * block_width, 1
        )
        return ((query_acc, key_acc, value_acc), None)

    (query_grad, key_part, value_part), _ = lax.scan(
        both_step, (local_zeros, whole_zeros, whole_zeros), jnp.arange(key_count)
    )
    key_grad, value_grad = (
        lax.psum_scatter(
            key_part.astype(jnp.bfloat16), LON, scatter_dimension=1, tiled=True
        ).astype(jnp.float32),
        lax.psum_scatter(
            value_part.astype(jnp.bfloat16), LON, scatter_dimension=1, tiled=True
        ).astype(jnp.float32),
    )
    stacked = (
        jnp.stack([query_grad, key_grad, value_grad])
        .astype(jnp.bfloat16)
        .reshape(3, token_count, local_width)
    )
    first_grad = jnp.einsum(
        "kte,kde->td", stacked, input_weight, preferred_element_type=jnp.float32
    )
    grad_input = jnp.einsum("td,kte->kde", first_low, stacked, preferred_element_type=jnp.float32)
    first_in = head_share(first_grad)
    _, first_back = jax.vjp(layer_norm, start_sum, gain_one, shift_one)
    part_low, grad_gain_one, grad_shift_one = first_back(first_in)
    start_grad = middle_grad + part_low
    grad_lead = jnp.stack(
        [jnp.sum(start_grad * lead_rows[:, None], axis=0), jnp.sum(start_grad, axis=0)]
    )
    start_low = spread_rows(start_grad.astype(jnp.bfloat16))
    grad_mixer = outer_sum(mixed_low, start_low)
    mixed_grad = jnp.einsum(
        "td,ed->te", start_low, mixer_weight, preferred_element_type=jnp.float32
    ).astype(jnp.bfloat16)
    mixed_grad = mixed_grad.reshape(row_count, slot_width, head_count, HEAD_DIM)
    initial = (
        jnp.zeros(full_patch.shape, jnp.float32),
        jnp.zeros(full_variable.shape, jnp.float32),
        jnp.zeros(head_query.shape, jnp.float32),
        jnp.zeros(pair_weight.shape, jnp.float32),
    )
    mixer_step = partial(
        mixer_back,
        full_patch=full_patch,
        full_variable=full_variable,
        pair_weight=pair_weight,
        head_query=head_query,
    )
    (grad_patch, grad_variable, grad_query, grad_pair), slot_grads = lax.scan(
        mixer_step, initial, (patches, mixed_grad)
    )
    slot_total = head_total(slot_grads).reshape(row_count, slot_width, var_count, 2, 2)
    table_grads = jnp.einsum(
        "rjsa,rjvpx->svapjx", chosen.astype(jnp.float32), slot_total, precision=highest
    )
    side_grads = jnp.pad(
        table_grads[:, :, :, 0], ((0, 0), (0, 0), (0, 1), (0, 0), (0, 0))
    ) + jnp.pad(table_grads[:, :, :, 1], ((0, 0), (0, 0), (1, 0), (0, 0), (0, 0)))
    west_grad = side_grads[0].reshape(var_count, lat_count, 2 * slot_width)
    east_grad = side_grads[1].reshape(var_count, lat_count, 2 * slot_width)
    padded_grad = jnp.pad(west_grad, ((0, 0), (0, 0), (0, 2))) + jnp.pad(
        east_grad, ((0, 0), (0, 0), (2, 0))
    )
    rim_values = jnp.stack([padded_grad[:, :, 0], padded_grad[:, :, -1]], axis=2)
    returned = extended(rim_values, ((LON, 2),), 1)
    pixel_grad = (
        padded_grad[:, :, 1:-1]
        + jnp.pad(returned[:, :, 0:1], ((0, 0), (0, 0), (0, 2 * slot_width - 1)))
        + jnp.pad(returned[:, :, 3:4], ((0, 0), (0, 0), (2 * slot_width - 1, 0)))
    )
    sector_out = (
        lax.psum_scatter(
            grad_query.astype(jnp.bfloat16), LON, scatter_dimension=1, tiled=True
        ).astype(jnp.float32),
        lax.psum_scatter(
            grad_pair[:, :local_width].astype(jnp.bfloat16), LON, scatter_dimension=0, tiled=True
        ).astype(jnp.float32),
        lax.psum_scatter(
            grad_pair[:, local_width:].astype(jnp.bfloat16), LON, scatter_dimension=0, tiled=True
        ).astype(jnp.float32),
        lax.psum_scatter(
            grad_mixer.astype(jnp.bfloat16), LON, scatter_dimension=1, tiled=True
        ).astype(jnp.float32),
        lax.psum_scatter(
            grad_input.astype(jnp.bfloat16), LON, scatter_dimension=1, tiled=True
        ).astype(jnp.float32),
        lax.psum_scatter(
            grad_proj.astype(jnp.bfloat16), LON, scatter_dimension=1, tiled=True
        ).astype(jnp.float32),
        lax.psum_scatter(
            grad_up.astype(jnp.bfloat16), LON, scatter_dimension=0, tiled=True
        ).astype(jnp.float32),
        lax.psum_scatter(
            grad_up_bias.astype(jnp.bfloat16), LON, scatter_dimension=1, tiled=True
        ).astype(jnp.float32),
        lax.psum_scatter(
            grad_down.astype(jnp.bfloat16), LON, scatter_dimension=1, tiled=True
        ).astype(jnp.float32),
        lax.psum_scatter(
            grad_final_weight.astype(jnp.bfloat16), LON, scatter_dimension=0, tiled=True
        ).astype(jnp.float32),
    )
    shared_out = (
        lax.psum_scatter(grad_patch, (LON, HEAD), scatter_dimension=2, tiled=True),
        lax.psum_scatter(grad_variable, (LON, HEAD), scatter_dimension=1, tiled=True),
        lax.psum_scatter(grad_lead, (LON, HEAD), scatter_dimension=1, tiled=True),
        lax.psum_scatter(grad_gain_one, (LON, HEAD), scatter_dimension=0, tiled=True),
        lax.psum_scatter(grad_shift_one, (LON, HEAD), scatter_dimension=0, tiled=True),
        lax.psum_scatter(grad_gain_two, (LON, HEAD), scatter_dimension=0, tiled=True),
        lax.psum_scatter(grad_shift_two, (LON, HEAD), scatter_dimension=0, tiled=True),
    )
    return (
        predicted,
        pixel_grad,
        shared_out[0],
        shared_out[1],
        sector_out[0],
        sector_out[1],
        sector_out[2],
        sector_out[3],
        shared_out[2],
        shared_out[3],
        shared_out[4],
        sector_out[4],
        sector_out[5],
        shared_out[5],
        shared_out[6],
        sector_out[6],
        sector_out[7],
        sector_out[8],
        sector_out[9],
    )


MESH = pl.DeviceIdType.MESH
BOTH = (LON, HEAD)
LON_SIZE = 16
HEAD_SIZE = 2
CHUNK = 256
low = jnp.bfloat16
wide = jnp.float32


def planned(mesh):
    return mesh.shape[LON] == LON_SIZE and mesh.shape[HEAD] == HEAD_SIZE


def dot(left, right, left_dim=1, right_dim=0):
    return lax.dot_general(
        left, right, (((left_dim,), (right_dim,)), ((), ())), preferred_element_type=wide
    )


def position():
    lon = lax.axis_index(LON)
    x = lax.axis_index(HEAD)
    z = lax.div(lon, 4)
    y = lax.rem(lax.div(lon, 2), 2)
    c = lax.rem(lon, 2)
    return x, z, y, c


def partners(x, z, y, c):
    here = z * 4 + y * 2 + c
    across = {
        "x": (here, 1 - x),
        "y": (z * 4 + (1 - y) * 2 + c, x),
        "c": (z * 4 + y * 2 + 1 - c, x),
    }
    line = [(lax.rem(z + step, 4) * 4 + y * 2 + c, x) for step in (1, 2, 3)]
    return across, line


def sector_of(z, y, c, x, part, side):
    return (y * 2 + c) * 4 + x * 2 + part, side


def block_of(z, y, row):
    return row * 4 + z, y


def meet(peers, others=(), own=None):
    barrier = pltpu.get_barrier_semaphore()
    for device in peers:
        pl.semaphore_signal(barrier, inc=1, device_id=device, device_id_type=MESH)
    for device in others:

        @pl.when(jnp.logical_not(same(device, own)))
        def _():
            pl.semaphore_signal(barrier, inc=1, device_id=device, device_id_type=MESH)

    expected = len(peers)
    for device in others:
        expected = expected + 1 - same(device, own).astype(jnp.int32)
    pl.semaphore_wait(barrier, expected)


def same(device, own):
    return jnp.logical_and(device[0] == own[0], device[1] == own[1])


def post(source, target, send_sem, recv_sem, device, own):
    here = same(device, own)

    @pl.when(here)
    def _():
        pltpu.make_async_copy(source, target, recv_sem).start()

    @pl.when(jnp.logical_not(here))
    def _():
        remote(source, target, send_sem, recv_sem, device).start()


def settle(source, target, send_sem, recv_sem, device, own):
    @pl.when(jnp.logical_not(same(device, own)))
    def _():
        remote(source, target, send_sem, recv_sem, device).wait_send()


def remote(source, target, send_sem, recv_sem, device):
    return pltpu.make_async_remote_copy(
        src_ref=source,
        dst_ref=target,
        send_sem=send_sem,
        recv_sem=recv_sem,
        device_id=device,
        device_id_type=MESH,
    )


def gatherer(views, sems):
    own_sem, line_send, line_recv, hop_send, hop_recv = sems
    x, z, y, c = position()
    across, line = partners(x, z, y, c)

    def keep(number):
        source, target, span, _ = views(number)
        return pltpu.make_async_copy(source, target.at[x, z, y, c, span], own_sem.at[number])

    def along(number, d):
        source, target, span, _ = views(number)
        return remote(
            source,
            target.at[x, z, y, c, span],
            line_send.at[number, d],
            line_recv.at[number, d],
            line[d],
        )

    def hop(number, k):
        _, target, span, color = views(number)
        if k == 0:
            part, axis = target.at[x, :, y, c, span], "yx"[color]
        elif k == 1 and color == 0:
            part, axis = target.at[x, :, :, c, span], "x"
        elif k == 1:
            part, axis = target.at[:, :, y, c, span], "y"
        else:
            part, axis = target.at[:, :, :, c, span], "c"
        return remote(
            part, part, hop_send.at[number, k], hop_recv.at[number, k], across[axis]
        )

    def begin(number):
        keep(number).start()
        for d in range(3):
            along(number, d).start()

    def spread(number):
        keep(number).wait()
        for d in range(3):
            along(number, d).wait_recv()
        hop(number, 0).start()

    def widen(number):
        hop(number, 0).wait_recv()
        hop(number, 1).start()

    def pair_up(number):
        hop(number, 1).wait_recv()
        hop(number, 2).start()

    def close(number):
        hop(number, 2).wait_recv()

    def finish(number):
        for k in range(3):
            along(number, k).wait_send()
            hop(number, k).wait_send()

    return (begin, spread, widen, pair_up, close), finish


def reduce_kernel(chunks, count, *refs):
    ins = refs[:count]
    value_in, grad_in, lat_ref, shift_ref = refs[count : count + 4]
    out, value_out, pixel_out = refs[count + 4 : count + 7]
    buffers, sems = refs[count + 7 : count + 13], refs[count + 13 : count + 20]
    grad_out, field, edge, west_edge, east_edge = refs[count + 20 : count + 25]
    value_send, value_recv, grad_send, grad_recv, edge_send, edge_recv = refs[count + 25 :]
    x, z, y, c = position()
    across, line = partners(x, z, y, c)
    lon = z * 4 + y * 2 + c
    own = (lon, x)
    east, west = (lax.rem(lon + 1, 16), x), (lax.rem(lon + 15, 16), x)
    sources = [block_of(z, y, row) for row in range(4)]
    meet(list(across.values()) + line + [east, west], sources, own)
    letters = []
    for part in range(2):
        for side in range(2):
            device = sector_of(z, y, c, x, part, side)
            at = 2 * part + side
            letters.append(
                (value_in.at[side, part], value_out.at[z], value_send.at[at], value_recv.at[z])
                + (device, own)
            )
            letters.append(
                (grad_in.at[part], grad_out.at[z], grad_send.at[at], grad_recv.at[z])
                + (device, own)
            )
    for letter in letters:
        post(*letter)
    total = len(chunks)

    lat_count, var_count, lanes = field.shape
    half = lanes // 2
    column_count = pixel_out.shape[2]

    def paste(row):
        pltpu.make_async_copy(grad_in.at[0], grad_out.at[row], grad_recv.at[row]).wait()
        lat = lat_ref[row : row + 1, :]
        going_west = shift_ref[row : row + 1, :] < 0
        lat_both = jnp.concatenate([lat, lat], axis=1)
        both = []
        for py in range(2):
            k = 2 * py
            grads = jnp.concatenate(
                [
                    grad_out[row, k * var_count : (k + 1) * var_count, :],
                    grad_out[row, (k + 1) * var_count : (k + 2) * var_count, :],
                ],
                axis=1,
            )
            left = jnp.where(going_west, grads, 0.0)
            both.append(jnp.concatenate([left, grads - left], axis=1))

        def body(b, carry):
            piece = jnp.where(lat_both == b, both[0], 0.0) + jnp.where(
                lat_both == b - 1, both[1], 0.0
            )
            if row == 0:
                field[b] = piece
            else:
                field[b] += piece
            return carry

        lax.fori_loop(0, lat_count, body, 0)

    def thirds(values):
        one = values.astype(low)
        rest = values - one.astype(wide)
        two = rest.astype(low)
        return one, two, (rest - two.astype(wide)).astype(low)

    def columns_of(shape, axis):
        spot = lax.broadcasted_iota(jnp.int32, shape, axis)
        side, spot = lax.div(spot, half), lax.rem(spot, half)
        slots = half // 2
        return 2 * lax.rem(spot, slots) + 2 * side + lax.div(spot, slots) - 1

    def edges():
        kind = lax.broadcasted_iota(jnp.int32, (8, lanes), 0)
        wanted = columns_of((8, lanes), 1)
        pick = jnp.where(
            jnp.logical_or(
                jnp.logical_and(kind == 0, wanted == -1),
                jnp.logical_and(kind == 1, wanted == column_count),
            ),
            1.0,
            0.0,
        ).astype(low)
        flat = field[...].reshape(lat_count * var_count, lanes)
        one, two, three = thirds(flat)
        edge[...] = dot(pick, one, 1, 1) + dot(pick, two, 1, 1) + dot(pick, three, 1, 1)
        remote(edge, west_edge, edge_send.at[0], edge_recv.at[0], east).start()
        remote(edge, east_edge, edge_send.at[1], edge_recv.at[1], west).start()

    def pixels():
        remote(edge, west_edge, edge_send.at[0], edge_recv.at[0], east).wait()
        remote(edge, east_edge, edge_send.at[1], edge_recv.at[1], west).wait()
        wanted = columns_of((lanes, column_count), 0)
        column = lax.broadcasted_iota(jnp.int32, (lanes, column_count), 1)
        place = jnp.where(wanted == column, 1.0, 0.0).astype(low)
        kind = lax.broadcasted_iota(jnp.int32, (8, column_count), 0)
        column = lax.broadcasted_iota(jnp.int32, (8, column_count), 1)
        from_west = jnp.logical_and(kind == 1, column == 0)
        from_east = jnp.logical_and(kind == 0, column == column_count - 1)
        west_place = jnp.where(from_west, 1.0, 0.0).astype(low)
        east_place = jnp.where(from_east, 1.0, 0.0).astype(low)
        borders = None
        for values, target in ((west_edge[...], west_place), (east_edge[...], east_place)):
            for part in thirds(values):
                piece = dot(part, target, 0, 0)
                borders = piece if borders is None else borders + piece
        pixel_out[...] = borders.reshape(pixel_out.shape)

        def body(b, carry):
            result = pixel_out[b]
            for part in thirds(field[b]):
                result = result + dot(part, place)
            pixel_out[b] = result
            return carry

        lax.fori_loop(0, lat_count, body, 0)

    extra = {3: lambda: paste(0), 4: lambda: paste(1), 5: lambda: paste(2), 6: lambda: paste(3)}
    extra.update({7: edges, 10: pixels})

    def source_of(pair, color, side, core):
        index, lead, offset = chunks[2 * pair + color][side]
        source = ins[index] if lead is None else ins[index].at[lead]
        return source.at[:, :, core, :, pl.ds(offset, CHUNK)]

    begin, stage_core, stage_first, stage_second, stage_third, finish = reducer(
        source_of, buffers, sems, out
    )
    plan = ((0, begin), (2, stage_core), (4, stage_first), (6, stage_second), (8, stage_third))
    for step in range(total + 8):
        for back, stage in plan:
            if 0 <= step - back < total:
                stage((step - back) // 2, (step - back) % 2)
        if step in extra:
            extra[step]()
    for k in range(total):
        finish(k // 2, k % 2)
    for letter in letters:
        settle(*letter)
    for row in range(4):
        pltpu.make_async_copy(value_in.at[0, 0], value_out.at[row], value_recv.at[row]).wait()


def reduce_all(items, values, grads, lat_lanes, shift_lanes, lat_count, number):
    chunks, views = [], []
    for index, item in enumerate(items):
        rows, columns = item.shape[-2:]
        lead = item.shape[:-2]
        item = item.reshape((-1, 4, 2, 2, rows // 16, columns))
        if not lead:
            views.append(item[0])
            for offset in range(0, columns // 2, CHUNK):
                chunks.append(((index, None, offset), (index, None, columns // 2 + offset)))
            continue
        views.append(item)
        for first in range(0, item.shape[0], 2):
            for offset in range(0, columns, CHUNK):
                chunks.append(((index, first, offset), (index, first + 1, offset)))
    rows = views[0].shape[-2]
    var_count = grads.shape[1] // 4
    lanes = 2 * lat_lanes.shape[1]
    columns = lat_lanes.shape[1]
    vmem = pl.BlockSpec(memory_space=pltpu.VMEM)
    hbm = pl.BlockSpec(memory_space=pl.ANY)
    count, total = len(views), len(chunks)
    sem = pltpu.SemaphoreType.DMA
    return pl.pallas_call(
        partial(reduce_kernel, chunks, count),
        out_shape=[
            jax.ShapeDtypeStruct((rows, total * CHUNK), wide),
            jax.ShapeDtypeStruct((4,) + values.shape[2:], values.dtype),
            jax.ShapeDtypeStruct((lat_count, var_count, columns), wide),
        ],
        in_specs=[hbm] * (count + 2) + [vmem] * 2,
        out_specs=[vmem, hbm, vmem],
        scratch_shapes=reducer_scratch(total, rows)
        + [
            pltpu.VMEM((4,) + grads.shape[1:], wide),
            pltpu.VMEM((lat_count, var_count, lanes), wide),
            pltpu.VMEM((8, lat_count * var_count), wide),
            pltpu.VMEM((8, lat_count * var_count), wide),
            pltpu.VMEM((8, lat_count * var_count), wide),
            sem((4,)),
            sem((4,)),
            sem((4,)),
            sem((4,)),
            sem((2,)),
            sem((2,)),
        ],
        compiler_params=pltpu.CompilerParams(
            collective_id=number, has_side_effects=True, vmem_limit_bytes=60 * 2**20
        ),
    )(*views, values, grads, lat_lanes, shift_lanes)


def diagonal(var_count, columns):
    column = lax.broadcasted_iota(jnp.int32, (var_count, columns), 1)
    row = lax.broadcasted_iota(jnp.int32, (var_count, columns), 0)
    return (lax.rem(column, var_count) == row) & (column < 5 * var_count)


def patch_kernel(field_ref, lat_ref, shift_ref, patch_ref):
    lat_count, var_count, _ = field_ref.shape
    row_count, lanes = lat_ref.shape
    slots = lanes // 2
    for r in range(row_count):
        lat = lat_ref[r : r + 1, :]
        west = shift_ref[r : r + 1, :] < 0

        def body(b, carry):
            top, bottom = carry
            wide_row = field_ref[b].astype(wide)
            chosen = jnp.where(west, wide_row[:, :lanes], wide_row[:, lanes:])
            return (jnp.where(lat == b, chosen, top), jnp.where(lat == b - 1, chosen, bottom))

        zero = jnp.zeros((var_count, lanes), wide)
        rows = lax.fori_loop(0, lat_count, body, (zero, zero), unroll=4)
        for py in range(2):
            for px in range(2):
                k = 2 * py + px
                patch_ref[r, k * var_count : (k + 1) * var_count, :] = rows[py][
                    :, px * slots : (px + 1) * slots
                ].astype(low)


def cut_patches(field, lat_lanes, shift_lanes):
    row_count, lanes = lat_lanes.shape
    return pl.pallas_call(
        patch_kernel,
        out_shape=jax.ShapeDtypeStruct((row_count, 4 * field.shape[1], lanes // 2), low),
    )(field, lat_lanes, shift_lanes)


def mixer_backward_kernel(
    patch_ref,
    prob_ref,
    score_ref,
    value_ref,
    grad_ref,
    pooled_ref,
    count_ref,
    cut_ref,
    patch_grad_ref,
):
    head_count, var_count, _ = prob_ref.shape
    padded, tokens = patch_ref.shape
    rest = padded - 5 * var_count
    mask = diagonal(var_count, padded)
    patch_grad_ref[...] = jnp.zeros_like(patch_grad_ref)

    def head_step(h, carry):
        start = pl.multiple_of(h * HEAD_DIM, HEAD_DIM)
        grads = grad_ref[pl.ds(start, HEAD_DIM), :]
        prob = prob_ref[h]
        back = dot(value_ref[pl.ds(start, HEAD_DIM), :], grads, 0, 0)
        pieces = [patch_ref[k * var_count : (k + 1) * var_count, :].astype(wide) for k in range(5)]
        backs = [back[k * var_count : (k + 1) * var_count, :] for k in range(5)]
        prob_grad = pieces[0] * backs[0]
        for k in range(1, 5):
            prob_grad = prob_grad + pieces[k] * backs[k]
        mean = jnp.sum(prob * prob_grad, axis=0, keepdims=True)
        delta = prob * (prob_grad - mean)
        upper = delta.astype(low)
        lower = (delta - upper.astype(wide)).astype(low)
        spread = jnp.where(mask, score_ref[pl.ds(h, 1), :], 0.0).astype(low)
        patch_grad_ref[...] += dot(spread, upper, 0, 0)
        for k in range(4):
            patch_grad_ref[k * var_count : (k + 1) * var_count, :] += prob * backs[k]
        patch = patch_ref[...]
        counts = dot(upper, patch, 1, 1) + dot(lower, patch, 1, 1)
        count_ref[pl.ds(h, 1), :] = jnp.sum(jnp.where(mask, counts, 0.0), axis=0, keepdims=True)
        pooled = jnp.concatenate(
            [(prob * piece).astype(low) for piece in pieces] + [jnp.zeros((rest, tokens), low)],
            axis=0,
        )
        pooled_ref[pl.ds(start, HEAD_DIM), :] = dot(grads, pooled, 1, 1)
        return carry

    lax.fori_loop(0, head_count, head_step, 0)
    parts, taps, width = cut_ref.shape
    for part in range(parts):
        cut_ref[part] = patch_grad_ref[:taps, part * width : (part + 1) * width]


def mixer_backward(patches, probs, score_table, value_table, mixed_grads):
    head_count, padded = score_table.shape
    var_count = probs.shape[1]
    tokens = patches.shape[1]
    return pl.pallas_call(
        mixer_backward_kernel,
        out_shape=[
            jax.ShapeDtypeStruct((head_count * HEAD_DIM, padded), wide),
            jax.ShapeDtypeStruct((head_count, padded), wide),
            jax.ShapeDtypeStruct((2, 4 * var_count, tokens // 2), wide),
        ],
        scratch_shapes=[pltpu.VMEM((padded, tokens), wide)],
        compiler_params=pltpu.CompilerParams(vmem_limit_bytes=40 * 2**20),
    )(patches, probs, score_table, value_table, mixed_grads)


def head_lanes(values, h):
    lane = lax.broadcasted_iota(jnp.int32, values.shape, values.ndim - 1)
    inside = lane < HEAD_DIM if h == 0 else lane >= HEAD_DIM
    return jnp.where(inside, values, jnp.zeros_like(values))


def plane_device(z, index):
    return z * 4 + lax.div(index, 2), lax.rem(index, 2)


def plane_meet(x, z, y, c):
    barrier = pltpu.get_barrier_semaphore()
    for flip in range(1, 8):
        there_y = 1 - y if flip & 4 else y
        there_c = 1 - c if flip & 2 else c
        there_x = 1 - x if flip & 1 else x
        device = (z * 4 + there_y * 2 + there_c, there_x)
        pl.semaphore_signal(barrier, inc=1, device_id=device, device_id_type=MESH)
    return barrier


def joined(left, right):
    return (left.astype(wide) + right.astype(wide)).astype(low)


def reducer(source_of, buffers, sems, out):
    mine, other, first_a, first_b, second, third = buffers
    own_sem, core_send, core_recv, hop_send, hop_recv, line_send, line_recv = sems
    x, z, y, c = position()
    across, line = partners(x, z, y, c)

    def keeps(pair, color):
        k = 2 * pair + color
        return [
            pltpu.make_async_copy(
                source_of(pair, color, side, c), mine.at[2 * k + side], own_sem.at[k, side]
            )
            for side in range(2)
        ]

    def swaps(pair, color):
        k = 2 * pair + color
        return [
            remote(
                source_of(pair, color, side, 1 - c),
                other.at[2 * k + side],
                core_send.at[k, side],
                core_recv.at[k, side],
                across["c"],
            )
            for side in range(2)
        ]

    def hop_one(pair, color):
        k = 2 * pair + color
        if color == 0:
            source, target, axis = mine.at[2 * k + 1 - x], first_a.at[pair], "x"
        else:
            source = mine.at[pl.ds(2 * k, 2), :, 1 - y]
            target, axis = first_b.at[pair], "y"
        return remote(source, target, hop_send.at[k, 0], hop_recv.at[k, 0], across[axis])

    def hop_two(pair, color):
        k = 2 * pair + color
        if color == 0:
            source, axis = mine.at[2 * k + x, :, 1 - y], "y"
        else:
            source, axis = mine.at[2 * k + 1 - x, :, y], "x"
        return remote(source, second.at[k], hop_send.at[k, 1], hop_recv.at[k, 1], across[axis])

    def along(pair, color):
        k = 2 * pair + color
        return [
            remote(
                mine.at[2 * k + x, lax.rem(z + d + 1, 4), y],
                third.at[k, d],
                line_send.at[k, d],
                line_recv.at[k, d],
                line[d],
            )
            for d in range(3)
        ]

    def begin(pair, color):
        for copy in swaps(pair, color) + keeps(pair, color):
            copy.start()

    def stage_core(pair, color):
        k = 2 * pair + color
        for copy in keeps(pair, color):
            copy.wait()
        for copy in swaps(pair, color):
            copy.wait_recv()

        def body(step, carry):
            side, row = lax.div(step, 4), lax.rem(step, 4)
            for part in range(2):
                mine[2 * k + side, row, part] = joined(
                    mine[2 * k + side, row, part], other[2 * k + side, row, part]
                )
            return carry

        lax.fori_loop(0, 8, body, 0)
        hop_one(pair, color).start()

    def stage_first(pair, color):
        k = 2 * pair + color
        hop_one(pair, color).wait_recv()

        def body(row, carry):
            for part in range(2):
                if color == 0:
                    mine[2 * k + x, row, part] = joined(
                        mine[2 * k + x, row, part], first_a[pair, row, part]
                    )
                else:
                    mine[2 * k + part, row, y] = joined(
                        mine[2 * k + part, row, y], first_b[pair, part, row]
                    )
            return carry

        lax.fori_loop(0, 4, body, 0)
        hop_two(pair, color).start()

    def stage_second(pair, color):
        k = 2 * pair + color
        hop_two(pair, color).wait_recv()

        def body(row, carry):
            mine[2 * k + x, row, y] = joined(mine[2 * k + x, row, y], second[k, row])
            return carry

        lax.fori_loop(0, 4, body, 0)
        for copy in along(pair, color):
            copy.start()

    def stage_third(pair, color):
        k = 2 * pair + color
        for copy in along(pair, color):
            copy.wait_recv()
        result = mine[2 * k + x, z, y].astype(wide)
        for d in range(3):
            result = result + third[k, d].astype(wide)
        start = k * CHUNK
        if not isinstance(k, int):
            start = pl.multiple_of(start, CHUNK)
        out[:, pl.ds(start, CHUNK)] = result

    def finish(pair, color):
        hop_one(pair, color).wait_send()
        hop_two(pair, color).wait_send()
        for copy in swaps(pair, color) + along(pair, color):
            copy.wait_send()

    return begin, stage_core, stage_first, stage_second, stage_third, finish


def reducer_scratch(total, rows):
    sem = pltpu.SemaphoreType.DMA
    pairs = (total + 1) // 2
    return [
        pltpu.VMEM((2 * total, 4, 2, rows, CHUNK), low),
        pltpu.VMEM((2 * total, 4, 2, rows, CHUNK), low),
        pltpu.VMEM((pairs, 4, 2, rows, CHUNK), low),
        pltpu.VMEM((pairs, 2, 4, rows, CHUNK), low),
        pltpu.VMEM((total, 4, rows, CHUNK), low),
        pltpu.VMEM((total, 3, rows, CHUNK), low),
    ] + [
        sem((total, 2)),
        sem((total, 2)),
        sem((total, 2)),
        sem((total, 2)),
        sem((total, 2)),
        sem((total, 3)),
        sem((total, 3)),
    ]


def attend_back_kernel(
    joint,
    tag_ref,
    crop_ref,
    out_ref,
    total_ref,
    source,
    feed_ref,
    stacked,
    sums,
    grads,
    result,
    key_acc,
    value_acc,
    *rest
):
    buffers, sems = rest[:6], rest[6:13]
    in_own, in_send, in_recv, back_own, back_send, back_recv = rest[13:]
    x, z, y, c = position()
    across, line = partners(x, z, y, c)
    me = y * 4 + c * 2 + x
    peers, kinds, share, lanes = joint.shape
    slots = peers * share
    scale = HEAD_DIM ** (-0.5)
    each = feed_ref.shape[-1] // CHUNK

    def source_of(pair, color, side, core):
        k = 2 * pair + color
        offset = pl.multiple_of(lax.rem(k, each) * CHUNK, CHUNK)
        return feed_ref.at[lax.div(k, each), side, :, :, core, :, pl.ds(offset, CHUNK)]

    begin, stage_core, stage_first, stage_second, stage_third, finish = reducer(
        source_of, buffers, sems, sums
    )
    keep = pltpu.make_async_copy(source.at[me], grads.at[me], in_own)
    keep.start()
    barrier = plane_meet(x, z, y, c)
    for device in line:
        pl.semaphore_signal(barrier, inc=1, device_id=device, device_id_type=MESH)
    pl.semaphore_wait(barrier, peers - 1 + len(line))

    def inward(there):
        return remote(
            source.at[there],
            grads.at[me],
            in_send.at[there],
            in_recv.at[me],
            plane_device(z, there),
        )

    def outward(there, part):
        span = pl.ds(0, 1) if part == 0 else pl.ds(1, 2)
        return remote(
            result.at[there, span],
            stacked.at[me, span],
            back_send.at[there, part],
            back_recv.at[me, part],
            plane_device(z, there),
        )

    for step in range(1, peers):
        inward(lax.rem(me + step, peers)).start()
    key_acc[...] = jnp.zeros_like(key_acc)
    value_acc[...] = jnp.zeros_like(value_acc)
    pairs = feed_ref.shape[0] * each // 2

    def attention(index):
        span = pl.ds(pl.multiple_of(index * share, share), share)
        queries = joint[index, 0]
        keys = joint[:, 1].reshape(slots, lanes)
        values = joint[:, 2].reshape(slots, lanes)
        grad = grads[index]
        product = grad.astype(wide) * out_ref[span, :]
        allowed = crop_ref[span, :] == tag_ref[0:1, :]
        query_grad = None
        for h in range(2):
            query_part, grad_part = head_lanes(queries, h), head_lanes(grad, h)
            scores = jnp.where(allowed, dot(query_part, keys, 1, 1), masked_score)
            weights = jnp.exp(scores - total_ref[h, span, :])
            weight_grads = dot(grad_part, values, 1, 1)
            delta = jnp.sum(head_lanes(product, h), axis=1, keepdims=True)
            score_grads = (weights * (weight_grads - delta)).astype(low)
            weights = weights.astype(low)
            value_acc[...] += dot(grad_part, weights, 0, 0)
            key_acc[...] += dot(query_part, score_grads, 0, 0)
            part = head_lanes(dot(score_grads, keys), h)
            query_grad = part if query_grad is None else query_grad + part
        result[index, 0] = (query_grad * scale).astype(low)

    def step_body(step, carry):
        @pl.when(step < pairs)
        def _():
            begin(step, 0)
            begin(step, 1)

        for back, stage in ((1, stage_core), (2, stage_first), (3, stage_second), (4, stage_third)):

            @pl.when(jnp.logical_and(step >= back, step < pairs + back))
            def _():
                stage(step - back, 0)
                stage(step - back, 1)

        @pl.when(step < peers)
        def _():
            index = lax.rem(me + step, peers)

            @pl.when(step == 0)
            def _():
                keep.wait()

            @pl.when(step > 0)
            def _():
                pltpu.make_async_copy(
                    grads.at[index], grads.at[index], in_recv.at[index]
                ).wait()

            attention(index)

            @pl.when(step > 0)
            def _():
                outward(index, 0).start()

        @pl.when(step == peers - 1)
        def _():
            for index in range(peers):
                span = slice(index * share, (index + 1) * share)
                result[index, 1] = key_acc[:, span].T.astype(low)
                result[index, 2] = value_acc[:, span].T.astype(low)
            for other in range(1, peers):
                outward(lax.rem(me + other, peers), 1).start()
            pltpu.make_async_copy(result.at[me], stacked.at[me], back_own).start()

        return carry

    lax.fori_loop(0, pairs + 4, step_body, 0)

    def finish_body(pair, carry):
        finish(pair, 0)
        finish(pair, 1)
        return carry

    lax.fori_loop(0, pairs, finish_body, 0)
    for step in range(1, peers):
        there = lax.rem(me + step, peers)
        inward(there).wait_send()
        for part in range(2):
            outward(there, part).wait_send()
            span = pl.ds(0, 1) if part == 0 else pl.ds(1, 2)
            pltpu.make_async_copy(
                result.at[there, span], stacked.at[there, span], back_recv.at[there, part]
            ).wait()
    pltpu.make_async_copy(result.at[me], stacked.at[me], back_own).wait()


def attend_back(joint, tags, crops, outputs, totals, source, feed_grads, number):
    peers, kinds, share, lanes = joint.shape
    slots = peers * share
    sides, halves, rows, columns = feed_grads.shape
    total = sides * columns // CHUNK
    sem = pltpu.SemaphoreType.DMA
    vmem = pl.BlockSpec(memory_space=pltpu.VMEM)
    hbm = pl.BlockSpec(memory_space=pl.ANY)
    return pl.pallas_call(
        attend_back_kernel,
        out_shape=[
            jax.ShapeDtypeStruct(joint.shape, low),
            jax.ShapeDtypeStruct((rows // 16, total * CHUNK), wide),
        ],
        in_specs=[vmem] * 5 + [hbm] * 2,
        out_specs=[hbm, vmem],
        scratch_shapes=[
            pltpu.VMEM((peers, share, lanes), low),
            pltpu.VMEM(joint.shape, low),
            pltpu.VMEM((lanes, slots), wide),
            pltpu.VMEM((lanes, slots), wide),
        ]
        + reducer_scratch(total, rows // 16)
        + [
            sem,
            sem((peers,)),
            sem((peers,)),
            sem,
            sem((peers, 2)),
            sem((peers, 2)),
        ],
        compiler_params=pltpu.CompilerParams(
            collective_id=number, has_side_effects=True, vmem_limit_bytes=60 * 2**20
        ),
    )(
        joint,
        tags,
        crops,
        outputs,
        totals,
        source,
        feed_grads.reshape(sides, halves, 4, 2, 2, rows // 16, columns),
    )


def whole(array):
    rank = len(array.shape)
    return pl.BlockSpec(array.shape, lambda *_: (0,) * rank)


def norm_parts(values):
    center = values - jnp.mean(values, axis=-1, keepdims=True)
    inverse = lax.rsqrt(jnp.mean(center * center, axis=-1, keepdims=True) + epsilon)
    return center * inverse, inverse


def norm_back(values, gain, grads):
    normed, inverse = norm_parts(values)
    scaled = grads * gain
    inner = (
        scaled
        - jnp.mean(scaled, axis=-1, keepdims=True)
        - normed * jnp.mean(scaled * normed, axis=-1, keepdims=True)
    )
    return (
        inner * inverse,
        jnp.sum(grads * normed, axis=0, keepdims=True),
        jnp.sum(grads, axis=0, keepdims=True),
    )


def front_kernel(items, *refs):
    arrays, refs = refs[:8], refs[8:]
    cut_in, grad_in, hour_ref, refs = refs[0], refs[1], refs[2], refs[3:]
    outs, grad_out, received, refs = refs[:8], refs[8], refs[9], refs[10:]
    joint, wide_ref, total_ref, tag_ref, crop_ref, refs = refs[:5] + (refs[5:],)
    patch_ref, prob_ref, mixed_ref, value_table, key_table, score_table, refs = refs[:6] + (
        refs[6:],
    )
    full_ref, vector_ref, query_ref, start_ref, low_ref, lead_ref, keep_ref, refs = refs[:7] + (
        refs[7:],
    )
    cut_ref, misc_ref, small_ref, weight_a, weight_b, projected, sending, turned, refs = refs[
        :8
    ] + (refs[8:],)
    gather_sems, refs = refs[:5], refs[5:]
    post_send, post_recv, load_sem, own_sem, send_sem, recv_sem, out_own, out_send, out_recv = refs
    x, z, y, c = position()
    across, line = partners(x, z, y, c)
    own = (z * 4 + y * 2 + c, x)
    me = y * 4 + c * 2 + x
    peers, kinds, share, lanes = joint.shape
    slots = peers * share
    head_count, var_count, tokens = prob_ref.shape
    padded = patch_ref.shape[0]
    taps = 4 * var_count
    halves = 2
    half_width = weight_a.shape[-1]

    everyone = [across["x"], across["y"], across["c"]] + line
    for flip in (3, 5, 6, 7):
        there_y = 1 - y if flip & 4 else y
        there_c = 1 - c if flip & 2 else c
        there_x = 1 - x if flip & 1 else x
        everyone.append((z * 4 + there_y * 2 + there_c, there_x))
    sources = [sector_of(z, y, c, x, part, side) for part in range(2) for side in range(2)]
    meet(everyone, sources, own)
    letters = []
    for part in range(2):
        row = 2 * x + part
        letters.append(
            (cut_in.at[part], cut_ref.at[c], post_send.at[part], post_recv.at[c])
            + (block_of(z, y, row), own)
        )
    for row in range(4):
        letters.append(
            (grad_in.at[row], grad_out.at[x, c], post_send.at[2 + row])
            + (post_recv.at[2 + 2 * x + c], block_of(z, y, row), own)
        )
    for letter in letters:
        post(*letter)

    def views(number):
        index, lead, first, rows, color = items[number]
        source, target = arrays[index], outs[index]
        if lead is not None:
            source, target = source.at[lead], target.at[lead]
        return source.at[pl.ds(first, rows)], target, pl.ds(first, rows), color

    stages, finish = gatherer(views, gather_sems)

    def load(source, target, spot):
        return pltpu.make_async_copy(source, target, load_sem.at[spot])

    def ask_small():
        load(outs[0], misc_ref, 0).start()
        load(outs[1], small_ref, 1).start()
        load(outs[2], weight_a, 2).start()
        load(outs[3], weight_b, 3).start()

    def read_small():
        load(outs[0], misc_ref, 0).wait()
        load(outs[1], small_ref, 1).wait()
        sector = small_ref.shape[4] // 2
        for lon in range(16):
            at = (lon // 4, lon // 2 % 2, lon % 2)
            for side in range(2):
                rows = slice((2 * lon + side) * sector, (2 * lon + side + 1) * sector)
                for half in range(2):
                    full_ref[rows, half * 128 : (half + 1) * 128] = small_ref[
                        (side,) + at + (slice(half * sector, (half + 1) * sector),)
                    ]
        upper = full_ref[:, 128:]
        vector_ref[...] = upper.astype(wide).T[taps + var_count - 128 : taps + var_count - 120]
        lane = lax.broadcasted_iota(jnp.int32, upper.shape, 1)
        full_ref[:, 128:] = jnp.where(lane < taps + var_count - 128, upper.astype(wide), 0.0).astype(
            low
        )
        kind = lax.broadcasted_iota(jnp.int32, (16, 128), 0)
        across_rows = lax.broadcasted_iota(jnp.int32, (128, 128), 0)
        across_lanes = lax.broadcasted_iota(jnp.int32, (128, 128), 1)
        queries = [None, None]
        for lon in range(16):
            at = (lon // 4, lon // 2 % 2, lon % 2)
            span = slice(lon * 128, (lon + 1) * 128)
            block = misc_ref[(0,) + at + (slice(0, 16),)].astype(wide)
            tag = jnp.sum(jnp.where(kind == z, block, 0.0), axis=0, keepdims=True)
            crop = jnp.sum(jnp.where(kind == 4 + z, block, 0.0), axis=0, keepdims=True)
            tag_ref[0:1, span] = tag
            for row, target in ((crop, crop_ref), (tag, turned)):
                target[span, :] = jnp.sum(
                    jnp.where(across_rows == across_lanes, row, 0.0), axis=1, keepdims=True
                )
            for side in range(2):
                block = misc_ref[(side,) + at + (slice(0, 16),)].astype(wide)[8:16]
                queries[side] = block if lon == 0 else queries[side] + block
        query_ref[...] = jnp.concatenate(queries, axis=0)
        mine = pl.ds(pl.multiple_of(me * share, share), share)
        keep_ref[...] = jnp.where(turned[mine, :] >= 0.0, 1.0, 0.0)
        crops = crop_ref[mine, :]
        hours = jnp.zeros((tokens, 1), wide)
        for k in range(8):
            hours = hours + jnp.where(crops == float(k), hour_ref[0:1, k : k + 1], 0.0)
        lead_ref[...] = hours
        for part in range(2):
            pltpu.make_async_copy(cut_in.at[part], cut_ref.at[part], post_recv.at[part]).wait()
            patch_ref[:taps, part * 128 : (part + 1) * 128] = cut_ref[part]
        patch_ref[taps : taps + var_count, :] = jnp.ones((var_count, tokens), low)
        patch_ref[taps + var_count :, :] = jnp.zeros((padded - taps - var_count, tokens), low)

    def tables(weight, spot, table):
        load(outs[spot], weight, spot).wait()
        for side in range(halves):
            product = dot(weight[side].reshape(-1, half_width), full_ref[...], 0, 0)
            table[side * half_width : (side + 1) * half_width, :] = product.astype(table.dtype)

    def score():
        tables(weight_a, 2, key_table)
        wide_query = jnp.concatenate([query_ref[...]] * (head_count * HEAD_DIM // 128), axis=1)
        head = lax.div(lax.broadcasted_iota(jnp.int32, wide_query.shape, 1), HEAD_DIM)
        row = lax.broadcasted_iota(jnp.int32, wide_query.shape, 0)
        wide_query = jnp.where(head == row, wide_query, 0.0).astype(low)
        rest, result = key_table[...], None
        for _ in range(3):
            part = rest.astype(low)
            rest = rest - part.astype(wide)
            piece = dot(wide_query, part)
            result = piece if result is None else result + piece
        score_table[...] = result * HEAD_DIM ** (-0.5)

    def ask_back():
        load(outs[4], weight_a, 2).start()

    def heads(first):
        mask = diagonal(var_count, padded)

        def head_step(h, carry):
            spread = jnp.where(mask, score_table[pl.ds(h, 1), :], 0.0)
            upper = spread.astype(low)
            lower = (spread - upper.astype(wide)).astype(low)
            patch = patch_ref[...]
            scores = dot(upper, patch) + dot(lower, patch)
            raised = jnp.exp(scores - jnp.max(scores, axis=0, keepdims=True))
            prob = raised / jnp.sum(raised, axis=0, keepdims=True)
            prob_ref[h] = prob
            pooled = jnp.concatenate(
                [
                    (prob * patch_ref[k * var_count : (k + 1) * var_count, :].astype(wide)).astype(
                        low
                    )
                    for k in range(5)
                ]
                + [jnp.zeros((padded - 5 * var_count, tokens), low)],
                axis=0,
            )
            start = pl.multiple_of(h * HEAD_DIM, HEAD_DIM)
            mixed_ref[pl.ds(start, HEAD_DIM), :] = dot(
                value_table[pl.ds(start, HEAD_DIM), :], pooled
            ).astype(low)
            return carry

        lax.fori_loop(first, first + 4, head_step, 0)

    def begin_block():
        load(outs[4], weight_a, 2).wait()
        total = lead_ref[...] * vector_ref[0:1] + vector_ref[1:2]
        mixed = mixed_ref[...].T
        for side in range(halves):
            total = total + dot(
                mixed[:, side * half_width : (side + 1) * half_width],
                weight_a[side].reshape(-1, half_width),
                1,
                1,
            )
        start_ref[...] = total
        normed, _ = norm_parts(total)
        low_ref[...] = (normed * vector_ref[2:3] + vector_ref[3:4]).astype(low)

    def ask_input(kind):
        target = weight_b if kind % 2 == 0 else weight_a
        load(outs[5].at[kind], target, 3 - kind % 2).start()

    def project(kind):
        target = weight_b if kind % 2 == 0 else weight_a
        load(outs[5].at[kind], target, 3 - kind % 2).wait()
        pairs = half_width // lanes
        for side in range(halves):
            result = dot(low_ref[...], target[side].reshape(-1, half_width)).astype(low)
            if kind == 0:
                result = result * low(HEAD_DIM ** (-0.5))
            for pair in range(pairs):
                projected[side * pairs + pair, kind] = result[
                    :, pair * lanes : (pair + 1) * lanes
                ]

    def inward(step):
        there = lax.rem(me + step, peers)
        return remote(
            projected.at[there],
            joint.at[me],
            send_sem.at[there],
            recv_sem.at[me],
            plane_device(z, there),
        )

    def outward(index):
        return remote(
            sending.at[index],
            received.at[me],
            out_send.at[index],
            out_recv.at[me],
            plane_device(z, index),
        )

    def send_heads():
        pltpu.make_async_copy(projected.at[me], joint.at[me], own_sem).start()
        for step in range(1, peers):
            inward(step).start()

    def take_heads():
        pltpu.make_async_copy(projected.at[me], joint.at[me], own_sem).wait()
        for step in range(1, peers):
            there = lax.rem(me + step, peers)
            pltpu.make_async_copy(joint.at[there], joint.at[there], recv_sem.at[there]).wait()

    def attention(first, count):
        def block(step, carry):
            index = lax.rem(me + 1 + step, peers)
            span = pl.ds(pl.multiple_of(index * share, share), share)
            queries = joint[index, 0]
            keys = joint[:, 1].reshape(slots, lanes)
            values = joint[:, 2].reshape(slots, lanes)
            allowed = crop_ref[span, :] == tag_ref[0:1, :]
            result = None
            for h in range(2):
                scores = dot(head_lanes(queries, h), keys, 1, 1)
                scores = jnp.where(allowed, scores, masked_score)
                largest = jnp.max(scores, axis=1, keepdims=True)
                weights = jnp.exp(scores - largest)
                total = jnp.sum(weights, axis=1, keepdims=True)
                weights = (weights * (1.0 / total)).astype(low)
                part = head_lanes(dot(weights, values), h)
                result = part if result is None else result + part
                total_ref[h, span, :] = largest + jnp.log(total)
            wide_ref[span, :] = result
            sending[index] = result.astype(low)

            @pl.when(step < peers - 1)
            def _():
                outward(index).start()

            return carry

        lax.fori_loop(first, first + count, block, 0)

    ready = {}
    for number, item in enumerate(items):
        ready[item[:2]] = number + 8
    at = ready[(3, None)]
    extra = {at: [ask_small, read_small], at + 1: [score]}
    extra[at + 2] = [lambda: tables(weight_b, 3, value_table), ask_back]
    for quarter in range(4):
        extra.setdefault(at + 3 + quarter // 2, []).append(partial(heads, 4 * quarter))
    at = max(at + 5, ready[(5, 2)])
    extra.setdefault(at, []).extend([partial(ask_input, 0), begin_block, partial(ask_input, 1)])
    extra[at + 1] = [partial(project, 0), partial(ask_input, 2), partial(project, 1)]
    extra[at + 2] = [partial(project, 2), send_heads]
    at += 5
    extra[at] = [take_heads]
    for step in range(4):
        extra.setdefault(at + step, []).append(partial(attention, 2 * step, 2))
    total = len(items)
    for step in range(max(total + 8, max(extra) + 1)):
        for back, stage in enumerate(stages):
            if 0 <= step - 2 * back < total:
                stage(step - 2 * back)
        for work in extra.get(step, []):
            work()
    last = pltpu.make_async_copy(sending.at[me], received.at[me], out_own)
    last.start()
    for number in range(total):
        finish(number)
    for letter in letters:
        settle(*letter)
    for side in range(2):
        for part in range(2):
            pltpu.make_async_copy(
                grad_in.at[0], grad_out.at[side, part], post_recv.at[2 + 2 * side + part]
            ).wait()
    for step in range(1, peers):
        there = lax.rem(me + step, peers)
        inward(step).wait_send()
        outward(there).wait_send()
        pltpu.make_async_copy(sending.at[there], received.at[there], out_recv.at[there]).wait()
    last.wait()


def front(arrays, cut, grads, hours, head_count, number):
    items = []
    for index, array in enumerate(arrays):
        for lead in range(array.shape[0]) if array.ndim == 3 else (None,):
            rows = array.shape[-2]
            if rows % 64:
                items.append((index, lead, 0, rows, 0))
                continue
            for color in range(2):
                items.append((index, lead, color * rows // 2, rows // 2, color))
    width = arrays[2].shape[1]
    model = 2 * width
    var_count = cut.shape[1] // 4
    tokens = 2 * cut.shape[2]
    padded = 2 * arrays[1].shape[1]
    slots = 8 * tokens
    sem = pltpu.SemaphoreType.DMA
    vmem = pl.BlockSpec(memory_space=pltpu.VMEM)
    hbm = pl.BlockSpec(memory_space=pl.ANY)
    block = (2, 4, 2, 2)

    def all_of(array):
        return array.shape[:-2] + block + array.shape[-2:]

    low_outs = [all_of(a) for a in arrays] + [(2, 2) + grads.shape[1:], (8, tokens, 128)]
    vmem_outs = [
        ((8, 3, tokens, 128), low),
        ((slots, 128), wide),
        ((2, slots, 1), wide),
        ((8, slots), wide),
        ((slots, 1), wide),
        ((padded, tokens), low),
        ((head_count, var_count, tokens), wide),
        ((model, tokens), low),
        ((model, padded), low),
        ((model, padded), wide),
        ((head_count, padded), wide),
        ((model, padded), low),
        ((8, model), wide),
        ((head_count, 128), wide),
        ((tokens, model), wide),
        ((tokens, model), low),
        ((tokens, 1), wide),
        ((tokens, 1), wide),
    ]
    result = pl.pallas_call(
        partial(front_kernel, items),
        out_shape=[jax.ShapeDtypeStruct(shape, low) for shape in low_outs]
        + [jax.ShapeDtypeStruct(shape, dtype) for shape, dtype in vmem_outs],
        in_specs=[hbm] * (len(arrays) + 2) + [vmem],
        out_specs=[hbm] * len(low_outs) + [vmem] * len(vmem_outs),
        scratch_shapes=[
            pltpu.VMEM(cut.shape, low),
            pltpu.VMEM(all_of(arrays[0]), low),
            pltpu.VMEM(all_of(arrays[1]), low),
            pltpu.VMEM(all_of(arrays[2]), low),
            pltpu.VMEM(all_of(arrays[2]), low),
            pltpu.VMEM((8, 3, tokens, 128), low),
            pltpu.VMEM((8, tokens, 128), low),
            pltpu.VMEM((slots, 1), wide),
            sem((len(items),)),
        ]
        + [sem((len(items), 3))] * 4
        + [sem((6,)), sem((6,)), sem((4,)), sem, sem((8,)), sem((8,)), sem, sem((8,)), sem((8,))],
        compiler_params=pltpu.CompilerParams(
            collective_id=number, has_side_effects=True, vmem_limit_bytes=58 * 2**20
        ),
    )(*arrays, cut, grads, hours)
    count = len(arrays)
    gathered = [
        g.reshape(a.shape[:-2] + (2, 16 * a.shape[-2], a.shape[-1]))
        for g, a in zip(result, arrays)
    ]
    return gathered, result[count:]


def feed_kernel(
    attended_ref,
    proj_ref,
    start_ref,
    vector_ref,
    up_ref,
    down_ref,
    bias_ref,
    final_ref,
    masked_ref,
    keep_ref,
    predicted_ref,
    middle_grad_ref,
    unit_ref,
    grad_feed_ref,
    grad_proj_ref,
    grad_final_ref,
    grad_bias_ref,
    grad_vector_ref,
    flat,
    middle,
    second,
    second_turned,
    active,
    slope,
    total,
    grad_low,
    grad_turned,
    grad_final,
):
    step = pl.program_id(0)
    count = active.shape[0]
    row_count, units, share, lanes = attended_ref.shape
    _, halves, _, half_width = proj_ref.shape
    tokens = row_count * share

    @pl.when(step == 0)
    def _():
        for unit in range(units):
            flat[:, unit * lanes : (unit + 1) * lanes] = attended_ref[:, unit].reshape(
                tokens, lanes
            )
        result = start_ref[...]
        for side in range(halves):
            result = result + dot(
                flat[:, side * half_width : (side + 1) * half_width], proj_ref[0, side], 1, 1
            )
        middle[...] = result
        normed, _ = norm_parts(result)
        normed = (normed * vector_ref[4:5] + vector_ref[5:6]).astype(low)
        second[...] = normed
        second_turned[...] = normed.T
        total[...] = result

    @pl.when(step < count)
    def _():
        hidden = dot(second[...], up_ref[0, 0]) + bias_ref[...]
        share_of = 0.5 * (1.0 + lax.erf(hidden * (0.5**0.5)))
        fired = (hidden * share_of).astype(low)
        active[step] = fired
        slope[step] = share_of + hidden * jnp.exp(-0.5 * hidden * hidden) * (
            0.5 / 1.2533141373155003
        )
        total[...] += dot(fired, down_ref[0, 0], 1, 1)

    @pl.when(step == count - 1)
    def _():
        final_low = total[...].astype(low)
        final_turned = final_low.T
        grads = None
        for side in range(halves):
            predicted_ref[side] = (dot(final_low, final_ref[side]) * keep_ref[...]).astype(low)
            part = dot(masked_ref[side], final_ref[side], 1, 1)
            grads = part if grads is None else grads + part
            grad_final_ref[side] = dot(final_turned, masked_ref[side]).astype(low)
        grad_final[...] = grads
        grad_low[...] = grads.astype(low)
        grad_turned[...] = grads.astype(low).T
        total[...] = jnp.zeros_like(total)

    @pl.when(step >= count)
    def _():
        block = step - count
        hidden_grad = dot(grad_low[...], down_ref[0, 0]) * slope[block]
        hidden_low = hidden_grad.astype(low)
        grad_bias_ref[...] = jnp.sum(hidden_low.astype(wide), axis=0, keepdims=True)
        total[...] += dot(hidden_low, up_ref[0, 0], 1, 1)
        grad_feed_ref[0, 0] = dot(second_turned[...], hidden_low).astype(low)
        grad_feed_ref[1, 0] = dot(grad_turned[...], active[block]).astype(low)

    @pl.when(step == 2 * count - 1)
    def _():
        part, grad_gain, grad_shift = norm_back(middle[...], vector_ref[4:5], total[...])
        result = grad_final[...] + part
        middle_grad_ref[...] = result
        grad_vector_ref[0:1] = grad_gain
        grad_vector_ref[1:2] = grad_shift
        result_low = result.astype(low)
        result_turned = result_low.T
        pairs = half_width // lanes
        for side in range(halves):
            span = slice(side * half_width, (side + 1) * half_width)
            grad_proj_ref[side] = dot(result_turned, flat[:, span]).astype(low)
            out = dot(result_low, proj_ref[0, side]).astype(low)
            for pair in range(pairs):
                unit_ref[:, side * pairs + pair] = out[
                    :, pair * lanes : (pair + 1) * lanes
                ].reshape(row_count, share, lanes)


def feed(attended, start, vectors, late, up_bias, final_weight, masked, keep):
    blocks, halves, model, block = late.shape
    half_width = block
    each = blocks // 2
    full = each * block
    tokens = start.shape[0]
    count = halves * each

    def block_of_kind(kind):
        def block_at(i):
            j = lax.rem(i, count)
            return (kind * each + lax.rem(j, each), lax.div(j, each), 0, 0)

        return pl.BlockSpec((1, 1, model, block), block_at)

    def late_block(i):
        j = lax.max(i - count, 0)
        return (0, lax.div(j, each), 0, lax.rem(j, each))

    def fixed(shape, dtype):
        rank = len(shape)
        return jax.ShapeDtypeStruct(shape, dtype), pl.BlockSpec(shape, lambda i: (0,) * rank)

    outs = [
        fixed((halves, tokens, 128), low),
        fixed((tokens, model), wide),
        fixed(attended.shape, low),
        (
            jax.ShapeDtypeStruct((2, halves, model, full), low),
            pl.BlockSpec((2, 1, model, block), late_block),
        ),
        fixed((halves, model, half_width), low),
        fixed((halves, model, 128), low),
        (
            jax.ShapeDtypeStruct((1, halves * full), wide),
            pl.BlockSpec((1, block), lambda i: (0, lax.max(i - count, 0))),
        ),
        fixed((2, model), wide),
    ]
    return pl.pallas_call(
        feed_kernel,
        grid=(2 * count,),
        out_shape=[shape for shape, _ in outs],
        in_specs=[
            whole(attended),
            pl.BlockSpec((1, halves, model, block), lambda i: (blocks - 1, 0, 0, 0)),
            whole(start),
            whole(vectors),
            block_of_kind(0),
            block_of_kind(1),
            pl.BlockSpec((1, block), lambda i: (0, lax.rem(i, count))),
            whole(final_weight),
            whole(masked),
            whole(keep),
        ],
        out_specs=[spec for _, spec in outs],
        scratch_shapes=[
            pltpu.VMEM((tokens, model), low),
            pltpu.VMEM((tokens, model), wide),
            pltpu.VMEM((tokens, model), low),
            pltpu.VMEM((model, tokens), low),
            pltpu.VMEM((count, tokens, block), low),
            pltpu.VMEM((count, tokens, block), wide),
            pltpu.VMEM((tokens, model), wide),
            pltpu.VMEM((tokens, model), low),
            pltpu.VMEM((model, tokens), low),
            pltpu.VMEM((tokens, model), wide),
        ],
        compiler_params=pltpu.CompilerParams(vmem_limit_bytes=56 * 2**20),
    )(attended, late, start, vectors, late, late, up_bias, final_weight, masked, keep)


def return_kernel(
    grads_ref,
    weight_ref,
    low_ref,
    start_ref,
    middle_grad_ref,
    vector_ref,
    lead_ref,
    back_ref,
    mixed_ref,
    grad_input_ref,
    grad_mixer_ref,
    mixed_grad_ref,
    grad_vector_ref,
    turned,
    total,
):
    step = pl.program_id(0)
    halves, _, half_width = back_ref.shape
    row_count, _, _, share, lanes = grads_ref.shape
    tokens = row_count * share
    pairs = half_width // lanes

    @pl.when(step == 0)
    def _():
        turned[...] = low_ref[...].T
        total[...] = jnp.zeros_like(total)

    kind, side = lax.div(step, halves), lax.rem(step, halves)
    piece = jnp.concatenate(
        [grads_ref[:, side * pairs + pair, kind].reshape(tokens, lanes) for pair in range(pairs)],
        axis=1,
    )
    total[...] += dot(piece, weight_ref[0, 0], 1, 1)
    grad_input_ref[0, 0] = dot(turned[...], piece).astype(low)

    @pl.when(step == pl.num_programs(0) - 1)
    def _():
        part, grad_gain, grad_shift = norm_back(start_ref[...], vector_ref[2:3], total[...])
        result = middle_grad_ref[...] + part
        grad_vector_ref[0:1] = jnp.sum(result * lead_ref[...], axis=0, keepdims=True)
        grad_vector_ref[1:2] = jnp.sum(result, axis=0, keepdims=True)
        grad_vector_ref[2:3] = grad_gain
        grad_vector_ref[3:4] = grad_shift
        result_low = result.astype(low)
        result_turned = result_low.T
        for half in range(halves):
            span = slice(half * half_width, (half + 1) * half_width)
            grad_mixer_ref[half] = dot(result_turned, mixed_ref[span, :], 1, 1).astype(low)
            mixed_grad_ref[span, :] = dot(result_low, back_ref[half]).astype(low).T


def go_back(grads, weights, first_low, start, middle_grad, vectors, lead_column, back_weight, mixed):
    kinds, halves, model, half_width = weights.shape
    tokens = start.shape[0]
    block = pl.BlockSpec((1, 1, model, half_width), lambda i: (i // halves, i % halves, 0, 0))
    return pl.pallas_call(
        return_kernel,
        grid=(kinds * halves,),
        out_shape=[
            jax.ShapeDtypeStruct(weights.shape, low),
            jax.ShapeDtypeStruct((halves, model, half_width), low),
            jax.ShapeDtypeStruct((model, tokens), low),
            jax.ShapeDtypeStruct((4, model), wide),
        ],
        in_specs=[
            whole(grads),
            block,
            whole(first_low),
            whole(start),
            whole(middle_grad),
            whole(vectors),
            whole(lead_column),
            whole(back_weight),
            whole(mixed),
        ],
        out_specs=[
            block,
            pl.BlockSpec((halves, model, half_width), lambda i: (0, 0, 0)),
            pl.BlockSpec((model, tokens), lambda i: (0, 0)),
            pl.BlockSpec((4, model), lambda i: (0, 0)),
        ],
        scratch_shapes=[pltpu.VMEM((model, tokens), low), pltpu.VMEM((tokens, model), wide)],
        compiler_params=pltpu.CompilerParams(vmem_limit_bytes=50 * 2**20),
    )(grads, weights, first_low, start, middle_grad, vectors, lead_column, back_weight, mixed)


def einsum(spec, left, right):
    return jnp.einsum(spec, left, right, preferred_element_type=wide)


def fast_local(
    pixels,
    crop_starts,
    crop_shifts,
    slot_crops,
    occupied,
    lead_hours,
    patch_weight,
    variable_embed,
    mixer_query,
    mixer_keys,
    mixer_values,
    mixer_output,
    lead_embed,
    first_gain,
    first_bias,
    attention_in,
    attention_out,
    second_gain,
    second_bias,
    expand_weight,
    expand_bias,
    reduce_weight,
    output_weight,
    cotangent,
):
    lon, head = lax.axis_index(LON), lax.axis_index(HEAD)
    row_count, slot_width = slot_crops.shape
    share = slot_width // HEAD_SIZE
    tokens = row_count * share
    var_count, lat_count, column_count = pixels.shape
    head_half, query_width = mixer_query.shape
    head_count = HEAD_SIZE * head_half
    half_width = head_half * HEAD_DIM
    out_half = output_weight.shape[1]
    slice_width = patch_weight.shape[2]
    model = slice_width * LON_SIZE * HEAD_SIZE
    block_rows = model // LON_SIZE
    taps = 4 * var_count
    pairs = half_width // 128
    scale = HEAD_DIM ** (-0.5)

    last = lax.slice_in_dim(pixels, column_count - 1, column_count, axis=2)
    up = [(i, (i + 1) % LON_SIZE) for i in range(LON_SIZE)]
    down = [(j, i) for i, j in up]
    before = lax.ppermute(last, LON, up)
    after = lax.ppermute(pixels[:, :, :1], LON, down)
    lat_slot = crop_lookup(crop_starts, slot_crops)
    shift_slot = crop_lookup(crop_shifts, slot_crops)
    lat_lanes = jnp.tile(lat_slot, (1, 2))
    shift_lanes = jnp.tile(shift_slot, (1, 2))
    wanted = jnp.arange(2 * 2 * slot_width)
    side, wanted = wanted // (2 * slot_width), wanted % (2 * slot_width)
    wanted = 2 * (wanted % slot_width) + 2 * side + wanted // slot_width - 1
    select = (jnp.arange(column_count)[:, None] == wanted[None, :]).astype(low)
    field = einsum("vac,cn->avn", pixels, select)
    field = field + jnp.where(wanted == -1, jnp.transpose(before, (1, 0, 2)).astype(wide), 0.0)
    field = field + jnp.where(
        wanted == column_count, jnp.transpose(after, (1, 0, 2)).astype(wide), 0.0
    )
    field = field.astype(low)
    pair_rows = row_count // HEAD_SIZE
    cut = cut_patches(
        field,
        block_slice(lat_lanes, head, pair_rows, 0),
        block_slice(shift_lanes, head, pair_rows, 0),
    )
    masked = cotangent * occupied[:, :, None].astype(low)
    masked = jnp.pad(masked, ((0, 0), (0, 0), (0, 128 - out_half)))
    late = jnp.concatenate(
        [
            jnp.transpose(part.reshape(block_rows, -1, half_width), (1, 0, 2))
            for part in (expand_weight, reduce_weight.T, attention_out.T)
        ]
    )
    padded = 256
    small = jnp.concatenate(
        [
            jnp.transpose(patch_weight, (1, 0, 2)).reshape(taps, slice_width),
            variable_embed,
            lead_embed,
            first_gain[None],
            first_bias[None],
            second_gain[None],
            second_bias[None],
            jnp.zeros((padded - taps - var_count - 6, slice_width), low),
        ]
    ).T
    small = jnp.concatenate([small[:, :128], small[:, 128:]])
    tags = jnp.where(occupied == 1, slot_crops, -1).astype(low)
    lane = jnp.arange(128) % (LON_SIZE * query_width) // query_width
    spread = jnp.tile(jnp.concatenate([mixer_query, expand_bias]), (1, 128 // query_width))
    spread = jnp.where(lane == lon, spread, 0)
    misc = jnp.concatenate([tags, slot_crops.astype(low), spread])
    out_block = jnp.pad(output_weight, ((0, 0), (0, 128 - out_half)))
    my_row = lax.div(lon, LON_SIZE // row_count)
    hours = lax.dynamic_index_in_dim(lead_hours, my_row, 0).astype(wide) / 100.0
    hours = jnp.pad(hours, ((0, 0), (0, 128 - hours.shape[1])))
    gathered, made = front(
        [
            misc,
            small,
            mixer_keys,
            mixer_values,
            mixer_output.T,
            attention_in,
            out_block,
            late,
        ],
        cut,
        masked,
        hours,
        head_count,
        1,
    )
    misc_all, _, key_weight, value_weight, mixer_weight, input_weight, final_weight, late = gathered
    masked, attended, joint, attended_wide, totals, tag_row, crop_column = made[:7]
    patches, probs, mixed, value_table, key_table, score_table = made[7:13]
    patch_full, vectors, query, start_sum, first_low, lead_column, keep_mask = made[13:]
    masked = masked.reshape(HEAD_SIZE, tokens, 128)
    attended = attended[None]
    query = query[:, :HEAD_DIM]
    bias_rows = expand_bias.shape[0]
    up_bias = misc_all.reshape(HEAD_SIZE, LON_SIZE, -1, 128)[:, :, 2 * row_count + head_half :]
    up_bias = jnp.sum(up_bias[..., : LON_SIZE * query_width].astype(wide), axis=1)
    units = HEAD_SIZE * pairs
    (
        predicted,
        middle_grad,
        out_grads,
        grad_feed,
        grad_proj,
        grad_out,
        grad_up_bias,
        second_vectors,
    ) = feed(
        attended,
        start_sum,
        vectors,
        late,
        up_bias.reshape(1, -1),
        final_weight,
        masked,
        keep_mask,
    )
    stacked, feed_sums = attend_back(
        joint,
        tag_row,
        crop_column,
        attended_wide,
        totals,
        out_grads.reshape(units, tokens, 128),
        grad_feed,
        4,
    )
    stacked = stacked[None]
    grad_input, grad_mixer, mixed_grads, first_vectors = go_back(
        stacked,
        input_weight,
        first_low,
        start_sum,
        middle_grad,
        vectors,
        lead_column,
        mixer_weight,
        mixed,
    )
    pooled_grads, counts, cut_grads = mixer_backward(
        patches, probs, score_table, value_table, mixed_grads
    )
    counts = counts * scale
    pooled_low = pooled_grads.astype(low)
    grad_values = dot(patch_full, pooled_low, 1, 1).astype(low)
    key_low = (query[:, :, None] * counts[:, None, :]).astype(low).reshape(model, padded)
    grad_small = einsum(
        "xde,xem->dm", key_weight, key_low.reshape(HEAD_SIZE, half_width, padded)
    ) + einsum("xde,xem->dm", value_weight, pooled_low.reshape(HEAD_SIZE, half_width, padded))
    head_sums = einsum("dm,hm->dh", patch_full.astype(wide), counts)
    grad_query = jnp.sum(
        key_table.reshape(head_count, HEAD_DIM, padded) * counts[:, None, :], axis=2
    )

    vector_grads = jnp.concatenate([first_vectors, second_vectors]).T
    spot = taps + var_count
    grad_small = jnp.concatenate(
        [grad_small[:, :spot], vector_grads, jnp.zeros((model, padded - spot - 6), wide)], axis=1
    )
    grad_small = jnp.transpose(
        grad_small.reshape(LON_SIZE, HEAD_SIZE, slice_width, 2, 128), (0, 3, 2, 1, 4)
    ).reshape(model, HEAD_SIZE, 128)
    head_block = head_sums.reshape(model, HEAD_SIZE, head_half)
    bias_cols = expand_bias.shape[1]
    bias_block = jnp.transpose(
        grad_up_bias.reshape(HEAD_SIZE, bias_rows, LON_SIZE, bias_cols), (2, 1, 0, 3)
    )
    bias_block = jnp.pad(
        bias_block, ((0, 0), (0, block_rows - bias_rows), (0, 0), (0, 0))
    ).reshape(model, HEAD_SIZE, bias_cols)
    query_block = jnp.transpose(
        grad_query.reshape(HEAD_SIZE, head_half, LON_SIZE, query_width), (2, 1, 0, 3)
    )
    query_block = jnp.pad(
        query_block, ((0, 0), (0, block_rows - head_half), (0, 0), (0, 0))
    ).reshape(model, HEAD_SIZE, query_width)
    extra = head_half + bias_cols + query_width
    filler = jnp.zeros((model, 128 - out_half - extra), wide)
    tail = jnp.stack(
        [
            jnp.concatenate(
                [
                    grad_small[:, side],
                    grad_out[side, :, :out_half].astype(wide),
                    head_block[:, side],
                    bias_block[:, side],
                    query_block[:, side],
                    filler,
                ],
                axis=1,
            )
            for side in range(2)
        ]
    ).astype(low)
    sums, predicted, pixel_grad = reduce_all(
        [grad_proj, grad_input, grad_mixer, grad_values, tail],
        predicted.reshape(HEAD_SIZE, 2, slot_width, 128),
        cut_grads,
        lat_lanes,
        shift_lanes,
        lat_count,
        2,
    )
    predicted = predicted[:, :, :out_half]
    full_half = expand_weight.shape[1]
    place = [0]

    def take(width):
        begin = place[0]
        place[0] = begin + width
        return sums[:, begin : begin + width]

    out_up = feed_sums[:, :full_half]
    out_down = feed_sums[:, full_half:].T
    out_proj = take(half_width).T
    out_input = jnp.stack([take(half_width) for _ in range(3)])
    out_mixer = take(half_width).T
    out_values = take(half_width)
    tail_small = take(128)
    tail_rest = take(128)
    tail_small = jnp.concatenate([tail_small[:slice_width], tail_small[slice_width:]], axis=1).T
    out_patch = jnp.transpose(tail_small[:taps].reshape(4, var_count, slice_width), (1, 0, 2))
    out_variable = tail_small[taps:spot]
    out_lead = tail_small[spot : spot + 2]
    out_final = tail_rest[:, :out_half]
    at = out_half
    my_heads = tail_rest[:, at : at + head_half]
    at += head_half
    out_bias = tail_rest[:bias_rows, at : at + bias_cols]
    at += bias_cols
    out_query = tail_rest[:head_half, at : at + query_width]
    my_query = block_slice(query, head, head_half, 0)
    out_keys = (my_heads[:, :, None] * my_query[None]).reshape(block_rows, half_width)

    pixel_grad = jnp.transpose(pixel_grad, (1, 0, 2))
    return (
        predicted,
        pixel_grad,
        out_patch,
        out_variable,
        out_query,
        out_keys,
        out_values,
        out_mixer,
        out_lead,
        tail_small[spot + 2],
        tail_small[spot + 3],
        out_input,
        out_proj,
        tail_small[spot + 4],
        tail_small[spot + 5],
        out_up,
        out_bias,
        out_down,
        out_final,
    )


def solution(mesh):
    body = fast_local if planned(mesh) else local
    placed = (
        P(None, None, LON),
        P(),
        P(),
        P(None, LON),
        P(None, LON),
        P(),
        P(None, None, (LON, HEAD)),
        P(None, (LON, HEAD)),
        P(HEAD, LON),
        P(LON, HEAD),
        P(LON, HEAD),
        P(HEAD, LON),
        P(None, (LON, HEAD)),
        P((LON, HEAD)),
        P((LON, HEAD)),
        P(None, LON, HEAD),
        P(HEAD, LON),
        P((LON, HEAD)),
        P((LON, HEAD)),
        P(LON, HEAD),
        P(HEAD, LON),
        P(HEAD, LON),
        P(LON, HEAD),
        P(None, LON, HEAD),
    )
    return jax.shard_map(
        body,
        mesh=mesh,
        in_specs=placed,
        out_specs=(
            P(None, LON, HEAD),
            P(None, None, LON),
            P(None, None, (LON, HEAD)),
            P(None, (LON, HEAD)),
            P(HEAD, LON),
            P(LON, HEAD),
            P(LON, HEAD),
            P(HEAD, LON),
            P(None, (LON, HEAD)),
            P((LON, HEAD)),
            P((LON, HEAD)),
            P(None, LON, HEAD),
            P(HEAD, LON),
            P((LON, HEAD)),
            P((LON, HEAD)),
            P(LON, HEAD),
            P(HEAD, LON),
            P(HEAD, LON),
            P(LON, HEAD),
        ),
        check_vma=False,
    )
```

```python
from functools import partial

import jax
import jax.numpy as jnp
from jax import lax
from jax.experimental import pallas as pl
from jax.experimental.pallas import tpu as pltpu
from jax.sharding import PartitionSpec as P

HEAD_DIM = 64
LON, HEAD = "lon", "head"


epsilon = 1e-05
masked_score = -1e30
highest = lax.Precision.HIGHEST


def extended(array, sides, width):
    for axis, dim in sides:
        count, length = (lax.axis_size(axis), array.shape[dim])
        up = [(i, (i + 1) % count) for i in range(count)]
        down = [(j, i) for i, j in up]
        last = lax.slice_in_dim(array, length - width, length, axis=dim)
        leading = lax.slice_in_dim(array, 0, width, axis=dim)
        before = lax.ppermute(last, axis, up)
        after = lax.ppermute(leading, axis, down)
        array = jnp.concatenate([before, array, after], axis=dim)
    return array


def layer_norm(values, gain_vector, shift_vector):
    center = values - jnp.mean(values, axis=-1, keepdims=True)
    spread = jnp.mean(center * center, axis=-1, keepdims=True)
    return center * lax.rsqrt(spread + epsilon) * gain_vector + shift_vector


def head_total(partial_sum):
    return lax.psum(partial_sum.astype(jnp.bfloat16), HEAD).astype(jnp.float32)


def head_share(partial_sum):
    return lax.psum_scatter(
        partial_sum.astype(jnp.bfloat16), HEAD, scatter_dimension=0, tiled=True
    ).astype(jnp.float32)


def head_rows(values):
    return lax.all_gather(values, HEAD, axis=0, tiled=True)


def reduce_rows(partial_sum):
    return head_share(partial_sum)


def spread_rows(values):
    return head_rows(values)


def crop_lookup(crop_table, slot_numbers):
    numbers = jnp.arange(crop_table.shape[1], dtype=jnp.int32)
    picked = slot_numbers[:, :, None] == numbers[None, None, :]
    return jnp.sum(jnp.where(picked, crop_table[:, None, :], 0), axis=2)


def outer_sum(left_rows, right_rows):
    return jnp.einsum("ti,tj->ij", left_rows, right_rows, preferred_element_type=jnp.float32)


def block_slice(values, block_index, block_width, axis_number):
    return lax.dynamic_slice_in_dim(values, block_index * block_width, block_width, axis_number)


def block_scores(queries, query_crops, key_block, key_tags):
    scores = jnp.einsum(
        "rqhd,rkhd->rhqk", queries, key_block, preferred_element_type=jnp.float32
    ) * HEAD_DIM ** (-0.5)
    matched = query_crops[:, None, :, None] == key_tags[:, None, None, :]
    return (jnp.where(matched, scores, masked_score), matched)


def key_stats(queries, query_crops, key_rows, key_tags, block_width):
    row_count, slot_count, head_count, head_size = queries.shape

    def key_step(carried, block_index):
        largest, totals = carried
        scores, matched = block_scores(
            queries,
            query_crops,
            block_slice(key_rows, block_index, block_width, 1),
            block_slice(key_tags, block_index, block_width, 1),
        )
        raised = jnp.maximum(largest, jnp.max(scores, axis=-1))
        totals = totals * jnp.exp(largest - raised) + jnp.sum(
            jnp.where(matched, jnp.exp(scores - raised[..., None]), 0.0), axis=-1
        )
        return ((raised, totals), None)

    initial = (
        jnp.full((row_count, head_count, slot_count), masked_score, jnp.float32),
        jnp.zeros((row_count, head_count, slot_count), jnp.float32),
    )
    (largest, totals), _ = lax.scan(key_step, initial, jnp.arange(key_rows.shape[1] // block_width))
    return largest + jnp.log(totals)


def attend(queries, query_crops, key_rows, value_rows, key_tags, log_totals, block_width):

    def attend_step(running, block_index):
        scores, matched = block_scores(
            queries,
            query_crops,
            block_slice(key_rows, block_index, block_width, 1),
            block_slice(key_tags, block_index, block_width, 1),
        )
        weights = jnp.where(matched, jnp.exp(scores - log_totals[..., None]), 0.0).astype(
            jnp.bfloat16
        )
        value_block = block_slice(value_rows, block_index, block_width, 1)
        return (
            running
            + jnp.einsum(
                "rhqk,rkhd->rqhd", weights, value_block, preferred_element_type=jnp.float32
            ),
            None,
        )

    outputs, _ = lax.scan(
        attend_step,
        jnp.zeros(queries.shape, jnp.float32),
        jnp.arange(key_rows.shape[1] // block_width),
    )
    return outputs


def score_grads(
    queries, query_crops, out_grads, log_totals, deltas, key_block, value_block, key_tags
):
    scores, matched = block_scores(queries, query_crops, key_block, key_tags)
    weights = jnp.where(matched, jnp.exp(scores - log_totals[..., None]), 0.0)
    weight_grads = jnp.einsum(
        "rqhd,rkhd->rhqk", out_grads, value_block, preferred_element_type=jnp.float32
    )
    score_delta = (weights * (weight_grads - deltas[..., None])).astype(jnp.bfloat16)
    return (score_delta, weights.astype(jnp.bfloat16))


def mixer_row(patch_row, full_patch, full_variable, pair_weight, head_query):
    embedded = jnp.einsum(
        "svk,vkd->svd", patch_row, full_patch, preferred_element_type=jnp.float32
    ) + full_variable.astype(jnp.float32)
    embedded = embedded.astype(jnp.bfloat16)
    slot_count, var_count, model_width = embedded.shape
    head_count, head_size = head_query.shape
    local_width = head_count * head_size
    paired = jnp.dot(
        embedded.reshape(slot_count * var_count, model_width),
        pair_weight,
        preferred_element_type=jnp.float32,
    ).astype(jnp.bfloat16)
    key_rows = paired[:, :local_width].reshape(slot_count, var_count, head_count, head_size)
    value_rows = paired[:, local_width:].reshape(slot_count, var_count, head_count, head_size)
    scores = jnp.einsum(
        "svhd,hd->shv", key_rows, head_query, preferred_element_type=jnp.float32
    ) * HEAD_DIM ** (-0.5)
    weights = jax.nn.softmax(scores, axis=-1)
    return (embedded, key_rows, value_rows, weights)


def mixer_back(carried, inputs, full_patch, full_variable, pair_weight, head_query):
    patch_row, mixed_grad = inputs
    embedded, key_rows, value_rows, weights = mixer_row(
        patch_row, full_patch, full_variable, pair_weight, head_query
    )
    slot_count, var_count, model_width = embedded.shape
    local_width = key_rows.shape[2] * key_rows.shape[3]
    mixed_wide = mixed_grad.astype(jnp.float32)
    value_grads = jnp.einsum("shv,shd->svhd", weights, mixed_wide, precision=highest).astype(
        jnp.bfloat16
    )
    weight_grads = jnp.einsum(
        "shd,svhd->shv", mixed_wide, value_rows.astype(jnp.float32), precision=highest
    )
    score_delta = (
        weights
        * (weight_grads - jnp.sum(weights * weight_grads, axis=-1, keepdims=True))
        * HEAD_DIM ** (-0.5)
    )
    key_grads = jnp.einsum(
        "shv,hd->svhd", score_delta, head_query.astype(jnp.float32), precision=highest
    ).astype(jnp.bfloat16)
    query_grad = jnp.einsum(
        "shv,svhd->hd", score_delta, key_rows.astype(jnp.float32), precision=highest
    )
    pair_grads = jnp.concatenate(
        [
            key_grads.reshape(slot_count * var_count, local_width),
            value_grads.reshape(slot_count * var_count, local_width),
        ],
        axis=1,
    )
    embed_grad = jnp.einsum(
        "ne,de->nd", pair_grads, pair_weight, preferred_element_type=jnp.float32
    )
    pair_weight_grad = outer_sum(embedded.reshape(slot_count * var_count, model_width), pair_grads)
    embed_grad = embed_grad.reshape(slot_count, var_count, model_width)
    patch_grad = jnp.einsum(
        "svk,svd->vkd", patch_row.astype(jnp.float32), embed_grad, precision=highest
    )
    variable_grad = jnp.sum(embed_grad, axis=0)
    slot_grad = jnp.einsum(
        "svd,vkd->svk", embed_grad, full_patch.astype(jnp.float32), precision=highest
    )
    patch_acc, variable_acc, query_acc, pair_acc = carried
    return (
        (
            patch_acc + patch_grad,
            variable_acc + variable_grad,
            query_acc + query_grad,
            pair_acc + pair_weight_grad,
        ),
        slot_grad,
    )


def local(
    pixels,
    crop_starts,
    crop_shifts,
    slot_crops,
    occupied,
    lead_hours,
    patch_weight,
    variable_embed,
    mixer_query,
    mixer_keys,
    mixer_values,
    mixer_output,
    lead_embed,
    first_gain,
    first_bias,
    attention_in,
    attention_out,
    second_gain,
    second_bias,
    expand_weight,
    expand_bias,
    reduce_weight,
    output_weight,
    cotangent,
):
    shared = (
        lax.all_gather(patch_weight, (LON, HEAD), axis=2, tiled=True),
        lax.all_gather(variable_embed, (LON, HEAD), axis=1, tiled=True),
        lax.all_gather(lead_embed, (LON, HEAD), axis=1, tiled=True),
        lax.all_gather(first_gain, (LON, HEAD), axis=0, tiled=True),
        lax.all_gather(first_bias, (LON, HEAD), axis=0, tiled=True),
        lax.all_gather(second_gain, (LON, HEAD), axis=0, tiled=True),
        lax.all_gather(second_bias, (LON, HEAD), axis=0, tiled=True),
    )
    full_patch, full_variable, full_lead, gain_first, shift_first, gain_second, shift_second = (
        shared
    )
    sector = (
        lax.all_gather(mixer_query, LON, axis=1, tiled=True),
        lax.all_gather(mixer_keys, LON, axis=0, tiled=True),
        lax.all_gather(mixer_values, LON, axis=0, tiled=True),
        lax.all_gather(mixer_output, LON, axis=1, tiled=True),
        lax.all_gather(attention_in, LON, axis=1, tiled=True),
        lax.all_gather(attention_out, LON, axis=1, tiled=True),
        lax.all_gather(expand_weight, LON, axis=0, tiled=True),
        lax.all_gather(expand_bias, LON, axis=1, tiled=True),
        lax.all_gather(reduce_weight, LON, axis=1, tiled=True),
        lax.all_gather(output_weight, LON, axis=0, tiled=True),
    )
    (
        head_query,
        key_weight,
        value_weight,
        mixer_weight,
        input_weight,
        output_proj,
        up_weight,
        up_bias,
        down_weight,
        final_weight,
    ) = sector
    row_count, slot_width = slot_crops.shape
    token_count = row_count * slot_width
    local_width = key_weight.shape[1]
    head_count = local_width // HEAD_DIM
    pair_weight = jnp.concatenate([key_weight, value_weight], axis=1)
    gain_one = gain_first.astype(jnp.float32)
    shift_one = shift_first.astype(jnp.float32)
    gain_two = gain_second.astype(jnp.float32)
    shift_two = shift_second.astype(jnp.float32)
    lat_slot = crop_lookup(crop_starts, slot_crops)
    shift_slot = crop_lookup(crop_shifts, slot_crops)
    lead_slot = crop_lookup(lead_hours, slot_crops).astype(jnp.float32).reshape(token_count) / 100.0
    share_count = token_count // lax.axis_size(HEAD)
    lead_rows = lax.dynamic_slice_in_dim(
        lead_slot, lax.axis_index(HEAD) * share_count, share_count
    )
    padded = extended(pixels, ((LON, 2),), 1)
    var_count, lat_count = (pixels.shape[0], pixels.shape[1])
    west_pairs = padded[:, :, : 2 * slot_width].reshape(var_count, lat_count, slot_width, 2)
    east_pairs = padded[:, :, 2:].reshape(var_count, lat_count, slot_width, 2)
    side_pairs = jnp.stack([west_pairs, east_pairs])
    tables = jnp.stack([side_pairs[:, :, :-1], side_pairs[:, :, 1:]], axis=3)
    lat_index = jnp.arange(lat_count - 1, dtype=jnp.int32)
    side_shift = 2 * jnp.arange(2, dtype=jnp.int32) - 1
    chosen = (lat_slot[:, :, None, None] == lat_index[None, None, None, :]) & (
        shift_slot[:, :, None, None] == side_shift[None, None, :, None]
    )
    patches = jnp.einsum(
        "rjsa,svapjx->rjvpx",
        chosen.astype(jnp.bfloat16),
        tables,
        preferred_element_type=jnp.float32,
    )
    patches = patches.astype(jnp.bfloat16).reshape(row_count, slot_width, var_count, 4)

    def mixer_forward(patch_row):
        embedded, key_rows, value_rows, weights = mixer_row(
            patch_row, full_patch, full_variable, pair_weight, head_query
        )
        return jnp.einsum(
            "shv,svhd->shd", weights, value_rows.astype(jnp.float32), precision=highest
        ).astype(jnp.bfloat16)

    mixed_low = lax.map(mixer_forward, patches).reshape(token_count, local_width)
    start_sum = reduce_rows(jnp.dot(mixed_low, mixer_weight, preferred_element_type=jnp.float32))
    start_sum = (
        start_sum
        + lead_rows[:, None] * full_lead[0].astype(jnp.float32)
        + full_lead[1].astype(jnp.float32)
    )
    first_low = spread_rows(layer_norm(start_sum, gain_one, shift_one).astype(jnp.bfloat16))
    projected = jnp.einsum(
        "td,kde->kte", first_low, input_weight, preferred_element_type=jnp.float32
    ).astype(jnp.bfloat16)
    projected = projected.reshape(3, row_count, slot_width, head_count, HEAD_DIM)
    queries, key_local, value_local = (projected[0], projected[1], projected[2])
    query_crops = slot_crops.astype(jnp.float32)
    key_tags = jnp.where(occupied == 1, slot_crops, -1).astype(jnp.bfloat16)
    key_all, value_all, tag_all = (
        lax.all_gather(key_local, LON, axis=1, tiled=True),
        lax.all_gather(value_local, LON, axis=1, tiled=True),
        lax.all_gather(key_tags, LON, axis=1, tiled=True),
    )
    block_width = min(512, key_all.shape[1])
    tag_wide = tag_all.astype(jnp.float32)
    log_totals = key_stats(queries, query_crops, key_all, tag_wide, block_width)
    attended = attend(queries, query_crops, key_all, value_all, tag_wide, log_totals, block_width)
    attended_low = attended.astype(jnp.bfloat16).reshape(token_count, local_width)
    middle = start_sum + reduce_rows(
        jnp.dot(attended_low, output_proj, preferred_element_type=jnp.float32)
    )
    second_low = spread_rows(layer_norm(middle, gain_two, shift_two).astype(jnp.bfloat16))
    hidden = jnp.dot(second_low, up_weight, preferred_element_type=jnp.float32) + up_bias.reshape(
        -1
    ).astype(jnp.float32)
    active = jax.nn.gelu(hidden, approximate=False).astype(jnp.bfloat16)
    final_sum = middle + reduce_rows(
        jnp.dot(active, down_weight, preferred_element_type=jnp.float32)
    )
    final_low = spread_rows(final_sum.astype(jnp.bfloat16))
    keep_mask = occupied.reshape(token_count, 1)
    predicted = (
        jnp.dot(final_low, final_weight, preferred_element_type=jnp.float32)
        * keep_mask.astype(jnp.float32)
    ).astype(jnp.bfloat16)
    predicted = predicted.reshape(row_count, slot_width, -1)
    masked_grad = (cotangent * occupied[:, :, None].astype(jnp.bfloat16)).reshape(token_count, -1)
    grad_final_weight = outer_sum(final_low, masked_grad)
    part_top = jnp.einsum(
        "to,do->td", masked_grad, final_weight, preferred_element_type=jnp.float32
    )
    final_grad = reduce_rows(part_top)
    final_grad_low = spread_rows(final_grad.astype(jnp.bfloat16))
    grad_down = outer_sum(active, final_grad_low)
    active_grad = jnp.einsum(
        "td,fd->tf", final_grad_low, down_weight, preferred_element_type=jnp.float32
    )
    _, gelu_back = jax.vjp(partial(jax.nn.gelu, approximate=False), hidden)
    hidden_grad = gelu_back(active_grad)[0].astype(jnp.bfloat16)
    grad_up = outer_sum(second_low, hidden_grad)
    grad_up_bias = jnp.sum(hidden_grad.astype(jnp.float32), axis=0).reshape(up_bias.shape)
    second_grad = jnp.einsum(
        "tf,df->td", hidden_grad, up_weight, preferred_element_type=jnp.float32
    )
    second_in = head_share(second_grad)
    _, second_back = jax.vjp(layer_norm, middle, gain_two, shift_two)
    part_mid, grad_gain_two, grad_shift_two = second_back(second_in)
    middle_grad = final_grad + part_mid
    middle_low = spread_rows(middle_grad.astype(jnp.bfloat16))
    grad_proj = outer_sum(attended_low, middle_low)
    out_grads = jnp.einsum(
        "td,ed->te", middle_low, output_proj, preferred_element_type=jnp.float32
    ).astype(jnp.bfloat16)
    out_grads = out_grads.reshape(row_count, slot_width, head_count, HEAD_DIM)
    deltas = jnp.transpose(jnp.sum(out_grads.astype(jnp.float32) * attended, axis=-1), (0, 2, 1))
    back_keys, back_values, back_raw = (
        lax.all_gather(key_local, LON, axis=1, tiled=True),
        lax.all_gather(value_local, LON, axis=1, tiled=True),
        lax.all_gather(key_tags, LON, axis=1, tiled=True),
    )
    back_tags = back_raw.astype(jnp.float32)
    scale = HEAD_DIM ** (-0.5)
    key_count = back_keys.shape[1] // block_width
    local_zeros = jnp.zeros(queries.shape, jnp.float32)
    whole_zeros = jnp.zeros(back_keys.shape, jnp.float32)

    def both_step(running, block_index):
        query_acc, key_acc, value_acc = running
        key_block = block_slice(back_keys, block_index, block_width, 1)
        score_delta, weights_low = score_grads(
            queries,
            query_crops,
            out_grads,
            log_totals,
            deltas,
            key_block,
            block_slice(back_values, block_index, block_width, 1),
            block_slice(back_tags, block_index, block_width, 1),
        )
        query_acc = (
            query_acc
            + jnp.einsum(
                "rhqk,rkhd->rqhd", score_delta, key_block, preferred_element_type=jnp.float32
            )
            * scale
        )
        key_piece = (
            jnp.einsum("rhqk,rqhd->rkhd", score_delta, queries, preferred_element_type=jnp.float32)
            * scale
        )
        value_piece = jnp.einsum(
            "rhqk,rqhd->rkhd", weights_low, out_grads, preferred_element_type=jnp.float32
        )
        key_acc = lax.dynamic_update_slice_in_dim(key_acc, key_piece, block_index * block_width, 1)
        value_acc = lax.dynamic_update_slice_in_dim(
            value_acc, value_piece, block_index * block_width, 1
        )
        return ((query_acc, key_acc, value_acc), None)

    (query_grad, key_part, value_part), _ = lax.scan(
        both_step, (local_zeros, whole_zeros, whole_zeros), jnp.arange(key_count)
    )
    key_grad, value_grad = (
        lax.psum_scatter(
            key_part.astype(jnp.bfloat16), LON, scatter_dimension=1, tiled=True
        ).astype(jnp.float32),
        lax.psum_scatter(
            value_part.astype(jnp.bfloat16), LON, scatter_dimension=1, tiled=True
        ).astype(jnp.float32),
    )
    stacked = (
        jnp.stack([query_grad, key_grad, value_grad])
        .astype(jnp.bfloat16)
        .reshape(3, token_count, local_width)
    )
    first_grad = jnp.einsum(
        "kte,kde->td", stacked, input_weight, preferred_element_type=jnp.float32
    )
    grad_input = jnp.einsum("td,kte->kde", first_low, stacked, preferred_element_type=jnp.float32)
    first_in = head_share(first_grad)
    _, first_back = jax.vjp(layer_norm, start_sum, gain_one, shift_one)
    part_low, grad_gain_one, grad_shift_one = first_back(first_in)
    start_grad = middle_grad + part_low
    grad_lead = jnp.stack(
        [jnp.sum(start_grad * lead_rows[:, None], axis=0), jnp.sum(start_grad, axis=0)]
    )
    start_low = spread_rows(start_grad.astype(jnp.bfloat16))
    grad_mixer = outer_sum(mixed_low, start_low)
    mixed_grad = jnp.einsum(
        "td,ed->te", start_low, mixer_weight, preferred_element_type=jnp.float32
    ).astype(jnp.bfloat16)
    mixed_grad = mixed_grad.reshape(row_count, slot_width, head_count, HEAD_DIM)
    initial = (
        jnp.zeros(full_patch.shape, jnp.float32),
        jnp.zeros(full_variable.shape, jnp.float32),
        jnp.zeros(head_query.shape, jnp.float32),
        jnp.zeros(pair_weight.shape, jnp.float32),
    )
    mixer_step = partial(
        mixer_back,
        full_patch=full_patch,
        full_variable=full_variable,
        pair_weight=pair_weight,
        head_query=head_query,
    )
    (grad_patch, grad_variable, grad_query, grad_pair), slot_grads = lax.scan(
        mixer_step, initial, (patches, mixed_grad)
    )
    slot_total = head_total(slot_grads).reshape(row_count, slot_width, var_count, 2, 2)
    table_grads = jnp.einsum(
        "rjsa,rjvpx->svapjx", chosen.astype(jnp.float32), slot_total, precision=highest
    )
    side_grads = jnp.pad(
        table_grads[:, :, :, 0], ((0, 0), (0, 0), (0, 1), (0, 0), (0, 0))
    ) + jnp.pad(table_grads[:, :, :, 1], ((0, 0), (0, 0), (1, 0), (0, 0), (0, 0)))
    west_grad = side_grads[0].reshape(var_count, lat_count, 2 * slot_width)
    east_grad = side_grads[1].reshape(var_count, lat_count, 2 * slot_width)
    padded_grad = jnp.pad(west_grad, ((0, 0), (0, 0), (0, 2))) + jnp.pad(
        east_grad, ((0, 0), (0, 0), (2, 0))
    )
    rim_values = jnp.stack([padded_grad[:, :, 0], padded_grad[:, :, -1]], axis=2)
    returned = extended(rim_values, ((LON, 2),), 1)
    pixel_grad = (
        padded_grad[:, :, 1:-1]
        + jnp.pad(returned[:, :, 0:1], ((0, 0), (0, 0), (0, 2 * slot_width - 1)))
        + jnp.pad(returned[:, :, 3:4], ((0, 0), (0, 0), (2 * slot_width - 1, 0)))
    )
    sector_out = (
        lax.psum_scatter(
            grad_query.astype(jnp.bfloat16), LON, scatter_dimension=1, tiled=True
        ).astype(jnp.float32),
        lax.psum_scatter(
            grad_pair[:, :local_width].astype(jnp.bfloat16), LON, scatter_dimension=0, tiled=True
        ).astype(jnp.float32),
        lax.psum_scatter(
            grad_pair[:, local_width:].astype(jnp.bfloat16), LON, scatter_dimension=0, tiled=True
        ).astype(jnp.float32),
        lax.psum_scatter(
            grad_mixer.astype(jnp.bfloat16), LON, scatter_dimension=1, tiled=True
        ).astype(jnp.float32),
        lax.psum_scatter(
            grad_input.astype(jnp.bfloat16), LON, scatter_dimension=1, tiled=True
        ).astype(jnp.float32),
        lax.psum_scatter(
            grad_proj.astype(jnp.bfloat16), LON, scatter_dimension=1, tiled=True
        ).astype(jnp.float32),
        lax.psum_scatter(
            grad_up.astype(jnp.bfloat16), LON, scatter_dimension=0, tiled=True
        ).astype(jnp.float32),
        lax.psum_scatter(
            grad_up_bias.astype(jnp.bfloat16), LON, scatter_dimension=1, tiled=True
        ).astype(jnp.float32),
        lax.psum_scatter(
            grad_down.astype(jnp.bfloat16), LON, scatter_dimension=1, tiled=True
        ).astype(jnp.float32),
        lax.psum_scatter(
            grad_final_weight.astype(jnp.bfloat16), LON, scatter_dimension=0, tiled=True
        ).astype(jnp.float32),
    )
    shared_out = (
        lax.psum_scatter(grad_patch, (LON, HEAD), scatter_dimension=2, tiled=True),
        lax.psum_scatter(grad_variable, (LON, HEAD), scatter_dimension=1, tiled=True),
        lax.psum_scatter(grad_lead, (LON, HEAD), scatter_dimension=1, tiled=True),
        lax.psum_scatter(grad_gain_one, (LON, HEAD), scatter_dimension=0, tiled=True),
        lax.psum_scatter(grad_shift_one, (LON, HEAD), scatter_dimension=0, tiled=True),
        lax.psum_scatter(grad_gain_two, (LON, HEAD), scatter_dimension=0, tiled=True),
        lax.psum_scatter(grad_shift_two, (LON, HEAD), scatter_dimension=0, tiled=True),
    )
    return (
        predicted,
        pixel_grad,
        shared_out[0],
        shared_out[1],
        sector_out[0],
        sector_out[1],
        sector_out[2],
        sector_out[3],
        shared_out[2],
        shared_out[3],
        shared_out[4],
        sector_out[4],
        sector_out[5],
        shared_out[5],
        shared_out[6],
        sector_out[6],
        sector_out[7],
        sector_out[8],
        sector_out[9],
    )


MESH = pl.DeviceIdType.MESH
BOTH = (LON, HEAD)
LON_SIZE = 16
HEAD_SIZE = 2
CHUNK = 256
low = jnp.bfloat16
wide = jnp.float32


def planned(mesh):
    return mesh.shape[LON] == LON_SIZE and mesh.shape[HEAD] == HEAD_SIZE


def dot(left, right, left_dim=1, right_dim=0):
    return lax.dot_general(
        left, right, (((left_dim,), (right_dim,)), ((), ())), preferred_element_type=wide
    )


def position():
    lon = lax.axis_index(LON)
    x = lax.axis_index(HEAD)
    z = lax.div(lon, 4)
    y = lax.rem(lax.div(lon, 2), 2)
    c = lax.rem(lon, 2)
    return x, z, y, c


def partners(x, z, y, c):
    here = z * 4 + y * 2 + c
    across = {
        "x": (here, 1 - x),
        "y": (z * 4 + (1 - y) * 2 + c, x),
        "c": (z * 4 + y * 2 + 1 - c, x),
    }
    line = [(lax.rem(z + step, 4) * 4 + y * 2 + c, x) for step in (1, 2, 3)]
    return across, line


def sector_of(z, y, c, x, part, side):
    return (y * 2 + c) * 4 + x * 2 + part, side


def block_of(z, y, row):
    return row * 4 + z, y


def meet(peers, others=(), own=None):
    barrier = pltpu.get_barrier_semaphore()
    for device in peers:
        pl.semaphore_signal(barrier, inc=1, device_id=device, device_id_type=MESH)
    for device in others:

        @pl.when(jnp.logical_not(same(device, own)))
        def _():
            pl.semaphore_signal(barrier, inc=1, device_id=device, device_id_type=MESH)

    expected = len(peers)
    for device in others:
        expected = expected + 1 - same(device, own).astype(jnp.int32)
    pl.semaphore_wait(barrier, expected)


def same(device, own):
    return jnp.logical_and(device[0] == own[0], device[1] == own[1])


def post(source, target, send_sem, recv_sem, device, own):
    here = same(device, own)

    @pl.when(here)
    def _():
        pltpu.make_async_copy(source, target, recv_sem).start()

    @pl.when(jnp.logical_not(here))
    def _():
        remote(source, target, send_sem, recv_sem, device).start()


def settle(source, target, send_sem, recv_sem, device, own):
    @pl.when(jnp.logical_not(same(device, own)))
    def _():
        remote(source, target, send_sem, recv_sem, device).wait_send()


def remote(source, target, send_sem, recv_sem, device):
    return pltpu.make_async_remote_copy(
        src_ref=source,
        dst_ref=target,
        send_sem=send_sem,
        recv_sem=recv_sem,
        device_id=device,
        device_id_type=MESH,
    )


def gatherer(views, sems):
    own_sem, line_send, line_recv, hop_send, hop_recv = sems
    x, z, y, c = position()
    across, line = partners(x, z, y, c)

    def keep(number):
        source, target, span, _ = views(number)
        return pltpu.make_async_copy(source, target.at[x, z, y, c, span], own_sem.at[number])

    def along(number, d):
        source, target, span, _ = views(number)
        return remote(
            source,
            target.at[x, z, y, c, span],
            line_send.at[number, d],
            line_recv.at[number, d],
            line[d],
        )

    def hop(number, k):
        _, target, span, color = views(number)
        if k == 0:
            part, axis = target.at[x, :, y, c, span], "yx"[color]
        elif k == 1 and color == 0:
            part, axis = target.at[x, :, :, c, span], "x"
        elif k == 1:
            part, axis = target.at[:, :, y, c, span], "y"
        else:
            part, axis = target.at[:, :, :, c, span], "c"
        return remote(
            part, part, hop_send.at[number, k], hop_recv.at[number, k], across[axis]
        )

    def begin(number):
        keep(number).start()
        for d in range(3):
            along(number, d).start()

    def spread(number):
        keep(number).wait()
        for d in range(3):
            along(number, d).wait_recv()
        hop(number, 0).start()

    def widen(number):
        hop(number, 0).wait_recv()
        hop(number, 1).start()

    def pair_up(number):
        hop(number, 1).wait_recv()
        hop(number, 2).start()

    def close(number):
        hop(number, 2).wait_recv()

    def finish(number):
        for k in range(3):
            along(number, k).wait_send()
            hop(number, k).wait_send()

    return (begin, spread, widen, pair_up, close), finish


def reduce_kernel(chunks, count, *refs):
    ins, refs = refs[:count], refs[count:]
    value_in, key_weight, value_weight, lat_ref, shift_ref, refs = refs[:5] + (refs[5:],)
    patch_ref, prob_ref, score_table, value_table, key_table, mixed_grad, refs = refs[:6] + (
        refs[6:],
    )
    full_ref, query_ref, first_ref, second_ref, rest_ref, refs = refs[:5] + (refs[5:],)
    out, value_out, pixel_out, refs = refs[:3] + (refs[3:],)
    buffers, sems, refs = refs[:6], refs[6:13], refs[13:]
    grad_out, field, edge, west_edge, east_edge, refs = refs[:5] + (refs[5:],)
    value_send, value_recv, grad_send, grad_recv, edge_send, edge_recv, refs = refs[:6] + (
        refs[6:],
    )
    grad_in, pooled_ref, count_ref, patch_grad, weight_a, weight_b, key_low, query_grad = refs[:8]
    values_ref, tail_ref, load_sem = refs[8:]
    ins = ins + (values_ref, tail_ref)
    x, z, y, c = position()
    across, line = partners(x, z, y, c)
    lon = z * 4 + y * 2 + c
    own = (lon, x)
    east, west = (lax.rem(lon + 1, 16), x), (lax.rem(lon + 15, 16), x)
    sources = [block_of(z, y, row) for row in range(4)]
    meet(list(across.values()) + line + [east, west], sources, own)
    letters = []
    for part in range(2):
        for side in range(2):
            device = sector_of(z, y, c, x, part, side)
            at = 2 * part + side
            letters.append(
                (grad_in.at[part], grad_out.at[z], grad_send.at[at], grad_recv.at[z])
                + (device, own)
            )
            letters.append(
                (value_in.at[side, part], value_out.at[z], value_send.at[at], value_recv.at[z])
                + (device, own)
            )
    for letter in letters[1::2]:
        post(*letter)
    total = len(chunks)
    loads = [
        pltpu.make_async_copy(key_weight, weight_a, load_sem.at[0]),
        pltpu.make_async_copy(value_weight, weight_b, load_sem.at[1]),
    ]
    for copy in loads:
        copy.start()
    head_total, var_total, tokens = prob_ref.shape
    padded = patch_ref.shape[0]
    scale = HEAD_DIM ** (-0.5)

    def halves_of(values):
        upper = values.astype(low)
        return upper, (values - upper.astype(wide)).astype(low)

    def heads(first):
        mask = diagonal(var_total, padded)
        if first == 0:
            patch_grad[...] = jnp.zeros_like(patch_grad)
            query_grad[...] = jnp.zeros_like(query_grad)

        def head_step(h, carry):
            span = pl.ds(pl.multiple_of(h * HEAD_DIM, HEAD_DIM), HEAD_DIM)
            grads = mixed_grad[span, :]
            prob = prob_ref[h]
            back = dot(value_table[span, :], grads, 0, 0)
            pieces = [
                patch_ref[k * var_total : (k + 1) * var_total, :].astype(wide) for k in range(5)
            ]
            backs = [back[k * var_total : (k + 1) * var_total, :] for k in range(5)]
            prob_grad = pieces[0] * backs[0]
            for k in range(1, 5):
                prob_grad = prob_grad + pieces[k] * backs[k]
            mean = jnp.sum(prob * prob_grad, axis=0, keepdims=True)
            upper, lower = halves_of(prob * (prob_grad - mean))
            spread = jnp.where(mask, score_table[pl.ds(h, 1), :], 0.0).astype(low)
            patch_grad[...] += dot(spread, upper, 0, 0)
            for k in range(4):
                patch_grad[k * var_total : (k + 1) * var_total, :] += prob * backs[k]
            patch = patch_ref[...]
            counts = dot(upper, patch, 1, 1) + dot(lower, patch, 1, 1)
            counts = jnp.sum(jnp.where(mask, counts, 0.0), axis=0, keepdims=True) * scale
            count_ref[pl.ds(h, 1), :] = counts
            table = key_table[span, :].astype(low)
            upper, lower = halves_of(counts)
            query_grad[pl.ds(h, 1), :HEAD_DIM] = dot(upper, table, 1, 1) + dot(lower, table, 1, 1)
            pooled = jnp.concatenate(
                [(prob * piece).astype(low) for piece in pieces]
                + [jnp.zeros((padded - 5 * var_total, tokens), low)],
                axis=0,
            )
            pooled_ref[span, :] = dot(grads, pooled, 1, 1).astype(low)
            return carry

        lax.fori_loop(first, first + head_total // 4, head_step, 0)

    def send_cut():
        taps = 4 * var_total
        for part in range(2):
            grad_in[part] = patch_grad[:taps, part * 128 : (part + 1) * 128]
        for letter in letters[0::2]:
            post(*letter)

    def value_grads():
        rows = full_ref.shape[0] // 4
        for part in range(4):
            piece = dot(full_ref[part * rows : (part + 1) * rows, :], pooled_ref[...], 1, 1)
            values_ref[part] = piece.astype(low).reshape(values_ref.shape[1:])

    def tail_grads():
        for copy in loads:
            copy.wait()
        half_width = weight_a.shape[-1]
        wide_query = jnp.concatenate([query_ref[...]] * (head_total * HEAD_DIM // 128), axis=1)
        head = lax.div(lax.broadcasted_iota(jnp.int32, wide_query.shape, 1), HEAD_DIM)
        row = lax.broadcasted_iota(jnp.int32, wide_query.shape, 0)
        wide_query = jnp.where(head == row, wide_query, 0.0).astype(low)
        count_parts = halves_of(count_ref[...])
        key_low[...] = sum(dot(wide_query, part, 0, 0) for part in count_parts).astype(low)
        spots = lax.broadcasted_iota(jnp.int32, (8, padded), 1) - 5 * var_total
        kinds = lax.broadcasted_iota(jnp.int32, (8, padded), 0)
        vectors = jnp.concatenate(
            [first_ref[...], second_ref[...], jnp.zeros((2, first_ref.shape[1]), wide)], axis=0
        )
        result = dot(vectors.astype(low), jnp.where(spots == kinds, 1.0, 0.0).astype(low), 0, 0)
        for side in range(2):
            span = slice(side * half_width, (side + 1) * half_width)
            result = result + dot(weight_a[side], key_low[span, :])
            result = result + dot(weight_b[side], pooled_ref[span, :])
        result = result.astype(low)
        sector = tail_ref.shape[-2] // 2
        for place in range(16):
            at = (place // 4, place // 2 % 2, place % 2)
            for side in range(2):
                first = (2 * place + side) * sector
                for half in range(2):
                    tail_ref[
                        (side,) + at + (slice(half * sector, (half + 1) * sector), slice(0, 128))
                    ] = result[first : first + sector, half * 128 : (half + 1) * 128]

    def rest_grads():
        used = rest_ref.shape[2] - 32
        head_half = head_total // 2
        model = full_ref.shape[0]
        count_parts = halves_of(count_ref[...])
        head = lax.broadcasted_iota(jnp.int32, (head_total, 128), 0)
        lane = lax.broadcasted_iota(jnp.int32, (head_total, 128), 1)
        rows = lax.broadcasted_iota(jnp.int32, (model, head_total), 0)
        columns = lax.broadcasted_iota(jnp.int32, (model, head_total), 1)
        inner = lax.rem(rows, model // 16)
        sectors = lax.div(lax.broadcasted_iota(jnp.int32, (model, 128), 0), model // 16)
        lanes_at = lax.broadcasted_iota(jnp.int32, (model, 128), 1)
        source_lane = lax.broadcasted_iota(jnp.int32, (128, 128), 0)
        target_lane = lax.broadcasted_iota(jnp.int32, (128, 128), 1)
        query_at = used + head_half + 4
        move = jnp.where(target_lane == query_at + lax.rem(source_lane, 4), 1.0, 0.0).astype(low)
        for side in range(2):
            spot = used + head - head_half * side
            inside = lax.div(head, head_half) == side
            target = jnp.where(jnp.logical_and(inside, lane == spot), 1.0, 0.0).astype(low)
            sums = sum(dot(part, target, 0, 0) for part in count_parts)
            result = rest_ref[side].astype(wide)
            for part in halves_of(sums):
                result = result + dot(full_ref[...], part)
            chosen = jnp.logical_and(inner < head_half, columns == inner + head_half * side)
            spread = dot(jnp.where(chosen, 1.0, 0.0).astype(low), query_grad[...].astype(low))
            spread = jnp.where(lax.div(lanes_at, 4) == sectors, spread, 0.0).astype(low)
            result = result + dot(spread, move)
            tail_ref[side, :, :, :, :, 128:] = result.astype(low).reshape(
                tail_ref.shape[1:-1] + (128,)
            )

    lat_count, var_count, lanes = field.shape
    half = lanes // 2
    column_count = pixel_out.shape[2]

    def paste(row):
        pltpu.make_async_copy(grad_in.at[0], grad_out.at[row], grad_recv.at[row]).wait()
        lat = lat_ref[row : row + 1, :]
        going_west = shift_ref[row : row + 1, :] < 0
        lat_both = jnp.concatenate([lat, lat], axis=1)
        both = []
        for py in range(2):
            k = 2 * py
            grads = jnp.concatenate(
                [
                    grad_out[row, k * var_count : (k + 1) * var_count, :],
                    grad_out[row, (k + 1) * var_count : (k + 2) * var_count, :],
                ],
                axis=1,
            )
            left = jnp.where(going_west, grads, 0.0)
            both.append(jnp.concatenate([left, grads - left], axis=1))

        def body(b, carry):
            piece = jnp.where(lat_both == b, both[0], 0.0) + jnp.where(
                lat_both == b - 1, both[1], 0.0
            )
            if row == 0:
                field[b] = piece
            else:
                field[b] += piece
            return carry

        lax.fori_loop(0, lat_count, body, 0)

    def thirds(values):
        one = values.astype(low)
        rest = values - one.astype(wide)
        two = rest.astype(low)
        return one, two, (rest - two.astype(wide)).astype(low)

    def edges():
        kind = lax.broadcasted_iota(jnp.int32, (8, lanes), 0)
        wanted = columns_of((8, lanes), 1, half)
        pick = jnp.where(
            jnp.logical_or(
                jnp.logical_and(kind == 0, wanted == -1),
                jnp.logical_and(kind == 1, wanted == column_count),
            ),
            1.0,
            0.0,
        ).astype(low)
        flat = field[...].reshape(lat_count * var_count, lanes)
        one, two, three = thirds(flat)
        edge[...] = dot(pick, one, 1, 1) + dot(pick, two, 1, 1) + dot(pick, three, 1, 1)
        remote(edge, west_edge, edge_send.at[0], edge_recv.at[0], east).start()
        remote(edge, east_edge, edge_send.at[1], edge_recv.at[1], west).start()

    def pixels():
        remote(edge, west_edge, edge_send.at[0], edge_recv.at[0], east).wait()
        remote(edge, east_edge, edge_send.at[1], edge_recv.at[1], west).wait()
        wanted = columns_of((lanes, column_count), 0, half)
        column = lax.broadcasted_iota(jnp.int32, (lanes, column_count), 1)
        place = jnp.where(wanted == column, 1.0, 0.0).astype(low)
        kind = lax.broadcasted_iota(jnp.int32, (8, column_count), 0)
        column = lax.broadcasted_iota(jnp.int32, (8, column_count), 1)
        from_west = jnp.logical_and(kind == 1, column == 0)
        from_east = jnp.logical_and(kind == 0, column == column_count - 1)
        west_place = jnp.where(from_west, 1.0, 0.0).astype(low)
        east_place = jnp.where(from_east, 1.0, 0.0).astype(low)
        borders = None
        for values, target in ((west_edge[...], west_place), (east_edge[...], east_place)):
            for part in thirds(values):
                piece = dot(part, target, 0, 0)
                borders = piece if borders is None else borders + piece
        pixel_out[...] = borders.reshape(pixel_out.shape)

        def body(b, carry):
            result = pixel_out[b]
            for part in thirds(field[b]):
                result = result + dot(part, place)
            pixel_out[b] = result
            return carry

        lax.fori_loop(0, lat_count, body, 0)

    quarter = head_total // 4
    extra = {step: partial(heads, step * quarter) for step in range(4)}
    extra.update({4: send_cut, 5: value_grads, 6: tail_grads, 7: rest_grads})
    extra.update({8 + row: partial(paste, row) for row in range(4)})
    extra.update({12: edges, 15: pixels})

    def source_of(pair, color, side, core):
        index, lead, offset = chunks[2 * pair + color][side]
        source = ins[index] if lead is None else ins[index].at[lead]
        return source.at[:, :, core, :, pl.ds(offset, CHUNK)]

    begin, stage_core, stage_first, stage_second, stage_third, finish = reducer(
        source_of, buffers, sems, out
    )
    plan = ((0, begin), (2, stage_core), (4, stage_first), (6, stage_second), (8, stage_third))
    for step in range(total + 8):
        for back, stage in plan:
            if 0 <= step - back < total:
                stage((step - back) // 2, (step - back) % 2)
        if step in extra:
            extra[step]()
    for k in range(total):
        finish(k // 2, k % 2)
    for letter in letters:
        settle(*letter)
    for row in range(4):
        pltpu.make_async_copy(value_in.at[0, 0], value_out.at[row], value_recv.at[row]).wait()


def reduce_all(items, values, weights, lat_lanes, shift_lanes, mixer, rest, lat_count, number):
    chunks, views = [], []
    for index, item in enumerate(items):
        rows, columns = item.shape[-2:]
        views.append(item.reshape((-1, 4, 2, 2, rows // 16, columns)))
        for first in range(0, views[index].shape[0], 2):
            for offset in range(0, columns, CHUNK):
                chunks.append(((index, first, offset), (index, first + 1, offset)))
    count = len(views)
    half = weights[0].shape[-1]
    for offset in range(0, half, CHUNK):
        chunks.append(((count, None, offset), (count, None, half + offset)))
    chunks.append(((count + 1, 0, 0), (count + 1, 1, 0)))
    total = len(chunks)
    rows = views[0].shape[-2]
    probs = mixer[1]
    head_count, var_count, tokens = probs.shape
    padded = mixer[0].shape[0]
    model = head_count * HEAD_DIM
    lanes = 2 * lat_lanes.shape[1]
    columns = lat_lanes.shape[1]
    cut = (4, 4 * var_count, 128)
    vmem = pl.BlockSpec(memory_space=pltpu.VMEM)
    hbm = pl.BlockSpec(memory_space=pl.ANY)
    sem = pltpu.SemaphoreType.DMA
    return pl.pallas_call(
        partial(reduce_kernel, chunks, count),
        out_shape=[
            jax.ShapeDtypeStruct((rows, total * CHUNK), wide),
            jax.ShapeDtypeStruct((4,) + values.shape[2:], values.dtype),
            jax.ShapeDtypeStruct((lat_count, var_count, columns), wide),
        ],
        in_specs=[hbm] * (count + 3) + [vmem] * (2 + len(mixer) + len(rest)),
        out_specs=[vmem, hbm, vmem],
        scratch_shapes=reducer_scratch(total, rows)
        + [
            pltpu.VMEM(cut, wide),
            pltpu.VMEM((lat_count, var_count, lanes), wide),
            pltpu.VMEM((8, lat_count * var_count), wide),
            pltpu.VMEM((8, lat_count * var_count), wide),
            pltpu.VMEM((8, lat_count * var_count), wide),
            sem((4,)),
            sem((4,)),
            sem((4,)),
            sem((4,)),
            sem((2,)),
            sem((2,)),
            pltpu.VMEM((2,) + cut[1:], wide),
            pltpu.VMEM((model, padded), low),
            pltpu.VMEM((head_count, padded), wide),
            pltpu.VMEM((padded, tokens), wide),
            pltpu.VMEM(weights[0].shape, low),
            pltpu.VMEM(weights[0].shape, low),
            pltpu.VMEM((model, padded), low),
            pltpu.VMEM((head_count, 128), wide),
            pltpu.VMEM((4, 2, 2, rows, 2 * half), low),
            pltpu.VMEM((2, 4, 2, 2, rows, CHUNK), low),
            sem((2,)),
        ],
        compiler_params=pltpu.CompilerParams(
            collective_id=number, has_side_effects=True, vmem_limit_bytes=60 * 2**20
        ),
    )(*views, values, *weights, lat_lanes, shift_lanes, *mixer, *rest)


def diagonal(var_count, columns):
    column = lax.broadcasted_iota(jnp.int32, (var_count, columns), 1)
    row = lax.broadcasted_iota(jnp.int32, (var_count, columns), 0)
    return (lax.rem(column, var_count) == row) & (column < 5 * var_count)


def head_lanes(values, h):
    lane = lax.broadcasted_iota(jnp.int32, values.shape, values.ndim - 1)
    inside = lane < HEAD_DIM if h == 0 else lane >= HEAD_DIM
    return jnp.where(inside, values, jnp.zeros_like(values))


def plane_device(z, index):
    return z * 4 + lax.div(index, 2), lax.rem(index, 2)


def plane_meet(x, z, y, c):
    barrier = pltpu.get_barrier_semaphore()
    for flip in range(1, 8):
        there_y = 1 - y if flip & 4 else y
        there_c = 1 - c if flip & 2 else c
        there_x = 1 - x if flip & 1 else x
        device = (z * 4 + there_y * 2 + there_c, there_x)
        pl.semaphore_signal(barrier, inc=1, device_id=device, device_id_type=MESH)
    return barrier


def joined(left, right):
    return (left.astype(wide) + right.astype(wide)).astype(low)


def reducer(source_of, buffers, sems, out):
    mine, other, first_a, first_b, second, third = buffers
    own_sem, core_send, core_recv, hop_send, hop_recv, line_send, line_recv = sems
    x, z, y, c = position()
    across, line = partners(x, z, y, c)

    def keeps(pair, color):
        k = 2 * pair + color
        return [
            pltpu.make_async_copy(
                source_of(pair, color, side, c), mine.at[2 * k + side], own_sem.at[k, side]
            )
            for side in range(2)
        ]

    def swaps(pair, color):
        k = 2 * pair + color
        return [
            remote(
                source_of(pair, color, side, 1 - c),
                other.at[2 * k + side],
                core_send.at[k, side],
                core_recv.at[k, side],
                across["c"],
            )
            for side in range(2)
        ]

    def hop_one(pair, color):
        k = 2 * pair + color
        if color == 0:
            source, target, axis = mine.at[2 * k + 1 - x], first_a.at[pair], "x"
        else:
            source = mine.at[pl.ds(2 * k, 2), :, 1 - y]
            target, axis = first_b.at[pair], "y"
        return remote(source, target, hop_send.at[k, 0], hop_recv.at[k, 0], across[axis])

    def hop_two(pair, color):
        k = 2 * pair + color
        if color == 0:
            source, axis = mine.at[2 * k + x, :, 1 - y], "y"
        else:
            source, axis = mine.at[2 * k + 1 - x, :, y], "x"
        return remote(source, second.at[k], hop_send.at[k, 1], hop_recv.at[k, 1], across[axis])

    def along(pair, color):
        k = 2 * pair + color
        return [
            remote(
                mine.at[2 * k + x, lax.rem(z + d + 1, 4), y],
                third.at[k, d],
                line_send.at[k, d],
                line_recv.at[k, d],
                line[d],
            )
            for d in range(3)
        ]

    def begin(pair, color):
        for copy in swaps(pair, color) + keeps(pair, color):
            copy.start()

    def stage_core(pair, color):
        k = 2 * pair + color
        for copy in keeps(pair, color):
            copy.wait()
        for copy in swaps(pair, color):
            copy.wait_recv()

        def body(step, carry):
            side, row = lax.div(step, 4), lax.rem(step, 4)
            for part in range(2):
                mine[2 * k + side, row, part] = joined(
                    mine[2 * k + side, row, part], other[2 * k + side, row, part]
                )
            return carry

        lax.fori_loop(0, 8, body, 0)
        hop_one(pair, color).start()

    def stage_first(pair, color):
        k = 2 * pair + color
        hop_one(pair, color).wait_recv()

        def body(row, carry):
            for part in range(2):
                if color == 0:
                    mine[2 * k + x, row, part] = joined(
                        mine[2 * k + x, row, part], first_a[pair, row, part]
                    )
                else:
                    mine[2 * k + part, row, y] = joined(
                        mine[2 * k + part, row, y], first_b[pair, part, row]
                    )
            return carry

        lax.fori_loop(0, 4, body, 0)
        hop_two(pair, color).start()

    def stage_second(pair, color):
        k = 2 * pair + color
        hop_two(pair, color).wait_recv()

        def body(row, carry):
            mine[2 * k + x, row, y] = joined(mine[2 * k + x, row, y], second[k, row])
            return carry

        lax.fori_loop(0, 4, body, 0)
        for copy in along(pair, color):
            copy.start()

    def stage_third(pair, color):
        k = 2 * pair + color
        for copy in along(pair, color):
            copy.wait_recv()
        result = mine[2 * k + x, z, y].astype(wide)
        for d in range(3):
            result = result + third[k, d].astype(wide)
        start = k * CHUNK
        if not isinstance(k, int):
            start = pl.multiple_of(start, CHUNK)
        out[:, pl.ds(start, CHUNK)] = result

    def finish(pair, color):
        hop_one(pair, color).wait_send()
        hop_two(pair, color).wait_send()
        for copy in swaps(pair, color) + along(pair, color):
            copy.wait_send()

    return begin, stage_core, stage_first, stage_second, stage_third, finish


def reducer_scratch(total, rows):
    sem = pltpu.SemaphoreType.DMA
    pairs = (total + 1) // 2
    return [
        pltpu.VMEM((2 * total, 4, 2, rows, CHUNK), low),
        pltpu.VMEM((2 * total, 4, 2, rows, CHUNK), low),
        pltpu.VMEM((pairs, 4, 2, rows, CHUNK), low),
        pltpu.VMEM((pairs, 2, 4, rows, CHUNK), low),
        pltpu.VMEM((total, 4, rows, CHUNK), low),
        pltpu.VMEM((total, 3, rows, CHUNK), low),
    ] + [
        sem((total, 2)),
        sem((total, 2)),
        sem((total, 2)),
        sem((total, 2)),
        sem((total, 2)),
        sem((total, 3)),
        sem((total, 3)),
    ]


def attend_back_kernel(
    joint,
    tag_ref,
    crop_ref,
    out_ref,
    total_ref,
    source,
    feed_ref,
    stacked,
    sums,
    grads,
    result,
    key_acc,
    value_acc,
    *rest
):
    buffers, sems = rest[:6], rest[6:13]
    in_own, in_send, in_recv, back_own, back_send, back_recv = rest[13:]
    x, z, y, c = position()
    across, line = partners(x, z, y, c)
    me = y * 4 + c * 2 + x
    peers, kinds, share, lanes = joint.shape
    slots = peers * share
    scale = HEAD_DIM ** (-0.5)
    each = feed_ref.shape[-1] // CHUNK

    def source_of(pair, color, side, core):
        k = 2 * pair + color
        offset = pl.multiple_of(lax.rem(k, each) * CHUNK, CHUNK)
        return feed_ref.at[lax.div(k, each), side, :, :, core, :, pl.ds(offset, CHUNK)]

    begin, stage_core, stage_first, stage_second, stage_third, finish = reducer(
        source_of, buffers, sems, sums
    )
    keep = pltpu.make_async_copy(source.at[me], grads.at[me], in_own)
    keep.start()
    barrier = plane_meet(x, z, y, c)
    for device in line:
        pl.semaphore_signal(barrier, inc=1, device_id=device, device_id_type=MESH)
    pl.semaphore_wait(barrier, peers - 1 + len(line))

    def inward(there):
        return remote(
            source.at[there],
            grads.at[me],
            in_send.at[there],
            in_recv.at[me],
            plane_device(z, there),
        )

    def outward(there, part):
        span = pl.ds(0, 1) if part == 0 else pl.ds(1, 2)
        return remote(
            result.at[there, span],
            stacked.at[me, span],
            back_send.at[there, part],
            back_recv.at[me, part],
            plane_device(z, there),
        )

    for step in range(1, peers):
        inward(lax.rem(me + step, peers)).start()
    key_acc[...] = jnp.zeros_like(key_acc)
    value_acc[...] = jnp.zeros_like(value_acc)
    pairs = feed_ref.shape[0] * each // 2

    def attention(index):
        span = pl.ds(pl.multiple_of(index * share, share), share)
        queries = joint[index, 0]
        keys = joint[:, 1].reshape(slots, lanes)
        values = joint[:, 2].reshape(slots, lanes)
        grad = grads[index]
        product = grad.astype(wide) * out_ref[span, :]
        allowed = crop_ref[span, :] == tag_ref[0:1, :]
        query_grad = None
        for h in range(2):
            query_part, grad_part = head_lanes(queries, h), head_lanes(grad, h)
            scores = jnp.where(allowed, dot(query_part, keys, 1, 1), masked_score)
            weights = jnp.exp(scores - total_ref[h, span, :])
            weight_grads = dot(grad_part, values, 1, 1)
            delta = jnp.sum(head_lanes(product, h), axis=1, keepdims=True)
            score_grads = (weights * (weight_grads - delta)).astype(low)
            weights = weights.astype(low)
            value_acc[...] += dot(grad_part, weights, 0, 0)
            key_acc[...] += dot(query_part, score_grads, 0, 0)
            part = head_lanes(dot(score_grads, keys), h)
            query_grad = part if query_grad is None else query_grad + part
        result[index, 0] = (query_grad * scale).astype(low)

    def step_body(step, carry):
        @pl.when(step < pairs)
        def _():
            begin(step, 0)
            begin(step, 1)

        for back, stage in ((1, stage_core), (2, stage_first), (3, stage_second), (4, stage_third)):

            @pl.when(jnp.logical_and(step >= back, step < pairs + back))
            def _():
                stage(step - back, 0)
                stage(step - back, 1)

        @pl.when(step < peers)
        def _():
            index = lax.rem(me + step, peers)

            @pl.when(step == 0)
            def _():
                keep.wait()

            @pl.when(step > 0)
            def _():
                pltpu.make_async_copy(
                    grads.at[index], grads.at[index], in_recv.at[index]
                ).wait()

            attention(index)

            @pl.when(step > 0)
            def _():
                outward(index, 0).start()

        @pl.when(step == peers - 1)
        def _():
            for index in range(peers):
                span = slice(index * share, (index + 1) * share)
                result[index, 1] = key_acc[:, span].T.astype(low)
                result[index, 2] = value_acc[:, span].T.astype(low)
            for other in range(1, peers):
                outward(lax.rem(me + other, peers), 1).start()
            pltpu.make_async_copy(result.at[me], stacked.at[me], back_own).start()

        return carry

    lax.fori_loop(0, pairs + 4, step_body, 0)

    def finish_body(pair, carry):
        finish(pair, 0)
        finish(pair, 1)
        return carry

    lax.fori_loop(0, pairs, finish_body, 0)
    for step in range(1, peers):
        there = lax.rem(me + step, peers)
        inward(there).wait_send()
        for part in range(2):
            outward(there, part).wait_send()
            span = pl.ds(0, 1) if part == 0 else pl.ds(1, 2)
            pltpu.make_async_copy(
                result.at[there, span], stacked.at[there, span], back_recv.at[there, part]
            ).wait()
    pltpu.make_async_copy(result.at[me], stacked.at[me], back_own).wait()


def attend_back(joint, tags, crops, outputs, totals, source, feed_grads, number):
    peers, kinds, share, lanes = joint.shape
    slots = peers * share
    sides, halves, rows, columns = feed_grads.shape
    total = sides * columns // CHUNK
    sem = pltpu.SemaphoreType.DMA
    vmem = pl.BlockSpec(memory_space=pltpu.VMEM)
    hbm = pl.BlockSpec(memory_space=pl.ANY)
    return pl.pallas_call(
        attend_back_kernel,
        out_shape=[
            jax.ShapeDtypeStruct(joint.shape, low),
            jax.ShapeDtypeStruct((rows // 16, total * CHUNK), wide),
        ],
        in_specs=[vmem] * 5 + [hbm] * 2,
        out_specs=[hbm, vmem],
        scratch_shapes=[
            pltpu.VMEM((peers, share, lanes), low),
            pltpu.VMEM(joint.shape, low),
            pltpu.VMEM((lanes, slots), wide),
            pltpu.VMEM((lanes, slots), wide),
        ]
        + reducer_scratch(total, rows // 16)
        + [
            sem,
            sem((peers,)),
            sem((peers,)),
            sem,
            sem((peers, 2)),
            sem((peers, 2)),
        ],
        compiler_params=pltpu.CompilerParams(
            collective_id=number, has_side_effects=True, vmem_limit_bytes=60 * 2**20
        ),
    )(
        joint,
        tags,
        crops,
        outputs,
        totals,
        source,
        feed_grads.reshape(sides, halves, 4, 2, 2, rows // 16, columns),
    )


def whole(array):
    rank = len(array.shape)
    return pl.BlockSpec(array.shape, lambda *_: (0,) * rank)


def norm_parts(values):
    center = values - jnp.mean(values, axis=-1, keepdims=True)
    inverse = lax.rsqrt(jnp.mean(center * center, axis=-1, keepdims=True) + epsilon)
    return center * inverse, inverse


def norm_back(values, gain, grads):
    normed, inverse = norm_parts(values)
    scaled = grads * gain
    inner = (
        scaled
        - jnp.mean(scaled, axis=-1, keepdims=True)
        - normed * jnp.mean(scaled * normed, axis=-1, keepdims=True)
    )
    return (
        inner * inverse,
        jnp.sum(grads * normed, axis=0, keepdims=True),
        jnp.sum(grads, axis=0, keepdims=True),
    )


def columns_of(shape, axis, half):
    spot = lax.broadcasted_iota(jnp.int32, shape, axis)
    side, spot = lax.div(spot, half), lax.rem(spot, half)
    slots = half // 2
    return 2 * lax.rem(spot, slots) + 2 * side + lax.div(spot, slots) - 1


def front_kernel(items, *refs):
    arrays, refs = refs[:8], refs[8:]
    grad_in, hour_ref, pixel_ref, lat_ref, shift_ref, refs = refs[:5] + (refs[5:],)
    outs, grad_out, received, refs = refs[:8], refs[8], refs[9], refs[10:]
    joint, wide_ref, total_ref, tag_ref, crop_ref, refs = refs[:5] + (refs[5:],)
    patch_ref, prob_ref, mixed_ref, value_table, key_table, score_table, refs = refs[:6] + (
        refs[6:],
    )
    full_ref, vector_ref, query_ref, start_ref, low_ref, lead_ref, keep_ref, refs = refs[:7] + (
        refs[7:],
    )
    cut_ref, misc_ref, small_ref, weight_a, weight_b, projected, sending, turned, refs = refs[
        :8
    ] + (refs[8:],)
    gather_sems, refs = refs[:5], refs[5:]
    post_send, post_recv, load_sem, own_sem, send_sem, recv_sem, out_own, refs = refs[:7] + (
        refs[7:],
    )
    out_send, out_recv, cut_in, cut_rows, field, edge, west_edge, east_edge, edge_send, edge_recv = refs
    x, z, y, c = position()
    across, line = partners(x, z, y, c)
    lon = z * 4 + y * 2 + c
    own = (lon, x)
    east, west = (lax.rem(lon + 1, 16), x), (lax.rem(lon + 15, 16), x)
    me = y * 4 + c * 2 + x
    peers, kinds, share, lanes = joint.shape
    slots = peers * share
    head_count, var_count, tokens = prob_ref.shape
    padded = patch_ref.shape[0]
    taps = 4 * var_count
    halves = 2
    half_width = weight_a.shape[-1]

    everyone = [across["x"], across["y"], across["c"]] + line
    for flip in (3, 5, 6, 7):
        there_y = 1 - y if flip & 4 else y
        there_c = 1 - c if flip & 2 else c
        there_x = 1 - x if flip & 1 else x
        everyone.append((z * 4 + there_y * 2 + there_c, there_x))
    sources = [sector_of(z, y, c, x, part, side) for part in range(2) for side in range(2)]
    meet(everyone + [east, west], sources, own)
    letters = []
    for part in range(2):
        row = 2 * x + part
        letters.append(
            (cut_in.at[part], cut_ref.at[c], post_send.at[part], post_recv.at[c])
            + (block_of(z, y, row), own)
        )
    for row in range(4):
        letters.append(
            (grad_in.at[row], grad_out.at[x, c], post_send.at[2 + row])
            + (post_recv.at[2 + 2 * x + c], block_of(z, y, row), own)
        )
    for letter in letters[2:]:
        post(*letter)
    var_total, lat_count, column_count = pixel_ref.shape
    half = lat_ref.shape[1]

    def edge_copies():
        return [
            remote(edge, west_edge, edge_send.at[0], edge_recv.at[0], east),
            remote(edge, east_edge, edge_send.at[1], edge_recv.at[1], west),
        ]

    def send_edges():
        kind = lax.broadcasted_iota(jnp.int32, (16, column_count), 0)
        column = lax.broadcasted_iota(jnp.int32, (16, column_count), 1)
        pick = jnp.where(column == kind * (column_count - 1), 1.0, 0.0).astype(low)
        flat = pixel_ref[...].reshape(var_total * lat_count, column_count)
        edge[...] = dot(pick, flat, 1, 1).astype(low)
        for copy in edge_copies():
            copy.start()

    def make_field():
        for copy in edge_copies():
            copy.wait()
        wanted = columns_of((column_count, 2 * half), 1, half)
        column = lax.broadcasted_iota(jnp.int32, (column_count, 2 * half), 0)
        select = jnp.where(wanted == column, 1.0, 0.0).astype(low)
        kind = lax.broadcasted_iota(jnp.int32, (16, 2 * half), 0)
        wanted = columns_of((16, 2 * half), 1, half)
        from_west = jnp.logical_and(kind == 1, wanted == -1)
        from_east = jnp.logical_and(kind == 0, wanted == column_count)
        flat = pixel_ref[...].reshape(var_total * lat_count, column_count)
        result = dot(flat, select)
        for values, place in ((west_edge, from_west), (east_edge, from_east)):
            result = result + dot(values[...], jnp.where(place, 1.0, 0.0).astype(low), 0, 0)
        field[...] = result.astype(low).reshape(field.shape)

    def cut_row(part):
        lat = jnp.where(x == 0, lat_ref[part : part + 1, :], lat_ref[part + 2 : part + 3, :])
        shift = jnp.where(x == 0, shift_ref[part : part + 1, :], shift_ref[part + 2 : part + 3, :])
        row = lax.broadcasted_iota(jnp.int32, (lat_count, half), 0)
        slots = half // 2

        def body(v, carry):
            values = field[v].astype(wide)
            chosen = jnp.where(shift < 0, values[:, :half], values[:, half:])
            for py in range(2):
                taken = jnp.sum(jnp.where(row == lat + py, chosen, 0.0), axis=0, keepdims=True)
                for px in range(2):
                    spot = pl.ds((2 * py + px) * var_total + v, 1)
                    cut_rows[part, spot, :] = taken[:, px * slots : (px + 1) * slots]
            return carry

        lax.fori_loop(0, var_total, body, 0)

    def send_cut():
        cut_in[...] = cut_rows[...].astype(low)
        for letter in letters[:2]:
            post(*letter)

    def views(number):
        index, lead, first, rows, color = items[number]
        source, target = arrays[index], outs[index]
        if lead is not None:
            source, target = source.at[lead], target.at[lead]
        return source.at[pl.ds(first, rows)], target, pl.ds(first, rows), color

    stages, finish = gatherer(views, gather_sems)

    def load(source, target, spot):
        return pltpu.make_async_copy(source, target, load_sem.at[spot])

    def ask_small():
        load(outs[0], misc_ref, 0).start()
        load(outs[1], small_ref, 1).start()
        load(outs[2], weight_a, 2).start()
        load(outs[3], weight_b, 3).start()

    def read_small():
        load(outs[0], misc_ref, 0).wait()
        load(outs[1], small_ref, 1).wait()
        sector = small_ref.shape[4] // 2
        for lon in range(16):
            at = (lon // 4, lon // 2 % 2, lon % 2)
            for side in range(2):
                rows = slice((2 * lon + side) * sector, (2 * lon + side + 1) * sector)
                for half in range(2):
                    full_ref[rows, half * 128 : (half + 1) * 128] = small_ref[
                        (side,) + at + (slice(half * sector, (half + 1) * sector),)
                    ]
        upper = full_ref[:, 128:]
        vector_ref[...] = upper.astype(wide).T[taps + var_count - 128 : taps + var_count - 120]
        lane = lax.broadcasted_iota(jnp.int32, upper.shape, 1)
        full_ref[:, 128:] = jnp.where(lane < taps + var_count - 128, upper.astype(wide), 0.0).astype(
            low
        )
        kind = lax.broadcasted_iota(jnp.int32, (16, 128), 0)
        across_rows = lax.broadcasted_iota(jnp.int32, (128, 128), 0)
        across_lanes = lax.broadcasted_iota(jnp.int32, (128, 128), 1)
        queries = [None, None]
        for lon in range(16):
            at = (lon // 4, lon // 2 % 2, lon % 2)
            span = slice(lon * 128, (lon + 1) * 128)
            block = misc_ref[(0,) + at + (slice(0, 16),)].astype(wide)
            tag = jnp.sum(jnp.where(kind == z, block, 0.0), axis=0, keepdims=True)
            crop = jnp.sum(jnp.where(kind == 4 + z, block, 0.0), axis=0, keepdims=True)
            tag_ref[0:1, span] = tag
            for row, target in ((crop, crop_ref), (tag, turned)):
                target[span, :] = jnp.sum(
                    jnp.where(across_rows == across_lanes, row, 0.0), axis=1, keepdims=True
                )
            for side in range(2):
                block = misc_ref[(side,) + at + (slice(0, 16),)].astype(wide)[8:16]
                queries[side] = block if lon == 0 else queries[side] + block
        query_ref[...] = jnp.concatenate(queries, axis=0)
        mine = pl.ds(pl.multiple_of(me * share, share), share)
        keep_ref[...] = jnp.where(turned[mine, :] >= 0.0, 1.0, 0.0)
        crops = crop_ref[mine, :]
        hours = jnp.zeros((tokens, 1), wide)
        for k in range(8):
            hours = hours + jnp.where(crops == float(k), hour_ref[0:1, k : k + 1], 0.0)
        lead_ref[...] = hours
        for part in range(2):
            pltpu.make_async_copy(cut_in.at[part], cut_ref.at[part], post_recv.at[part]).wait()
            patch_ref[:taps, part * 128 : (part + 1) * 128] = cut_ref[part]
        patch_ref[taps : taps + var_count, :] = jnp.ones((var_count, tokens), low)
        patch_ref[taps + var_count :, :] = jnp.zeros((padded - taps - var_count, tokens), low)

    def tables(weight, spot, table):
        load(outs[spot], weight, spot).wait()
        for side in range(halves):
            product = dot(weight[side].reshape(-1, half_width), full_ref[...], 0, 0)
            table[side * half_width : (side + 1) * half_width, :] = product.astype(table.dtype)

    def score():
        tables(weight_a, 2, key_table)
        wide_query = jnp.concatenate([query_ref[...]] * (head_count * HEAD_DIM // 128), axis=1)
        head = lax.div(lax.broadcasted_iota(jnp.int32, wide_query.shape, 1), HEAD_DIM)
        row = lax.broadcasted_iota(jnp.int32, wide_query.shape, 0)
        wide_query = jnp.where(head == row, wide_query, 0.0).astype(low)
        rest, result = key_table[...], None
        for _ in range(3):
            part = rest.astype(low)
            rest = rest - part.astype(wide)
            piece = dot(wide_query, part)
            result = piece if result is None else result + piece
        score_table[...] = result * HEAD_DIM ** (-0.5)

    def ask_back():
        load(outs[4], weight_a, 2).start()

    def heads(first):
        mask = diagonal(var_count, padded)

        def head_step(h, carry):
            spread = jnp.where(mask, score_table[pl.ds(h, 1), :], 0.0)
            upper = spread.astype(low)
            lower = (spread - upper.astype(wide)).astype(low)
            patch = patch_ref[...]
            scores = dot(upper, patch) + dot(lower, patch)
            raised = jnp.exp(scores - jnp.max(scores, axis=0, keepdims=True))
            prob = raised / jnp.sum(raised, axis=0, keepdims=True)
            prob_ref[h] = prob
            pooled = jnp.concatenate(
                [
                    (prob * patch_ref[k * var_count : (k + 1) * var_count, :].astype(wide)).astype(
                        low
                    )
                    for k in range(5)
                ]
                + [jnp.zeros((padded - 5 * var_count, tokens), low)],
                axis=0,
            )
            start = pl.multiple_of(h * HEAD_DIM, HEAD_DIM)
            mixed_ref[pl.ds(start, HEAD_DIM), :] = dot(
                value_table[pl.ds(start, HEAD_DIM), :], pooled
            ).astype(low)
            return carry

        lax.fori_loop(first, first + 4, head_step, 0)

    def begin_block():
        load(outs[4], weight_a, 2).wait()
        total = lead_ref[...] * vector_ref[0:1] + vector_ref[1:2]
        mixed = mixed_ref[...].T
        for side in range(halves):
            total = total + dot(
                mixed[:, side * half_width : (side + 1) * half_width],
                weight_a[side].reshape(-1, half_width),
                1,
                1,
            )
        start_ref[...] = total
        normed, _ = norm_parts(total)
        low_ref[...] = (normed * vector_ref[2:3] + vector_ref[3:4]).astype(low)

    def ask_input(kind):
        target = weight_b if kind % 2 == 0 else weight_a
        load(outs[5].at[kind], target, 3 - kind % 2).start()

    def project(kind):
        target = weight_b if kind % 2 == 0 else weight_a
        load(outs[5].at[kind], target, 3 - kind % 2).wait()
        pairs = half_width // lanes
        for side in range(halves):
            result = dot(low_ref[...], target[side].reshape(-1, half_width)).astype(low)
            if kind == 0:
                result = result * low(HEAD_DIM ** (-0.5))
            for pair in range(pairs):
                projected[side * pairs + pair, kind] = result[
                    :, pair * lanes : (pair + 1) * lanes
                ]

    def inward(step):
        there = lax.rem(me + step, peers)
        return remote(
            projected.at[there],
            joint.at[me],
            send_sem.at[there],
            recv_sem.at[me],
            plane_device(z, there),
        )

    def outward(index):
        return remote(
            sending.at[index],
            received.at[me],
            out_send.at[index],
            out_recv.at[me],
            plane_device(z, index),
        )

    def send_heads():
        pltpu.make_async_copy(projected.at[me], joint.at[me], own_sem).start()
        for step in range(1, peers):
            inward(step).start()

    def take_heads():
        pltpu.make_async_copy(projected.at[me], joint.at[me], own_sem).wait()
        for step in range(1, peers):
            there = lax.rem(me + step, peers)
            pltpu.make_async_copy(joint.at[there], joint.at[there], recv_sem.at[there]).wait()

    def attention(first, count):
        def block(step, carry):
            index = lax.rem(me + 1 + step, peers)
            span = pl.ds(pl.multiple_of(index * share, share), share)
            queries = joint[index, 0]
            keys = joint[:, 1].reshape(slots, lanes)
            values = joint[:, 2].reshape(slots, lanes)
            allowed = crop_ref[span, :] == tag_ref[0:1, :]
            result = None
            for h in range(2):
                scores = dot(head_lanes(queries, h), keys, 1, 1)
                scores = jnp.where(allowed, scores, masked_score)
                largest = jnp.max(scores, axis=1, keepdims=True)
                weights = jnp.exp(scores - largest)
                total = jnp.sum(weights, axis=1, keepdims=True)
                weights = (weights * (1.0 / total)).astype(low)
                part = head_lanes(dot(weights, values), h)
                result = part if result is None else result + part
                total_ref[h, span, :] = largest + jnp.log(total)
            wide_ref[span, :] = result
            sending[index] = result.astype(low)

            @pl.when(step < peers - 1)
            def _():
                outward(index).start()

            return carry

        lax.fori_loop(first, first + count, block, 0)

    ready = {}
    for number, item in enumerate(items):
        ready[item[:2]] = number + 8
    at = ready[(3, None)]
    extra = {0: [send_edges], 3: [make_field], 4: [partial(cut_row, 0)], 5: [partial(cut_row, 1)]}
    extra.update({6: [send_cut], at: [ask_small, read_small], at + 1: [score]})
    extra[at + 2] = [lambda: tables(weight_b, 3, value_table), ask_back]
    for quarter in range(4):
        extra.setdefault(at + 3 + quarter // 2, []).append(partial(heads, 4 * quarter))
    at = max(at + 5, ready[(5, 2)])
    extra.setdefault(at, []).extend([partial(ask_input, 0), begin_block, partial(ask_input, 1)])
    extra[at + 1] = [partial(project, 0), partial(ask_input, 2), partial(project, 1)]
    extra[at + 2] = [partial(project, 2), send_heads]
    at += 5
    extra[at] = [take_heads]
    for step in range(4):
        extra.setdefault(at + step, []).append(partial(attention, 2 * step, 2))
    total = len(items)
    for step in range(max(total + 8, max(extra) + 1)):
        for back, stage in enumerate(stages):
            if 0 <= step - 2 * back < total:
                stage(step - 2 * back)
        for work in extra.get(step, []):
            work()
    last = pltpu.make_async_copy(sending.at[me], received.at[me], out_own)
    last.start()
    for number in range(total):
        finish(number)
    for letter in letters:
        settle(*letter)
    for side in range(2):
        for part in range(2):
            pltpu.make_async_copy(
                grad_in.at[0], grad_out.at[side, part], post_recv.at[2 + 2 * side + part]
            ).wait()
    for step in range(1, peers):
        there = lax.rem(me + step, peers)
        inward(step).wait_send()
        outward(there).wait_send()
        pltpu.make_async_copy(sending.at[there], received.at[there], out_recv.at[there]).wait()
    last.wait()


def front(arrays, grads, hours, pixels, lat_lanes, shift_lanes, head_count, number):
    items = []
    for index, array in enumerate(arrays):
        for lead in range(array.shape[0]) if array.ndim == 3 else (None,):
            rows = array.shape[-2]
            if rows % 64:
                items.append((index, lead, 0, rows, 0))
                continue
            for color in range(2):
                items.append((index, lead, color * rows // 2, rows // 2, color))
    width = arrays[2].shape[1]
    model = 2 * width
    var_count, lat_count = pixels.shape[:2]
    tokens = lat_lanes.shape[1]
    cut_shape = (2, 4 * var_count, tokens // 2)
    padded = 2 * arrays[1].shape[1]
    slots = 8 * tokens
    sem = pltpu.SemaphoreType.DMA
    vmem = pl.BlockSpec(memory_space=pltpu.VMEM)
    hbm = pl.BlockSpec(memory_space=pl.ANY)
    block = (2, 4, 2, 2)

    def all_of(array):
        return array.shape[:-2] + block + array.shape[-2:]

    low_outs = [all_of(a) for a in arrays] + [(2, 2) + grads.shape[1:], (8, tokens, 128)]
    vmem_outs = [
        ((8, 3, tokens, 128), low),
        ((slots, 128), wide),
        ((2, slots, 1), wide),
        ((8, slots), wide),
        ((slots, 1), wide),
        ((padded, tokens), low),
        ((head_count, var_count, tokens), wide),
        ((model, tokens), low),
        ((model, padded), low),
        ((model, padded), wide),
        ((head_count, padded), wide),
        ((model, padded), low),
        ((8, model), wide),
        ((head_count, 128), wide),
        ((tokens, model), wide),
        ((tokens, model), low),
        ((tokens, 1), wide),
        ((tokens, 1), wide),
    ]
    result = pl.pallas_call(
        partial(front_kernel, items),
        out_shape=[jax.ShapeDtypeStruct(shape, low) for shape in low_outs]
        + [jax.ShapeDtypeStruct(shape, dtype) for shape, dtype in vmem_outs],
        in_specs=[hbm] * (len(arrays) + 1) + [vmem] * 4,
        out_specs=[hbm] * len(low_outs) + [vmem] * len(vmem_outs),
        scratch_shapes=[
            pltpu.VMEM(cut_shape, low),
            pltpu.VMEM(all_of(arrays[0]), low),
            pltpu.VMEM(all_of(arrays[1]), low),
            pltpu.VMEM(all_of(arrays[2]), low),
            pltpu.VMEM(all_of(arrays[2]), low),
            pltpu.VMEM((8, 3, tokens, 128), low),
            pltpu.VMEM((8, tokens, 128), low),
            pltpu.VMEM((slots, 1), wide),
            sem((len(items),)),
        ]
        + [sem((len(items), 3))] * 4
        + [sem((6,)), sem((6,)), sem((4,)), sem, sem((8,)), sem((8,)), sem, sem((8,)), sem((8,))]
        + [
            pltpu.VMEM(cut_shape, low),
            pltpu.VMEM(cut_shape, wide),
            pltpu.VMEM((var_count, lat_count, 2 * tokens), low),
            pltpu.VMEM((16, var_count * lat_count), low),
            pltpu.VMEM((16, var_count * lat_count), low),
            pltpu.VMEM((16, var_count * lat_count), low),
            sem((2,)),
            sem((2,)),
        ],
        compiler_params=pltpu.CompilerParams(
            collective_id=number, has_side_effects=True, vmem_limit_bytes=58 * 2**20
        ),
    )(*arrays, grads, hours, pixels, lat_lanes, shift_lanes)
    count = len(arrays)
    gathered = [
        g.reshape(a.shape[:-2] + (2, 16 * a.shape[-2], a.shape[-1]))
        for g, a in zip(result, arrays)
    ]
    return gathered, result[count:]


def feed_kernel(
    attended_ref,
    proj_ref,
    start_ref,
    vector_ref,
    up_ref,
    down_ref,
    bias_ref,
    final_ref,
    masked_ref,
    keep_ref,
    predicted_ref,
    middle_grad_ref,
    unit_ref,
    grad_feed_ref,
    grad_proj_ref,
    grad_final_ref,
    grad_bias_ref,
    grad_vector_ref,
    flat,
    middle,
    second,
    second_turned,
    active,
    slope,
    total,
    grad_low,
    grad_turned,
    grad_final,
):
    step = pl.program_id(0)
    count = active.shape[0]
    row_count, units, share, lanes = attended_ref.shape
    _, halves, _, half_width = proj_ref.shape
    tokens = row_count * share

    @pl.when(step == 0)
    def _():
        for unit in range(units):
            flat[:, unit * lanes : (unit + 1) * lanes] = attended_ref[:, unit].reshape(
                tokens, lanes
            )
        result = start_ref[...]
        for side in range(halves):
            result = result + dot(
                flat[:, side * half_width : (side + 1) * half_width], proj_ref[0, side], 1, 1
            )
        middle[...] = result
        normed, _ = norm_parts(result)
        normed = (normed * vector_ref[4:5] + vector_ref[5:6]).astype(low)
        second[...] = normed
        second_turned[...] = normed.T
        total[...] = result

    @pl.when(step < count)
    def _():
        hidden = dot(second[...], up_ref[0, 0]) + bias_ref[...]
        share_of = 0.5 * (1.0 + lax.erf(hidden * (0.5**0.5)))
        fired = (hidden * share_of).astype(low)
        active[step] = fired
        slope[step] = share_of + hidden * jnp.exp(-0.5 * hidden * hidden) * (
            0.5 / 1.2533141373155003
        )
        total[...] += dot(fired, down_ref[0, 0], 1, 1)

    @pl.when(step == count - 1)
    def _():
        final_low = total[...].astype(low)
        final_turned = final_low.T
        grads = None
        for side in range(halves):
            predicted_ref[side] = (dot(final_low, final_ref[side]) * keep_ref[...]).astype(low)
            part = dot(masked_ref[side], final_ref[side], 1, 1)
            grads = part if grads is None else grads + part
            grad_final_ref[side] = dot(final_turned, masked_ref[side]).astype(low)
        grad_final[...] = grads
        grad_low[...] = grads.astype(low)
        grad_turned[...] = grads.astype(low).T
        total[...] = jnp.zeros_like(total)

    @pl.when(step >= count)
    def _():
        block = step - count
        hidden_grad = dot(grad_low[...], down_ref[0, 0]) * slope[block]
        hidden_low = hidden_grad.astype(low)
        grad_bias_ref[...] = jnp.sum(hidden_low.astype(wide), axis=0, keepdims=True)
        total[...] += dot(hidden_low, up_ref[0, 0], 1, 1)
        grad_feed_ref[0, 0] = dot(second_turned[...], hidden_low).astype(low)
        grad_feed_ref[1, 0] = dot(grad_turned[...], active[block]).astype(low)

    @pl.when(step == 2 * count - 1)
    def _():
        part, grad_gain, grad_shift = norm_back(middle[...], vector_ref[4:5], total[...])
        result = grad_final[...] + part
        middle_grad_ref[...] = result
        grad_vector_ref[0:1] = grad_gain
        grad_vector_ref[1:2] = grad_shift
        result_low = result.astype(low)
        result_turned = result_low.T
        pairs = half_width // lanes
        for side in range(halves):
            span = slice(side * half_width, (side + 1) * half_width)
            grad_proj_ref[side] = dot(result_turned, flat[:, span]).astype(low)
            out = dot(result_low, proj_ref[0, side]).astype(low)
            for pair in range(pairs):
                unit_ref[:, side * pairs + pair] = out[
                    :, pair * lanes : (pair + 1) * lanes
                ].reshape(row_count, share, lanes)


def feed(attended, start, vectors, late, up_bias, final_weight, masked, keep):
    blocks, halves, model, block = late.shape
    half_width = block
    each = blocks // 2
    full = each * block
    tokens = start.shape[0]
    count = halves * each

    def block_of_kind(kind):
        def block_at(i):
            j = lax.rem(i, count)
            return (kind * each + lax.rem(j, each), lax.div(j, each), 0, 0)

        return pl.BlockSpec((1, 1, model, block), block_at)

    def late_block(i):
        j = lax.max(i - count, 0)
        return (0, lax.div(j, each), 0, lax.rem(j, each))

    def fixed(shape, dtype):
        rank = len(shape)
        return jax.ShapeDtypeStruct(shape, dtype), pl.BlockSpec(shape, lambda i: (0,) * rank)

    outs = [
        fixed((halves, tokens, 128), low),
        fixed((tokens, model), wide),
        fixed(attended.shape, low),
        (
            jax.ShapeDtypeStruct((2, halves, model, full), low),
            pl.BlockSpec((2, 1, model, block), late_block),
        ),
        fixed((halves, model, half_width), low),
        fixed((halves, model, 128), low),
        (
            jax.ShapeDtypeStruct((1, halves * full), wide),
            pl.BlockSpec((1, block), lambda i: (0, lax.max(i - count, 0))),
        ),
        fixed((2, model), wide),
    ]
    return pl.pallas_call(
        feed_kernel,
        grid=(2 * count,),
        out_shape=[shape for shape, _ in outs],
        in_specs=[
            whole(attended),
            pl.BlockSpec((1, halves, model, block), lambda i: (blocks - 1, 0, 0, 0)),
            whole(start),
            whole(vectors),
            block_of_kind(0),
            block_of_kind(1),
            pl.BlockSpec((1, block), lambda i: (0, lax.rem(i, count))),
            whole(final_weight),
            whole(masked),
            whole(keep),
        ],
        out_specs=[spec for _, spec in outs],
        scratch_shapes=[
            pltpu.VMEM((tokens, model), low),
            pltpu.VMEM((tokens, model), wide),
            pltpu.VMEM((tokens, model), low),
            pltpu.VMEM((model, tokens), low),
            pltpu.VMEM((count, tokens, block), low),
            pltpu.VMEM((count, tokens, block), wide),
            pltpu.VMEM((tokens, model), wide),
            pltpu.VMEM((tokens, model), low),
            pltpu.VMEM((model, tokens), low),
            pltpu.VMEM((tokens, model), wide),
        ],
        compiler_params=pltpu.CompilerParams(vmem_limit_bytes=56 * 2**20),
    )(attended, late, start, vectors, late, late, up_bias, final_weight, masked, keep)


def return_kernel(
    grads_ref,
    weight_ref,
    low_ref,
    start_ref,
    middle_grad_ref,
    vector_ref,
    lead_ref,
    back_ref,
    mixed_ref,
    grad_input_ref,
    grad_mixer_ref,
    mixed_grad_ref,
    grad_vector_ref,
    turned,
    total,
):
    step = pl.program_id(0)
    halves, _, half_width = back_ref.shape
    row_count, _, _, share, lanes = grads_ref.shape
    tokens = row_count * share
    pairs = half_width // lanes

    @pl.when(step == 0)
    def _():
        turned[...] = low_ref[...].T
        total[...] = jnp.zeros_like(total)

    kind, side = lax.div(step, halves), lax.rem(step, halves)
    piece = jnp.concatenate(
        [grads_ref[:, side * pairs + pair, kind].reshape(tokens, lanes) for pair in range(pairs)],
        axis=1,
    )
    total[...] += dot(piece, weight_ref[0, 0], 1, 1)
    grad_input_ref[0, 0] = dot(turned[...], piece).astype(low)

    @pl.when(step == pl.num_programs(0) - 1)
    def _():
        part, grad_gain, grad_shift = norm_back(start_ref[...], vector_ref[2:3], total[...])
        result = middle_grad_ref[...] + part
        grad_vector_ref[0:1] = jnp.sum(result * lead_ref[...], axis=0, keepdims=True)
        grad_vector_ref[1:2] = jnp.sum(result, axis=0, keepdims=True)
        grad_vector_ref[2:3] = grad_gain
        grad_vector_ref[3:4] = grad_shift
        result_low = result.astype(low)
        result_turned = result_low.T
        for half in range(halves):
            span = slice(half * half_width, (half + 1) * half_width)
            grad_mixer_ref[half] = dot(result_turned, mixed_ref[span, :], 1, 1).astype(low)
            mixed_grad_ref[span, :] = dot(result_low, back_ref[half]).astype(low).T


def go_back(grads, weights, first_low, start, middle_grad, vectors, lead_column, back_weight, mixed):
    kinds, halves, model, half_width = weights.shape
    tokens = start.shape[0]
    block = pl.BlockSpec((1, 1, model, half_width), lambda i: (i // halves, i % halves, 0, 0))
    return pl.pallas_call(
        return_kernel,
        grid=(kinds * halves,),
        out_shape=[
            jax.ShapeDtypeStruct(weights.shape, low),
            jax.ShapeDtypeStruct((halves, model, half_width), low),
            jax.ShapeDtypeStruct((model, tokens), low),
            jax.ShapeDtypeStruct((4, model), wide),
        ],
        in_specs=[
            whole(grads),
            block,
            whole(first_low),
            whole(start),
            whole(middle_grad),
            whole(vectors),
            whole(lead_column),
            whole(back_weight),
            whole(mixed),
        ],
        out_specs=[
            block,
            pl.BlockSpec((halves, model, half_width), lambda i: (0, 0, 0)),
            pl.BlockSpec((model, tokens), lambda i: (0, 0)),
            pl.BlockSpec((4, model), lambda i: (0, 0)),
        ],
        scratch_shapes=[pltpu.VMEM((model, tokens), low), pltpu.VMEM((tokens, model), wide)],
        compiler_params=pltpu.CompilerParams(vmem_limit_bytes=50 * 2**20),
    )(grads, weights, first_low, start, middle_grad, vectors, lead_column, back_weight, mixed)


def einsum(spec, left, right):
    return jnp.einsum(spec, left, right, preferred_element_type=wide)


def fast_local(
    pixels,
    crop_starts,
    crop_shifts,
    slot_crops,
    occupied,
    lead_hours,
    patch_weight,
    variable_embed,
    mixer_query,
    mixer_keys,
    mixer_values,
    mixer_output,
    lead_embed,
    first_gain,
    first_bias,
    attention_in,
    attention_out,
    second_gain,
    second_bias,
    expand_weight,
    expand_bias,
    reduce_weight,
    output_weight,
    cotangent,
):
    lon, head = lax.axis_index(LON), lax.axis_index(HEAD)
    row_count, slot_width = slot_crops.shape
    share = slot_width // HEAD_SIZE
    tokens = row_count * share
    var_count, lat_count, column_count = pixels.shape
    head_half, query_width = mixer_query.shape
    head_count = HEAD_SIZE * head_half
    half_width = head_half * HEAD_DIM
    out_half = output_weight.shape[1]
    slice_width = patch_weight.shape[2]
    model = slice_width * LON_SIZE * HEAD_SIZE
    block_rows = model // LON_SIZE
    taps = 4 * var_count
    pairs = half_width // 128
    scale = HEAD_DIM ** (-0.5)

    lat_lanes = jnp.tile(crop_lookup(crop_starts, slot_crops), (1, 2))
    shift_lanes = jnp.tile(crop_lookup(crop_shifts, slot_crops), (1, 2))
    masked = cotangent * occupied[:, :, None].astype(low)
    masked = jnp.pad(masked, ((0, 0), (0, 0), (0, 128 - out_half)))
    late = jnp.concatenate(
        [
            jnp.transpose(part.reshape(block_rows, -1, half_width), (1, 0, 2))
            for part in (expand_weight, reduce_weight.T, attention_out.T)
        ]
    )
    padded = 256
    small = jnp.concatenate(
        [
            jnp.transpose(patch_weight, (1, 0, 2)).reshape(taps, slice_width),
            variable_embed,
            jnp.concatenate(
                [
                    lead_embed.reshape(-1),
                    first_gain,
                    first_bias,
                    second_gain,
                    second_bias,
                    jnp.zeros(((padded - taps - var_count - 6) * slice_width,), low),
                ]
            ).reshape(-1, slice_width),
        ]
    ).T
    small = jnp.concatenate([small[:, :128], small[:, 128:]])
    tags = jnp.where(occupied == 1, slot_crops, -1).astype(low)
    lane = jnp.arange(128) % (LON_SIZE * query_width) // query_width
    spread = jnp.tile(jnp.concatenate([mixer_query, expand_bias]), (1, 128 // query_width))
    spread = jnp.where(lane == lon, spread, 0)
    misc = jnp.concatenate([tags, slot_crops.astype(low), spread])
    out_block = jnp.pad(output_weight, ((0, 0), (0, 128 - out_half)))
    my_row = lax.div(lon, LON_SIZE // row_count)
    hours = lax.dynamic_index_in_dim(lead_hours, my_row, 0).astype(wide) / 100.0
    hours = jnp.pad(hours, ((0, 0), (0, 128 - hours.shape[1])))
    gathered, made = front(
        [
            misc,
            small,
            mixer_keys,
            mixer_values,
            mixer_output.T,
            attention_in,
            out_block,
            late,
        ],
        masked,
        hours,
        pixels,
        lat_lanes,
        shift_lanes,
        head_count,
        1,
    )
    misc_all, _, key_weight, value_weight, mixer_weight, input_weight, final_weight, late = gathered
    masked, attended, joint, attended_wide, totals, tag_row, crop_column = made[:7]
    patches, probs, mixed, value_table, key_table, score_table = made[7:13]
    patch_full, vectors, query, start_sum, first_low, lead_column, keep_mask = made[13:]
    masked = masked.reshape(HEAD_SIZE, tokens, 128)
    attended = attended[None]
    query_wide, query = query, query[:, :HEAD_DIM]
    bias_rows = expand_bias.shape[0]
    up_bias = misc_all.reshape(HEAD_SIZE, LON_SIZE, -1, 128)[:, :, 2 * row_count + head_half :]
    up_bias = jnp.sum(up_bias[..., : LON_SIZE * query_width].astype(wide), axis=1)
    units = HEAD_SIZE * pairs
    (
        predicted,
        middle_grad,
        out_grads,
        grad_feed,
        grad_proj,
        grad_out,
        grad_up_bias,
        second_vectors,
    ) = feed(
        attended,
        start_sum,
        vectors,
        late,
        up_bias.reshape(1, -1),
        final_weight,
        masked,
        keep_mask,
    )
    stacked, feed_sums = attend_back(
        joint,
        tag_row,
        crop_column,
        attended_wide,
        totals,
        out_grads.reshape(units, tokens, 128),
        grad_feed,
        4,
    )
    stacked = stacked[None]
    grad_input, grad_mixer, mixed_grads, first_vectors = go_back(
        stacked,
        input_weight,
        first_low,
        start_sum,
        middle_grad,
        vectors,
        lead_column,
        mixer_weight,
        mixed,
    )
    bias_cols = expand_bias.shape[1]
    bias_block = jnp.transpose(
        grad_up_bias.reshape(HEAD_SIZE, bias_rows, LON_SIZE, bias_cols), (0, 2, 1, 3)
    )
    bias_at = out_half + head_half
    bias_block = jnp.pad(
        bias_block,
        (
            (0, 0),
            (0, 0),
            (0, block_rows - bias_rows),
            (bias_at, 128 - bias_at - bias_cols),
        ),
    ).reshape(HEAD_SIZE, model, 128)
    rest = grad_out + bias_block.astype(low)
    spot = taps + var_count
    sums, predicted, pixel_grad = reduce_all(
        [grad_proj, grad_input, grad_mixer],
        predicted.reshape(HEAD_SIZE, 2, slot_width, 128),
        (key_weight, value_weight),
        lat_lanes,
        shift_lanes,
        (patches, probs, score_table, value_table, key_table, mixed_grads),
        (patch_full, query_wide, first_vectors, second_vectors, rest),
        lat_count,
        2,
    )
    predicted = predicted[:, :, :out_half]
    full_half = expand_weight.shape[1]
    place = [0]

    def take(width):
        begin = place[0]
        place[0] = begin + width
        return sums[:, begin : begin + width]

    out_up = feed_sums[:, :full_half]
    out_down = feed_sums[:, full_half:].T
    out_proj = take(half_width).T
    out_input = jnp.stack([take(half_width) for _ in range(3)])
    out_mixer = take(half_width).T
    out_values = take(half_width)
    tail_small = take(128)
    tail_rest = take(128)
    tail_small = jnp.concatenate([tail_small[:slice_width], tail_small[slice_width:]], axis=1).T
    out_patch = jnp.transpose(tail_small[:taps].reshape(4, var_count, slice_width), (1, 0, 2))
    out_variable = tail_small[taps:spot]
    out_lead = tail_small[spot : spot + 2]
    out_final = tail_rest[:, :out_half]
    at = out_half
    my_heads = tail_rest[:, at : at + head_half]
    at += head_half
    out_bias = tail_rest[:bias_rows, at : at + bias_cols]
    at += bias_cols
    out_query = tail_rest[:head_half, at : at + query_width]
    my_query = block_slice(query, head, head_half, 0)
    out_keys = (my_heads[:, :, None] * my_query[None]).reshape(block_rows, half_width)

    pixel_grad = jnp.transpose(pixel_grad, (1, 0, 2))
    return (
        predicted,
        pixel_grad,
        out_patch,
        out_variable,
        out_query,
        out_keys,
        out_values,
        out_mixer,
        out_lead,
        tail_small[spot + 2],
        tail_small[spot + 3],
        out_input,
        out_proj,
        tail_small[spot + 4],
        tail_small[spot + 5],
        out_up,
        out_bias,
        out_down,
        out_final,
    )


def solution(mesh):
    body = fast_local if planned(mesh) else local
    placed = (
        P(None, None, LON),
        P(),
        P(),
        P(None, LON),
        P(None, LON),
        P(),
        P(None, None, (LON, HEAD)),
        P(None, (LON, HEAD)),
        P(HEAD, LON),
        P(LON, HEAD),
        P(LON, HEAD),
        P(HEAD, LON),
        P(None, (LON, HEAD)),
        P((LON, HEAD)),
        P((LON, HEAD)),
        P(None, LON, HEAD),
        P(HEAD, LON),
        P((LON, HEAD)),
        P((LON, HEAD)),
        P(LON, HEAD),
        P(HEAD, LON),
        P(HEAD, LON),
        P(LON, HEAD),
        P(None, LON, HEAD),
    )
    return jax.shard_map(
        body,
        mesh=mesh,
        in_specs=placed,
        out_specs=(
            P(None, LON, HEAD),
            P(None, None, LON),
            P(None, None, (LON, HEAD)),
            P(None, (LON, HEAD)),
            P(HEAD, LON),
            P(LON, HEAD),
            P(LON, HEAD),
            P(HEAD, LON),
            P(None, (LON, HEAD)),
            P((LON, HEAD)),
            P((LON, HEAD)),
            P(None, LON, HEAD),
            P(HEAD, LON),
            P((LON, HEAD)),
            P((LON, HEAD)),
            P(LON, HEAD),
            P(HEAD, LON),
            P(HEAD, LON),
            P(LON, HEAD),
        ),
        check_vma=False,
    )
```

```python
from functools import partial

import jax
import jax.numpy as jnp
from jax import lax
from jax.experimental import pallas as pl
from jax.experimental.pallas import tpu as pltpu
from jax.sharding import PartitionSpec as P

HEAD_DIM = 64
LON, HEAD = "lon", "head"


epsilon = 1e-05
masked_score = -1e30
highest = lax.Precision.HIGHEST


def extended(array, sides, width):
    for axis, dim in sides:
        count, length = (lax.axis_size(axis), array.shape[dim])
        up = [(i, (i + 1) % count) for i in range(count)]
        down = [(j, i) for i, j in up]
        last = lax.slice_in_dim(array, length - width, length, axis=dim)
        leading = lax.slice_in_dim(array, 0, width, axis=dim)
        before = lax.ppermute(last, axis, up)
        after = lax.ppermute(leading, axis, down)
        array = jnp.concatenate([before, array, after], axis=dim)
    return array


def layer_norm(values, gain_vector, shift_vector):
    center = values - jnp.mean(values, axis=-1, keepdims=True)
    spread = jnp.mean(center * center, axis=-1, keepdims=True)
    return center * lax.rsqrt(spread + epsilon) * gain_vector + shift_vector


def head_total(partial_sum):
    return lax.psum(partial_sum.astype(jnp.bfloat16), HEAD).astype(jnp.float32)


def head_share(partial_sum):
    return lax.psum_scatter(
        partial_sum.astype(jnp.bfloat16), HEAD, scatter_dimension=0, tiled=True
    ).astype(jnp.float32)


def head_rows(values):
    return lax.all_gather(values, HEAD, axis=0, tiled=True)


def reduce_rows(partial_sum):
    return head_share(partial_sum)


def spread_rows(values):
    return head_rows(values)


def crop_lookup(crop_table, slot_numbers):
    numbers = jnp.arange(crop_table.shape[1], dtype=jnp.int32)
    picked = slot_numbers[:, :, None] == numbers[None, None, :]
    return jnp.sum(jnp.where(picked, crop_table[:, None, :], 0), axis=2)


def outer_sum(left_rows, right_rows):
    return jnp.einsum("ti,tj->ij", left_rows, right_rows, preferred_element_type=jnp.float32)


def block_slice(values, block_index, block_width, axis_number):
    return lax.dynamic_slice_in_dim(values, block_index * block_width, block_width, axis_number)


def block_scores(queries, query_crops, key_block, key_tags):
    scores = jnp.einsum(
        "rqhd,rkhd->rhqk", queries, key_block, preferred_element_type=jnp.float32
    ) * HEAD_DIM ** (-0.5)
    matched = query_crops[:, None, :, None] == key_tags[:, None, None, :]
    return (jnp.where(matched, scores, masked_score), matched)


def key_stats(queries, query_crops, key_rows, key_tags, block_width):
    row_count, slot_count, head_count, head_size = queries.shape

    def key_step(carried, block_index):
        largest, totals = carried
        scores, matched = block_scores(
            queries,
            query_crops,
            block_slice(key_rows, block_index, block_width, 1),
            block_slice(key_tags, block_index, block_width, 1),
        )
        raised = jnp.maximum(largest, jnp.max(scores, axis=-1))
        totals = totals * jnp.exp(largest - raised) + jnp.sum(
            jnp.where(matched, jnp.exp(scores - raised[..., None]), 0.0), axis=-1
        )
        return ((raised, totals), None)

    initial = (
        jnp.full((row_count, head_count, slot_count), masked_score, jnp.float32),
        jnp.zeros((row_count, head_count, slot_count), jnp.float32),
    )
    (largest, totals), _ = lax.scan(key_step, initial, jnp.arange(key_rows.shape[1] // block_width))
    return largest + jnp.log(totals)


def attend(queries, query_crops, key_rows, value_rows, key_tags, log_totals, block_width):

    def attend_step(running, block_index):
        scores, matched = block_scores(
            queries,
            query_crops,
            block_slice(key_rows, block_index, block_width, 1),
            block_slice(key_tags, block_index, block_width, 1),
        )
        weights = jnp.where(matched, jnp.exp(scores - log_totals[..., None]), 0.0).astype(
            jnp.bfloat16
        )
        value_block = block_slice(value_rows, block_index, block_width, 1)
        return (
            running
            + jnp.einsum(
                "rhqk,rkhd->rqhd", weights, value_block, preferred_element_type=jnp.float32
            ),
            None,
        )

    outputs, _ = lax.scan(
        attend_step,
        jnp.zeros(queries.shape, jnp.float32),
        jnp.arange(key_rows.shape[1] // block_width),
    )
    return outputs


def score_grads(
    queries, query_crops, out_grads, log_totals, deltas, key_block, value_block, key_tags
):
    scores, matched = block_scores(queries, query_crops, key_block, key_tags)
    weights = jnp.where(matched, jnp.exp(scores - log_totals[..., None]), 0.0)
    weight_grads = jnp.einsum(
        "rqhd,rkhd->rhqk", out_grads, value_block, preferred_element_type=jnp.float32
    )
    score_delta = (weights * (weight_grads - deltas[..., None])).astype(jnp.bfloat16)
    return (score_delta, weights.astype(jnp.bfloat16))


def mixer_row(patch_row, full_patch, full_variable, pair_weight, head_query):
    embedded = jnp.einsum(
        "svk,vkd->svd", patch_row, full_patch, preferred_element_type=jnp.float32
    ) + full_variable.astype(jnp.float32)
    embedded = embedded.astype(jnp.bfloat16)
    slot_count, var_count, model_width = embedded.shape
    head_count, head_size = head_query.shape
    local_width = head_count * head_size
    paired = jnp.dot(
        embedded.reshape(slot_count * var_count, model_width),
        pair_weight,
        preferred_element_type=jnp.float32,
    ).astype(jnp.bfloat16)
    key_rows = paired[:, :local_width].reshape(slot_count, var_count, head_count, head_size)
    value_rows = paired[:, local_width:].reshape(slot_count, var_count, head_count, head_size)
    scores = jnp.einsum(
        "svhd,hd->shv", key_rows, head_query, preferred_element_type=jnp.float32
    ) * HEAD_DIM ** (-0.5)
    weights = jax.nn.softmax(scores, axis=-1)
    return (embedded, key_rows, value_rows, weights)


def mixer_back(carried, inputs, full_patch, full_variable, pair_weight, head_query):
    patch_row, mixed_grad = inputs
    embedded, key_rows, value_rows, weights = mixer_row(
        patch_row, full_patch, full_variable, pair_weight, head_query
    )
    slot_count, var_count, model_width = embedded.shape
    local_width = key_rows.shape[2] * key_rows.shape[3]
    mixed_wide = mixed_grad.astype(jnp.float32)
    value_grads = jnp.einsum("shv,shd->svhd", weights, mixed_wide, precision=highest).astype(
        jnp.bfloat16
    )
    weight_grads = jnp.einsum(
        "shd,svhd->shv", mixed_wide, value_rows.astype(jnp.float32), precision=highest
    )
    score_delta = (
        weights
        * (weight_grads - jnp.sum(weights * weight_grads, axis=-1, keepdims=True))
        * HEAD_DIM ** (-0.5)
    )
    key_grads = jnp.einsum(
        "shv,hd->svhd", score_delta, head_query.astype(jnp.float32), precision=highest
    ).astype(jnp.bfloat16)
    query_grad = jnp.einsum(
        "shv,svhd->hd", score_delta, key_rows.astype(jnp.float32), precision=highest
    )
    pair_grads = jnp.concatenate(
        [
            key_grads.reshape(slot_count * var_count, local_width),
            value_grads.reshape(slot_count * var_count, local_width),
        ],
        axis=1,
    )
    embed_grad = jnp.einsum(
        "ne,de->nd", pair_grads, pair_weight, preferred_element_type=jnp.float32
    )
    pair_weight_grad = outer_sum(embedded.reshape(slot_count * var_count, model_width), pair_grads)
    embed_grad = embed_grad.reshape(slot_count, var_count, model_width)
    patch_grad = jnp.einsum(
        "svk,svd->vkd", patch_row.astype(jnp.float32), embed_grad, precision=highest
    )
    variable_grad = jnp.sum(embed_grad, axis=0)
    slot_grad = jnp.einsum(
        "svd,vkd->svk", embed_grad, full_patch.astype(jnp.float32), precision=highest
    )
    patch_acc, variable_acc, query_acc, pair_acc = carried
    return (
        (
            patch_acc + patch_grad,
            variable_acc + variable_grad,
            query_acc + query_grad,
            pair_acc + pair_weight_grad,
        ),
        slot_grad,
    )


def local(
    pixels,
    crop_starts,
    crop_shifts,
    slot_crops,
    occupied,
    lead_hours,
    patch_weight,
    variable_embed,
    mixer_query,
    mixer_keys,
    mixer_values,
    mixer_output,
    lead_embed,
    first_gain,
    first_bias,
    attention_in,
    attention_out,
    second_gain,
    second_bias,
    expand_weight,
    expand_bias,
    reduce_weight,
    output_weight,
    cotangent,
):
    shared = (
        lax.all_gather(patch_weight, (LON, HEAD), axis=2, tiled=True),
        lax.all_gather(variable_embed, (LON, HEAD), axis=1, tiled=True),
        lax.all_gather(lead_embed, (LON, HEAD), axis=1, tiled=True),
        lax.all_gather(first_gain, (LON, HEAD), axis=0, tiled=True),
        lax.all_gather(first_bias, (LON, HEAD), axis=0, tiled=True),
        lax.all_gather(second_gain, (LON, HEAD), axis=0, tiled=True),
        lax.all_gather(second_bias, (LON, HEAD), axis=0, tiled=True),
    )
    full_patch, full_variable, full_lead, gain_first, shift_first, gain_second, shift_second = (
        shared
    )
    sector = (
        lax.all_gather(mixer_query, LON, axis=1, tiled=True),
        lax.all_gather(mixer_keys, LON, axis=0, tiled=True),
        lax.all_gather(mixer_values, LON, axis=0, tiled=True),
        lax.all_gather(mixer_output, LON, axis=1, tiled=True),
        lax.all_gather(attention_in, LON, axis=1, tiled=True),
        lax.all_gather(attention_out, LON, axis=1, tiled=True),
        lax.all_gather(expand_weight, LON, axis=0, tiled=True),
        lax.all_gather(expand_bias, LON, axis=1, tiled=True),
        lax.all_gather(reduce_weight, LON, axis=1, tiled=True),
        lax.all_gather(output_weight, LON, axis=0, tiled=True),
    )
    (
        head_query,
        key_weight,
        value_weight,
        mixer_weight,
        input_weight,
        output_proj,
        up_weight,
        up_bias,
        down_weight,
        final_weight,
    ) = sector
    row_count, slot_width = slot_crops.shape
    token_count = row_count * slot_width
    local_width = key_weight.shape[1]
    head_count = local_width // HEAD_DIM
    pair_weight = jnp.concatenate([key_weight, value_weight], axis=1)
    gain_one = gain_first.astype(jnp.float32)
    shift_one = shift_first.astype(jnp.float32)
    gain_two = gain_second.astype(jnp.float32)
    shift_two = shift_second.astype(jnp.float32)
    lat_slot = crop_lookup(crop_starts, slot_crops)
    shift_slot = crop_lookup(crop_shifts, slot_crops)
    lead_slot = crop_lookup(lead_hours, slot_crops).astype(jnp.float32).reshape(token_count) / 100.0
    share_count = token_count // lax.axis_size(HEAD)
    lead_rows = lax.dynamic_slice_in_dim(
        lead_slot, lax.axis_index(HEAD) * share_count, share_count
    )
    padded = extended(pixels, ((LON, 2),), 1)
    var_count, lat_count = (pixels.shape[0], pixels.shape[1])
    west_pairs = padded[:, :, : 2 * slot_width].reshape(var_count, lat_count, slot_width, 2)
    east_pairs = padded[:, :, 2:].reshape(var_count, lat_count, slot_width, 2)
    side_pairs = jnp.stack([west_pairs, east_pairs])
    tables = jnp.stack([side_pairs[:, :, :-1], side_pairs[:, :, 1:]], axis=3)
    lat_index = jnp.arange(lat_count - 1, dtype=jnp.int32)
    side_shift = 2 * jnp.arange(2, dtype=jnp.int32) - 1
    chosen = (lat_slot[:, :, None, None] == lat_index[None, None, None, :]) & (
        shift_slot[:, :, None, None] == side_shift[None, None, :, None]
    )
    patches = jnp.einsum(
        "rjsa,svapjx->rjvpx",
        chosen.astype(jnp.bfloat16),
        tables,
        preferred_element_type=jnp.float32,
    )
    patches = patches.astype(jnp.bfloat16).reshape(row_count, slot_width, var_count, 4)

    def mixer_forward(patch_row):
        embedded, key_rows, value_rows, weights = mixer_row(
            patch_row, full_patch, full_variable, pair_weight, head_query
        )
        return jnp.einsum(
            "shv,svhd->shd", weights, value_rows.astype(jnp.float32), precision=highest
        ).astype(jnp.bfloat16)

    mixed_low = lax.map(mixer_forward, patches).reshape(token_count, local_width)
    start_sum = reduce_rows(jnp.dot(mixed_low, mixer_weight, preferred_element_type=jnp.float32))
    start_sum = (
        start_sum
        + lead_rows[:, None] * full_lead[0].astype(jnp.float32)
        + full_lead[1].astype(jnp.float32)
    )
    first_low = spread_rows(layer_norm(start_sum, gain_one, shift_one).astype(jnp.bfloat16))
    projected = jnp.einsum(
        "td,kde->kte", first_low, input_weight, preferred_element_type=jnp.float32
    ).astype(jnp.bfloat16)
    projected = projected.reshape(3, row_count, slot_width, head_count, HEAD_DIM)
    queries, key_local, value_local = (projected[0], projected[1], projected[2])
    query_crops = slot_crops.astype(jnp.float32)
    key_tags = jnp.where(occupied == 1, slot_crops, -1).astype(jnp.bfloat16)
    key_all, value_all, tag_all = (
        lax.all_gather(key_local, LON, axis=1, tiled=True),
        lax.all_gather(value_local, LON, axis=1, tiled=True),
        lax.all_gather(key_tags, LON, axis=1, tiled=True),
    )
    block_width = min(512, key_all.shape[1])
    tag_wide = tag_all.astype(jnp.float32)
    log_totals = key_stats(queries, query_crops, key_all, tag_wide, block_width)
    attended = attend(queries, query_crops, key_all, value_all, tag_wide, log_totals, block_width)
    attended_low = attended.astype(jnp.bfloat16).reshape(token_count, local_width)
    middle = start_sum + reduce_rows(
        jnp.dot(attended_low, output_proj, preferred_element_type=jnp.float32)
    )
    second_low = spread_rows(layer_norm(middle, gain_two, shift_two).astype(jnp.bfloat16))
    hidden = jnp.dot(second_low, up_weight, preferred_element_type=jnp.float32) + up_bias.reshape(
        -1
    ).astype(jnp.float32)
    active = jax.nn.gelu(hidden, approximate=False).astype(jnp.bfloat16)
    final_sum = middle + reduce_rows(
        jnp.dot(active, down_weight, preferred_element_type=jnp.float32)
    )
    final_low = spread_rows(final_sum.astype(jnp.bfloat16))
    keep_mask = occupied.reshape(token_count, 1)
    predicted = (
        jnp.dot(final_low, final_weight, preferred_element_type=jnp.float32)
        * keep_mask.astype(jnp.float32)
    ).astype(jnp.bfloat16)
    predicted = predicted.reshape(row_count, slot_width, -1)
    masked_grad = (cotangent * occupied[:, :, None].astype(jnp.bfloat16)).reshape(token_count, -1)
    grad_final_weight = outer_sum(final_low, masked_grad)
    part_top = jnp.einsum(
        "to,do->td", masked_grad, final_weight, preferred_element_type=jnp.float32
    )
    final_grad = reduce_rows(part_top)
    final_grad_low = spread_rows(final_grad.astype(jnp.bfloat16))
    grad_down = outer_sum(active, final_grad_low)
    active_grad = jnp.einsum(
        "td,fd->tf", final_grad_low, down_weight, preferred_element_type=jnp.float32
    )
    _, gelu_back = jax.vjp(partial(jax.nn.gelu, approximate=False), hidden)
    hidden_grad = gelu_back(active_grad)[0].astype(jnp.bfloat16)
    grad_up = outer_sum(second_low, hidden_grad)
    grad_up_bias = jnp.sum(hidden_grad.astype(jnp.float32), axis=0).reshape(up_bias.shape)
    second_grad = jnp.einsum(
        "tf,df->td", hidden_grad, up_weight, preferred_element_type=jnp.float32
    )
    second_in = head_share(second_grad)
    _, second_back = jax.vjp(layer_norm, middle, gain_two, shift_two)
    part_mid, grad_gain_two, grad_shift_two = second_back(second_in)
    middle_grad = final_grad + part_mid
    middle_low = spread_rows(middle_grad.astype(jnp.bfloat16))
    grad_proj = outer_sum(attended_low, middle_low)
    out_grads = jnp.einsum(
        "td,ed->te", middle_low, output_proj, preferred_element_type=jnp.float32
    ).astype(jnp.bfloat16)
    out_grads = out_grads.reshape(row_count, slot_width, head_count, HEAD_DIM)
    deltas = jnp.transpose(jnp.sum(out_grads.astype(jnp.float32) * attended, axis=-1), (0, 2, 1))
    back_keys, back_values, back_raw = (
        lax.all_gather(key_local, LON, axis=1, tiled=True),
        lax.all_gather(value_local, LON, axis=1, tiled=True),
        lax.all_gather(key_tags, LON, axis=1, tiled=True),
    )
    back_tags = back_raw.astype(jnp.float32)
    scale = HEAD_DIM ** (-0.5)
    key_count = back_keys.shape[1] // block_width
    local_zeros = jnp.zeros(queries.shape, jnp.float32)
    whole_zeros = jnp.zeros(back_keys.shape, jnp.float32)

    def both_step(running, block_index):
        query_acc, key_acc, value_acc = running
        key_block = block_slice(back_keys, block_index, block_width, 1)
        score_delta, weights_low = score_grads(
            queries,
            query_crops,
            out_grads,
            log_totals,
            deltas,
            key_block,
            block_slice(back_values, block_index, block_width, 1),
            block_slice(back_tags, block_index, block_width, 1),
        )
        query_acc = (
            query_acc
            + jnp.einsum(
                "rhqk,rkhd->rqhd", score_delta, key_block, preferred_element_type=jnp.float32
            )
            * scale
        )
        key_piece = (
            jnp.einsum("rhqk,rqhd->rkhd", score_delta, queries, preferred_element_type=jnp.float32)
            * scale
        )
        value_piece = jnp.einsum(
            "rhqk,rqhd->rkhd", weights_low, out_grads, preferred_element_type=jnp.float32
        )
        key_acc = lax.dynamic_update_slice_in_dim(key_acc, key_piece, block_index * block_width, 1)
        value_acc = lax.dynamic_update_slice_in_dim(
            value_acc, value_piece, block_index * block_width, 1
        )
        return ((query_acc, key_acc, value_acc), None)

    (query_grad, key_part, value_part), _ = lax.scan(
        both_step, (local_zeros, whole_zeros, whole_zeros), jnp.arange(key_count)
    )
    key_grad, value_grad = (
        lax.psum_scatter(
            key_part.astype(jnp.bfloat16), LON, scatter_dimension=1, tiled=True
        ).astype(jnp.float32),
        lax.psum_scatter(
            value_part.astype(jnp.bfloat16), LON, scatter_dimension=1, tiled=True
        ).astype(jnp.float32),
    )
    stacked = (
        jnp.stack([query_grad, key_grad, value_grad])
        .astype(jnp.bfloat16)
        .reshape(3, token_count, local_width)
    )
    first_grad = jnp.einsum(
        "kte,kde->td", stacked, input_weight, preferred_element_type=jnp.float32
    )
    grad_input = jnp.einsum("td,kte->kde", first_low, stacked, preferred_element_type=jnp.float32)
    first_in = head_share(first_grad)
    _, first_back = jax.vjp(layer_norm, start_sum, gain_one, shift_one)
    part_low, grad_gain_one, grad_shift_one = first_back(first_in)
    start_grad = middle_grad + part_low
    grad_lead = jnp.stack(
        [jnp.sum(start_grad * lead_rows[:, None], axis=0), jnp.sum(start_grad, axis=0)]
    )
    start_low = spread_rows(start_grad.astype(jnp.bfloat16))
    grad_mixer = outer_sum(mixed_low, start_low)
    mixed_grad = jnp.einsum(
        "td,ed->te", start_low, mixer_weight, preferred_element_type=jnp.float32
    ).astype(jnp.bfloat16)
    mixed_grad = mixed_grad.reshape(row_count, slot_width, head_count, HEAD_DIM)
    initial = (
        jnp.zeros(full_patch.shape, jnp.float32),
        jnp.zeros(full_variable.shape, jnp.float32),
        jnp.zeros(head_query.shape, jnp.float32),
        jnp.zeros(pair_weight.shape, jnp.float32),
    )
    mixer_step = partial(
        mixer_back,
        full_patch=full_patch,
        full_variable=full_variable,
        pair_weight=pair_weight,
        head_query=head_query,
    )
    (grad_patch, grad_variable, grad_query, grad_pair), slot_grads = lax.scan(
        mixer_step, initial, (patches, mixed_grad)
    )
    slot_total = head_total(slot_grads).reshape(row_count, slot_width, var_count, 2, 2)
    table_grads = jnp.einsum(
        "rjsa,rjvpx->svapjx", chosen.astype(jnp.float32), slot_total, precision=highest
    )
    side_grads = jnp.pad(
        table_grads[:, :, :, 0], ((0, 0), (0, 0), (0, 1), (0, 0), (0, 0))
    ) + jnp.pad(table_grads[:, :, :, 1], ((0, 0), (0, 0), (1, 0), (0, 0), (0, 0)))
    west_grad = side_grads[0].reshape(var_count, lat_count, 2 * slot_width)
    east_grad = side_grads[1].reshape(var_count, lat_count, 2 * slot_width)
    padded_grad = jnp.pad(west_grad, ((0, 0), (0, 0), (0, 2))) + jnp.pad(
        east_grad, ((0, 0), (0, 0), (2, 0))
    )
    rim_values = jnp.stack([padded_grad[:, :, 0], padded_grad[:, :, -1]], axis=2)
    returned = extended(rim_values, ((LON, 2),), 1)
    pixel_grad = (
        padded_grad[:, :, 1:-1]
        + jnp.pad(returned[:, :, 0:1], ((0, 0), (0, 0), (0, 2 * slot_width - 1)))
        + jnp.pad(returned[:, :, 3:4], ((0, 0), (0, 0), (2 * slot_width - 1, 0)))
    )
    sector_out = (
        lax.psum_scatter(
            grad_query.astype(jnp.bfloat16), LON, scatter_dimension=1, tiled=True
        ).astype(jnp.float32),
        lax.psum_scatter(
            grad_pair[:, :local_width].astype(jnp.bfloat16), LON, scatter_dimension=0, tiled=True
        ).astype(jnp.float32),
        lax.psum_scatter(
            grad_pair[:, local_width:].astype(jnp.bfloat16), LON, scatter_dimension=0, tiled=True
        ).astype(jnp.float32),
        lax.psum_scatter(
            grad_mixer.astype(jnp.bfloat16), LON, scatter_dimension=1, tiled=True
        ).astype(jnp.float32),
        lax.psum_scatter(
            grad_input.astype(jnp.bfloat16), LON, scatter_dimension=1, tiled=True
        ).astype(jnp.float32),
        lax.psum_scatter(
            grad_proj.astype(jnp.bfloat16), LON, scatter_dimension=1, tiled=True
        ).astype(jnp.float32),
        lax.psum_scatter(
            grad_up.astype(jnp.bfloat16), LON, scatter_dimension=0, tiled=True
        ).astype(jnp.float32),
        lax.psum_scatter(
            grad_up_bias.astype(jnp.bfloat16), LON, scatter_dimension=1, tiled=True
        ).astype(jnp.float32),
        lax.psum_scatter(
            grad_down.astype(jnp.bfloat16), LON, scatter_dimension=1, tiled=True
        ).astype(jnp.float32),
        lax.psum_scatter(
            grad_final_weight.astype(jnp.bfloat16), LON, scatter_dimension=0, tiled=True
        ).astype(jnp.float32),
    )
    shared_out = (
        lax.psum_scatter(grad_patch, (LON, HEAD), scatter_dimension=2, tiled=True),
        lax.psum_scatter(grad_variable, (LON, HEAD), scatter_dimension=1, tiled=True),
        lax.psum_scatter(grad_lead, (LON, HEAD), scatter_dimension=1, tiled=True),
        lax.psum_scatter(grad_gain_one, (LON, HEAD), scatter_dimension=0, tiled=True),
        lax.psum_scatter(grad_shift_one, (LON, HEAD), scatter_dimension=0, tiled=True),
        lax.psum_scatter(grad_gain_two, (LON, HEAD), scatter_dimension=0, tiled=True),
        lax.psum_scatter(grad_shift_two, (LON, HEAD), scatter_dimension=0, tiled=True),
    )
    return (
        predicted,
        pixel_grad,
        shared_out[0],
        shared_out[1],
        sector_out[0],
        sector_out[1],
        sector_out[2],
        sector_out[3],
        shared_out[2],
        shared_out[3],
        shared_out[4],
        sector_out[4],
        sector_out[5],
        shared_out[5],
        shared_out[6],
        sector_out[6],
        sector_out[7],
        sector_out[8],
        sector_out[9],
    )


MESH = pl.DeviceIdType.MESH
BOTH = (LON, HEAD)
LON_SIZE = 16
HEAD_SIZE = 2
CHUNK = 256
low = jnp.bfloat16
wide = jnp.float32


def planned(mesh):
    return mesh.shape[LON] == LON_SIZE and mesh.shape[HEAD] == HEAD_SIZE


def dot(left, right, left_dim=1, right_dim=0):
    return lax.dot_general(
        left, right, (((left_dim,), (right_dim,)), ((), ())), preferred_element_type=wide
    )


def position():
    lon = lax.axis_index(LON)
    x = lax.axis_index(HEAD)
    z = lax.div(lon, 4)
    y = lax.rem(lax.div(lon, 2), 2)
    c = lax.rem(lon, 2)
    return x, z, y, c


def partners(x, z, y, c):
    here = z * 4 + y * 2 + c
    across = {
        "x": (here, 1 - x),
        "y": (z * 4 + (1 - y) * 2 + c, x),
        "c": (z * 4 + y * 2 + 1 - c, x),
    }
    line = [(lax.rem(z + step, 4) * 4 + y * 2 + c, x) for step in (1, 2, 3)]
    return across, line


def sector_of(z, y, c, x, part, side):
    return (y * 2 + c) * 4 + x * 2 + part, side


def block_of(z, y, row):
    return row * 4 + z, y


def meet(peers, others=(), own=None):
    barrier = pltpu.get_barrier_semaphore()
    for device in peers:
        pl.semaphore_signal(barrier, inc=1, device_id=device, device_id_type=MESH)
    for device in others:

        @pl.when(jnp.logical_not(same(device, own)))
        def _():
            pl.semaphore_signal(barrier, inc=1, device_id=device, device_id_type=MESH)

    expected = len(peers)
    for device in others:
        expected = expected + 1 - same(device, own).astype(jnp.int32)
    pl.semaphore_wait(barrier, expected)


def same(device, own):
    return jnp.logical_and(device[0] == own[0], device[1] == own[1])


def post(source, target, send_sem, recv_sem, device, own):
    here = same(device, own)

    @pl.when(here)
    def _():
        pltpu.make_async_copy(source, target, recv_sem).start()

    @pl.when(jnp.logical_not(here))
    def _():
        remote(source, target, send_sem, recv_sem, device).start()


def settle(source, target, send_sem, recv_sem, device, own):
    @pl.when(jnp.logical_not(same(device, own)))
    def _():
        remote(source, target, send_sem, recv_sem, device).wait_send()


def remote(source, target, send_sem, recv_sem, device):
    return pltpu.make_async_remote_copy(
        src_ref=source,
        dst_ref=target,
        send_sem=send_sem,
        recv_sem=recv_sem,
        device_id=device,
        device_id_type=MESH,
    )


def gatherer(views, sems):
    own_sem, line_send, line_recv, hop_send, hop_recv = sems
    x, z, y, c = position()
    across, line = partners(x, z, y, c)

    def keep(number):
        source, target, span, _ = views(number)
        return pltpu.make_async_copy(source, target.at[x, z, y, c, span], own_sem.at[number])

    def along(number, d):
        source, target, span, _ = views(number)
        return remote(
            source,
            target.at[x, z, y, c, span],
            line_send.at[number, d],
            line_recv.at[number, d],
            line[d],
        )

    def hop(number, k):
        _, target, span, color = views(number)
        if k == 0:
            part, axis = target.at[x, :, y, c, span], "yx"[color]
        elif k == 1 and color == 0:
            part, axis = target.at[x, :, :, c, span], "x"
        elif k == 1:
            part, axis = target.at[:, :, y, c, span], "y"
        else:
            part, axis = target.at[:, :, :, c, span], "c"
        return remote(
            part, part, hop_send.at[number, k], hop_recv.at[number, k], across[axis]
        )

    def begin(number):
        keep(number).start()
        for d in range(3):
            along(number, d).start()

    def spread(number):
        keep(number).wait()
        for d in range(3):
            along(number, d).wait_recv()
        hop(number, 0).start()

    def widen(number):
        hop(number, 0).wait_recv()
        hop(number, 1).start()

    def pair_up(number):
        hop(number, 1).wait_recv()
        hop(number, 2).start()

    def close(number):
        hop(number, 2).wait_recv()

    def finish(number):
        for k in range(3):
            along(number, k).wait_send()
            hop(number, k).wait_send()

    return (begin, spread, widen, pair_up, close), finish


def reduce_kernel(chunks, count, *refs):
    ins, refs = refs[:count], refs[count:]
    value_in, key_weight, value_weight, input_weight, back_weight, refs = refs[:5] + (refs[5:],)
    lat_ref, shift_ref, refs = refs[:2] + (refs[2:],)
    patch_ref, prob_ref, score_table, value_table, key_table, mixed_ref, refs = refs[:6] + (
        refs[6:],
    )
    full_ref, query_ref, second_ref, rest_ref, bias_ref, refs = refs[:5] + (refs[5:],)
    stacked_ref, low_ref, start_ref, middle_ref, vector_ref, lead_ref, refs = refs[:6] + (refs[6:],)
    out, value_out, pixel_out, refs = refs[:3] + (refs[3:],)
    buffers, sems, refs = refs[:6], refs[6:13], refs[13:]
    grad_out, field, edge, west_edge, east_edge, refs = refs[:5] + (refs[5:],)
    value_send, value_recv, grad_send, grad_recv, edge_send, edge_recv, refs = refs[:6] + (
        refs[6:],
    )
    grad_in, pooled_ref, count_ref, patch_grad, weight_a, weight_b, key_low, query_grad = refs[:8]
    input_ref, mixer_ref, values_ref, tail_ref, load_sem, first_ref, mixed_grad, turned, total_ref = (
        refs[8:]
    )
    ins = ins + (input_ref, mixer_ref, values_ref, tail_ref)
    x, z, y, c = position()
    across, line = partners(x, z, y, c)
    lon = z * 4 + y * 2 + c
    own = (lon, x)
    east, west = (lax.rem(lon + 1, 16), x), (lax.rem(lon + 15, 16), x)
    sources = [block_of(z, y, row) for row in range(4)]
    meet(list(across.values()) + line + [east, west], sources, own)
    letters = []
    for part in range(2):
        for side in range(2):
            device = sector_of(z, y, c, x, part, side)
            at = 2 * part + side
            letters.append(
                (grad_in.at[part], grad_out.at[z], grad_send.at[at], grad_recv.at[z])
                + (device, own)
            )
            letters.append(
                (value_in.at[side, part], value_out.at[z], value_send.at[at], value_recv.at[z])
                + (device, own)
            )
    for letter in letters[1::2]:
        post(*letter)
    total = len(chunks)
    weights = (weight_a, weight_b)
    queue = [input_weight.at[0], input_weight.at[1], input_weight.at[2], back_weight]
    queue += [key_weight, value_weight]

    def load(number):
        return pltpu.make_async_copy(queue[number], weights[number % 2], load_sem.at[number % 2])

    load(0).start()
    load(1).start()
    half_width = weight_a.shape[-1]

    def input_grads(kind):
        if kind == 0:
            turned[...] = low_ref[...].T
            total_ref[...] = jnp.zeros_like(total_ref)
        load(kind).wait()
        pairs = half_width // stacked_ref.shape[-1]
        for side in range(2):
            piece = jnp.concatenate(
                [stacked_ref[side * pairs + pair, kind] for pair in range(pairs)], axis=1
            )
            total_ref[...] += dot(piece, weights[kind % 2][side], 1, 1)
            grads = dot(turned[...], piece).astype(low)
            input_ref[2 * kind + side] = grads.reshape(input_ref.shape[1:])
        load(kind + 2).start()

    def start_grads():
        part, grad_gain, grad_shift = norm_back(start_ref[...], vector_ref[2:3], total_ref[...])
        result = middle_ref[...] + part
        first_ref[0:1] = jnp.sum(result * lead_ref[...], axis=0, keepdims=True)
        first_ref[1:2] = jnp.sum(result, axis=0, keepdims=True)
        first_ref[2:3] = grad_gain
        first_ref[3:4] = grad_shift
        result_low = result.astype(low)
        turned[...] = result_low.T
        load(3).wait()
        for side in range(2):
            span = slice(side * half_width, (side + 1) * half_width)
            grads = dot(turned[...], mixed_ref[span, :], 1, 1).astype(low)
            mixer_ref[side] = grads.reshape(mixer_ref.shape[1:])
            mixed_grad[span, :] = dot(result_low, weight_b[side]).astype(low).T
        load(5).start()
    head_total, var_total, tokens = prob_ref.shape
    padded = patch_ref.shape[0]
    scale = HEAD_DIM ** (-0.5)

    def halves_of(values):
        upper = values.astype(low)
        return upper, (values - upper.astype(wide)).astype(low)

    def heads(first):
        mask = diagonal(var_total, padded)
        if first == 0:
            patch_grad[...] = jnp.zeros_like(patch_grad)
            query_grad[...] = jnp.zeros_like(query_grad)

        def head_step(h, carry):
            span = pl.ds(pl.multiple_of(h * HEAD_DIM, HEAD_DIM), HEAD_DIM)
            grads = mixed_grad[span, :]
            prob = prob_ref[h]
            back = dot(value_table[span, :], grads, 0, 0)
            pieces = [
                patch_ref[k * var_total : (k + 1) * var_total, :].astype(wide) for k in range(5)
            ]
            backs = [back[k * var_total : (k + 1) * var_total, :] for k in range(5)]
            prob_grad = pieces[0] * backs[0]
            for k in range(1, 5):
                prob_grad = prob_grad + pieces[k] * backs[k]
            mean = jnp.sum(prob * prob_grad, axis=0, keepdims=True)
            upper, lower = halves_of(prob * (prob_grad - mean))
            spread = jnp.where(mask, score_table[pl.ds(h, 1), :], 0.0).astype(low)
            patch_grad[...] += dot(spread, upper, 0, 0)
            for k in range(4):
                patch_grad[k * var_total : (k + 1) * var_total, :] += prob * backs[k]
            patch = patch_ref[...]
            counts = dot(upper, patch, 1, 1) + dot(lower, patch, 1, 1)
            counts = jnp.sum(jnp.where(mask, counts, 0.0), axis=0, keepdims=True) * scale
            count_ref[pl.ds(h, 1), :] = counts
            table = key_table[span, :].astype(low)
            upper, lower = halves_of(counts)
            query_grad[pl.ds(h, 1), :HEAD_DIM] = dot(upper, table, 1, 1) + dot(lower, table, 1, 1)
            pooled = jnp.concatenate(
                [(prob * piece).astype(low) for piece in pieces]
                + [jnp.zeros((padded - 5 * var_total, tokens), low)],
                axis=0,
            )
            pooled_ref[span, :] = dot(grads, pooled, 1, 1).astype(low)
            return carry

        lax.fori_loop(first, first + head_total // 4, head_step, 0)

    def send_cut():
        taps = 4 * var_total
        for part in range(2):
            grad_in[part] = patch_grad[:taps, part * 128 : (part + 1) * 128]
        for letter in letters[0::2]:
            post(*letter)

    def value_grads():
        rows = full_ref.shape[0] // 4
        for part in range(4):
            piece = dot(full_ref[part * rows : (part + 1) * rows, :], pooled_ref[...], 1, 1)
            values_ref[part] = piece.astype(low).reshape(values_ref.shape[1:])

    def tail_grads():
        load(4).wait()
        load(5).wait()
        wide_query = jnp.concatenate([query_ref[...]] * (head_total * HEAD_DIM // 128), axis=1)
        head = lax.div(lax.broadcasted_iota(jnp.int32, wide_query.shape, 1), HEAD_DIM)
        row = lax.broadcasted_iota(jnp.int32, wide_query.shape, 0)
        wide_query = jnp.where(head == row, wide_query, 0.0).astype(low)
        count_parts = halves_of(count_ref[...])
        key_low[...] = sum(dot(wide_query, part, 0, 0) for part in count_parts).astype(low)
        spots = lax.broadcasted_iota(jnp.int32, (8, padded), 1) - 5 * var_total
        kinds = lax.broadcasted_iota(jnp.int32, (8, padded), 0)
        vectors = jnp.concatenate(
            [first_ref[...], second_ref[...], jnp.zeros((2, first_ref.shape[1]), wide)], axis=0
        )
        result = dot(vectors.astype(low), jnp.where(spots == kinds, 1.0, 0.0).astype(low), 0, 0)
        for side in range(2):
            span = slice(side * half_width, (side + 1) * half_width)
            result = result + dot(weight_a[side], key_low[span, :])
            result = result + dot(weight_b[side], pooled_ref[span, :])
        result = result.astype(low)
        sector = tail_ref.shape[-2] // 2
        for place in range(16):
            at = (place // 4, place // 2 % 2, place % 2)
            for side in range(2):
                first = (2 * place + side) * sector
                for half in range(2):
                    tail_ref[
                        (side,) + at + (slice(half * sector, (half + 1) * sector), slice(0, 128))
                    ] = result[first : first + sector, half * 128 : (half + 1) * 128]

    def rest_grads():
        used = rest_ref.shape[2] - 32
        head_half = head_total // 2
        model = full_ref.shape[0]
        count_parts = halves_of(count_ref[...])
        head = lax.broadcasted_iota(jnp.int32, (head_total, 128), 0)
        lane = lax.broadcasted_iota(jnp.int32, (head_total, 128), 1)
        rows = lax.broadcasted_iota(jnp.int32, (model, head_total), 0)
        columns = lax.broadcasted_iota(jnp.int32, (model, head_total), 1)
        inner = lax.rem(rows, model // 16)
        sectors = lax.div(lax.broadcasted_iota(jnp.int32, (model, 128), 0), model // 16)
        lanes_at = lax.broadcasted_iota(jnp.int32, (model, 128), 1)
        source_lane = lax.broadcasted_iota(jnp.int32, (128, 128), 0)
        target_lane = lax.broadcasted_iota(jnp.int32, (128, 128), 1)
        query_at = used + head_half + 4
        move = jnp.where(target_lane == query_at + lax.rem(source_lane, 4), 1.0, 0.0).astype(low)
        for side in range(2):
            spot = used + head - head_half * side
            inside = lax.div(head, head_half) == side
            target = jnp.where(jnp.logical_and(inside, lane == spot), 1.0, 0.0).astype(low)
            sums = sum(dot(part, target, 0, 0) for part in count_parts)
            result = rest_ref[side].astype(wide) + bias_ref[side]
            for part in halves_of(sums):
                result = result + dot(full_ref[...], part)
            chosen = jnp.logical_and(inner < head_half, columns == inner + head_half * side)
            spread = dot(jnp.where(chosen, 1.0, 0.0).astype(low), query_grad[...].astype(low))
            spread = jnp.where(lax.div(lanes_at, 4) == sectors, spread, 0.0).astype(low)
            result = result + dot(spread, move)
            tail_ref[side, :, :, :, :, 128:] = result.astype(low).reshape(
                tail_ref.shape[1:-1] + (128,)
            )

    lat_count, var_count, lanes = field.shape
    half = lanes // 2
    column_count = pixel_out.shape[2]

    def paste(row):
        pltpu.make_async_copy(grad_in.at[0], grad_out.at[row], grad_recv.at[row]).wait()
        lat = lat_ref[row : row + 1, :]
        going_west = shift_ref[row : row + 1, :] < 0
        lat_both = jnp.concatenate([lat, lat], axis=1)
        both = []
        for py in range(2):
            k = 2 * py
            grads = jnp.concatenate(
                [
                    grad_out[row, k * var_count : (k + 1) * var_count, :],
                    grad_out[row, (k + 1) * var_count : (k + 2) * var_count, :],
                ],
                axis=1,
            )
            left = jnp.where(going_west, grads, 0.0)
            both.append(jnp.concatenate([left, grads - left], axis=1))

        def body(b, carry):
            piece = jnp.where(lat_both == b, both[0], 0.0) + jnp.where(
                lat_both == b - 1, both[1], 0.0
            )
            if row == 0:
                field[b] = piece
            else:
                field[b] += piece
            return carry

        lax.fori_loop(0, lat_count, body, 0)

    def thirds(values):
        one = values.astype(low)
        rest = values - one.astype(wide)
        two = rest.astype(low)
        return one, two, (rest - two.astype(wide)).astype(low)

    def edges():
        kind = lax.broadcasted_iota(jnp.int32, (8, lanes), 0)
        wanted = columns_of((8, lanes), 1, half)
        pick = jnp.where(
            jnp.logical_or(
                jnp.logical_and(kind == 0, wanted == -1),
                jnp.logical_and(kind == 1, wanted == column_count),
            ),
            1.0,
            0.0,
        ).astype(low)
        flat = field[...].reshape(lat_count * var_count, lanes)
        one, two, three = thirds(flat)
        edge[...] = dot(pick, one, 1, 1) + dot(pick, two, 1, 1) + dot(pick, three, 1, 1)
        remote(edge, west_edge, edge_send.at[0], edge_recv.at[0], east).start()
        remote(edge, east_edge, edge_send.at[1], edge_recv.at[1], west).start()

    def pixels():
        remote(edge, west_edge, edge_send.at[0], edge_recv.at[0], east).wait()
        remote(edge, east_edge, edge_send.at[1], edge_recv.at[1], west).wait()
        wanted = columns_of((lanes, column_count), 0, half)
        column = lax.broadcasted_iota(jnp.int32, (lanes, column_count), 1)
        place = jnp.where(wanted == column, 1.0, 0.0).astype(low)
        kind = lax.broadcasted_iota(jnp.int32, (8, column_count), 0)
        column = lax.broadcasted_iota(jnp.int32, (8, column_count), 1)
        from_west = jnp.logical_and(kind == 1, column == 0)
        from_east = jnp.logical_and(kind == 0, column == column_count - 1)
        west_place = jnp.where(from_west, 1.0, 0.0).astype(low)
        east_place = jnp.where(from_east, 1.0, 0.0).astype(low)
        borders = None
        for values, target in ((west_edge[...], west_place), (east_edge[...], east_place)):
            for part in thirds(values):
                piece = dot(part, target, 0, 0)
                borders = piece if borders is None else borders + piece
        pixel_out[...] = borders.reshape(pixel_out.shape)

        def body(b, carry):
            result = pixel_out[b]
            for part in thirds(field[b]):
                result = result + dot(part, place)
            pixel_out[b] = result
            return carry

        lax.fori_loop(0, lat_count, body, 0)

    quarter = head_total // 4
    extra = {kind: partial(input_grads, kind) for kind in range(3)}
    extra[3] = start_grads
    extra.update({4 + step: partial(heads, step * quarter) for step in range(4)})
    extra.update({8: lambda: (send_cut(), value_grads()), 9: tail_grads, 10: rest_grads})
    extra.update({12 + row: partial(paste, row) for row in range(3)})
    extra.update({15: lambda: (paste(3), edges()), 18: pixels})

    def source_of(pair, color, side, core):
        index, lead, offset = chunks[2 * pair + color][side]
        source = ins[index] if lead is None else ins[index].at[lead]
        return source.at[:, :, core, :, pl.ds(offset, CHUNK)]

    begin, stage_core, stage_first, stage_second, stage_third, finish = reducer(
        source_of, buffers, sems, out
    )
    plan = ((0, begin), (2, stage_core), (4, stage_first), (6, stage_second), (8, stage_third))
    for step in range(total + 8):
        for back, stage in plan:
            if 0 <= step - back < total:
                stage((step - back) // 2, (step - back) % 2)
        if step in extra:
            extra[step]()
    for k in range(total):
        finish(k // 2, k % 2)
    for letter in letters:
        settle(*letter)
    for row in range(4):
        pltpu.make_async_copy(value_in.at[0, 0], value_out.at[row], value_recv.at[row]).wait()


def reduce_all(item, values, weights, lat_lanes, shift_lanes, mixer, rest, block, lat_count, number):
    chunks = []
    model, half = item.shape[-2:]
    views = [item.reshape((-1, 4, 2, 2, model // 16, half))]
    kinds = weights[2].shape[0]
    for index, leads in ((0, 1), (1, kinds), (2, 1)):
        for first in range(0, 2 * leads, 2):
            for offset in range(0, half, CHUNK):
                chunks.append(((index, first, offset), (index, first + 1, offset)))
    count = len(views)
    for offset in range(0, half, CHUNK):
        chunks.append(((3, None, offset), (3, None, half + offset)))
    chunks.append(((4, 0, 0), (4, 1, 0)))
    total = len(chunks)
    rows = views[0].shape[-2]
    probs = mixer[1]
    head_count, var_count, tokens = probs.shape
    padded = mixer[0].shape[0]
    lanes = 2 * lat_lanes.shape[1]
    columns = lat_lanes.shape[1]
    cut = (4, 4 * var_count, 128)
    vmem = pl.BlockSpec(memory_space=pltpu.VMEM)
    hbm = pl.BlockSpec(memory_space=pl.ANY)
    sem = pltpu.SemaphoreType.DMA
    return pl.pallas_call(
        partial(reduce_kernel, chunks, count),
        out_shape=[
            jax.ShapeDtypeStruct((rows, total * CHUNK), wide),
            jax.ShapeDtypeStruct((4,) + values.shape[2:], values.dtype),
            jax.ShapeDtypeStruct((lat_count, var_count, columns), wide),
        ],
        in_specs=[hbm] * (count + 5) + [vmem] * (2 + len(mixer) + len(rest) + len(block)),
        out_specs=[vmem, hbm, vmem],
        scratch_shapes=reducer_scratch(total, rows)
        + [
            pltpu.VMEM(cut, wide),
            pltpu.VMEM((lat_count, var_count, lanes), wide),
            pltpu.VMEM((8, lat_count * var_count), wide),
            pltpu.VMEM((8, lat_count * var_count), wide),
            pltpu.VMEM((8, lat_count * var_count), wide),
            sem((4,)),
            sem((4,)),
            sem((4,)),
            sem((4,)),
            sem((2,)),
            sem((2,)),
            pltpu.VMEM((2,) + cut[1:], wide),
            pltpu.VMEM((model, padded), low),
            pltpu.VMEM((head_count, padded), wide),
            pltpu.VMEM((padded, tokens), wide),
            pltpu.VMEM(weights[0].shape, low),
            pltpu.VMEM(weights[0].shape, low),
            pltpu.VMEM((model, padded), low),
            pltpu.VMEM((head_count, 128), wide),
            pltpu.VMEM((2 * kinds, 4, 2, 2, rows, half), low),
            pltpu.VMEM((2, 4, 2, 2, rows, half), low),
            pltpu.VMEM((4, 2, 2, rows, 2 * half), low),
            pltpu.VMEM((2, 4, 2, 2, rows, CHUNK), low),
            sem((2,)),
            pltpu.VMEM((4, model), wide),
            pltpu.VMEM((model, tokens), low),
            pltpu.VMEM((model, tokens), low),
            pltpu.VMEM((tokens, model), wide),
        ],
        compiler_params=pltpu.CompilerParams(
            collective_id=number, has_side_effects=True, vmem_limit_bytes=60 * 2**20
        ),
    )(*views, values, *weights, lat_lanes, shift_lanes, *mixer, *rest, *block)


def diagonal(var_count, columns):
    column = lax.broadcasted_iota(jnp.int32, (var_count, columns), 1)
    row = lax.broadcasted_iota(jnp.int32, (var_count, columns), 0)
    return (lax.rem(column, var_count) == row) & (column < 5 * var_count)


def head_lanes(values, h):
    lane = lax.broadcasted_iota(jnp.int32, values.shape, values.ndim - 1)
    inside = lane < HEAD_DIM if h == 0 else lane >= HEAD_DIM
    return jnp.where(inside, values, jnp.zeros_like(values))


def plane_device(z, index):
    return z * 4 + lax.div(index, 2), lax.rem(index, 2)


def plane_meet(x, z, y, c):
    barrier = pltpu.get_barrier_semaphore()
    for flip in range(1, 8):
        there_y = 1 - y if flip & 4 else y
        there_c = 1 - c if flip & 2 else c
        there_x = 1 - x if flip & 1 else x
        device = (z * 4 + there_y * 2 + there_c, there_x)
        pl.semaphore_signal(barrier, inc=1, device_id=device, device_id_type=MESH)
    return barrier


def joined(left, right):
    return (left.astype(wide) + right.astype(wide)).astype(low)


def reducer(source_of, buffers, sems, out):
    mine, other, first_a, first_b, second, third = buffers
    own_sem, core_send, core_recv, hop_send, hop_recv, line_send, line_recv = sems
    x, z, y, c = position()
    across, line = partners(x, z, y, c)

    def keeps(pair, color):
        k = 2 * pair + color
        return [
            pltpu.make_async_copy(
                source_of(pair, color, side, c), mine.at[2 * k + side], own_sem.at[k, side]
            )
            for side in range(2)
        ]

    def swaps(pair, color):
        k = 2 * pair + color
        return [
            remote(
                source_of(pair, color, side, 1 - c),
                other.at[2 * k + side],
                core_send.at[k, side],
                core_recv.at[k, side],
                across["c"],
            )
            for side in range(2)
        ]

    def hop_one(pair, color):
        k = 2 * pair + color
        if color == 0:
            source, target, axis = mine.at[2 * k + 1 - x], first_a.at[pair], "x"
        else:
            source = mine.at[pl.ds(2 * k, 2), :, 1 - y]
            target, axis = first_b.at[pair], "y"
        return remote(source, target, hop_send.at[k, 0], hop_recv.at[k, 0], across[axis])

    def hop_two(pair, color):
        k = 2 * pair + color
        if color == 0:
            source, axis = mine.at[2 * k + x, :, 1 - y], "y"
        else:
            source, axis = mine.at[2 * k + 1 - x, :, y], "x"
        return remote(source, second.at[k], hop_send.at[k, 1], hop_recv.at[k, 1], across[axis])

    def along(pair, color):
        k = 2 * pair + color
        return [
            remote(
                mine.at[2 * k + x, lax.rem(z + d + 1, 4), y],
                third.at[k, d],
                line_send.at[k, d],
                line_recv.at[k, d],
                line[d],
            )
            for d in range(3)
        ]

    def begin(pair, color):
        for copy in swaps(pair, color) + keeps(pair, color):
            copy.start()

    def stage_core(pair, color):
        k = 2 * pair + color
        for copy in keeps(pair, color):
            copy.wait()
        for copy in swaps(pair, color):
            copy.wait_recv()

        def body(step, carry):
            side, row = lax.div(step, 4), lax.rem(step, 4)
            for part in range(2):
                mine[2 * k + side, row, part] = joined(
                    mine[2 * k + side, row, part], other[2 * k + side, row, part]
                )
            return carry

        lax.fori_loop(0, 8, body, 0)
        hop_one(pair, color).start()

    def stage_first(pair, color):
        k = 2 * pair + color
        hop_one(pair, color).wait_recv()

        def body(row, carry):
            for part in range(2):
                if color == 0:
                    mine[2 * k + x, row, part] = joined(
                        mine[2 * k + x, row, part], first_a[pair, row, part]
                    )
                else:
                    mine[2 * k + part, row, y] = joined(
                        mine[2 * k + part, row, y], first_b[pair, part, row]
                    )
            return carry

        lax.fori_loop(0, 4, body, 0)
        hop_two(pair, color).start()

    def stage_second(pair, color):
        k = 2 * pair + color
        hop_two(pair, color).wait_recv()

        def body(row, carry):
            mine[2 * k + x, row, y] = joined(mine[2 * k + x, row, y], second[k, row])
            return carry

        lax.fori_loop(0, 4, body, 0)
        for copy in along(pair, color):
            copy.start()

    def stage_third(pair, color):
        k = 2 * pair + color
        for copy in along(pair, color):
            copy.wait_recv()
        result = mine[2 * k + x, z, y].astype(wide)
        for d in range(3):
            result = result + third[k, d].astype(wide)
        start = k * CHUNK
        if not isinstance(k, int):
            start = pl.multiple_of(start, CHUNK)
        out[:, pl.ds(start, CHUNK)] = result

    def finish(pair, color):
        hop_one(pair, color).wait_send()
        hop_two(pair, color).wait_send()
        for copy in swaps(pair, color) + along(pair, color):
            copy.wait_send()

    return begin, stage_core, stage_first, stage_second, stage_third, finish


def reducer_scratch(total, rows):
    sem = pltpu.SemaphoreType.DMA
    pairs = (total + 1) // 2
    return [
        pltpu.VMEM((2 * total, 4, 2, rows, CHUNK), low),
        pltpu.VMEM((2 * total, 4, 2, rows, CHUNK), low),
        pltpu.VMEM((pairs, 4, 2, rows, CHUNK), low),
        pltpu.VMEM((pairs, 2, 4, rows, CHUNK), low),
        pltpu.VMEM((total, 4, rows, CHUNK), low),
        pltpu.VMEM((total, 3, rows, CHUNK), low),
    ] + [
        sem((total, 2)),
        sem((total, 2)),
        sem((total, 2)),
        sem((total, 2)),
        sem((total, 2)),
        sem((total, 3)),
        sem((total, 3)),
    ]


def attend_back_kernel(
    joint,
    tag_ref,
    crop_ref,
    out_ref,
    total_ref,
    source,
    feed_ref,
    stacked,
    sums,
    grads,
    result,
    key_acc,
    value_acc,
    *rest
):
    buffers, sems = rest[:6], rest[6:13]
    in_own, in_send, in_recv, back_own, back_send, back_recv = rest[13:]
    x, z, y, c = position()
    across, line = partners(x, z, y, c)
    me = y * 4 + c * 2 + x
    peers, kinds, share, lanes = joint.shape
    slots = peers * share
    scale = HEAD_DIM ** (-0.5)
    each = feed_ref.shape[-1] // CHUNK

    def source_of(pair, color, side, core):
        k = 2 * pair + color
        offset = pl.multiple_of(lax.rem(k, each) * CHUNK, CHUNK)
        return feed_ref.at[lax.div(k, each), side, :, :, core, :, pl.ds(offset, CHUNK)]

    begin, stage_core, stage_first, stage_second, stage_third, finish = reducer(
        source_of, buffers, sems, sums
    )
    keep = pltpu.make_async_copy(source.at[me], grads.at[me], in_own)
    keep.start()
    barrier = plane_meet(x, z, y, c)
    for device in line:
        pl.semaphore_signal(barrier, inc=1, device_id=device, device_id_type=MESH)
    pl.semaphore_wait(barrier, peers - 1 + len(line))

    def inward(there):
        return remote(
            source.at[there],
            grads.at[me],
            in_send.at[there],
            in_recv.at[me],
            plane_device(z, there),
        )

    def outward(there, part):
        span = pl.ds(0, 1) if part == 0 else pl.ds(1, 2)
        return remote(
            result.at[there, span],
            stacked.at[me, span],
            back_send.at[there, part],
            back_recv.at[me, part],
            plane_device(z, there),
        )

    for step in range(1, peers):
        inward(lax.rem(me + step, peers)).start()
    key_acc[...] = jnp.zeros_like(key_acc)
    value_acc[...] = jnp.zeros_like(value_acc)
    pairs = feed_ref.shape[0] * each // 2

    def attention(index):
        span = pl.ds(pl.multiple_of(index * share, share), share)
        queries = joint[index, 0]
        keys = joint[:, 1].reshape(slots, lanes)
        values = joint[:, 2].reshape(slots, lanes)
        grad = grads[index]
        product = grad.astype(wide) * out_ref[span, :]
        allowed = crop_ref[span, :] == tag_ref[0:1, :]
        query_grad = None
        for h in range(2):
            query_part, grad_part = head_lanes(queries, h), head_lanes(grad, h)
            scores = jnp.where(allowed, dot(query_part, keys, 1, 1), masked_score)
            weights = jnp.exp(scores - total_ref[h, span, :])
            weight_grads = dot(grad_part, values, 1, 1)
            delta = jnp.sum(head_lanes(product, h), axis=1, keepdims=True)
            score_grads = (weights * (weight_grads - delta)).astype(low)
            weights = weights.astype(low)
            value_acc[...] += dot(grad_part, weights, 0, 0)
            key_acc[...] += dot(query_part, score_grads, 0, 0)
            part = head_lanes(dot(score_grads, keys), h)
            query_grad = part if query_grad is None else query_grad + part
        result[index, 0] = (query_grad * scale).astype(low)

    def step_body(step, carry):
        @pl.when(step < pairs)
        def _():
            begin(step, 0)
            begin(step, 1)

        for back, stage in ((1, stage_core), (2, stage_first), (3, stage_second), (4, stage_third)):

            @pl.when(jnp.logical_and(step >= back, step < pairs + back))
            def _():
                stage(step - back, 0)
                stage(step - back, 1)

        @pl.when(step < peers)
        def _():
            index = lax.rem(me + step, peers)

            @pl.when(step == 0)
            def _():
                keep.wait()

            @pl.when(step > 0)
            def _():
                pltpu.make_async_copy(
                    grads.at[index], grads.at[index], in_recv.at[index]
                ).wait()

            attention(index)

            @pl.when(step > 0)
            def _():
                outward(index, 0).start()

        @pl.when(step == peers - 1)
        def _():
            for index in range(peers):
                span = slice(index * share, (index + 1) * share)
                result[index, 1] = key_acc[:, span].T.astype(low)
                result[index, 2] = value_acc[:, span].T.astype(low)
            for other in range(1, peers):
                outward(lax.rem(me + other, peers), 1).start()
            pltpu.make_async_copy(result.at[me], stacked.at[me], back_own).start()

        return carry

    lax.fori_loop(0, pairs + 4, step_body, 0)

    def finish_body(pair, carry):
        finish(pair, 0)
        finish(pair, 1)
        return carry

    lax.fori_loop(0, pairs, finish_body, 0)
    for step in range(1, peers):
        there = lax.rem(me + step, peers)
        inward(there).wait_send()
        for part in range(2):
            outward(there, part).wait_send()
            span = pl.ds(0, 1) if part == 0 else pl.ds(1, 2)
            pltpu.make_async_copy(
                result.at[there, span], stacked.at[there, span], back_recv.at[there, part]
            ).wait()
    pltpu.make_async_copy(result.at[me], stacked.at[me], back_own).wait()


def attend_back(joint, tags, crops, outputs, totals, source, feed_grads, number):
    peers, kinds, share, lanes = joint.shape
    slots = peers * share
    sides, halves, rows, columns = feed_grads.shape
    total = sides * columns // CHUNK
    sem = pltpu.SemaphoreType.DMA
    vmem = pl.BlockSpec(memory_space=pltpu.VMEM)
    hbm = pl.BlockSpec(memory_space=pl.ANY)
    return pl.pallas_call(
        attend_back_kernel,
        out_shape=[
            jax.ShapeDtypeStruct(joint.shape, low),
            jax.ShapeDtypeStruct((rows // 16, total * CHUNK), wide),
        ],
        in_specs=[vmem] * 5 + [hbm] * 2,
        out_specs=[hbm, vmem],
        scratch_shapes=[
            pltpu.VMEM((peers, share, lanes), low),
            pltpu.VMEM(joint.shape, low),
            pltpu.VMEM((lanes, slots), wide),
            pltpu.VMEM((lanes, slots), wide),
        ]
        + reducer_scratch(total, rows // 16)
        + [
            sem,
            sem((peers,)),
            sem((peers,)),
            sem,
            sem((peers, 2)),
            sem((peers, 2)),
        ],
        compiler_params=pltpu.CompilerParams(
            collective_id=number, has_side_effects=True, vmem_limit_bytes=60 * 2**20
        ),
    )(
        joint,
        tags,
        crops,
        outputs,
        totals,
        source,
        feed_grads.reshape(sides, halves, 4, 2, 2, rows // 16, columns),
    )


def whole(array):
    rank = len(array.shape)
    return pl.BlockSpec(array.shape, lambda *_: (0,) * rank)


def norm_parts(values):
    center = values - jnp.mean(values, axis=-1, keepdims=True)
    inverse = lax.rsqrt(jnp.mean(center * center, axis=-1, keepdims=True) + epsilon)
    return center * inverse, inverse


def norm_back(values, gain, grads):
    normed, inverse = norm_parts(values)
    scaled = grads * gain
    inner = (
        scaled
        - jnp.mean(scaled, axis=-1, keepdims=True)
        - normed * jnp.mean(scaled * normed, axis=-1, keepdims=True)
    )
    return (
        inner * inverse,
        jnp.sum(grads * normed, axis=0, keepdims=True),
        jnp.sum(grads, axis=0, keepdims=True),
    )


def columns_of(shape, axis, half):
    spot = lax.broadcasted_iota(jnp.int32, shape, axis)
    side, spot = lax.div(spot, half), lax.rem(spot, half)
    slots = half // 2
    return 2 * lax.rem(spot, slots) + 2 * side + lax.div(spot, slots) - 1


def front_kernel(items, *refs):
    arrays, refs = refs[:8], refs[8:]
    grad_in, hour_ref, pixel_ref, lat_ref, shift_ref, refs = refs[:5] + (refs[5:],)
    outs, grad_out, received, refs = refs[:8], refs[8], refs[9], refs[10:]
    joint, wide_ref, total_ref, tag_ref, crop_ref, refs = refs[:5] + (refs[5:],)
    patch_ref, prob_ref, mixed_ref, value_table, key_table, score_table, refs = refs[:6] + (
        refs[6:],
    )
    full_ref, vector_ref, query_ref, start_ref, low_ref, lead_ref, keep_ref, refs = refs[:7] + (
        refs[7:],
    )
    cut_ref, misc_ref, small_ref, weight_a, weight_b, projected, sending, turned, refs = refs[
        :8
    ] + (refs[8:],)
    gather_sems, refs = refs[:5], refs[5:]
    post_send, post_recv, load_sem, own_sem, send_sem, recv_sem, out_own, refs = refs[:7] + (
        refs[7:],
    )
    out_send, out_recv, cut_in, cut_rows, field, edge, west_edge, east_edge, edge_send, edge_recv = refs
    x, z, y, c = position()
    across, line = partners(x, z, y, c)
    lon = z * 4 + y * 2 + c
    own = (lon, x)
    east, west = (lax.rem(lon + 1, 16), x), (lax.rem(lon + 15, 16), x)
    me = y * 4 + c * 2 + x
    peers, kinds, share, lanes = joint.shape
    slots = peers * share
    head_count, var_count, tokens = prob_ref.shape
    padded = patch_ref.shape[0]
    taps = 4 * var_count
    halves = 2
    half_width = weight_a.shape[-1]

    everyone = [across["x"], across["y"], across["c"]] + line
    for flip in (3, 5, 6, 7):
        there_y = 1 - y if flip & 4 else y
        there_c = 1 - c if flip & 2 else c
        there_x = 1 - x if flip & 1 else x
        everyone.append((z * 4 + there_y * 2 + there_c, there_x))
    sources = [sector_of(z, y, c, x, part, side) for part in range(2) for side in range(2)]
    meet(everyone + [east, west], sources, own)
    letters = []
    for part in range(2):
        row = 2 * x + part
        letters.append(
            (cut_in.at[part], cut_ref.at[c], post_send.at[part], post_recv.at[c])
            + (block_of(z, y, row), own)
        )
    for row in range(4):
        letters.append(
            (grad_in.at[row], grad_out.at[x, c], post_send.at[2 + row])
            + (post_recv.at[2 + 2 * x + c], block_of(z, y, row), own)
        )
    for letter in letters[2:]:
        post(*letter)
    var_total, lat_count, column_count = pixel_ref.shape
    half = lat_ref.shape[1]

    def edge_copies():
        return [
            remote(edge, west_edge, edge_send.at[0], edge_recv.at[0], east),
            remote(edge, east_edge, edge_send.at[1], edge_recv.at[1], west),
        ]

    def send_edges():
        kind = lax.broadcasted_iota(jnp.int32, (16, column_count), 0)
        column = lax.broadcasted_iota(jnp.int32, (16, column_count), 1)
        pick = jnp.where(column == kind * (column_count - 1), 1.0, 0.0).astype(low)
        flat = pixel_ref[...].reshape(var_total * lat_count, column_count)
        edge[...] = dot(pick, flat, 1, 1).astype(low)
        for copy in edge_copies():
            copy.start()

    def make_field():
        for copy in edge_copies():
            copy.wait()
        wanted = columns_of((column_count, 2 * half), 1, half)
        column = lax.broadcasted_iota(jnp.int32, (column_count, 2 * half), 0)
        select = jnp.where(wanted == column, 1.0, 0.0).astype(low)
        kind = lax.broadcasted_iota(jnp.int32, (16, 2 * half), 0)
        wanted = columns_of((16, 2 * half), 1, half)
        from_west = jnp.logical_and(kind == 1, wanted == -1)
        from_east = jnp.logical_and(kind == 0, wanted == column_count)
        flat = pixel_ref[...].reshape(var_total * lat_count, column_count)
        result = dot(flat, select)
        for values, place in ((west_edge, from_west), (east_edge, from_east)):
            result = result + dot(values[...], jnp.where(place, 1.0, 0.0).astype(low), 0, 0)
        field[...] = result.astype(low).reshape(field.shape)

    def cut_row(part):
        lat = jnp.where(x == 0, lat_ref[part : part + 1, :], lat_ref[part + 2 : part + 3, :])
        shift = jnp.where(x == 0, shift_ref[part : part + 1, :], shift_ref[part + 2 : part + 3, :])
        row = lax.broadcasted_iota(jnp.int32, (lat_count, half), 0)
        slots = half // 2

        def body(v, carry):
            values = field[v].astype(wide)
            chosen = jnp.where(shift < 0, values[:, :half], values[:, half:])
            for py in range(2):
                taken = jnp.sum(jnp.where(row == lat + py, chosen, 0.0), axis=0, keepdims=True)
                for px in range(2):
                    spot = pl.ds((2 * py + px) * var_total + v, 1)
                    cut_rows[part, spot, :] = taken[:, px * slots : (px + 1) * slots]
            return carry

        lax.fori_loop(0, var_total, body, 0)

    def send_cut():
        cut_in[...] = cut_rows[...].astype(low)
        for letter in letters[:2]:
            post(*letter)

    def views(number):
        index, lead, first, rows, color = items[number]
        source, target = arrays[index], outs[index]
        if lead is not None:
            source, target = source.at[lead], target.at[lead]
        return source.at[pl.ds(first, rows)], target, pl.ds(first, rows), color

    stages, finish = gatherer(views, gather_sems)

    def load(source, target, spot):
        return pltpu.make_async_copy(source, target, load_sem.at[spot])

    def ask_small():
        load(outs[0], misc_ref, 0).start()
        load(outs[1], small_ref, 1).start()
        load(outs[2], weight_a, 2).start()
        load(outs[3], weight_b, 3).start()

    def read_small():
        load(outs[0], misc_ref, 0).wait()
        load(outs[1], small_ref, 1).wait()
        sector = small_ref.shape[4] // 2
        for lon in range(16):
            at = (lon // 4, lon // 2 % 2, lon % 2)
            for side in range(2):
                rows = slice((2 * lon + side) * sector, (2 * lon + side + 1) * sector)
                for half in range(2):
                    full_ref[rows, half * 128 : (half + 1) * 128] = small_ref[
                        (side,) + at + (slice(half * sector, (half + 1) * sector),)
                    ]
        upper = full_ref[:, 128:]
        vector_ref[...] = upper.astype(wide).T[taps + var_count - 128 : taps + var_count - 120]
        lane = lax.broadcasted_iota(jnp.int32, upper.shape, 1)
        full_ref[:, 128:] = jnp.where(lane < taps + var_count - 128, upper.astype(wide), 0.0).astype(
            low
        )
        kind = lax.broadcasted_iota(jnp.int32, (16, 128), 0)
        across_rows = lax.broadcasted_iota(jnp.int32, (128, 128), 0)
        across_lanes = lax.broadcasted_iota(jnp.int32, (128, 128), 1)
        queries = [None, None]
        for lon in range(16):
            at = (lon // 4, lon // 2 % 2, lon % 2)
            span = slice(lon * 128, (lon + 1) * 128)
            block = misc_ref[(0,) + at + (slice(0, 16),)].astype(wide)
            tag = jnp.sum(jnp.where(kind == z, block, 0.0), axis=0, keepdims=True)
            crop = jnp.sum(jnp.where(kind == 4 + z, block, 0.0), axis=0, keepdims=True)
            tag_ref[0:1, span] = tag
            for row, target in ((crop, crop_ref), (tag, turned)):
                target[span, :] = jnp.sum(
                    jnp.where(across_rows == across_lanes, row, 0.0), axis=1, keepdims=True
                )
            for side in range(2):
                block = misc_ref[(side,) + at + (slice(0, 16),)].astype(wide)[8:16]
                queries[side] = block if lon == 0 else queries[side] + block
        query_ref[...] = jnp.concatenate(queries, axis=0)
        mine = pl.ds(pl.multiple_of(me * share, share), share)
        keep_ref[...] = jnp.where(turned[mine, :] >= 0.0, 1.0, 0.0)
        crops = crop_ref[mine, :]
        hours = jnp.zeros((tokens, 1), wide)
        for k in range(8):
            hours = hours + jnp.where(crops == float(k), hour_ref[0:1, k : k + 1], 0.0)
        lead_ref[...] = hours
        for part in range(2):
            pltpu.make_async_copy(cut_in.at[part], cut_ref.at[part], post_recv.at[part]).wait()
            patch_ref[:taps, part * 128 : (part + 1) * 128] = cut_ref[part]
        patch_ref[taps : taps + var_count, :] = jnp.ones((var_count, tokens), low)
        patch_ref[taps + var_count :, :] = jnp.zeros((padded - taps - var_count, tokens), low)

    def tables(weight, spot, table):
        load(outs[spot], weight, spot).wait()
        for side in range(halves):
            product = dot(weight[side].reshape(-1, half_width), full_ref[...], 0, 0)
            table[side * half_width : (side + 1) * half_width, :] = product.astype(table.dtype)

    def score():
        tables(weight_a, 2, key_table)
        wide_query = jnp.concatenate([query_ref[...]] * (head_count * HEAD_DIM // 128), axis=1)
        head = lax.div(lax.broadcasted_iota(jnp.int32, wide_query.shape, 1), HEAD_DIM)
        row = lax.broadcasted_iota(jnp.int32, wide_query.shape, 0)
        wide_query = jnp.where(head == row, wide_query, 0.0).astype(low)
        rest, result = key_table[...], None
        for _ in range(3):
            part = rest.astype(low)
            rest = rest - part.astype(wide)
            piece = dot(wide_query, part)
            result = piece if result is None else result + piece
        score_table[...] = result * HEAD_DIM ** (-0.5)

    def ask_back():
        load(outs[4], weight_a, 2).start()

    def heads(first):
        mask = diagonal(var_count, padded)

        def head_step(h, carry):
            spread = jnp.where(mask, score_table[pl.ds(h, 1), :], 0.0)
            upper = spread.astype(low)
            lower = (spread - upper.astype(wide)).astype(low)
            patch = patch_ref[...]
            scores = dot(upper, patch) + dot(lower, patch)
            raised = jnp.exp(scores - jnp.max(scores, axis=0, keepdims=True))
            prob = raised / jnp.sum(raised, axis=0, keepdims=True)
            prob_ref[h] = prob
            pooled = jnp.concatenate(
                [
                    (prob * patch_ref[k * var_count : (k + 1) * var_count, :].astype(wide)).astype(
                        low
                    )
                    for k in range(5)
                ]
                + [jnp.zeros((padded - 5 * var_count, tokens), low)],
                axis=0,
            )
            start = pl.multiple_of(h * HEAD_DIM, HEAD_DIM)
            mixed_ref[pl.ds(start, HEAD_DIM), :] = dot(
                value_table[pl.ds(start, HEAD_DIM), :], pooled
            ).astype(low)
            return carry

        lax.fori_loop(first, first + 4, head_step, 0)

    def begin_block():
        load(outs[4], weight_a, 2).wait()
        total = lead_ref[...] * vector_ref[0:1] + vector_ref[1:2]
        mixed = mixed_ref[...].T
        for side in range(halves):
            total = total + dot(
                mixed[:, side * half_width : (side + 1) * half_width],
                weight_a[side].reshape(-1, half_width),
                1,
                1,
            )
        start_ref[...] = total
        normed, _ = norm_parts(total)
        low_ref[...] = (normed * vector_ref[2:3] + vector_ref[3:4]).astype(low)

    def ask_input(kind):
        target = weight_b if kind % 2 == 0 else weight_a
        load(outs[5].at[kind], target, 3 - kind % 2).start()

    def project(kind):
        target = weight_b if kind % 2 == 0 else weight_a
        load(outs[5].at[kind], target, 3 - kind % 2).wait()
        pairs = half_width // lanes
        for side in range(halves):
            result = dot(low_ref[...], target[side].reshape(-1, half_width)).astype(low)
            if kind == 0:
                result = result * low(HEAD_DIM ** (-0.5))
            for pair in range(pairs):
                projected[side * pairs + pair, kind] = result[
                    :, pair * lanes : (pair + 1) * lanes
                ]

    def inward(step):
        there = lax.rem(me + step, peers)
        return remote(
            projected.at[there],
            joint.at[me],
            send_sem.at[there],
            recv_sem.at[me],
            plane_device(z, there),
        )

    def outward(index):
        return remote(
            sending.at[index],
            received.at[me],
            out_send.at[index],
            out_recv.at[me],
            plane_device(z, index),
        )

    def send_heads():
        pltpu.make_async_copy(projected.at[me], joint.at[me], own_sem).start()
        for step in range(1, peers):
            inward(step).start()

    def take_heads():
        pltpu.make_async_copy(projected.at[me], joint.at[me], own_sem).wait()
        for step in range(1, peers):
            there = lax.rem(me + step, peers)
            pltpu.make_async_copy(joint.at[there], joint.at[there], recv_sem.at[there]).wait()

    def attention(first, count):
        def block(step, carry):
            index = lax.rem(me + 1 + step, peers)
            span = pl.ds(pl.multiple_of(index * share, share), share)
            queries = joint[index, 0]
            keys = joint[:, 1].reshape(slots, lanes)
            values = joint[:, 2].reshape(slots, lanes)
            allowed = crop_ref[span, :] == tag_ref[0:1, :]
            result = None
            for h in range(2):
                scores = dot(head_lanes(queries, h), keys, 1, 1)
                scores = jnp.where(allowed, scores, masked_score)
                largest = jnp.max(scores, axis=1, keepdims=True)
                weights = jnp.exp(scores - largest)
                total = jnp.sum(weights, axis=1, keepdims=True)
                weights = (weights * (1.0 / total)).astype(low)
                part = head_lanes(dot(weights, values), h)
                result = part if result is None else result + part
                total_ref[h, span, :] = largest + jnp.log(total)
            wide_ref[span, :] = result
            sending[index] = result.astype(low)

            @pl.when(step < peers - 1)
            def _():
                outward(index).start()

            return carry

        lax.fori_loop(first, first + count, block, 0)

    ready = {}
    for number, item in enumerate(items):
        ready[item[:2]] = number + 8
    at = ready[(3, None)]
    extra = {0: [send_edges], 3: [make_field], 4: [partial(cut_row, 0)], 5: [partial(cut_row, 1)]}
    extra.update({6: [send_cut], at: [ask_small, read_small], at + 1: [score]})
    extra[at + 2] = [lambda: tables(weight_b, 3, value_table), ask_back]
    for quarter in range(4):
        extra.setdefault(at + 3 + quarter // 2, []).append(partial(heads, 4 * quarter))
    at = max(at + 5, ready[(5, 2)])
    extra.setdefault(at, []).extend([partial(ask_input, 0), begin_block, partial(ask_input, 1)])
    extra[at + 1] = [partial(project, 0), partial(ask_input, 2), partial(project, 1)]
    extra[at + 2] = [partial(project, 2), send_heads]
    at += 5
    extra[at] = [take_heads]
    for step in range(4):
        extra.setdefault(at + step, []).append(partial(attention, 2 * step, 2))
    total = len(items)
    for step in range(max(total + 8, max(extra) + 1)):
        for back, stage in enumerate(stages):
            if 0 <= step - 2 * back < total:
                stage(step - 2 * back)
        for work in extra.get(step, []):
            work()
    last = pltpu.make_async_copy(sending.at[me], received.at[me], out_own)
    last.start()
    for number in range(total):
        finish(number)
    for letter in letters:
        settle(*letter)
    for side in range(2):
        for part in range(2):
            pltpu.make_async_copy(
                grad_in.at[0], grad_out.at[side, part], post_recv.at[2 + 2 * side + part]
            ).wait()
    for step in range(1, peers):
        there = lax.rem(me + step, peers)
        inward(step).wait_send()
        outward(there).wait_send()
        pltpu.make_async_copy(sending.at[there], received.at[there], out_recv.at[there]).wait()
    last.wait()


def front(arrays, grads, hours, pixels, lat_lanes, shift_lanes, head_count, number):
    items = []
    for index, array in enumerate(arrays):
        for lead in range(array.shape[0]) if array.ndim == 3 else (None,):
            rows = array.shape[-2]
            if rows % 64:
                items.append((index, lead, 0, rows, 0))
                continue
            for color in range(2):
                items.append((index, lead, color * rows // 2, rows // 2, color))
    width = arrays[2].shape[1]
    model = 2 * width
    var_count, lat_count = pixels.shape[:2]
    tokens = lat_lanes.shape[1]
    cut_shape = (2, 4 * var_count, tokens // 2)
    padded = 2 * arrays[1].shape[1]
    slots = 8 * tokens
    sem = pltpu.SemaphoreType.DMA
    vmem = pl.BlockSpec(memory_space=pltpu.VMEM)
    hbm = pl.BlockSpec(memory_space=pl.ANY)
    block = (2, 4, 2, 2)

    def all_of(array):
        return array.shape[:-2] + block + array.shape[-2:]

    low_outs = [all_of(a) for a in arrays] + [(2, 2) + grads.shape[1:], (8, tokens, 128)]
    vmem_outs = [
        ((8, 3, tokens, 128), low),
        ((slots, 128), wide),
        ((2, slots, 1), wide),
        ((8, slots), wide),
        ((slots, 1), wide),
        ((padded, tokens), low),
        ((head_count, var_count, tokens), wide),
        ((model, tokens), low),
        ((model, padded), low),
        ((model, padded), wide),
        ((head_count, padded), wide),
        ((model, padded), low),
        ((8, model), wide),
        ((head_count, 128), wide),
        ((tokens, model), wide),
        ((tokens, model), low),
        ((tokens, 1), wide),
        ((tokens, 1), wide),
    ]
    result = pl.pallas_call(
        partial(front_kernel, items),
        out_shape=[jax.ShapeDtypeStruct(shape, low) for shape in low_outs]
        + [jax.ShapeDtypeStruct(shape, dtype) for shape, dtype in vmem_outs],
        in_specs=[hbm] * (len(arrays) + 1) + [vmem] * 4,
        out_specs=[hbm] * len(low_outs) + [vmem] * len(vmem_outs),
        scratch_shapes=[
            pltpu.VMEM(cut_shape, low),
            pltpu.VMEM(all_of(arrays[0]), low),
            pltpu.VMEM(all_of(arrays[1]), low),
            pltpu.VMEM(all_of(arrays[2]), low),
            pltpu.VMEM(all_of(arrays[2]), low),
            pltpu.VMEM((8, 3, tokens, 128), low),
            pltpu.VMEM((8, tokens, 128), low),
            pltpu.VMEM((slots, 1), wide),
            sem((len(items),)),
        ]
        + [sem((len(items), 3))] * 4
        + [sem((6,)), sem((6,)), sem((4,)), sem, sem((8,)), sem((8,)), sem, sem((8,)), sem((8,))]
        + [
            pltpu.VMEM(cut_shape, low),
            pltpu.VMEM(cut_shape, wide),
            pltpu.VMEM((var_count, lat_count, 2 * tokens), low),
            pltpu.VMEM((16, var_count * lat_count), low),
            pltpu.VMEM((16, var_count * lat_count), low),
            pltpu.VMEM((16, var_count * lat_count), low),
            sem((2,)),
            sem((2,)),
        ],
        compiler_params=pltpu.CompilerParams(
            collective_id=number, has_side_effects=True, vmem_limit_bytes=58 * 2**20
        ),
    )(*arrays, grads, hours, pixels, lat_lanes, shift_lanes)
    count = len(arrays)
    gathered = [
        g.reshape(a.shape[:-2] + (2, 16 * a.shape[-2], a.shape[-1]))
        for g, a in zip(result, arrays)
    ]
    return gathered, result[count:]


def feed_kernel(
    attended_ref,
    proj_ref,
    start_ref,
    vector_ref,
    up_ref,
    down_ref,
    bias_ref,
    final_ref,
    masked_ref,
    keep_ref,
    predicted_ref,
    middle_grad_ref,
    unit_ref,
    grad_feed_ref,
    grad_proj_ref,
    grad_final_ref,
    grad_bias_ref,
    grad_vector_ref,
    flat,
    middle,
    second,
    second_turned,
    active,
    slope,
    total,
    grad_low,
    grad_turned,
    grad_final,
):
    step = pl.program_id(0)
    count = active.shape[0]
    row_count, units, share, lanes = attended_ref.shape
    _, halves, _, half_width = proj_ref.shape
    tokens = row_count * share

    @pl.when(step == 0)
    def _():
        for unit in range(units):
            flat[:, unit * lanes : (unit + 1) * lanes] = attended_ref[:, unit].reshape(
                tokens, lanes
            )
        result = start_ref[...]
        for side in range(halves):
            result = result + dot(
                flat[:, side * half_width : (side + 1) * half_width], proj_ref[0, side], 1, 1
            )
        middle[...] = result
        normed, _ = norm_parts(result)
        normed = (normed * vector_ref[4:5] + vector_ref[5:6]).astype(low)
        second[...] = normed
        second_turned[...] = normed.T
        total[...] = result

    @pl.when(step < count)
    def _():
        hidden = dot(second[...], up_ref[0, 0]) + bias_ref[...]
        share_of = 0.5 * (1.0 + lax.erf(hidden * (0.5**0.5)))
        fired = (hidden * share_of).astype(low)
        active[step] = fired
        slope[step] = share_of + hidden * jnp.exp(-0.5 * hidden * hidden) * (
            0.5 / 1.2533141373155003
        )
        total[...] += dot(fired, down_ref[0, 0], 1, 1)

    @pl.when(step == count - 1)
    def _():
        final_low = total[...].astype(low)
        final_turned = final_low.T
        grads = None
        for side in range(halves):
            predicted_ref[side] = (dot(final_low, final_ref[side]) * keep_ref[...]).astype(low)
            part = dot(masked_ref[side], final_ref[side], 1, 1)
            grads = part if grads is None else grads + part
            grad_final_ref[side] = dot(final_turned, masked_ref[side]).astype(low)
        grad_final[...] = grads
        grad_low[...] = grads.astype(low)
        grad_turned[...] = grads.astype(low).T
        total[...] = jnp.zeros_like(total)

    @pl.when(step >= count)
    def _():
        block = step - count
        hidden_grad = dot(grad_low[...], down_ref[0, 0]) * slope[block]
        hidden_low = hidden_grad.astype(low)
        grad_bias_ref[...] = jnp.sum(hidden_low.astype(wide), axis=0, keepdims=True)
        total[...] += dot(hidden_low, up_ref[0, 0], 1, 1)
        grad_feed_ref[0, 0] = dot(second_turned[...], hidden_low).astype(low)
        grad_feed_ref[1, 0] = dot(grad_turned[...], active[block]).astype(low)

    @pl.when(step == 2 * count - 1)
    def _():
        part, grad_gain, grad_shift = norm_back(middle[...], vector_ref[4:5], total[...])
        result = grad_final[...] + part
        middle_grad_ref[...] = result
        grad_vector_ref[0:1] = grad_gain
        grad_vector_ref[1:2] = grad_shift
        result_low = result.astype(low)
        result_turned = result_low.T
        pairs = half_width // lanes
        for side in range(halves):
            span = slice(side * half_width, (side + 1) * half_width)
            grad_proj_ref[side] = dot(result_turned, flat[:, span]).astype(low)
            out = dot(result_low, proj_ref[0, side]).astype(low)
            for pair in range(pairs):
                unit_ref[:, side * pairs + pair] = out[
                    :, pair * lanes : (pair + 1) * lanes
                ].reshape(row_count, share, lanes)


def feed(attended, start, vectors, late, up_bias, final_weight, masked, keep):
    blocks, halves, model, block = late.shape
    half_width = block
    each = blocks // 2
    full = each * block
    tokens = start.shape[0]
    count = halves * each

    def block_of_kind(kind):
        def block_at(i):
            j = lax.rem(i, count)
            return (kind * each + lax.rem(j, each), lax.div(j, each), 0, 0)

        return pl.BlockSpec((1, 1, model, block), block_at)

    def late_block(i):
        j = lax.max(i - count, 0)
        return (0, lax.div(j, each), 0, lax.rem(j, each))

    def fixed(shape, dtype):
        rank = len(shape)
        return jax.ShapeDtypeStruct(shape, dtype), pl.BlockSpec(shape, lambda i: (0,) * rank)

    outs = [
        fixed((halves, tokens, 128), low),
        fixed((tokens, model), wide),
        fixed(attended.shape, low),
        (
            jax.ShapeDtypeStruct((2, halves, model, full), low),
            pl.BlockSpec((2, 1, model, block), late_block),
        ),
        fixed((halves, model, half_width), low),
        fixed((halves, model, 128), low),
        (
            jax.ShapeDtypeStruct((1, halves * full), wide),
            pl.BlockSpec((1, block), lambda i: (0, lax.max(i - count, 0))),
        ),
        fixed((2, model), wide),
    ]
    return pl.pallas_call(
        feed_kernel,
        grid=(2 * count,),
        out_shape=[shape for shape, _ in outs],
        in_specs=[
            whole(attended),
            pl.BlockSpec((1, halves, model, block), lambda i: (blocks - 1, 0, 0, 0)),
            whole(start),
            whole(vectors),
            block_of_kind(0),
            block_of_kind(1),
            pl.BlockSpec((1, block), lambda i: (0, lax.rem(i, count))),
            whole(final_weight),
            whole(masked),
            whole(keep),
        ],
        out_specs=[spec for _, spec in outs],
        scratch_shapes=[
            pltpu.VMEM((tokens, model), low),
            pltpu.VMEM((tokens, model), wide),
            pltpu.VMEM((tokens, model), low),
            pltpu.VMEM((model, tokens), low),
            pltpu.VMEM((count, tokens, block), low),
            pltpu.VMEM((count, tokens, block), wide),
            pltpu.VMEM((tokens, model), wide),
            pltpu.VMEM((tokens, model), low),
            pltpu.VMEM((model, tokens), low),
            pltpu.VMEM((tokens, model), wide),
        ],
        compiler_params=pltpu.CompilerParams(vmem_limit_bytes=56 * 2**20),
    )(attended, late, start, vectors, late, late, up_bias, final_weight, masked, keep)


def einsum(spec, left, right):
    return jnp.einsum(spec, left, right, preferred_element_type=wide)


def fast_local(
    pixels,
    crop_starts,
    crop_shifts,
    slot_crops,
    occupied,
    lead_hours,
    patch_weight,
    variable_embed,
    mixer_query,
    mixer_keys,
    mixer_values,
    mixer_output,
    lead_embed,
    first_gain,
    first_bias,
    attention_in,
    attention_out,
    second_gain,
    second_bias,
    expand_weight,
    expand_bias,
    reduce_weight,
    output_weight,
    cotangent,
):
    lon, head = lax.axis_index(LON), lax.axis_index(HEAD)
    row_count, slot_width = slot_crops.shape
    share = slot_width // HEAD_SIZE
    tokens = row_count * share
    var_count, lat_count, column_count = pixels.shape
    head_half, query_width = mixer_query.shape
    head_count = HEAD_SIZE * head_half
    half_width = head_half * HEAD_DIM
    out_half = output_weight.shape[1]
    slice_width = patch_weight.shape[2]
    model = slice_width * LON_SIZE * HEAD_SIZE
    block_rows = model // LON_SIZE
    taps = 4 * var_count
    pairs = half_width // 128
    scale = HEAD_DIM ** (-0.5)

    lat_lanes = jnp.tile(crop_lookup(crop_starts, slot_crops), (1, 2))
    shift_lanes = jnp.tile(crop_lookup(crop_shifts, slot_crops), (1, 2))
    masked = cotangent * occupied[:, :, None].astype(low)
    masked = jnp.pad(masked, ((0, 0), (0, 0), (0, 128 - out_half)))
    late = jnp.concatenate(
        [
            jnp.transpose(part.reshape(block_rows, -1, half_width), (1, 0, 2))
            for part in (expand_weight, reduce_weight.T, attention_out.T)
        ]
    )
    padded = 256
    small = jnp.concatenate(
        [
            jnp.transpose(patch_weight, (1, 0, 2)).reshape(taps, slice_width),
            variable_embed,
            jnp.concatenate(
                [
                    lead_embed.reshape(-1),
                    first_gain,
                    first_bias,
                    second_gain,
                    second_bias,
                    jnp.zeros(((padded - taps - var_count - 6) * slice_width,), low),
                ]
            ).reshape(-1, slice_width),
        ]
    ).T
    small = jnp.concatenate([small[:, :128], small[:, 128:]])
    tags = jnp.where(occupied == 1, slot_crops, -1).astype(low)
    lane = jnp.arange(128) % (LON_SIZE * query_width) // query_width
    spread = jnp.tile(jnp.concatenate([mixer_query, expand_bias]), (1, 128 // query_width))
    spread = jnp.where(lane == lon, spread, 0)
    misc = jnp.concatenate([tags, slot_crops.astype(low), spread])
    out_block = jnp.pad(output_weight, ((0, 0), (0, 128 - out_half)))
    my_row = lax.div(lon, LON_SIZE // row_count)
    hours = lax.dynamic_index_in_dim(lead_hours, my_row, 0).astype(wide) / 100.0
    hours = jnp.pad(hours, ((0, 0), (0, 128 - hours.shape[1])))
    gathered, made = front(
        [
            misc,
            small,
            mixer_keys,
            mixer_values,
            mixer_output.T,
            attention_in,
            out_block,
            late,
        ],
        masked,
        hours,
        pixels,
        lat_lanes,
        shift_lanes,
        head_count,
        1,
    )
    misc_all, _, key_weight, value_weight, mixer_weight, input_weight, final_weight, late = gathered
    masked, attended, joint, attended_wide, totals, tag_row, crop_column = made[:7]
    patches, probs, mixed, value_table, key_table, score_table = made[7:13]
    patch_full, vectors, query, start_sum, first_low, lead_column, keep_mask = made[13:]
    masked = masked.reshape(HEAD_SIZE, tokens, 128)
    attended = attended[None]
    query_wide, query = query, query[:, :HEAD_DIM]
    bias_rows = expand_bias.shape[0]
    up_bias = misc_all.reshape(HEAD_SIZE, LON_SIZE, -1, 128)[:, :, 2 * row_count + head_half :]
    up_bias = jnp.sum(up_bias[..., : LON_SIZE * query_width].astype(wide), axis=1)
    units = HEAD_SIZE * pairs
    (
        predicted,
        middle_grad,
        out_grads,
        grad_feed,
        grad_proj,
        grad_out,
        grad_up_bias,
        second_vectors,
    ) = feed(
        attended,
        start_sum,
        vectors,
        late,
        up_bias.reshape(1, -1),
        final_weight,
        masked,
        keep_mask,
    )
    stacked, feed_sums = attend_back(
        joint,
        tag_row,
        crop_column,
        attended_wide,
        totals,
        out_grads.reshape(units, tokens, 128),
        grad_feed,
        4,
    )
    bias_cols = expand_bias.shape[1]
    bias_block = jnp.transpose(
        grad_up_bias.reshape(HEAD_SIZE, bias_rows, LON_SIZE, bias_cols), (0, 2, 1, 3)
    )
    bias_at = out_half + head_half
    bias_block = jnp.pad(
        bias_block,
        (
            (0, 0),
            (0, 0),
            (0, block_rows - bias_rows),
            (bias_at, 128 - bias_at - bias_cols),
        ),
    ).reshape(HEAD_SIZE, model, 128)
    spot = taps + var_count
    sums, predicted, pixel_grad = reduce_all(
        grad_proj,
        predicted.reshape(HEAD_SIZE, 2, slot_width, 128),
        (key_weight, value_weight, input_weight, mixer_weight),
        lat_lanes,
        shift_lanes,
        (patches, probs, score_table, value_table, key_table, mixed),
        (patch_full, query_wide, second_vectors, grad_out, bias_block),
        (stacked, first_low, start_sum, middle_grad, vectors, lead_column),
        lat_count,
        2,
    )
    predicted = predicted[:, :, :out_half]
    full_half = expand_weight.shape[1]
    place = [0]

    def take(width):
        begin = place[0]
        place[0] = begin + width
        return sums[:, begin : begin + width]

    out_up = feed_sums[:, :full_half]
    out_down = feed_sums[:, full_half:].T
    out_proj = take(half_width).T
    out_input = jnp.stack([take(half_width) for _ in range(3)])
    out_mixer = take(half_width).T
    out_values = take(half_width)
    tail_small = take(128)
    tail_rest = take(128)
    tail_small = jnp.concatenate([tail_small[:slice_width], tail_small[slice_width:]], axis=1).T
    out_patch = jnp.transpose(tail_small[:taps].reshape(4, var_count, slice_width), (1, 0, 2))
    out_variable = tail_small[taps:spot]
    out_lead = tail_small[spot : spot + 2]
    out_final = tail_rest[:, :out_half]
    at = out_half
    my_heads = tail_rest[:, at : at + head_half]
    at += head_half
    out_bias = tail_rest[:bias_rows, at : at + bias_cols]
    at += bias_cols
    out_query = tail_rest[:head_half, at : at + query_width]
    my_query = block_slice(query, head, head_half, 0)
    out_keys = (my_heads[:, :, None] * my_query[None]).reshape(block_rows, half_width)

    pixel_grad = jnp.transpose(pixel_grad, (1, 0, 2))
    return (
        predicted,
        pixel_grad,
        out_patch,
        out_variable,
        out_query,
        out_keys,
        out_values,
        out_mixer,
        out_lead,
        tail_small[spot + 2],
        tail_small[spot + 3],
        out_input,
        out_proj,
        tail_small[spot + 4],
        tail_small[spot + 5],
        out_up,
        out_bias,
        out_down,
        out_final,
    )


def solution(mesh):
    body = fast_local if planned(mesh) else local
    placed = (
        P(None, None, LON),
        P(),
        P(),
        P(None, LON),
        P(None, LON),
        P(),
        P(None, None, (LON, HEAD)),
        P(None, (LON, HEAD)),
        P(HEAD, LON),
        P(LON, HEAD),
        P(LON, HEAD),
        P(HEAD, LON),
        P(None, (LON, HEAD)),
        P((LON, HEAD)),
        P((LON, HEAD)),
        P(None, LON, HEAD),
        P(HEAD, LON),
        P((LON, HEAD)),
        P((LON, HEAD)),
        P(LON, HEAD),
        P(HEAD, LON),
        P(HEAD, LON),
        P(LON, HEAD),
        P(None, LON, HEAD),
    )
    return jax.shard_map(
        body,
        mesh=mesh,
        in_specs=placed,
        out_specs=(
            P(None, LON, HEAD),
            P(None, None, LON),
            P(None, None, (LON, HEAD)),
            P(None, (LON, HEAD)),
            P(HEAD, LON),
            P(LON, HEAD),
            P(LON, HEAD),
            P(HEAD, LON),
            P(None, (LON, HEAD)),
            P((LON, HEAD)),
            P((LON, HEAD)),
            P(None, LON, HEAD),
            P(HEAD, LON),
            P((LON, HEAD)),
            P((LON, HEAD)),
            P(LON, HEAD),
            P(HEAD, LON),
            P(HEAD, LON),
            P(LON, HEAD),
        ),
        check_vma=False,
    )
```

```python
from functools import partial

import jax
import jax.numpy as jnp
from jax import lax
from jax.experimental import pallas as pl
from jax.experimental.pallas import tpu as pltpu
from jax.sharding import PartitionSpec as P

HEAD_DIM = 64
LON, HEAD = "lon", "head"


epsilon = 1e-05
masked_score = -1e30
highest = lax.Precision.HIGHEST


def extended(array, sides, width):
    for axis, dim in sides:
        count, length = (lax.axis_size(axis), array.shape[dim])
        up = [(i, (i + 1) % count) for i in range(count)]
        down = [(j, i) for i, j in up]
        last = lax.slice_in_dim(array, length - width, length, axis=dim)
        leading = lax.slice_in_dim(array, 0, width, axis=dim)
        before = lax.ppermute(last, axis, up)
        after = lax.ppermute(leading, axis, down)
        array = jnp.concatenate([before, array, after], axis=dim)
    return array


def layer_norm(values, gain_vector, shift_vector):
    center = values - jnp.mean(values, axis=-1, keepdims=True)
    spread = jnp.mean(center * center, axis=-1, keepdims=True)
    return center * lax.rsqrt(spread + epsilon) * gain_vector + shift_vector


def head_total(partial_sum):
    return lax.psum(partial_sum.astype(jnp.bfloat16), HEAD).astype(jnp.float32)


def head_share(partial_sum):
    return lax.psum_scatter(
        partial_sum.astype(jnp.bfloat16), HEAD, scatter_dimension=0, tiled=True
    ).astype(jnp.float32)


def head_rows(values):
    return lax.all_gather(values, HEAD, axis=0, tiled=True)


def reduce_rows(partial_sum):
    return head_share(partial_sum)


def spread_rows(values):
    return head_rows(values)


def crop_lookup(crop_table, slot_numbers):
    numbers = jnp.arange(crop_table.shape[1], dtype=jnp.int32)
    picked = slot_numbers[:, :, None] == numbers[None, None, :]
    return jnp.sum(jnp.where(picked, crop_table[:, None, :], 0), axis=2)


def outer_sum(left_rows, right_rows):
    return jnp.einsum("ti,tj->ij", left_rows, right_rows, preferred_element_type=jnp.float32)


def block_slice(values, block_index, block_width, axis_number):
    return lax.dynamic_slice_in_dim(values, block_index * block_width, block_width, axis_number)


def block_scores(queries, query_crops, key_block, key_tags):
    scores = jnp.einsum(
        "rqhd,rkhd->rhqk", queries, key_block, preferred_element_type=jnp.float32
    ) * HEAD_DIM ** (-0.5)
    matched = query_crops[:, None, :, None] == key_tags[:, None, None, :]
    return (jnp.where(matched, scores, masked_score), matched)


def key_stats(queries, query_crops, key_rows, key_tags, block_width):
    row_count, slot_count, head_count, head_size = queries.shape

    def key_step(carried, block_index):
        largest, totals = carried
        scores, matched = block_scores(
            queries,
            query_crops,
            block_slice(key_rows, block_index, block_width, 1),
            block_slice(key_tags, block_index, block_width, 1),
        )
        raised = jnp.maximum(largest, jnp.max(scores, axis=-1))
        totals = totals * jnp.exp(largest - raised) + jnp.sum(
            jnp.where(matched, jnp.exp(scores - raised[..., None]), 0.0), axis=-1
        )
        return ((raised, totals), None)

    initial = (
        jnp.full((row_count, head_count, slot_count), masked_score, jnp.float32),
        jnp.zeros((row_count, head_count, slot_count), jnp.float32),
    )
    (largest, totals), _ = lax.scan(key_step, initial, jnp.arange(key_rows.shape[1] // block_width))
    return largest + jnp.log(totals)


def attend(queries, query_crops, key_rows, value_rows, key_tags, log_totals, block_width):

    def attend_step(running, block_index):
        scores, matched = block_scores(
            queries,
            query_crops,
            block_slice(key_rows, block_index, block_width, 1),
            block_slice(key_tags, block_index, block_width, 1),
        )
        weights = jnp.where(matched, jnp.exp(scores - log_totals[..., None]), 0.0).astype(
            jnp.bfloat16
        )
        value_block = block_slice(value_rows, block_index, block_width, 1)
        return (
            running
            + jnp.einsum(
                "rhqk,rkhd->rqhd", weights, value_block, preferred_element_type=jnp.float32
            ),
            None,
        )

    outputs, _ = lax.scan(
        attend_step,
        jnp.zeros(queries.shape, jnp.float32),
        jnp.arange(key_rows.shape[1] // block_width),
    )
    return outputs


def score_grads(
    queries, query_crops, out_grads, log_totals, deltas, key_block, value_block, key_tags
):
    scores, matched = block_scores(queries, query_crops, key_block, key_tags)
    weights = jnp.where(matched, jnp.exp(scores - log_totals[..., None]), 0.0)
    weight_grads = jnp.einsum(
        "rqhd,rkhd->rhqk", out_grads, value_block, preferred_element_type=jnp.float32
    )
    score_delta = (weights * (weight_grads - deltas[..., None])).astype(jnp.bfloat16)
    return (score_delta, weights.astype(jnp.bfloat16))


def mixer_row(patch_row, full_patch, full_variable, pair_weight, head_query):
    embedded = jnp.einsum(
        "svk,vkd->svd", patch_row, full_patch, preferred_element_type=jnp.float32
    ) + full_variable.astype(jnp.float32)
    embedded = embedded.astype(jnp.bfloat16)
    slot_count, var_count, model_width = embedded.shape
    head_count, head_size = head_query.shape
    local_width = head_count * head_size
    paired = jnp.dot(
        embedded.reshape(slot_count * var_count, model_width),
        pair_weight,
        preferred_element_type=jnp.float32,
    ).astype(jnp.bfloat16)
    key_rows = paired[:, :local_width].reshape(slot_count, var_count, head_count, head_size)
    value_rows = paired[:, local_width:].reshape(slot_count, var_count, head_count, head_size)
    scores = jnp.einsum(
        "svhd,hd->shv", key_rows, head_query, preferred_element_type=jnp.float32
    ) * HEAD_DIM ** (-0.5)
    weights = jax.nn.softmax(scores, axis=-1)
    return (embedded, key_rows, value_rows, weights)


def mixer_back(carried, inputs, full_patch, full_variable, pair_weight, head_query):
    patch_row, mixed_grad = inputs
    embedded, key_rows, value_rows, weights = mixer_row(
        patch_row, full_patch, full_variable, pair_weight, head_query
    )
    slot_count, var_count, model_width = embedded.shape
    local_width = key_rows.shape[2] * key_rows.shape[3]
    mixed_wide = mixed_grad.astype(jnp.float32)
    value_grads = jnp.einsum("shv,shd->svhd", weights, mixed_wide, precision=highest).astype(
        jnp.bfloat16
    )
    weight_grads = jnp.einsum(
        "shd,svhd->shv", mixed_wide, value_rows.astype(jnp.float32), precision=highest
    )
    score_delta = (
        weights
        * (weight_grads - jnp.sum(weights * weight_grads, axis=-1, keepdims=True))
        * HEAD_DIM ** (-0.5)
    )
    key_grads = jnp.einsum(
        "shv,hd->svhd", score_delta, head_query.astype(jnp.float32), precision=highest
    ).astype(jnp.bfloat16)
    query_grad = jnp.einsum(
        "shv,svhd->hd", score_delta, key_rows.astype(jnp.float32), precision=highest
    )
    pair_grads = jnp.concatenate(
        [
            key_grads.reshape(slot_count * var_count, local_width),
            value_grads.reshape(slot_count * var_count, local_width),
        ],
        axis=1,
    )
    embed_grad = jnp.einsum(
        "ne,de->nd", pair_grads, pair_weight, preferred_element_type=jnp.float32
    )
    pair_weight_grad = outer_sum(embedded.reshape(slot_count * var_count, model_width), pair_grads)
    embed_grad = embed_grad.reshape(slot_count, var_count, model_width)
    patch_grad = jnp.einsum(
        "svk,svd->vkd", patch_row.astype(jnp.float32), embed_grad, precision=highest
    )
    variable_grad = jnp.sum(embed_grad, axis=0)
    slot_grad = jnp.einsum(
        "svd,vkd->svk", embed_grad, full_patch.astype(jnp.float32), precision=highest
    )
    patch_acc, variable_acc, query_acc, pair_acc = carried
    return (
        (
            patch_acc + patch_grad,
            variable_acc + variable_grad,
            query_acc + query_grad,
            pair_acc + pair_weight_grad,
        ),
        slot_grad,
    )


def local(
    pixels,
    crop_starts,
    crop_shifts,
    slot_crops,
    occupied,
    lead_hours,
    patch_weight,
    variable_embed,
    mixer_query,
    mixer_keys,
    mixer_values,
    mixer_output,
    lead_embed,
    first_gain,
    first_bias,
    attention_in,
    attention_out,
    second_gain,
    second_bias,
    expand_weight,
    expand_bias,
    reduce_weight,
    output_weight,
    cotangent,
):
    shared = (
        lax.all_gather(patch_weight, (LON, HEAD), axis=2, tiled=True),
        lax.all_gather(variable_embed, (LON, HEAD), axis=1, tiled=True),
        lax.all_gather(lead_embed, (LON, HEAD), axis=1, tiled=True),
        lax.all_gather(first_gain, (LON, HEAD), axis=0, tiled=True),
        lax.all_gather(first_bias, (LON, HEAD), axis=0, tiled=True),
        lax.all_gather(second_gain, (LON, HEAD), axis=0, tiled=True),
        lax.all_gather(second_bias, (LON, HEAD), axis=0, tiled=True),
    )
    full_patch, full_variable, full_lead, gain_first, shift_first, gain_second, shift_second = (
        shared
    )
    sector = (
        lax.all_gather(mixer_query, LON, axis=1, tiled=True),
        lax.all_gather(mixer_keys, LON, axis=0, tiled=True),
        lax.all_gather(mixer_values, LON, axis=0, tiled=True),
        lax.all_gather(mixer_output, LON, axis=1, tiled=True),
        lax.all_gather(attention_in, LON, axis=1, tiled=True),
        lax.all_gather(attention_out, LON, axis=1, tiled=True),
        lax.all_gather(expand_weight, LON, axis=0, tiled=True),
        lax.all_gather(expand_bias, LON, axis=1, tiled=True),
        lax.all_gather(reduce_weight, LON, axis=1, tiled=True),
        lax.all_gather(output_weight, LON, axis=0, tiled=True),
    )
    (
        head_query,
        key_weight,
        value_weight,
        mixer_weight,
        input_weight,
        output_proj,
        up_weight,
        up_bias,
        down_weight,
        final_weight,
    ) = sector
    row_count, slot_width = slot_crops.shape
    token_count = row_count * slot_width
    local_width = key_weight.shape[1]
    head_count = local_width // HEAD_DIM
    pair_weight = jnp.concatenate([key_weight, value_weight], axis=1)
    gain_one = gain_first.astype(jnp.float32)
    shift_one = shift_first.astype(jnp.float32)
    gain_two = gain_second.astype(jnp.float32)
    shift_two = shift_second.astype(jnp.float32)
    lat_slot = crop_lookup(crop_starts, slot_crops)
    shift_slot = crop_lookup(crop_shifts, slot_crops)
    lead_slot = crop_lookup(lead_hours, slot_crops).astype(jnp.float32).reshape(token_count) / 100.0
    share_count = token_count // lax.axis_size(HEAD)
    lead_rows = lax.dynamic_slice_in_dim(
        lead_slot, lax.axis_index(HEAD) * share_count, share_count
    )
    padded = extended(pixels, ((LON, 2),), 1)
    var_count, lat_count = (pixels.shape[0], pixels.shape[1])
    west_pairs = padded[:, :, : 2 * slot_width].reshape(var_count, lat_count, slot_width, 2)
    east_pairs = padded[:, :, 2:].reshape(var_count, lat_count, slot_width, 2)
    side_pairs = jnp.stack([west_pairs, east_pairs])
    tables = jnp.stack([side_pairs[:, :, :-1], side_pairs[:, :, 1:]], axis=3)
    lat_index = jnp.arange(lat_count - 1, dtype=jnp.int32)
    side_shift = 2 * jnp.arange(2, dtype=jnp.int32) - 1
    chosen = (lat_slot[:, :, None, None] == lat_index[None, None, None, :]) & (
        shift_slot[:, :, None, None] == side_shift[None, None, :, None]
    )
    patches = jnp.einsum(
        "rjsa,svapjx->rjvpx",
        chosen.astype(jnp.bfloat16),
        tables,
        preferred_element_type=jnp.float32,
    )
    patches = patches.astype(jnp.bfloat16).reshape(row_count, slot_width, var_count, 4)

    def mixer_forward(patch_row):
        embedded, key_rows, value_rows, weights = mixer_row(
            patch_row, full_patch, full_variable, pair_weight, head_query
        )
        return jnp.einsum(
            "shv,svhd->shd", weights, value_rows.astype(jnp.float32), precision=highest
        ).astype(jnp.bfloat16)

    mixed_low = lax.map(mixer_forward, patches).reshape(token_count, local_width)
    start_sum = reduce_rows(jnp.dot(mixed_low, mixer_weight, preferred_element_type=jnp.float32))
    start_sum = (
        start_sum
        + lead_rows[:, None] * full_lead[0].astype(jnp.float32)
        + full_lead[1].astype(jnp.float32)
    )
    first_low = spread_rows(layer_norm(start_sum, gain_one, shift_one).astype(jnp.bfloat16))
    projected = jnp.einsum(
        "td,kde->kte", first_low, input_weight, preferred_element_type=jnp.float32
    ).astype(jnp.bfloat16)
    projected = projected.reshape(3, row_count, slot_width, head_count, HEAD_DIM)
    queries, key_local, value_local = (projected[0], projected[1], projected[2])
    query_crops = slot_crops.astype(jnp.float32)
    key_tags = jnp.where(occupied == 1, slot_crops, -1).astype(jnp.bfloat16)
    key_all, value_all, tag_all = (
        lax.all_gather(key_local, LON, axis=1, tiled=True),
        lax.all_gather(value_local, LON, axis=1, tiled=True),
        lax.all_gather(key_tags, LON, axis=1, tiled=True),
    )
    block_width = min(512, key_all.shape[1])
    tag_wide = tag_all.astype(jnp.float32)
    log_totals = key_stats(queries, query_crops, key_all, tag_wide, block_width)
    attended = attend(queries, query_crops, key_all, value_all, tag_wide, log_totals, block_width)
    attended_low = attended.astype(jnp.bfloat16).reshape(token_count, local_width)
    middle = start_sum + reduce_rows(
        jnp.dot(attended_low, output_proj, preferred_element_type=jnp.float32)
    )
    second_low = spread_rows(layer_norm(middle, gain_two, shift_two).astype(jnp.bfloat16))
    hidden = jnp.dot(second_low, up_weight, preferred_element_type=jnp.float32) + up_bias.reshape(
        -1
    ).astype(jnp.float32)
    active = jax.nn.gelu(hidden, approximate=False).astype(jnp.bfloat16)
    final_sum = middle + reduce_rows(
        jnp.dot(active, down_weight, preferred_element_type=jnp.float32)
    )
    final_low = spread_rows(final_sum.astype(jnp.bfloat16))
    keep_mask = occupied.reshape(token_count, 1)
    predicted = (
        jnp.dot(final_low, final_weight, preferred_element_type=jnp.float32)
        * keep_mask.astype(jnp.float32)
    ).astype(jnp.bfloat16)
    predicted = predicted.reshape(row_count, slot_width, -1)
    masked_grad = (cotangent * occupied[:, :, None].astype(jnp.bfloat16)).reshape(token_count, -1)
    grad_final_weight = outer_sum(final_low, masked_grad)
    part_top = jnp.einsum(
        "to,do->td", masked_grad, final_weight, preferred_element_type=jnp.float32
    )
    final_grad = reduce_rows(part_top)
    final_grad_low = spread_rows(final_grad.astype(jnp.bfloat16))
    grad_down = outer_sum(active, final_grad_low)
    active_grad = jnp.einsum(
        "td,fd->tf", final_grad_low, down_weight, preferred_element_type=jnp.float32
    )
    _, gelu_back = jax.vjp(partial(jax.nn.gelu, approximate=False), hidden)
    hidden_grad = gelu_back(active_grad)[0].astype(jnp.bfloat16)
    grad_up = outer_sum(second_low, hidden_grad)
    grad_up_bias = jnp.sum(hidden_grad.astype(jnp.float32), axis=0).reshape(up_bias.shape)
    second_grad = jnp.einsum(
        "tf,df->td", hidden_grad, up_weight, preferred_element_type=jnp.float32
    )
    second_in = head_share(second_grad)
    _, second_back = jax.vjp(layer_norm, middle, gain_two, shift_two)
    part_mid, grad_gain_two, grad_shift_two = second_back(second_in)
    middle_grad = final_grad + part_mid
    middle_low = spread_rows(middle_grad.astype(jnp.bfloat16))
    grad_proj = outer_sum(attended_low, middle_low)
    out_grads = jnp.einsum(
        "td,ed->te", middle_low, output_proj, preferred_element_type=jnp.float32
    ).astype(jnp.bfloat16)
    out_grads = out_grads.reshape(row_count, slot_width, head_count, HEAD_DIM)
    deltas = jnp.transpose(jnp.sum(out_grads.astype(jnp.float32) * attended, axis=-1), (0, 2, 1))
    back_keys, back_values, back_raw = (
        lax.all_gather(key_local, LON, axis=1, tiled=True),
        lax.all_gather(value_local, LON, axis=1, tiled=True),
        lax.all_gather(key_tags, LON, axis=1, tiled=True),
    )
    back_tags = back_raw.astype(jnp.float32)
    scale = HEAD_DIM ** (-0.5)
    key_count = back_keys.shape[1] // block_width
    local_zeros = jnp.zeros(queries.shape, jnp.float32)
    whole_zeros = jnp.zeros(back_keys.shape, jnp.float32)

    def both_step(running, block_index):
        query_acc, key_acc, value_acc = running
        key_block = block_slice(back_keys, block_index, block_width, 1)
        score_delta, weights_low = score_grads(
            queries,
            query_crops,
            out_grads,
            log_totals,
            deltas,
            key_block,
            block_slice(back_values, block_index, block_width, 1),
            block_slice(back_tags, block_index, block_width, 1),
        )
        query_acc = (
            query_acc
            + jnp.einsum(
                "rhqk,rkhd->rqhd", score_delta, key_block, preferred_element_type=jnp.float32
            )
            * scale
        )
        key_piece = (
            jnp.einsum("rhqk,rqhd->rkhd", score_delta, queries, preferred_element_type=jnp.float32)
            * scale
        )
        value_piece = jnp.einsum(
            "rhqk,rqhd->rkhd", weights_low, out_grads, preferred_element_type=jnp.float32
        )
        key_acc = lax.dynamic_update_slice_in_dim(key_acc, key_piece, block_index * block_width, 1)
        value_acc = lax.dynamic_update_slice_in_dim(
            value_acc, value_piece, block_index * block_width, 1
        )
        return ((query_acc, key_acc, value_acc), None)

    (query_grad, key_part, value_part), _ = lax.scan(
        both_step, (local_zeros, whole_zeros, whole_zeros), jnp.arange(key_count)
    )
    key_grad, value_grad = (
        lax.psum_scatter(
            key_part.astype(jnp.bfloat16), LON, scatter_dimension=1, tiled=True
        ).astype(jnp.float32),
        lax.psum_scatter(
            value_part.astype(jnp.bfloat16), LON, scatter_dimension=1, tiled=True
        ).astype(jnp.float32),
    )
    stacked = (
        jnp.stack([query_grad, key_grad, value_grad])
        .astype(jnp.bfloat16)
        .reshape(3, token_count, local_width)
    )
    first_grad = jnp.einsum(
        "kte,kde->td", stacked, input_weight, preferred_element_type=jnp.float32
    )
    grad_input = jnp.einsum("td,kte->kde", first_low, stacked, preferred_element_type=jnp.float32)
    first_in = head_share(first_grad)
    _, first_back = jax.vjp(layer_norm, start_sum, gain_one, shift_one)
    part_low, grad_gain_one, grad_shift_one = first_back(first_in)
    start_grad = middle_grad + part_low
    grad_lead = jnp.stack(
        [jnp.sum(start_grad * lead_rows[:, None], axis=0), jnp.sum(start_grad, axis=0)]
    )
    start_low = spread_rows(start_grad.astype(jnp.bfloat16))
    grad_mixer = outer_sum(mixed_low, start_low)
    mixed_grad = jnp.einsum(
        "td,ed->te", start_low, mixer_weight, preferred_element_type=jnp.float32
    ).astype(jnp.bfloat16)
    mixed_grad = mixed_grad.reshape(row_count, slot_width, head_count, HEAD_DIM)
    initial = (
        jnp.zeros(full_patch.shape, jnp.float32),
        jnp.zeros(full_variable.shape, jnp.float32),
        jnp.zeros(head_query.shape, jnp.float32),
        jnp.zeros(pair_weight.shape, jnp.float32),
    )
    mixer_step = partial(
        mixer_back,
        full_patch=full_patch,
        full_variable=full_variable,
        pair_weight=pair_weight,
        head_query=head_query,
    )
    (grad_patch, grad_variable, grad_query, grad_pair), slot_grads = lax.scan(
        mixer_step, initial, (patches, mixed_grad)
    )
    slot_total = head_total(slot_grads).reshape(row_count, slot_width, var_count, 2, 2)
    table_grads = jnp.einsum(
        "rjsa,rjvpx->svapjx", chosen.astype(jnp.float32), slot_total, precision=highest
    )
    side_grads = jnp.pad(
        table_grads[:, :, :, 0], ((0, 0), (0, 0), (0, 1), (0, 0), (0, 0))
    ) + jnp.pad(table_grads[:, :, :, 1], ((0, 0), (0, 0), (1, 0), (0, 0), (0, 0)))
    west_grad = side_grads[0].reshape(var_count, lat_count, 2 * slot_width)
    east_grad = side_grads[1].reshape(var_count, lat_count, 2 * slot_width)
    padded_grad = jnp.pad(west_grad, ((0, 0), (0, 0), (0, 2))) + jnp.pad(
        east_grad, ((0, 0), (0, 0), (2, 0))
    )
    rim_values = jnp.stack([padded_grad[:, :, 0], padded_grad[:, :, -1]], axis=2)
    returned = extended(rim_values, ((LON, 2),), 1)
    pixel_grad = (
        padded_grad[:, :, 1:-1]
        + jnp.pad(returned[:, :, 0:1], ((0, 0), (0, 0), (0, 2 * slot_width - 1)))
        + jnp.pad(returned[:, :, 3:4], ((0, 0), (0, 0), (2 * slot_width - 1, 0)))
    )
    sector_out = (
        lax.psum_scatter(
            grad_query.astype(jnp.bfloat16), LON, scatter_dimension=1, tiled=True
        ).astype(jnp.float32),
        lax.psum_scatter(
            grad_pair[:, :local_width].astype(jnp.bfloat16), LON, scatter_dimension=0, tiled=True
        ).astype(jnp.float32),
        lax.psum_scatter(
            grad_pair[:, local_width:].astype(jnp.bfloat16), LON, scatter_dimension=0, tiled=True
        ).astype(jnp.float32),
        lax.psum_scatter(
            grad_mixer.astype(jnp.bfloat16), LON, scatter_dimension=1, tiled=True
        ).astype(jnp.float32),
        lax.psum_scatter(
            grad_input.astype(jnp.bfloat16), LON, scatter_dimension=1, tiled=True
        ).astype(jnp.float32),
        lax.psum_scatter(
            grad_proj.astype(jnp.bfloat16), LON, scatter_dimension=1, tiled=True
        ).astype(jnp.float32),
        lax.psum_scatter(
            grad_up.astype(jnp.bfloat16), LON, scatter_dimension=0, tiled=True
        ).astype(jnp.float32),
        lax.psum_scatter(
            grad_up_bias.astype(jnp.bfloat16), LON, scatter_dimension=1, tiled=True
        ).astype(jnp.float32),
        lax.psum_scatter(
            grad_down.astype(jnp.bfloat16), LON, scatter_dimension=1, tiled=True
        ).astype(jnp.float32),
        lax.psum_scatter(
            grad_final_weight.astype(jnp.bfloat16), LON, scatter_dimension=0, tiled=True
        ).astype(jnp.float32),
    )
    shared_out = (
        lax.psum_scatter(grad_patch, (LON, HEAD), scatter_dimension=2, tiled=True),
        lax.psum_scatter(grad_variable, (LON, HEAD), scatter_dimension=1, tiled=True),
        lax.psum_scatter(grad_lead, (LON, HEAD), scatter_dimension=1, tiled=True),
        lax.psum_scatter(grad_gain_one, (LON, HEAD), scatter_dimension=0, tiled=True),
        lax.psum_scatter(grad_shift_one, (LON, HEAD), scatter_dimension=0, tiled=True),
        lax.psum_scatter(grad_gain_two, (LON, HEAD), scatter_dimension=0, tiled=True),
        lax.psum_scatter(grad_shift_two, (LON, HEAD), scatter_dimension=0, tiled=True),
    )
    return (
        predicted,
        pixel_grad,
        shared_out[0],
        shared_out[1],
        sector_out[0],
        sector_out[1],
        sector_out[2],
        sector_out[3],
        shared_out[2],
        shared_out[3],
        shared_out[4],
        sector_out[4],
        sector_out[5],
        shared_out[5],
        shared_out[6],
        sector_out[6],
        sector_out[7],
        sector_out[8],
        sector_out[9],
    )


MESH = pl.DeviceIdType.MESH
BOTH = (LON, HEAD)
LON_SIZE = 16
HEAD_SIZE = 2
CHUNK = 256
LATE_PAIRS = 1
low = jnp.bfloat16
wide = jnp.float32


def planned(mesh):
    return mesh.shape[LON] == LON_SIZE and mesh.shape[HEAD] == HEAD_SIZE


def dot(left, right, left_dim=1, right_dim=0):
    return lax.dot_general(
        left, right, (((left_dim,), (right_dim,)), ((), ())), preferred_element_type=wide
    )


def position():
    lon = lax.axis_index(LON)
    x = lax.axis_index(HEAD)
    z = lax.div(lon, 4)
    y = lax.rem(lax.div(lon, 2), 2)
    c = lax.rem(lon, 2)
    return x, z, y, c


def partners(x, z, y, c):
    here = z * 4 + y * 2 + c
    across = {
        "x": (here, 1 - x),
        "y": (z * 4 + (1 - y) * 2 + c, x),
        "c": (z * 4 + y * 2 + 1 - c, x),
    }
    line = [(lax.rem(z + step, 4) * 4 + y * 2 + c, x) for step in (1, 2, 3)]
    return across, line


def sector_of(z, y, c, x, part, side):
    return (y * 2 + c) * 4 + x * 2 + part, side


def block_of(z, y, row):
    return row * 4 + z, y


def meet(peers, others=(), own=None):
    barrier = pltpu.get_barrier_semaphore()
    for device in peers:
        pl.semaphore_signal(barrier, inc=1, device_id=device, device_id_type=MESH)
    for device in others:

        @pl.when(jnp.logical_not(same(device, own)))
        def _():
            pl.semaphore_signal(barrier, inc=1, device_id=device, device_id_type=MESH)

    expected = len(peers)
    for device in others:
        expected = expected + 1 - same(device, own).astype(jnp.int32)
    pl.semaphore_wait(barrier, expected)


def same(device, own):
    return jnp.logical_and(device[0] == own[0], device[1] == own[1])


def post(source, target, send_sem, recv_sem, device, own):
    here = same(device, own)

    @pl.when(here)
    def _():
        pltpu.make_async_copy(source, target, recv_sem).start()

    @pl.when(jnp.logical_not(here))
    def _():
        remote(source, target, send_sem, recv_sem, device).start()


def settle(source, target, send_sem, recv_sem, device, own):
    @pl.when(jnp.logical_not(same(device, own)))
    def _():
        remote(source, target, send_sem, recv_sem, device).wait_send()


def remote(source, target, send_sem, recv_sem, device):
    return pltpu.make_async_remote_copy(
        src_ref=source,
        dst_ref=target,
        send_sem=send_sem,
        recv_sem=recv_sem,
        device_id=device,
        device_id_type=MESH,
    )


def gatherer(views, sems):
    own_sem, line_send, line_recv, hop_send, hop_recv = sems
    x, z, y, c = position()
    across, line = partners(x, z, y, c)

    def keep(number):
        source, target, span, _ = views(number)
        return pltpu.make_async_copy(source, target.at[x, z, y, c, span], own_sem.at[number])

    def along(number, d):
        source, target, span, _ = views(number)
        return remote(
            source,
            target.at[x, z, y, c, span],
            line_send.at[number, d],
            line_recv.at[number, d],
            line[d],
        )

    def hop(number, k):
        _, target, span, color = views(number)
        if k == 0:
            part, axis = target.at[x, :, y, c, span], "yx"[color]
        elif k == 1 and color == 0:
            part, axis = target.at[x, :, :, c, span], "x"
        elif k == 1:
            part, axis = target.at[:, :, y, c, span], "y"
        else:
            part, axis = target.at[:, :, :, c, span], "c"
        return remote(
            part, part, hop_send.at[number, k], hop_recv.at[number, k], across[axis]
        )

    def begin(number):
        keep(number).start()
        for d in range(3):
            along(number, d).start()

    def spread(number):
        keep(number).wait()
        for d in range(3):
            along(number, d).wait_recv()
        hop(number, 0).start()

    def widen(number):
        hop(number, 0).wait_recv()
        hop(number, 1).start()

    def pair_up(number):
        hop(number, 1).wait_recv()
        hop(number, 2).start()

    def close(number):
        hop(number, 2).wait_recv()

    def finish(number):
        for k in range(3):
            along(number, k).wait_send()
            hop(number, k).wait_send()

    return (begin, spread, widen, pair_up, close), finish


def reduce_kernel(chunks, count, *refs):
    ins, refs = refs[:count], refs[count:]
    value_in, key_weight, value_weight, input_weight, back_weight, refs = refs[:5] + (refs[5:],)
    lat_ref, shift_ref, refs = refs[:2] + (refs[2:],)
    patch_ref, prob_ref, score_table, value_table, key_table, mixed_ref, refs = refs[:6] + (
        refs[6:],
    )
    full_ref, query_ref, second_ref, rest_ref, bias_ref, refs = refs[:5] + (refs[5:],)
    stacked_ref, low_ref, start_ref, middle_ref, vector_ref, lead_ref, refs = refs[:6] + (refs[6:],)
    out, value_out, pixel_out, refs = refs[:3] + (refs[3:],)
    buffers, sems, refs = refs[:6], refs[6:13], refs[13:]
    grad_out, field, edge, west_edge, east_edge, refs = refs[:5] + (refs[5:],)
    value_send, value_recv, grad_send, grad_recv, edge_send, edge_recv, refs = refs[:6] + (
        refs[6:],
    )
    grad_in, pooled_ref, count_ref, patch_grad, weight_a, weight_b, key_low, query_grad = refs[:8]
    input_ref, mixer_ref, values_ref, tail_ref, load_sem, first_ref, mixed_grad, turned, total_ref = (
        refs[8:]
    )
    ins = ins + (input_ref, mixer_ref, values_ref, tail_ref)
    x, z, y, c = position()
    across, line = partners(x, z, y, c)
    lon = z * 4 + y * 2 + c
    own = (lon, x)
    east, west = (lax.rem(lon + 1, 16), x), (lax.rem(lon + 15, 16), x)
    sources = [block_of(z, y, row) for row in range(4)]
    meet(list(across.values()) + line + [east, west], sources, own)
    letters = []
    for part in range(2):
        for side in range(2):
            device = sector_of(z, y, c, x, part, side)
            at = 2 * part + side
            letters.append(
                (grad_in.at[part], grad_out.at[z], grad_send.at[at], grad_recv.at[z])
                + (device, own)
            )
            letters.append(
                (value_in.at[side, part], value_out.at[z], value_send.at[at], value_recv.at[z])
                + (device, own)
            )
    for letter in letters[1::2]:
        post(*letter)
    total = len(chunks)
    weights = (weight_a, weight_b)
    queue = [input_weight.at[0], input_weight.at[1], input_weight.at[2], back_weight]
    queue += [key_weight, value_weight]

    def load(number):
        return pltpu.make_async_copy(queue[number], weights[number % 2], load_sem.at[number % 2])

    load(0).start()
    load(1).start()
    half_width = weight_a.shape[-1]

    def input_grads(kind):
        if kind == 0:
            turned[...] = low_ref[...].T
            total_ref[...] = jnp.zeros_like(total_ref)
        load(kind).wait()
        pairs = half_width // stacked_ref.shape[-1]
        for side in range(2):
            piece = jnp.concatenate(
                [stacked_ref[side * pairs + pair, kind] for pair in range(pairs)], axis=1
            )
            total_ref[...] += dot(piece, weights[kind % 2][side], 1, 1)
            grads = dot(turned[...], piece).astype(low)
            input_ref[2 * kind + side] = grads.reshape(input_ref.shape[1:])
        load(kind + 2).start()

    def start_grads():
        part, grad_gain, grad_shift = norm_back(start_ref[...], vector_ref[2:3], total_ref[...])
        result = middle_ref[...] + part
        first_ref[0:1] = jnp.sum(result * lead_ref[...], axis=0, keepdims=True)
        first_ref[1:2] = jnp.sum(result, axis=0, keepdims=True)
        first_ref[2:3] = grad_gain
        first_ref[3:4] = grad_shift
        result_low = result.astype(low)
        turned[...] = result_low.T
        load(3).wait()
        for side in range(2):
            span = slice(side * half_width, (side + 1) * half_width)
            grads = dot(turned[...], mixed_ref[span, :], 1, 1).astype(low)
            mixer_ref[side] = grads.reshape(mixer_ref.shape[1:])
            mixed_grad[span, :] = dot(result_low, weight_b[side]).astype(low).T
        load(5).start()
    head_total, var_total, tokens = prob_ref.shape
    padded = patch_ref.shape[0]
    scale = HEAD_DIM ** (-0.5)

    def halves_of(values):
        upper = values.astype(low)
        return upper, (values - upper.astype(wide)).astype(low)

    def heads(first):
        mask = diagonal(var_total, padded)
        if first == 0:
            patch_grad[...] = jnp.zeros_like(patch_grad)
            query_grad[...] = jnp.zeros_like(query_grad)

        def head_step(h, carry):
            span = pl.ds(pl.multiple_of(h * HEAD_DIM, HEAD_DIM), HEAD_DIM)
            grads = mixed_grad[span, :]
            prob = prob_ref[h]
            back = dot(value_table[span, :], grads, 0, 0)
            pieces = [
                patch_ref[k * var_total : (k + 1) * var_total, :].astype(wide) for k in range(5)
            ]
            backs = [back[k * var_total : (k + 1) * var_total, :] for k in range(5)]
            prob_grad = pieces[0] * backs[0]
            for k in range(1, 5):
                prob_grad = prob_grad + pieces[k] * backs[k]
            mean = jnp.sum(prob * prob_grad, axis=0, keepdims=True)
            upper, lower = halves_of(prob * (prob_grad - mean))
            spread = jnp.where(mask, score_table[pl.ds(h, 1), :], 0.0).astype(low)
            patch_grad[...] += dot(spread, upper, 0, 0)
            for k in range(4):
                patch_grad[k * var_total : (k + 1) * var_total, :] += prob * backs[k]
            patch = patch_ref[...]
            counts = dot(upper, patch, 1, 1) + dot(lower, patch, 1, 1)
            counts = jnp.sum(jnp.where(mask, counts, 0.0), axis=0, keepdims=True) * scale
            count_ref[pl.ds(h, 1), :] = counts
            table = key_table[span, :].astype(low)
            upper, lower = halves_of(counts)
            query_grad[pl.ds(h, 1), :HEAD_DIM] = dot(upper, table, 1, 1) + dot(lower, table, 1, 1)
            pooled = jnp.concatenate(
                [(prob * piece).astype(low) for piece in pieces]
                + [jnp.zeros((padded - 5 * var_total, tokens), low)],
                axis=0,
            )
            pooled_ref[span, :] = dot(grads, pooled, 1, 1).astype(low)
            return carry

        lax.fori_loop(first, first + head_total // 4, head_step, 0)

    def send_cut():
        taps = 4 * var_total
        for part in range(2):
            grad_in[part] = patch_grad[:taps, part * 128 : (part + 1) * 128]
        for letter in letters[0::2]:
            post(*letter)

    def value_grads():
        rows = full_ref.shape[0] // 4
        for part in range(4):
            piece = dot(full_ref[part * rows : (part + 1) * rows, :], pooled_ref[...], 1, 1)
            values_ref[part] = piece.astype(low).reshape(values_ref.shape[1:])

    def tail_grads():
        load(4).wait()
        load(5).wait()
        wide_query = jnp.concatenate([query_ref[...]] * (head_total * HEAD_DIM // 128), axis=1)
        head = lax.div(lax.broadcasted_iota(jnp.int32, wide_query.shape, 1), HEAD_DIM)
        row = lax.broadcasted_iota(jnp.int32, wide_query.shape, 0)
        wide_query = jnp.where(head == row, wide_query, 0.0).astype(low)
        count_parts = halves_of(count_ref[...])
        key_low[...] = sum(dot(wide_query, part, 0, 0) for part in count_parts).astype(low)
        spots = lax.broadcasted_iota(jnp.int32, (8, padded), 1) - 5 * var_total
        kinds = lax.broadcasted_iota(jnp.int32, (8, padded), 0)
        vectors = jnp.concatenate(
            [first_ref[...], second_ref[...], jnp.zeros((2, first_ref.shape[1]), wide)], axis=0
        )
        result = dot(vectors.astype(low), jnp.where(spots == kinds, 1.0, 0.0).astype(low), 0, 0)
        for side in range(2):
            span = slice(side * half_width, (side + 1) * half_width)
            result = result + dot(weight_a[side], key_low[span, :])
            result = result + dot(weight_b[side], pooled_ref[span, :])
        result = result.astype(low)
        sector = tail_ref.shape[-2] // 2
        for place in range(16):
            at = (place // 4, place // 2 % 2, place % 2)
            for side in range(2):
                first = (2 * place + side) * sector
                for half in range(2):
                    tail_ref[
                        (side,) + at + (slice(half * sector, (half + 1) * sector), slice(0, 128))
                    ] = result[first : first + sector, half * 128 : (half + 1) * 128]

    def rest_grads():
        used = rest_ref.shape[2] - 32
        head_half = head_total // 2
        model = full_ref.shape[0]
        count_parts = halves_of(count_ref[...])
        head = lax.broadcasted_iota(jnp.int32, (head_total, 128), 0)
        lane = lax.broadcasted_iota(jnp.int32, (head_total, 128), 1)
        rows = lax.broadcasted_iota(jnp.int32, (model, head_total), 0)
        columns = lax.broadcasted_iota(jnp.int32, (model, head_total), 1)
        inner = lax.rem(rows, model // 16)
        sectors = lax.div(lax.broadcasted_iota(jnp.int32, (model, 128), 0), model // 16)
        lanes_at = lax.broadcasted_iota(jnp.int32, (model, 128), 1)
        source_lane = lax.broadcasted_iota(jnp.int32, (128, 128), 0)
        target_lane = lax.broadcasted_iota(jnp.int32, (128, 128), 1)
        query_at = used + head_half + 4
        move = jnp.where(target_lane == query_at + lax.rem(source_lane, 4), 1.0, 0.0).astype(low)
        for side in range(2):
            spot = used + head - head_half * side
            inside = lax.div(head, head_half) == side
            target = jnp.where(jnp.logical_and(inside, lane == spot), 1.0, 0.0).astype(low)
            sums = sum(dot(part, target, 0, 0) for part in count_parts)
            result = rest_ref[side].astype(wide) + bias_ref[side].astype(wide)
            for part in halves_of(sums):
                result = result + dot(full_ref[...], part)
            chosen = jnp.logical_and(inner < head_half, columns == inner + head_half * side)
            spread = dot(jnp.where(chosen, 1.0, 0.0).astype(low), query_grad[...].astype(low))
            spread = jnp.where(lax.div(lanes_at, 4) == sectors, spread, 0.0).astype(low)
            result = result + dot(spread, move)
            tail_ref[side, :, :, :, :, 128:] = result.astype(low).reshape(
                tail_ref.shape[1:-1] + (128,)
            )

    lat_count, var_count, lanes = field.shape
    half = lanes // 2
    column_count = pixel_out.shape[2]

    def paste(row):
        pltpu.make_async_copy(grad_in.at[0], grad_out.at[row], grad_recv.at[row]).wait()
        lat = lat_ref[row : row + 1, :]
        going_west = shift_ref[row : row + 1, :] < 0
        lat_both = jnp.concatenate([lat, lat], axis=1)
        both = []
        for py in range(2):
            k = 2 * py
            grads = jnp.concatenate(
                [
                    grad_out[row, k * var_count : (k + 1) * var_count, :],
                    grad_out[row, (k + 1) * var_count : (k + 2) * var_count, :],
                ],
                axis=1,
            )
            left = jnp.where(going_west, grads, 0.0)
            both.append(jnp.concatenate([left, grads - left], axis=1))

        def body(b, carry):
            piece = jnp.where(lat_both == b, both[0], 0.0) + jnp.where(
                lat_both == b - 1, both[1], 0.0
            )
            if row == 0:
                field[b] = piece
            else:
                field[b] += piece
            return carry

        lax.fori_loop(0, lat_count, body, 0)

    def thirds(values):
        one = values.astype(low)
        rest = values - one.astype(wide)
        two = rest.astype(low)
        return one, two, (rest - two.astype(wide)).astype(low)

    def edges():
        kind = lax.broadcasted_iota(jnp.int32, (8, lanes), 0)
        wanted = columns_of((8, lanes), 1, half)
        pick = jnp.where(
            jnp.logical_or(
                jnp.logical_and(kind == 0, wanted == -1),
                jnp.logical_and(kind == 1, wanted == column_count),
            ),
            1.0,
            0.0,
        ).astype(low)
        flat = field[...].reshape(lat_count * var_count, lanes)
        one, two, three = thirds(flat)
        edge[...] = dot(pick, one, 1, 1) + dot(pick, two, 1, 1) + dot(pick, three, 1, 1)
        remote(edge, west_edge, edge_send.at[0], edge_recv.at[0], east).start()
        remote(edge, east_edge, edge_send.at[1], edge_recv.at[1], west).start()

    def pixels():
        remote(edge, west_edge, edge_send.at[0], edge_recv.at[0], east).wait()
        remote(edge, east_edge, edge_send.at[1], edge_recv.at[1], west).wait()
        wanted = columns_of((lanes, column_count), 0, half)
        column = lax.broadcasted_iota(jnp.int32, (lanes, column_count), 1)
        place = jnp.where(wanted == column, 1.0, 0.0).astype(low)
        kind = lax.broadcasted_iota(jnp.int32, (8, column_count), 0)
        column = lax.broadcasted_iota(jnp.int32, (8, column_count), 1)
        from_west = jnp.logical_and(kind == 1, column == 0)
        from_east = jnp.logical_and(kind == 0, column == column_count - 1)
        west_place = jnp.where(from_west, 1.0, 0.0).astype(low)
        east_place = jnp.where(from_east, 1.0, 0.0).astype(low)
        borders = None
        for values, target in ((west_edge[...], west_place), (east_edge[...], east_place)):
            for part in thirds(values):
                piece = dot(part, target, 0, 0)
                borders = piece if borders is None else borders + piece
        pixel_out[...] = borders.reshape(pixel_out.shape)

        def body(b, carry):
            result = pixel_out[b]
            for part in thirds(field[b]):
                result = result + dot(part, place)
            pixel_out[b] = result
            return carry

        lax.fori_loop(0, lat_count, body, 0)

    quarter = head_total // 4
    extra = {kind: partial(input_grads, kind) for kind in range(3)}
    extra[3] = start_grads
    extra.update({4 + step: partial(heads, step * quarter) for step in range(4)})
    extra.update({8: lambda: (send_cut(), value_grads()), 9: tail_grads, 10: rest_grads})
    extra.update({12 + row: partial(paste, row) for row in range(3)})
    extra.update({15: lambda: (paste(3), edges()), 18: pixels})

    def source_of(pair, color, side, core):
        index, lead, offset = chunks[2 * pair + color][side]
        source = ins[index] if lead is None else ins[index].at[lead]
        return source.at[:, :, core, :, pl.ds(offset, CHUNK)]

    begin, stage_core, stage_first, stage_second, stage_third, finish = reducer(
        source_of, buffers, sems, out
    )
    plan = ((0, begin), (2, stage_core), (4, stage_first), (6, stage_second), (8, stage_third))
    for step in range(total + 8):
        for back, stage in plan:
            if 0 <= step - back < total:
                stage((step - back) // 2, (step - back) % 2)
        if step in extra:
            extra[step]()
    for k in range(total):
        finish(k // 2, k % 2)
    for letter in letters:
        settle(*letter)
    for row in range(4):
        pltpu.make_async_copy(value_in.at[0, 0], value_out.at[row], value_recv.at[row]).wait()


def reduce_all(feed_grads, item, values, weights, lat_lanes, shift_lanes, mixer, rest, block, lat_count, number):
    chunks = []
    model, half = item.shape[-2:]
    views = [
        part.reshape((-1, 4, 2, 2, model // 16, part.shape[-1])) for part in (feed_grads, item)
    ]
    kinds = weights[2].shape[0]
    columns = feed_grads.shape[-1]
    for offset in range(columns - 2 * LATE_PAIRS * CHUNK, columns, CHUNK):
        chunks.append(((0, 2, offset), (0, 3, offset)))
    for index, leads in ((1, 1), (2, kinds), (3, 1)):
        for first in range(0, 2 * leads, 2):
            for offset in range(0, half, CHUNK):
                chunks.append(((index, first, offset), (index, first + 1, offset)))
    count = len(views)
    for offset in range(0, half, CHUNK):
        chunks.append(((4, None, offset), (4, None, half + offset)))
    chunks.append(((5, 0, 0), (5, 1, 0)))
    total = len(chunks)
    rows = views[0].shape[-2]
    probs = mixer[1]
    head_count, var_count, tokens = probs.shape
    padded = mixer[0].shape[0]
    lanes = 2 * lat_lanes.shape[1]
    columns = lat_lanes.shape[1]
    cut = (4, 4 * var_count, 128)
    vmem = pl.BlockSpec(memory_space=pltpu.VMEM)
    hbm = pl.BlockSpec(memory_space=pl.ANY)
    sem = pltpu.SemaphoreType.DMA
    return pl.pallas_call(
        partial(reduce_kernel, chunks, count),
        out_shape=[
            jax.ShapeDtypeStruct((rows, total * CHUNK), wide),
            jax.ShapeDtypeStruct((4,) + values.shape[2:], values.dtype),
            jax.ShapeDtypeStruct((lat_count, var_count, columns), wide),
        ],
        in_specs=[hbm] * (count + 5) + [vmem] * (2 + len(mixer) + len(rest) + len(block)),
        out_specs=[vmem, hbm, vmem],
        scratch_shapes=reducer_scratch(total, rows)
        + [
            pltpu.VMEM(cut, wide),
            pltpu.VMEM((lat_count, var_count, lanes), wide),
            pltpu.VMEM((8, lat_count * var_count), wide),
            pltpu.VMEM((8, lat_count * var_count), wide),
            pltpu.VMEM((8, lat_count * var_count), wide),
            sem((4,)),
            sem((4,)),
            sem((4,)),
            sem((4,)),
            sem((2,)),
            sem((2,)),
            pltpu.VMEM((2,) + cut[1:], wide),
            pltpu.VMEM((model, padded), low),
            pltpu.VMEM((head_count, padded), wide),
            pltpu.VMEM((padded, tokens), wide),
            pltpu.VMEM(weights[0].shape, low),
            pltpu.VMEM(weights[0].shape, low),
            pltpu.VMEM((model, padded), low),
            pltpu.VMEM((head_count, 128), wide),
            pltpu.VMEM((2 * kinds, 4, 2, 2, rows, half), low),
            pltpu.VMEM((2, 4, 2, 2, rows, half), low),
            pltpu.VMEM((4, 2, 2, rows, 2 * half), low),
            pltpu.VMEM((2, 4, 2, 2, rows, CHUNK), low),
            sem((2,)),
            pltpu.VMEM((4, model), wide),
            pltpu.VMEM((model, tokens), low),
            pltpu.VMEM((model, tokens), low),
            pltpu.VMEM((tokens, model), wide),
        ],
        compiler_params=pltpu.CompilerParams(
            collective_id=number, has_side_effects=True, vmem_limit_bytes=63 * 2**20
        ),
    )(*views, values, *weights, lat_lanes, shift_lanes, *mixer, *rest, *block)


def diagonal(var_count, columns):
    column = lax.broadcasted_iota(jnp.int32, (var_count, columns), 1)
    row = lax.broadcasted_iota(jnp.int32, (var_count, columns), 0)
    return (lax.rem(column, var_count) == row) & (column < 5 * var_count)


def head_lanes(values, h):
    lane = lax.broadcasted_iota(jnp.int32, values.shape, values.ndim - 1)
    inside = lane < HEAD_DIM if h == 0 else lane >= HEAD_DIM
    return jnp.where(inside, values, jnp.zeros_like(values))


def plane_device(z, index):
    return z * 4 + lax.div(index, 2), lax.rem(index, 2)


def plane_meet(x, z, y, c):
    barrier = pltpu.get_barrier_semaphore()
    for flip in range(1, 8):
        there_y = 1 - y if flip & 4 else y
        there_c = 1 - c if flip & 2 else c
        there_x = 1 - x if flip & 1 else x
        device = (z * 4 + there_y * 2 + there_c, there_x)
        pl.semaphore_signal(barrier, inc=1, device_id=device, device_id_type=MESH)
    return barrier


def joined(left, right):
    return (left.astype(wide) + right.astype(wide)).astype(low)


def reducer(source_of, buffers, sems, out):
    mine, other, first_a, first_b, second, third = buffers
    own_sem, core_send, core_recv, hop_send, hop_recv, line_send, line_recv = sems
    x, z, y, c = position()
    across, line = partners(x, z, y, c)

    def keeps(pair, color):
        k = 2 * pair + color
        return [
            pltpu.make_async_copy(
                source_of(pair, color, side, c), mine.at[2 * k + side], own_sem.at[k, side]
            )
            for side in range(2)
        ]

    def swaps(pair, color):
        k = 2 * pair + color
        return [
            remote(
                source_of(pair, color, side, 1 - c),
                other.at[2 * k + side],
                core_send.at[k, side],
                core_recv.at[k, side],
                across["c"],
            )
            for side in range(2)
        ]

    def hop_one(pair, color):
        k = 2 * pair + color
        if color == 0:
            source, target, axis = mine.at[2 * k + 1 - x], first_a.at[pair], "x"
        else:
            source = mine.at[pl.ds(2 * k, 2), :, 1 - y]
            target, axis = first_b.at[pair], "y"
        return remote(source, target, hop_send.at[k, 0], hop_recv.at[k, 0], across[axis])

    def hop_two(pair, color):
        k = 2 * pair + color
        if color == 0:
            source, axis = mine.at[2 * k + x, :, 1 - y], "y"
        else:
            source, axis = mine.at[2 * k + 1 - x, :, y], "x"
        return remote(source, second.at[k], hop_send.at[k, 1], hop_recv.at[k, 1], across[axis])

    def along(pair, color):
        k = 2 * pair + color
        return [
            remote(
                mine.at[2 * k + x, lax.rem(z + d + 1, 4), y],
                third.at[k, d],
                line_send.at[k, d],
                line_recv.at[k, d],
                line[d],
            )
            for d in range(3)
        ]

    def begin(pair, color):
        for copy in swaps(pair, color) + keeps(pair, color):
            copy.start()

    def stage_core(pair, color):
        k = 2 * pair + color
        for copy in keeps(pair, color):
            copy.wait()
        for copy in swaps(pair, color):
            copy.wait_recv()

        def body(step, carry):
            side, row = lax.div(step, 4), lax.rem(step, 4)
            for part in range(2):
                mine[2 * k + side, row, part] = joined(
                    mine[2 * k + side, row, part], other[2 * k + side, row, part]
                )
            return carry

        lax.fori_loop(0, 8, body, 0)
        hop_one(pair, color).start()

    def stage_first(pair, color):
        k = 2 * pair + color
        hop_one(pair, color).wait_recv()

        def body(row, carry):
            for part in range(2):
                if color == 0:
                    mine[2 * k + x, row, part] = joined(
                        mine[2 * k + x, row, part], first_a[pair, row, part]
                    )
                else:
                    mine[2 * k + part, row, y] = joined(
                        mine[2 * k + part, row, y], first_b[pair, part, row]
                    )
            return carry

        lax.fori_loop(0, 4, body, 0)
        hop_two(pair, color).start()

    def stage_second(pair, color):
        k = 2 * pair + color
        hop_two(pair, color).wait_recv()

        def body(row, carry):
            mine[2 * k + x, row, y] = joined(mine[2 * k + x, row, y], second[k, row])
            return carry

        lax.fori_loop(0, 4, body, 0)
        for copy in along(pair, color):
            copy.start()

    def stage_third(pair, color):
        k = 2 * pair + color
        for copy in along(pair, color):
            copy.wait_recv()
        result = mine[2 * k + x, z, y].astype(wide)
        for d in range(3):
            result = result + third[k, d].astype(wide)
        start = k * CHUNK
        if not isinstance(k, int):
            start = pl.multiple_of(start, CHUNK)
        out[:, pl.ds(start, CHUNK)] = result

    def finish(pair, color):
        hop_one(pair, color).wait_send()
        hop_two(pair, color).wait_send()
        for copy in swaps(pair, color) + along(pair, color):
            copy.wait_send()

    return begin, stage_core, stage_first, stage_second, stage_third, finish


def reducer_scratch(total, rows):
    sem = pltpu.SemaphoreType.DMA
    pairs = (total + 1) // 2
    return [
        pltpu.VMEM((2 * total, 4, 2, rows, CHUNK), low),
        pltpu.VMEM((2 * total, 4, 2, rows, CHUNK), low),
        pltpu.VMEM((pairs, 4, 2, rows, CHUNK), low),
        pltpu.VMEM((pairs, 2, 4, rows, CHUNK), low),
        pltpu.VMEM((total, 4, rows, CHUNK), low),
        pltpu.VMEM((total, 3, rows, CHUNK), low),
    ] + [
        sem((total, 2)),
        sem((total, 2)),
        sem((total, 2)),
        sem((total, 2)),
        sem((total, 2)),
        sem((total, 3)),
        sem((total, 3)),
    ]


def attend_back_kernel(
    joint,
    tag_ref,
    crop_ref,
    out_ref,
    total_ref,
    source,
    feed_ref,
    stacked,
    sums,
    grads,
    result,
    key_acc,
    value_acc,
    *rest
):
    buffers, sems = rest[:6], rest[6:13]
    in_own, in_send, in_recv, back_own, back_send, back_recv = rest[13:]
    x, z, y, c = position()
    across, line = partners(x, z, y, c)
    me = y * 4 + c * 2 + x
    peers, kinds, share, lanes = joint.shape
    slots = peers * share
    scale = HEAD_DIM ** (-0.5)
    each = feed_ref.shape[-1] // CHUNK

    def source_of(pair, color, side, core):
        k = 2 * pair + color
        offset = pl.multiple_of(lax.rem(k, each) * CHUNK, CHUNK)
        return feed_ref.at[lax.div(k, each), side, :, :, core, :, pl.ds(offset, CHUNK)]

    begin, stage_core, stage_first, stage_second, stage_third, finish = reducer(
        source_of, buffers, sems, sums
    )
    keep = pltpu.make_async_copy(source.at[me], grads.at[me], in_own)
    keep.start()
    barrier = plane_meet(x, z, y, c)
    for device in line:
        pl.semaphore_signal(barrier, inc=1, device_id=device, device_id_type=MESH)
    pl.semaphore_wait(barrier, peers - 1 + len(line))

    def inward(there):
        return remote(
            source.at[there],
            grads.at[me],
            in_send.at[there],
            in_recv.at[me],
            plane_device(z, there),
        )

    def outward(there, part):
        span = pl.ds(0, 1) if part == 0 else pl.ds(1, 2)
        return remote(
            result.at[there, span],
            stacked.at[me, span],
            back_send.at[there, part],
            back_recv.at[me, part],
            plane_device(z, there),
        )

    for step in range(1, peers):
        inward(lax.rem(me + step, peers)).start()
    key_acc[...] = jnp.zeros_like(key_acc)
    value_acc[...] = jnp.zeros_like(value_acc)
    pairs = feed_ref.shape[0] * each // 2 - LATE_PAIRS

    def attention(index):
        span = pl.ds(pl.multiple_of(index * share, share), share)
        queries = joint[index, 0]
        keys = joint[:, 1].reshape(slots, lanes)
        values = joint[:, 2].reshape(slots, lanes)
        grad = grads[index]
        product = grad.astype(wide) * out_ref[span, :]
        allowed = crop_ref[span, :] == tag_ref[0:1, :]
        query_grad = None
        for h in range(2):
            query_part, grad_part = head_lanes(queries, h), head_lanes(grad, h)
            scores = jnp.where(allowed, dot(query_part, keys, 1, 1), masked_score)
            weights = jnp.exp(scores - total_ref[h, span, :])
            weight_grads = dot(grad_part, values, 1, 1)
            delta = jnp.sum(head_lanes(product, h), axis=1, keepdims=True)
            score_grads = (weights * (weight_grads - delta)).astype(low)
            weights = weights.astype(low)
            value_acc[...] += dot(grad_part, weights, 0, 0)
            key_acc[...] += dot(query_part, score_grads, 0, 0)
            part = head_lanes(dot(score_grads, keys), h)
            query_grad = part if query_grad is None else query_grad + part
        result[index, 0] = (query_grad * scale).astype(low)

    def step_body(step, carry):
        @pl.when(step < pairs)
        def _():
            begin(step, 0)
            begin(step, 1)

        for back, stage in ((1, stage_core), (2, stage_first), (3, stage_second), (4, stage_third)):

            @pl.when(jnp.logical_and(step >= back, step < pairs + back))
            def _():
                stage(step - back, 0)
                stage(step - back, 1)

        @pl.when(step < peers)
        def _():
            index = lax.rem(me + step, peers)

            @pl.when(step == 0)
            def _():
                keep.wait()

            @pl.when(step > 0)
            def _():
                pltpu.make_async_copy(
                    grads.at[index], grads.at[index], in_recv.at[index]
                ).wait()

            attention(index)

            @pl.when(step > 0)
            def _():
                outward(index, 0).start()

        @pl.when(step == peers - 1)
        def _():
            for index in range(peers):
                span = slice(index * share, (index + 1) * share)
                result[index, 1] = key_acc[:, span].T.astype(low)
                result[index, 2] = value_acc[:, span].T.astype(low)
            for other in range(1, peers):
                outward(lax.rem(me + other, peers), 1).start()
            pltpu.make_async_copy(result.at[me], stacked.at[me], back_own).start()

        return carry

    lax.fori_loop(0, pairs + 4, step_body, 0)

    def finish_body(pair, carry):
        finish(pair, 0)
        finish(pair, 1)
        return carry

    lax.fori_loop(0, pairs, finish_body, 0)
    for step in range(1, peers):
        there = lax.rem(me + step, peers)
        inward(there).wait_send()
        for part in range(2):
            outward(there, part).wait_send()
            span = pl.ds(0, 1) if part == 0 else pl.ds(1, 2)
            pltpu.make_async_copy(
                result.at[there, span], stacked.at[there, span], back_recv.at[there, part]
            ).wait()
    pltpu.make_async_copy(result.at[me], stacked.at[me], back_own).wait()


def attend_back(joint, tags, crops, outputs, totals, source, feed_grads, number):
    peers, kinds, share, lanes = joint.shape
    slots = peers * share
    sides, halves, rows, columns = feed_grads.shape
    total = sides * columns // CHUNK - 2 * LATE_PAIRS
    sem = pltpu.SemaphoreType.DMA
    vmem = pl.BlockSpec(memory_space=pltpu.VMEM)
    hbm = pl.BlockSpec(memory_space=pl.ANY)
    return pl.pallas_call(
        attend_back_kernel,
        out_shape=[
            jax.ShapeDtypeStruct(joint.shape, low),
            jax.ShapeDtypeStruct((rows // 16, total * CHUNK), wide),
        ],
        in_specs=[vmem] * 5 + [hbm] * 2,
        out_specs=[hbm, vmem],
        scratch_shapes=[
            pltpu.VMEM((peers, share, lanes), low),
            pltpu.VMEM(joint.shape, low),
            pltpu.VMEM((lanes, slots), wide),
            pltpu.VMEM((lanes, slots), wide),
        ]
        + reducer_scratch(total, rows // 16)
        + [
            sem,
            sem((peers,)),
            sem((peers,)),
            sem,
            sem((peers, 2)),
            sem((peers, 2)),
        ],
        compiler_params=pltpu.CompilerParams(
            collective_id=number, has_side_effects=True, vmem_limit_bytes=60 * 2**20
        ),
    )(
        joint,
        tags,
        crops,
        outputs,
        totals,
        source,
        feed_grads.reshape(sides, halves, 4, 2, 2, rows // 16, columns),
    )


def whole(array):
    rank = len(array.shape)
    return pl.BlockSpec(array.shape, lambda *_: (0,) * rank)


def norm_parts(values):
    center = values - jnp.mean(values, axis=-1, keepdims=True)
    inverse = lax.rsqrt(jnp.mean(center * center, axis=-1, keepdims=True) + epsilon)
    return center * inverse, inverse


def norm_back(values, gain, grads):
    normed, inverse = norm_parts(values)
    scaled = grads * gain
    inner = (
        scaled
        - jnp.mean(scaled, axis=-1, keepdims=True)
        - normed * jnp.mean(scaled * normed, axis=-1, keepdims=True)
    )
    return (
        inner * inverse,
        jnp.sum(grads * normed, axis=0, keepdims=True),
        jnp.sum(grads, axis=0, keepdims=True),
    )


def columns_of(shape, axis, half):
    spot = lax.broadcasted_iota(jnp.int32, shape, axis)
    side, spot = lax.div(spot, half), lax.rem(spot, half)
    slots = half // 2
    return 2 * lax.rem(spot, slots) + 2 * side + lax.div(spot, slots) - 1


def front_kernel(items, *refs):
    arrays, refs = refs[:8], refs[8:]
    grad_in, hour_ref, pixel_ref, lat_ref, shift_ref, refs = refs[:5] + (refs[5:],)
    outs, grad_out, received, refs = refs[:8], refs[8], refs[9], refs[10:]
    joint, wide_ref, total_ref, tag_ref, crop_ref, refs = refs[:5] + (refs[5:],)
    patch_ref, prob_ref, mixed_ref, value_table, key_table, score_table, refs = refs[:6] + (
        refs[6:],
    )
    full_ref, vector_ref, query_ref, start_ref, low_ref, lead_ref, keep_ref, refs = refs[:7] + (
        refs[7:],
    )
    cut_ref, misc_ref, small_ref, weight_a, weight_b, projected, sending, turned, refs = refs[
        :8
    ] + (refs[8:],)
    gather_sems, refs = refs[:5], refs[5:]
    post_send, post_recv, load_sem, own_sem, send_sem, recv_sem, out_own, refs = refs[:7] + (
        refs[7:],
    )
    out_send, out_recv, cut_in, cut_rows, field, edge, west_edge, east_edge, edge_send, edge_recv = refs
    x, z, y, c = position()
    across, line = partners(x, z, y, c)
    lon = z * 4 + y * 2 + c
    own = (lon, x)
    east, west = (lax.rem(lon + 1, 16), x), (lax.rem(lon + 15, 16), x)
    me = y * 4 + c * 2 + x
    peers, kinds, share, lanes = joint.shape
    slots = peers * share
    head_count, var_count, tokens = prob_ref.shape
    padded = patch_ref.shape[0]
    taps = 4 * var_count
    halves = 2
    half_width = weight_a.shape[-1]

    everyone = [across["x"], across["y"], across["c"]] + line
    for flip in (3, 5, 6, 7):
        there_y = 1 - y if flip & 4 else y
        there_c = 1 - c if flip & 2 else c
        there_x = 1 - x if flip & 1 else x
        everyone.append((z * 4 + there_y * 2 + there_c, there_x))
    sources = [sector_of(z, y, c, x, part, side) for part in range(2) for side in range(2)]
    meet(everyone + [east, west], sources, own)
    letters = []
    for part in range(2):
        row = 2 * x + part
        letters.append(
            (cut_in.at[part], cut_ref.at[c], post_send.at[part], post_recv.at[c])
            + (block_of(z, y, row), own)
        )
    for row in range(4):
        letters.append(
            (grad_in.at[row], grad_out.at[x, c], post_send.at[2 + row])
            + (post_recv.at[2 + 2 * x + c], block_of(z, y, row), own)
        )
    for letter in letters[2:]:
        post(*letter)
    var_total, lat_count, column_count = pixel_ref.shape
    half = lat_ref.shape[1]

    def edge_copies():
        return [
            remote(edge, west_edge, edge_send.at[0], edge_recv.at[0], east),
            remote(edge, east_edge, edge_send.at[1], edge_recv.at[1], west),
        ]

    def send_edges():
        kind = lax.broadcasted_iota(jnp.int32, (16, column_count), 0)
        column = lax.broadcasted_iota(jnp.int32, (16, column_count), 1)
        pick = jnp.where(column == kind * (column_count - 1), 1.0, 0.0).astype(low)
        flat = pixel_ref[...].reshape(var_total * lat_count, column_count)
        edge[...] = dot(pick, flat, 1, 1).astype(low)
        for copy in edge_copies():
            copy.start()

    def make_field():
        for copy in edge_copies():
            copy.wait()
        wanted = columns_of((column_count, 2 * half), 1, half)
        column = lax.broadcasted_iota(jnp.int32, (column_count, 2 * half), 0)
        select = jnp.where(wanted == column, 1.0, 0.0).astype(low)
        kind = lax.broadcasted_iota(jnp.int32, (16, 2 * half), 0)
        wanted = columns_of((16, 2 * half), 1, half)
        from_west = jnp.logical_and(kind == 1, wanted == -1)
        from_east = jnp.logical_and(kind == 0, wanted == column_count)
        flat = pixel_ref[...].reshape(var_total * lat_count, column_count)
        result = dot(flat, select)
        for values, place in ((west_edge, from_west), (east_edge, from_east)):
            result = result + dot(values[...], jnp.where(place, 1.0, 0.0).astype(low), 0, 0)
        field[...] = result.astype(low).reshape(field.shape)

    def cut_row(part):
        lat = jnp.where(x == 0, lat_ref[part : part + 1, :], lat_ref[part + 2 : part + 3, :])
        shift = jnp.where(x == 0, shift_ref[part : part + 1, :], shift_ref[part + 2 : part + 3, :])
        row = lax.broadcasted_iota(jnp.int32, (lat_count, half), 0)
        slots = half // 2

        def body(v, carry):
            values = field[v].astype(wide)
            chosen = jnp.where(shift < 0, values[:, :half], values[:, half:])
            for py in range(2):
                taken = jnp.sum(jnp.where(row == lat + py, chosen, 0.0), axis=0, keepdims=True)
                for px in range(2):
                    spot = pl.ds((2 * py + px) * var_total + v, 1)
                    cut_rows[part, spot, :] = taken[:, px * slots : (px + 1) * slots]
            return carry

        lax.fori_loop(0, var_total, body, 0)

    def send_cut():
        cut_in[...] = cut_rows[...].astype(low)
        for letter in letters[:2]:
            post(*letter)

    def views(number):
        index, lead, first, rows, color = items[number]
        source, target = arrays[index], outs[index]
        if lead is not None:
            source, target = source.at[lead], target.at[lead]
        return source.at[pl.ds(first, rows)], target, pl.ds(first, rows), color

    stages, finish = gatherer(views, gather_sems)

    def load(source, target, spot):
        return pltpu.make_async_copy(source, target, load_sem.at[spot])

    def ask_small():
        load(outs[0], misc_ref, 0).start()
        load(outs[1], small_ref, 1).start()
        load(outs[2], weight_a, 2).start()
        load(outs[3], weight_b, 3).start()

    def read_small():
        load(outs[0], misc_ref, 0).wait()
        load(outs[1], small_ref, 1).wait()
        sector = small_ref.shape[4] // 2
        for lon in range(16):
            at = (lon // 4, lon // 2 % 2, lon % 2)
            for side in range(2):
                rows = slice((2 * lon + side) * sector, (2 * lon + side + 1) * sector)
                for half in range(2):
                    full_ref[rows, half * 128 : (half + 1) * 128] = small_ref[
                        (side,) + at + (slice(half * sector, (half + 1) * sector),)
                    ]
        upper = full_ref[:, 128:]
        vector_ref[...] = upper.astype(wide).T[taps + var_count - 128 : taps + var_count - 120]
        lane = lax.broadcasted_iota(jnp.int32, upper.shape, 1)
        full_ref[:, 128:] = jnp.where(lane < taps + var_count - 128, upper.astype(wide), 0.0).astype(
            low
        )
        kind = lax.broadcasted_iota(jnp.int32, (16, 128), 0)
        across_rows = lax.broadcasted_iota(jnp.int32, (128, 128), 0)
        across_lanes = lax.broadcasted_iota(jnp.int32, (128, 128), 1)
        queries = [None, None]
        for lon in range(16):
            at = (lon // 4, lon // 2 % 2, lon % 2)
            span = slice(lon * 128, (lon + 1) * 128)
            block = misc_ref[(0,) + at + (slice(0, 16),)].astype(wide)
            tag = jnp.sum(jnp.where(kind == z, block, 0.0), axis=0, keepdims=True)
            crop = jnp.sum(jnp.where(kind == 4 + z, block, 0.0), axis=0, keepdims=True)
            tag_ref[0:1, span] = tag
            for row, target in ((crop, crop_ref), (tag, turned)):
                target[span, :] = jnp.sum(
                    jnp.where(across_rows == across_lanes, row, 0.0), axis=1, keepdims=True
                )
            for side in range(2):
                block = misc_ref[(side,) + at + (slice(0, 16),)].astype(wide)[8:16]
                queries[side] = block if lon == 0 else queries[side] + block
        query_ref[...] = jnp.concatenate(queries, axis=0)
        mine = pl.ds(pl.multiple_of(me * share, share), share)
        keep_ref[...] = jnp.where(turned[mine, :] >= 0.0, 1.0, 0.0)
        crops = crop_ref[mine, :]
        hours = jnp.zeros((tokens, 1), wide)
        for k in range(8):
            hours = hours + jnp.where(crops == float(k), hour_ref[0:1, k : k + 1], 0.0)
        lead_ref[...] = hours
        for part in range(2):
            pltpu.make_async_copy(cut_in.at[part], cut_ref.at[part], post_recv.at[part]).wait()
            patch_ref[:taps, part * 128 : (part + 1) * 128] = cut_ref[part]
        patch_ref[taps : taps + var_count, :] = jnp.ones((var_count, tokens), low)
        patch_ref[taps + var_count :, :] = jnp.zeros((padded - taps - var_count, tokens), low)

    def tables(weight, spot, table):
        load(outs[spot], weight, spot).wait()
        for side in range(halves):
            product = dot(weight[side].reshape(-1, half_width), full_ref[...], 0, 0)
            table[side * half_width : (side + 1) * half_width, :] = product.astype(table.dtype)

    def score():
        tables(weight_a, 2, key_table)
        wide_query = jnp.concatenate([query_ref[...]] * (head_count * HEAD_DIM // 128), axis=1)
        head = lax.div(lax.broadcasted_iota(jnp.int32, wide_query.shape, 1), HEAD_DIM)
        row = lax.broadcasted_iota(jnp.int32, wide_query.shape, 0)
        wide_query = jnp.where(head == row, wide_query, 0.0).astype(low)
        rest, result = key_table[...], None
        for _ in range(3):
            part = rest.astype(low)
            rest = rest - part.astype(wide)
            piece = dot(wide_query, part)
            result = piece if result is None else result + piece
        score_table[...] = result * HEAD_DIM ** (-0.5)

    def ask_back():
        load(outs[4], weight_a, 2).start()

    def heads(first):
        mask = diagonal(var_count, padded)

        def head_step(h, carry):
            spread = jnp.where(mask, score_table[pl.ds(h, 1), :], 0.0)
            upper = spread.astype(low)
            lower = (spread - upper.astype(wide)).astype(low)
            patch = patch_ref[...]
            scores = dot(upper, patch) + dot(lower, patch)
            raised = jnp.exp(scores - jnp.max(scores, axis=0, keepdims=True))
            prob = raised / jnp.sum(raised, axis=0, keepdims=True)
            prob_ref[h] = prob
            pooled = jnp.concatenate(
                [
                    (prob * patch_ref[k * var_count : (k + 1) * var_count, :].astype(wide)).astype(
                        low
                    )
                    for k in range(5)
                ]
                + [jnp.zeros((padded - 5 * var_count, tokens), low)],
                axis=0,
            )
            start = pl.multiple_of(h * HEAD_DIM, HEAD_DIM)
            mixed_ref[pl.ds(start, HEAD_DIM), :] = dot(
                value_table[pl.ds(start, HEAD_DIM), :], pooled
            ).astype(low)
            return carry

        lax.fori_loop(first, first + 4, head_step, 0)

    def begin_block():
        load(outs[4], weight_a, 2).wait()
        total = lead_ref[...] * vector_ref[0:1] + vector_ref[1:2]
        mixed = mixed_ref[...].T
        for side in range(halves):
            total = total + dot(
                mixed[:, side * half_width : (side + 1) * half_width],
                weight_a[side].reshape(-1, half_width),
                1,
                1,
            )
        start_ref[...] = total
        normed, _ = norm_parts(total)
        low_ref[...] = (normed * vector_ref[2:3] + vector_ref[3:4]).astype(low)

    def ask_input(kind):
        target = weight_b if kind % 2 == 0 else weight_a
        load(outs[5].at[kind], target, 3 - kind % 2).start()

    def project(kind):
        target = weight_b if kind % 2 == 0 else weight_a
        load(outs[5].at[kind], target, 3 - kind % 2).wait()
        pairs = half_width // lanes
        for side in range(halves):
            result = dot(low_ref[...], target[side].reshape(-1, half_width)).astype(low)
            if kind == 0:
                result = result * low(HEAD_DIM ** (-0.5))
            for pair in range(pairs):
                projected[side * pairs + pair, kind] = result[
                    :, pair * lanes : (pair + 1) * lanes
                ]

    def inward(step):
        there = lax.rem(me + step, peers)
        return remote(
            projected.at[there],
            joint.at[me],
            send_sem.at[there],
            recv_sem.at[me],
            plane_device(z, there),
        )

    def outward(index):
        return remote(
            sending.at[index],
            received.at[me],
            out_send.at[index],
            out_recv.at[me],
            plane_device(z, index),
        )

    def send_heads():
        pltpu.make_async_copy(projected.at[me], joint.at[me], own_sem).start()
        for step in range(1, peers):
            inward(step).start()

    def take_heads():
        pltpu.make_async_copy(projected.at[me], joint.at[me], own_sem).wait()
        for step in range(1, peers):
            there = lax.rem(me + step, peers)
            pltpu.make_async_copy(joint.at[there], joint.at[there], recv_sem.at[there]).wait()

    def attention(first, count):
        def block(step, carry):
            index = lax.rem(me + 1 + step, peers)
            span = pl.ds(pl.multiple_of(index * share, share), share)
            queries = joint[index, 0]
            keys = joint[:, 1].reshape(slots, lanes)
            values = joint[:, 2].reshape(slots, lanes)
            allowed = crop_ref[span, :] == tag_ref[0:1, :]
            result = None
            for h in range(2):
                scores = dot(head_lanes(queries, h), keys, 1, 1)
                scores = jnp.where(allowed, scores, masked_score)
                largest = jnp.max(scores, axis=1, keepdims=True)
                weights = jnp.exp(scores - largest)
                total = jnp.sum(weights, axis=1, keepdims=True)
                weights = (weights * (1.0 / total)).astype(low)
                part = head_lanes(dot(weights, values), h)
                result = part if result is None else result + part
                total_ref[h, span, :] = largest + jnp.log(total)
            wide_ref[span, :] = result
            sending[index] = result.astype(low)

            @pl.when(step < peers - 1)
            def _():
                outward(index).start()

            return carry

        lax.fori_loop(first, first + count, block, 0)

    ready = {}
    for number, item in enumerate(items):
        ready[item[:2]] = number + 8
    at = ready[(3, None)]
    extra = {0: [send_edges], 3: [make_field], 4: [partial(cut_row, 0)], 5: [partial(cut_row, 1)]}
    extra.update({6: [send_cut], at: [ask_small, read_small], at + 1: [score]})
    extra[at + 2] = [lambda: tables(weight_b, 3, value_table), ask_back]
    for quarter in range(4):
        extra.setdefault(at + 3 + quarter // 2, []).append(partial(heads, 4 * quarter))
    at = max(at + 5, ready[(5, 2)])
    extra.setdefault(at, []).extend([partial(ask_input, 0), begin_block, partial(ask_input, 1)])
    extra[at + 1] = [partial(project, 0), partial(ask_input, 2), partial(project, 1)]
    extra[at + 2] = [partial(project, 2), send_heads]
    at += 5
    extra[at] = [take_heads]
    for step in range(4):
        extra.setdefault(at + step, []).append(partial(attention, 2 * step, 2))
    total = len(items)
    for step in range(max(total + 8, max(extra) + 1)):
        for back, stage in enumerate(stages):
            if 0 <= step - 2 * back < total:
                stage(step - 2 * back)
        for work in extra.get(step, []):
            work()
    last = pltpu.make_async_copy(sending.at[me], received.at[me], out_own)
    last.start()
    for number in range(total):
        finish(number)
    for letter in letters:
        settle(*letter)
    for side in range(2):
        for part in range(2):
            pltpu.make_async_copy(
                grad_in.at[0], grad_out.at[side, part], post_recv.at[2 + 2 * side + part]
            ).wait()
    for step in range(1, peers):
        there = lax.rem(me + step, peers)
        inward(step).wait_send()
        outward(there).wait_send()
        pltpu.make_async_copy(sending.at[there], received.at[there], out_recv.at[there]).wait()
    last.wait()


def front(arrays, grads, hours, pixels, lat_lanes, shift_lanes, head_count, number):
    items = []
    for index, array in enumerate(arrays):
        for lead in range(array.shape[0]) if array.ndim == 3 else (None,):
            rows = array.shape[-2]
            if rows % 64:
                items.append((index, lead, 0, rows, 0))
                continue
            for color in range(2):
                items.append((index, lead, color * rows // 2, rows // 2, color))
    width = arrays[2].shape[1]
    model = 2 * width
    var_count, lat_count = pixels.shape[:2]
    tokens = lat_lanes.shape[1]
    cut_shape = (2, 4 * var_count, tokens // 2)
    padded = 2 * arrays[1].shape[1]
    slots = 8 * tokens
    sem = pltpu.SemaphoreType.DMA
    vmem = pl.BlockSpec(memory_space=pltpu.VMEM)
    hbm = pl.BlockSpec(memory_space=pl.ANY)
    block = (2, 4, 2, 2)

    def all_of(array):
        return array.shape[:-2] + block + array.shape[-2:]

    low_outs = [all_of(a) for a in arrays] + [(2, 2) + grads.shape[1:], (8, tokens, 128)]
    vmem_outs = [
        ((8, 3, tokens, 128), low),
        ((slots, 128), wide),
        ((2, slots, 1), wide),
        ((8, slots), wide),
        ((slots, 1), wide),
        ((padded, tokens), low),
        ((head_count, var_count, tokens), wide),
        ((model, tokens), low),
        ((model, padded), low),
        ((model, padded), wide),
        ((head_count, padded), wide),
        ((model, padded), low),
        ((8, model), wide),
        ((head_count, 128), wide),
        ((tokens, model), wide),
        ((tokens, model), low),
        ((tokens, 1), wide),
        ((tokens, 1), wide),
    ]
    result = pl.pallas_call(
        partial(front_kernel, items),
        out_shape=[jax.ShapeDtypeStruct(shape, low) for shape in low_outs]
        + [jax.ShapeDtypeStruct(shape, dtype) for shape, dtype in vmem_outs],
        in_specs=[hbm] * (len(arrays) + 1) + [vmem] * 4,
        out_specs=[hbm] * len(low_outs) + [vmem] * len(vmem_outs),
        scratch_shapes=[
            pltpu.VMEM(cut_shape, low),
            pltpu.VMEM(all_of(arrays[0]), low),
            pltpu.VMEM(all_of(arrays[1]), low),
            pltpu.VMEM(all_of(arrays[2]), low),
            pltpu.VMEM(all_of(arrays[2]), low),
            pltpu.VMEM((8, 3, tokens, 128), low),
            pltpu.VMEM((8, tokens, 128), low),
            pltpu.VMEM((slots, 1), wide),
            sem((len(items),)),
        ]
        + [sem((len(items), 3))] * 4
        + [sem((6,)), sem((6,)), sem((4,)), sem, sem((8,)), sem((8,)), sem, sem((8,)), sem((8,))]
        + [
            pltpu.VMEM(cut_shape, low),
            pltpu.VMEM(cut_shape, wide),
            pltpu.VMEM((var_count, lat_count, 2 * tokens), low),
            pltpu.VMEM((16, var_count * lat_count), low),
            pltpu.VMEM((16, var_count * lat_count), low),
            pltpu.VMEM((16, var_count * lat_count), low),
            sem((2,)),
            sem((2,)),
        ],
        compiler_params=pltpu.CompilerParams(
            collective_id=number, has_side_effects=True, vmem_limit_bytes=58 * 2**20
        ),
    )(*arrays, grads, hours, pixels, lat_lanes, shift_lanes)
    count = len(arrays)
    gathered = [
        g.reshape(a.shape[:-2] + (2, 16 * a.shape[-2], a.shape[-1]))
        for g, a in zip(result, arrays)
    ]
    return gathered, result[count:]


def feed_kernel(
    attended_ref,
    proj_ref,
    start_ref,
    vector_ref,
    up_ref,
    down_ref,
    bias_ref,
    final_ref,
    masked_ref,
    keep_ref,
    predicted_ref,
    middle_grad_ref,
    unit_ref,
    grad_feed_ref,
    grad_proj_ref,
    grad_final_ref,
    grad_bias_ref,
    grad_vector_ref,
    flat,
    middle,
    second,
    second_turned,
    active,
    slope,
    total,
    grad_low,
    grad_turned,
    grad_final,
):
    step = pl.program_id(0)
    count = active.shape[0]
    row_count, units, share, lanes = attended_ref.shape
    _, halves, _, half_width = proj_ref.shape
    tokens = row_count * share

    @pl.when(step == 0)
    def _():
        for unit in range(units):
            flat[:, unit * lanes : (unit + 1) * lanes] = attended_ref[:, unit].reshape(
                tokens, lanes
            )
        result = start_ref[...]
        for side in range(halves):
            result = result + dot(
                flat[:, side * half_width : (side + 1) * half_width], proj_ref[0, side], 1, 1
            )
        middle[...] = result
        normed, _ = norm_parts(result)
        normed = (normed * vector_ref[4:5] + vector_ref[5:6]).astype(low)
        second[...] = normed
        second_turned[...] = normed.T
        total[...] = result

    @pl.when(step < count)
    def _():
        hidden = dot(second[...], up_ref[0, 0]) + bias_ref[...]
        share_of = 0.5 * (1.0 + lax.erf(hidden * (0.5**0.5)))
        fired = (hidden * share_of).astype(low)
        active[step] = fired
        slope[step] = share_of + hidden * jnp.exp(-0.5 * hidden * hidden) * (
            0.5 / 1.2533141373155003
        )
        total[...] += dot(fired, down_ref[0, 0], 1, 1)

    @pl.when(step == count - 1)
    def _():
        final_low = total[...].astype(low)
        final_turned = final_low.T
        grads = None
        for side in range(halves):
            predicted_ref[side] = (dot(final_low, final_ref[side]) * keep_ref[...]).astype(low)
            part = dot(masked_ref[side], final_ref[side], 1, 1)
            grads = part if grads is None else grads + part
            grad_final_ref[side] = dot(final_turned, masked_ref[side]).astype(low)
        grad_final[...] = grads
        grad_low[...] = grads.astype(low)
        grad_turned[...] = grads.astype(low).T
        total[...] = jnp.zeros_like(total)

    @pl.when(step >= count)
    def _():
        block = step - count
        hidden_grad = dot(grad_low[...], down_ref[0, 0]) * slope[block]
        hidden_low = hidden_grad.astype(low)
        grad_bias_ref[...] = jnp.sum(hidden_low.astype(wide), axis=0, keepdims=True)
        total[...] += dot(hidden_low, up_ref[0, 0], 1, 1)
        grad_feed_ref[0, 0] = dot(second_turned[...], hidden_low).astype(low)
        grad_feed_ref[1, 0] = dot(grad_turned[...], active[block]).astype(low)

    @pl.when(step == 2 * count - 1)
    def _():
        part, grad_gain, grad_shift = norm_back(middle[...], vector_ref[4:5], total[...])
        result = grad_final[...] + part
        middle_grad_ref[...] = result
        grad_vector_ref[0:1] = grad_gain
        grad_vector_ref[1:2] = grad_shift
        result_low = result.astype(low)
        result_turned = result_low.T
        pairs = half_width // lanes
        for side in range(halves):
            span = slice(side * half_width, (side + 1) * half_width)
            grad_proj_ref[side] = dot(result_turned, flat[:, span]).astype(low)
            out = dot(result_low, proj_ref[0, side]).astype(low)
            for pair in range(pairs):
                unit_ref[:, side * pairs + pair] = out[
                    :, pair * lanes : (pair + 1) * lanes
                ].reshape(row_count, share, lanes)


def feed(attended, start, vectors, late, up_bias, final_weight, masked, keep):
    blocks, halves, model, block = late.shape
    half_width = block
    each = blocks // 2
    full = each * block
    tokens = start.shape[0]
    count = halves * each

    def block_of_kind(kind):
        def block_at(i):
            j = lax.rem(i, count)
            return (kind * each + lax.rem(j, each), lax.div(j, each), 0, 0)

        return pl.BlockSpec((1, 1, model, block), block_at)

    def late_block(i):
        j = lax.max(i - count, 0)
        return (0, lax.div(j, each), 0, lax.rem(j, each))

    def fixed(shape, dtype):
        rank = len(shape)
        return jax.ShapeDtypeStruct(shape, dtype), pl.BlockSpec(shape, lambda i: (0,) * rank)

    outs = [
        fixed((halves, tokens, 128), low),
        fixed((tokens, model), wide),
        fixed(attended.shape, low),
        (
            jax.ShapeDtypeStruct((2, halves, model, full), low),
            pl.BlockSpec((2, 1, model, block), late_block),
        ),
        fixed((halves, model, half_width), low),
        fixed((halves, model, 128), low),
        (
            jax.ShapeDtypeStruct((1, halves * full), wide),
            pl.BlockSpec((1, block), lambda i: (0, lax.max(i - count, 0))),
        ),
        fixed((2, model), wide),
    ]
    return pl.pallas_call(
        feed_kernel,
        grid=(2 * count,),
        out_shape=[shape for shape, _ in outs],
        in_specs=[
            whole(attended),
            pl.BlockSpec((1, halves, model, block), lambda i: (blocks - 1, 0, 0, 0)),
            whole(start),
            whole(vectors),
            block_of_kind(0),
            block_of_kind(1),
            pl.BlockSpec((1, block), lambda i: (0, lax.rem(i, count))),
            whole(final_weight),
            whole(masked),
            whole(keep),
        ],
        out_specs=[spec for _, spec in outs],
        scratch_shapes=[
            pltpu.VMEM((tokens, model), low),
            pltpu.VMEM((tokens, model), wide),
            pltpu.VMEM((tokens, model), low),
            pltpu.VMEM((model, tokens), low),
            pltpu.VMEM((count, tokens, block), low),
            pltpu.VMEM((count, tokens, block), wide),
            pltpu.VMEM((tokens, model), wide),
            pltpu.VMEM((tokens, model), low),
            pltpu.VMEM((model, tokens), low),
            pltpu.VMEM((tokens, model), wide),
        ],
        compiler_params=pltpu.CompilerParams(vmem_limit_bytes=56 * 2**20),
    )(attended, late, start, vectors, late, late, up_bias, final_weight, masked, keep)


def einsum(spec, left, right):
    return jnp.einsum(spec, left, right, preferred_element_type=wide)


def fast_local(
    pixels,
    crop_starts,
    crop_shifts,
    slot_crops,
    occupied,
    lead_hours,
    patch_weight,
    variable_embed,
    mixer_query,
    mixer_keys,
    mixer_values,
    mixer_output,
    lead_embed,
    first_gain,
    first_bias,
    attention_in,
    attention_out,
    second_gain,
    second_bias,
    expand_weight,
    expand_bias,
    reduce_weight,
    output_weight,
    cotangent,
):
    lon, head = lax.axis_index(LON), lax.axis_index(HEAD)
    row_count, slot_width = slot_crops.shape
    share = slot_width // HEAD_SIZE
    tokens = row_count * share
    var_count, lat_count, column_count = pixels.shape
    head_half, query_width = mixer_query.shape
    head_count = HEAD_SIZE * head_half
    half_width = head_half * HEAD_DIM
    out_half = output_weight.shape[1]
    slice_width = patch_weight.shape[2]
    model = slice_width * LON_SIZE * HEAD_SIZE
    block_rows = model // LON_SIZE
    taps = 4 * var_count
    pairs = half_width // 128
    scale = HEAD_DIM ** (-0.5)

    lat_lanes = jnp.tile(crop_lookup(crop_starts, slot_crops), (1, 2))
    shift_lanes = jnp.tile(crop_lookup(crop_shifts, slot_crops), (1, 2))
    masked = cotangent * occupied[:, :, None].astype(low)
    masked = jnp.pad(masked, ((0, 0), (0, 0), (0, 128 - out_half)))
    late = jnp.concatenate(
        [
            jnp.transpose(part.reshape(block_rows, -1, half_width), (1, 0, 2))
            for part in (expand_weight, reduce_weight.T, attention_out.T)
        ]
    )
    padded = 256
    small = jnp.concatenate(
        [
            jnp.transpose(patch_weight, (1, 0, 2)).reshape(taps, slice_width),
            variable_embed,
            jnp.concatenate(
                [
                    lead_embed.reshape(-1),
                    first_gain,
                    first_bias,
                    second_gain,
                    second_bias,
                    jnp.zeros(((padded - taps - var_count - 6) * slice_width,), low),
                ]
            ).reshape(-1, slice_width),
        ]
    ).T
    small = jnp.concatenate([small[:, :128], small[:, 128:]])
    tags = jnp.where(occupied == 1, slot_crops, -1).astype(low)
    lane = jnp.arange(128) % (LON_SIZE * query_width) // query_width
    spread = jnp.tile(jnp.concatenate([mixer_query, expand_bias]), (1, 128 // query_width))
    spread = jnp.where(lane == lon, spread, 0)
    misc = jnp.concatenate([tags, slot_crops.astype(low), spread])
    out_block = jnp.pad(output_weight, ((0, 0), (0, 128 - out_half)))
    my_row = lax.div(lon, LON_SIZE // row_count)
    hours = lax.dynamic_index_in_dim(lead_hours, my_row, 0).astype(wide) / 100.0
    hours = jnp.pad(hours, ((0, 0), (0, 128 - hours.shape[1])))
    gathered, made = front(
        [
            misc,
            small,
            mixer_keys,
            mixer_values,
            mixer_output.T,
            attention_in,
            out_block,
            late,
        ],
        masked,
        hours,
        pixels,
        lat_lanes,
        shift_lanes,
        head_count,
        1,
    )
    misc_all, _, key_weight, value_weight, mixer_weight, input_weight, final_weight, late = gathered
    masked, attended, joint, attended_wide, totals, tag_row, crop_column = made[:7]
    patches, probs, mixed, value_table, key_table, score_table = made[7:13]
    patch_full, vectors, query, start_sum, first_low, lead_column, keep_mask = made[13:]
    masked = masked.reshape(HEAD_SIZE, tokens, 128)
    attended = attended[None]
    query_wide, query = query, query[:, :HEAD_DIM]
    bias_rows = expand_bias.shape[0]
    up_bias = misc_all.reshape(HEAD_SIZE, LON_SIZE, -1, 128)[:, :, 2 * row_count + head_half :]
    up_bias = jnp.sum(up_bias[..., : LON_SIZE * query_width].astype(wide), axis=1)
    units = HEAD_SIZE * pairs
    (
        predicted,
        middle_grad,
        out_grads,
        grad_feed,
        grad_proj,
        grad_out,
        grad_up_bias,
        second_vectors,
    ) = feed(
        attended,
        start_sum,
        vectors,
        late,
        up_bias.reshape(1, -1),
        final_weight,
        masked,
        keep_mask,
    )
    stacked, feed_sums = attend_back(
        joint,
        tag_row,
        crop_column,
        attended_wide,
        totals,
        out_grads.reshape(units, tokens, 128),
        grad_feed,
        4,
    )
    bias_cols = expand_bias.shape[1]
    bias_block = jnp.transpose(
        grad_up_bias.reshape(HEAD_SIZE, bias_rows, LON_SIZE, bias_cols), (0, 2, 1, 3)
    )
    bias_at = out_half + head_half
    bias_block = jnp.pad(
        bias_block,
        (
            (0, 0),
            (0, 0),
            (0, block_rows - bias_rows),
            (bias_at, 128 - bias_at - bias_cols),
        ),
    ).reshape(HEAD_SIZE, model, 128)
    spot = taps + var_count
    sums, predicted, pixel_grad = reduce_all(
        grad_feed,
        grad_proj,
        predicted.reshape(HEAD_SIZE, 2, slot_width, 128),
        (key_weight, value_weight, input_weight, mixer_weight),
        lat_lanes,
        shift_lanes,
        (patches, probs, score_table, value_table, key_table, mixed),
        (patch_full, query_wide, second_vectors, grad_out, bias_block.astype(low)),
        (stacked, first_low, start_sum, middle_grad, vectors, lead_column),
        lat_count,
        2,
    )
    predicted = predicted[:, :, :out_half]
    full_half = expand_weight.shape[1]
    place = [0]

    def take(width):
        begin = place[0]
        place[0] = begin + width
        return sums[:, begin : begin + width]

    out_up = feed_sums[:, :full_half]
    out_down = jnp.concatenate([feed_sums[:, full_half:], take(2 * LATE_PAIRS * CHUNK)], axis=1).T
    out_proj = take(half_width).T
    out_input = jnp.stack([take(half_width) for _ in range(3)])
    out_mixer = take(half_width).T
    out_values = take(half_width)
    tail_small = take(128)
    tail_rest = take(128)
    tail_small = jnp.concatenate([tail_small[:slice_width], tail_small[slice_width:]], axis=1).T
    out_patch = jnp.transpose(tail_small[:taps].reshape(4, var_count, slice_width), (1, 0, 2))
    out_variable = tail_small[taps:spot]
    out_lead = tail_small[spot : spot + 2]
    out_final = tail_rest[:, :out_half]
    at = out_half
    my_heads = tail_rest[:, at : at + head_half]
    at += head_half
    out_bias = tail_rest[:bias_rows, at : at + bias_cols]
    at += bias_cols
    out_query = tail_rest[:head_half, at : at + query_width]
    my_query = block_slice(query, head, head_half, 0)
    out_keys = (my_heads[:, :, None] * my_query[None]).reshape(block_rows, half_width)

    pixel_grad = jnp.transpose(pixel_grad, (1, 0, 2))
    return (
        predicted,
        pixel_grad,
        out_patch,
        out_variable,
        out_query,
        out_keys,
        out_values,
        out_mixer,
        out_lead,
        tail_small[spot + 2],
        tail_small[spot + 3],
        out_input,
        out_proj,
        tail_small[spot + 4],
        tail_small[spot + 5],
        out_up,
        out_bias,
        out_down,
        out_final,
    )


def solution(mesh):
    body = fast_local if planned(mesh) else local
    placed = (
        P(None, None, LON),
        P(),
        P(),
        P(None, LON),
        P(None, LON),
        P(),
        P(None, None, (LON, HEAD)),
        P(None, (LON, HEAD)),
        P(HEAD, LON),
        P(LON, HEAD),
        P(LON, HEAD),
        P(HEAD, LON),
        P(None, (LON, HEAD)),
        P((LON, HEAD)),
        P((LON, HEAD)),
        P(None, LON, HEAD),
        P(HEAD, LON),
        P((LON, HEAD)),
        P((LON, HEAD)),
        P(LON, HEAD),
        P(HEAD, LON),
        P(HEAD, LON),
        P(LON, HEAD),
        P(None, LON, HEAD),
    )
    return jax.shard_map(
        body,
        mesh=mesh,
        in_specs=placed,
        out_specs=(
            P(None, LON, HEAD),
            P(None, None, LON),
            P(None, None, (LON, HEAD)),
            P(None, (LON, HEAD)),
            P(HEAD, LON),
            P(LON, HEAD),
            P(LON, HEAD),
            P(HEAD, LON),
            P(None, (LON, HEAD)),
            P((LON, HEAD)),
            P((LON, HEAD)),
            P(None, LON, HEAD),
            P(HEAD, LON),
            P((LON, HEAD)),
            P((LON, HEAD)),
            P(LON, HEAD),
            P(HEAD, LON),
            P(HEAD, LON),
            P(LON, HEAD),
        ),
        check_vma=False,
    )
```

```python
from functools import partial

import jax
import jax.numpy as jnp
from jax import lax
from jax.experimental import pallas as pl
from jax.experimental.pallas import tpu as pltpu
from jax.sharding import PartitionSpec as P

HEAD_DIM = 64
LON, HEAD = "lon", "head"


epsilon = 1e-05
masked_score = -1e30
highest = lax.Precision.HIGHEST


def extended(array, sides, width):
    for axis, dim in sides:
        count, length = (lax.axis_size(axis), array.shape[dim])
        up = [(i, (i + 1) % count) for i in range(count)]
        down = [(j, i) for i, j in up]
        last = lax.slice_in_dim(array, length - width, length, axis=dim)
        leading = lax.slice_in_dim(array, 0, width, axis=dim)
        before = lax.ppermute(last, axis, up)
        after = lax.ppermute(leading, axis, down)
        array = jnp.concatenate([before, array, after], axis=dim)
    return array


def layer_norm(values, gain_vector, shift_vector):
    center = values - jnp.mean(values, axis=-1, keepdims=True)
    spread = jnp.mean(center * center, axis=-1, keepdims=True)
    return center * lax.rsqrt(spread + epsilon) * gain_vector + shift_vector


def head_total(partial_sum):
    return lax.psum(partial_sum.astype(jnp.bfloat16), HEAD).astype(jnp.float32)


def head_share(partial_sum):
    return lax.psum_scatter(
        partial_sum.astype(jnp.bfloat16), HEAD, scatter_dimension=0, tiled=True
    ).astype(jnp.float32)


def head_rows(values):
    return lax.all_gather(values, HEAD, axis=0, tiled=True)


def reduce_rows(partial_sum):
    return head_share(partial_sum)


def spread_rows(values):
    return head_rows(values)


def crop_lookup(crop_table, slot_numbers):
    numbers = jnp.arange(crop_table.shape[1], dtype=jnp.int32)
    picked = slot_numbers[:, :, None] == numbers[None, None, :]
    return jnp.sum(jnp.where(picked, crop_table[:, None, :], 0), axis=2)


def outer_sum(left_rows, right_rows):
    return jnp.einsum("ti,tj->ij", left_rows, right_rows, preferred_element_type=jnp.float32)


def block_slice(values, block_index, block_width, axis_number):
    return lax.dynamic_slice_in_dim(values, block_index * block_width, block_width, axis_number)


def block_scores(queries, query_crops, key_block, key_tags):
    scores = jnp.einsum(
        "rqhd,rkhd->rhqk", queries, key_block, preferred_element_type=jnp.float32
    ) * HEAD_DIM ** (-0.5)
    matched = query_crops[:, None, :, None] == key_tags[:, None, None, :]
    return (jnp.where(matched, scores, masked_score), matched)


def key_stats(queries, query_crops, key_rows, key_tags, block_width):
    row_count, slot_count, head_count, head_size = queries.shape

    def key_step(carried, block_index):
        largest, totals = carried
        scores, matched = block_scores(
            queries,
            query_crops,
            block_slice(key_rows, block_index, block_width, 1),
            block_slice(key_tags, block_index, block_width, 1),
        )
        raised = jnp.maximum(largest, jnp.max(scores, axis=-1))
        totals = totals * jnp.exp(largest - raised) + jnp.sum(
            jnp.where(matched, jnp.exp(scores - raised[..., None]), 0.0), axis=-1
        )
        return ((raised, totals), None)

    initial = (
        jnp.full((row_count, head_count, slot_count), masked_score, jnp.float32),
        jnp.zeros((row_count, head_count, slot_count), jnp.float32),
    )
    (largest, totals), _ = lax.scan(key_step, initial, jnp.arange(key_rows.shape[1] // block_width))
    return largest + jnp.log(totals)


def attend(queries, query_crops, key_rows, value_rows, key_tags, log_totals, block_width):

    def attend_step(running, block_index):
        scores, matched = block_scores(
            queries,
            query_crops,
            block_slice(key_rows, block_index, block_width, 1),
            block_slice(key_tags, block_index, block_width, 1),
        )
        weights = jnp.where(matched, jnp.exp(scores - log_totals[..., None]), 0.0).astype(
            jnp.bfloat16
        )
        value_block = block_slice(value_rows, block_index, block_width, 1)
        return (
            running
            + jnp.einsum(
                "rhqk,rkhd->rqhd", weights, value_block, preferred_element_type=jnp.float32
            ),
            None,
        )

    outputs, _ = lax.scan(
        attend_step,
        jnp.zeros(queries.shape, jnp.float32),
        jnp.arange(key_rows.shape[1] // block_width),
    )
    return outputs


def score_grads(
    queries, query_crops, out_grads, log_totals, deltas, key_block, value_block, key_tags
):
    scores, matched = block_scores(queries, query_crops, key_block, key_tags)
    weights = jnp.where(matched, jnp.exp(scores - log_totals[..., None]), 0.0)
    weight_grads = jnp.einsum(
        "rqhd,rkhd->rhqk", out_grads, value_block, preferred_element_type=jnp.float32
    )
    score_delta = (weights * (weight_grads - deltas[..., None])).astype(jnp.bfloat16)
    return (score_delta, weights.astype(jnp.bfloat16))


def mixer_row(patch_row, full_patch, full_variable, pair_weight, head_query):
    embedded = jnp.einsum(
        "svk,vkd->svd", patch_row, full_patch, preferred_element_type=jnp.float32
    ) + full_variable.astype(jnp.float32)
    embedded = embedded.astype(jnp.bfloat16)
    slot_count, var_count, model_width = embedded.shape
    head_count, head_size = head_query.shape
    local_width = head_count * head_size
    paired = jnp.dot(
        embedded.reshape(slot_count * var_count, model_width),
        pair_weight,
        preferred_element_type=jnp.float32,
    ).astype(jnp.bfloat16)
    key_rows = paired[:, :local_width].reshape(slot_count, var_count, head_count, head_size)
    value_rows = paired[:, local_width:].reshape(slot_count, var_count, head_count, head_size)
    scores = jnp.einsum(
        "svhd,hd->shv", key_rows, head_query, preferred_element_type=jnp.float32
    ) * HEAD_DIM ** (-0.5)
    weights = jax.nn.softmax(scores, axis=-1)
    return (embedded, key_rows, value_rows, weights)


def mixer_back(carried, inputs, full_patch, full_variable, pair_weight, head_query):
    patch_row, mixed_grad = inputs
    embedded, key_rows, value_rows, weights = mixer_row(
        patch_row, full_patch, full_variable, pair_weight, head_query
    )
    slot_count, var_count, model_width = embedded.shape
    local_width = key_rows.shape[2] * key_rows.shape[3]
    mixed_wide = mixed_grad.astype(jnp.float32)
    value_grads = jnp.einsum("shv,shd->svhd", weights, mixed_wide, precision=highest).astype(
        jnp.bfloat16
    )
    weight_grads = jnp.einsum(
        "shd,svhd->shv", mixed_wide, value_rows.astype(jnp.float32), precision=highest
    )
    score_delta = (
        weights
        * (weight_grads - jnp.sum(weights * weight_grads, axis=-1, keepdims=True))
        * HEAD_DIM ** (-0.5)
    )
    key_grads = jnp.einsum(
        "shv,hd->svhd", score_delta, head_query.astype(jnp.float32), precision=highest
    ).astype(jnp.bfloat16)
    query_grad = jnp.einsum(
        "shv,svhd->hd", score_delta, key_rows.astype(jnp.float32), precision=highest
    )
    pair_grads = jnp.concatenate(
        [
            key_grads.reshape(slot_count * var_count, local_width),
            value_grads.reshape(slot_count * var_count, local_width),
        ],
        axis=1,
    )
    embed_grad = jnp.einsum(
        "ne,de->nd", pair_grads, pair_weight, preferred_element_type=jnp.float32
    )
    pair_weight_grad = outer_sum(embedded.reshape(slot_count * var_count, model_width), pair_grads)
    embed_grad = embed_grad.reshape(slot_count, var_count, model_width)
    patch_grad = jnp.einsum(
        "svk,svd->vkd", patch_row.astype(jnp.float32), embed_grad, precision=highest
    )
    variable_grad = jnp.sum(embed_grad, axis=0)
    slot_grad = jnp.einsum(
        "svd,vkd->svk", embed_grad, full_patch.astype(jnp.float32), precision=highest
    )
    patch_acc, variable_acc, query_acc, pair_acc = carried
    return (
        (
            patch_acc + patch_grad,
            variable_acc + variable_grad,
            query_acc + query_grad,
            pair_acc + pair_weight_grad,
        ),
        slot_grad,
    )


def local(
    pixels,
    crop_starts,
    crop_shifts,
    slot_crops,
    occupied,
    lead_hours,
    patch_weight,
    variable_embed,
    mixer_query,
    mixer_keys,
    mixer_values,
    mixer_output,
    lead_embed,
    first_gain,
    first_bias,
    attention_in,
    attention_out,
    second_gain,
    second_bias,
    expand_weight,
    expand_bias,
    reduce_weight,
    output_weight,
    cotangent,
):
    shared = (
        lax.all_gather(patch_weight, (LON, HEAD), axis=2, tiled=True),
        lax.all_gather(variable_embed, (LON, HEAD), axis=1, tiled=True),
        lax.all_gather(lead_embed, (LON, HEAD), axis=1, tiled=True),
        lax.all_gather(first_gain, (LON, HEAD), axis=0, tiled=True),
        lax.all_gather(first_bias, (LON, HEAD), axis=0, tiled=True),
        lax.all_gather(second_gain, (LON, HEAD), axis=0, tiled=True),
        lax.all_gather(second_bias, (LON, HEAD), axis=0, tiled=True),
    )
    full_patch, full_variable, full_lead, gain_first, shift_first, gain_second, shift_second = (
        shared
    )
    sector = (
        lax.all_gather(mixer_query, LON, axis=1, tiled=True),
        lax.all_gather(mixer_keys, LON, axis=0, tiled=True),
        lax.all_gather(mixer_values, LON, axis=0, tiled=True),
        lax.all_gather(mixer_output, LON, axis=1, tiled=True),
        lax.all_gather(attention_in, LON, axis=1, tiled=True),
        lax.all_gather(attention_out, LON, axis=1, tiled=True),
        lax.all_gather(expand_weight, LON, axis=0, tiled=True),
        lax.all_gather(expand_bias, LON, axis=1, tiled=True),
        lax.all_gather(reduce_weight, LON, axis=1, tiled=True),
        lax.all_gather(output_weight, LON, axis=0, tiled=True),
    )
    (
        head_query,
        key_weight,
        value_weight,
        mixer_weight,
        input_weight,
        output_proj,
        up_weight,
        up_bias,
        down_weight,
        final_weight,
    ) = sector
    row_count, slot_width = slot_crops.shape
    token_count = row_count * slot_width
    local_width = key_weight.shape[1]
    head_count = local_width // HEAD_DIM
    pair_weight = jnp.concatenate([key_weight, value_weight], axis=1)
    gain_one = gain_first.astype(jnp.float32)
    shift_one = shift_first.astype(jnp.float32)
    gain_two = gain_second.astype(jnp.float32)
    shift_two = shift_second.astype(jnp.float32)
    lat_slot = crop_lookup(crop_starts, slot_crops)
    shift_slot = crop_lookup(crop_shifts, slot_crops)
    lead_slot = crop_lookup(lead_hours, slot_crops).astype(jnp.float32).reshape(token_count) / 100.0
    share_count = token_count // lax.axis_size(HEAD)
    lead_rows = lax.dynamic_slice_in_dim(
        lead_slot, lax.axis_index(HEAD) * share_count, share_count
    )
    padded = extended(pixels, ((LON, 2),), 1)
    var_count, lat_count = (pixels.shape[0], pixels.shape[1])
    west_pairs = padded[:, :, : 2 * slot_width].reshape(var_count, lat_count, slot_width, 2)
    east_pairs = padded[:, :, 2:].reshape(var_count, lat_count, slot_width, 2)
    side_pairs = jnp.stack([west_pairs, east_pairs])
    tables = jnp.stack([side_pairs[:, :, :-1], side_pairs[:, :, 1:]], axis=3)
    lat_index = jnp.arange(lat_count - 1, dtype=jnp.int32)
    side_shift = 2 * jnp.arange(2, dtype=jnp.int32) - 1
    chosen = (lat_slot[:, :, None, None] == lat_index[None, None, None, :]) & (
        shift_slot[:, :, None, None] == side_shift[None, None, :, None]
    )
    patches = jnp.einsum(
        "rjsa,svapjx->rjvpx",
        chosen.astype(jnp.bfloat16),
        tables,
        preferred_element_type=jnp.float32,
    )
    patches = patches.astype(jnp.bfloat16).reshape(row_count, slot_width, var_count, 4)

    def mixer_forward(patch_row):
        embedded, key_rows, value_rows, weights = mixer_row(
            patch_row, full_patch, full_variable, pair_weight, head_query
        )
        return jnp.einsum(
            "shv,svhd->shd", weights, value_rows.astype(jnp.float32), precision=highest
        ).astype(jnp.bfloat16)

    mixed_low = lax.map(mixer_forward, patches).reshape(token_count, local_width)
    start_sum = reduce_rows(jnp.dot(mixed_low, mixer_weight, preferred_element_type=jnp.float32))
    start_sum = (
        start_sum
        + lead_rows[:, None] * full_lead[0].astype(jnp.float32)
        + full_lead[1].astype(jnp.float32)
    )
    first_low = spread_rows(layer_norm(start_sum, gain_one, shift_one).astype(jnp.bfloat16))
    projected = jnp.einsum(
        "td,kde->kte", first_low, input_weight, preferred_element_type=jnp.float32
    ).astype(jnp.bfloat16)
    projected = projected.reshape(3, row_count, slot_width, head_count, HEAD_DIM)
    queries, key_local, value_local = (projected[0], projected[1], projected[2])
    query_crops = slot_crops.astype(jnp.float32)
    key_tags = jnp.where(occupied == 1, slot_crops, -1).astype(jnp.bfloat16)
    key_all, value_all, tag_all = (
        lax.all_gather(key_local, LON, axis=1, tiled=True),
        lax.all_gather(value_local, LON, axis=1, tiled=True),
        lax.all_gather(key_tags, LON, axis=1, tiled=True),
    )
    block_width = min(512, key_all.shape[1])
    tag_wide = tag_all.astype(jnp.float32)
    log_totals = key_stats(queries, query_crops, key_all, tag_wide, block_width)
    attended = attend(queries, query_crops, key_all, value_all, tag_wide, log_totals, block_width)
    attended_low = attended.astype(jnp.bfloat16).reshape(token_count, local_width)
    middle = start_sum + reduce_rows(
        jnp.dot(attended_low, output_proj, preferred_element_type=jnp.float32)
    )
    second_low = spread_rows(layer_norm(middle, gain_two, shift_two).astype(jnp.bfloat16))
    hidden = jnp.dot(second_low, up_weight, preferred_element_type=jnp.float32) + up_bias.reshape(
        -1
    ).astype(jnp.float32)
    active = jax.nn.gelu(hidden, approximate=False).astype(jnp.bfloat16)
    final_sum = middle + reduce_rows(
        jnp.dot(active, down_weight, preferred_element_type=jnp.float32)
    )
    final_low = spread_rows(final_sum.astype(jnp.bfloat16))
    keep_mask = occupied.reshape(token_count, 1)
    predicted = (
        jnp.dot(final_low, final_weight, preferred_element_type=jnp.float32)
        * keep_mask.astype(jnp.float32)
    ).astype(jnp.bfloat16)
    predicted = predicted.reshape(row_count, slot_width, -1)
    masked_grad = (cotangent * occupied[:, :, None].astype(jnp.bfloat16)).reshape(token_count, -1)
    grad_final_weight = outer_sum(final_low, masked_grad)
    part_top = jnp.einsum(
        "to,do->td", masked_grad, final_weight, preferred_element_type=jnp.float32
    )
    final_grad = reduce_rows(part_top)
    final_grad_low = spread_rows(final_grad.astype(jnp.bfloat16))
    grad_down = outer_sum(active, final_grad_low)
    active_grad = jnp.einsum(
        "td,fd->tf", final_grad_low, down_weight, preferred_element_type=jnp.float32
    )
    _, gelu_back = jax.vjp(partial(jax.nn.gelu, approximate=False), hidden)
    hidden_grad = gelu_back(active_grad)[0].astype(jnp.bfloat16)
    grad_up = outer_sum(second_low, hidden_grad)
    grad_up_bias = jnp.sum(hidden_grad.astype(jnp.float32), axis=0).reshape(up_bias.shape)
    second_grad = jnp.einsum(
        "tf,df->td", hidden_grad, up_weight, preferred_element_type=jnp.float32
    )
    second_in = head_share(second_grad)
    _, second_back = jax.vjp(layer_norm, middle, gain_two, shift_two)
    part_mid, grad_gain_two, grad_shift_two = second_back(second_in)
    middle_grad = final_grad + part_mid
    middle_low = spread_rows(middle_grad.astype(jnp.bfloat16))
    grad_proj = outer_sum(attended_low, middle_low)
    out_grads = jnp.einsum(
        "td,ed->te", middle_low, output_proj, preferred_element_type=jnp.float32
    ).astype(jnp.bfloat16)
    out_grads = out_grads.reshape(row_count, slot_width, head_count, HEAD_DIM)
    deltas = jnp.transpose(jnp.sum(out_grads.astype(jnp.float32) * attended, axis=-1), (0, 2, 1))
    back_keys, back_values, back_raw = (
        lax.all_gather(key_local, LON, axis=1, tiled=True),
        lax.all_gather(value_local, LON, axis=1, tiled=True),
        lax.all_gather(key_tags, LON, axis=1, tiled=True),
    )
    back_tags = back_raw.astype(jnp.float32)
    scale = HEAD_DIM ** (-0.5)
    key_count = back_keys.shape[1] // block_width
    local_zeros = jnp.zeros(queries.shape, jnp.float32)
    whole_zeros = jnp.zeros(back_keys.shape, jnp.float32)

    def both_step(running, block_index):
        query_acc, key_acc, value_acc = running
        key_block = block_slice(back_keys, block_index, block_width, 1)
        score_delta, weights_low = score_grads(
            queries,
            query_crops,
            out_grads,
            log_totals,
            deltas,
            key_block,
            block_slice(back_values, block_index, block_width, 1),
            block_slice(back_tags, block_index, block_width, 1),
        )
        query_acc = (
            query_acc
            + jnp.einsum(
                "rhqk,rkhd->rqhd", score_delta, key_block, preferred_element_type=jnp.float32
            )
            * scale
        )
        key_piece = (
            jnp.einsum("rhqk,rqhd->rkhd", score_delta, queries, preferred_element_type=jnp.float32)
            * scale
        )
        value_piece = jnp.einsum(
            "rhqk,rqhd->rkhd", weights_low, out_grads, preferred_element_type=jnp.float32
        )
        key_acc = lax.dynamic_update_slice_in_dim(key_acc, key_piece, block_index * block_width, 1)
        value_acc = lax.dynamic_update_slice_in_dim(
            value_acc, value_piece, block_index * block_width, 1
        )
        return ((query_acc, key_acc, value_acc), None)

    (query_grad, key_part, value_part), _ = lax.scan(
        both_step, (local_zeros, whole_zeros, whole_zeros), jnp.arange(key_count)
    )
    key_grad, value_grad = (
        lax.psum_scatter(
            key_part.astype(jnp.bfloat16), LON, scatter_dimension=1, tiled=True
        ).astype(jnp.float32),
        lax.psum_scatter(
            value_part.astype(jnp.bfloat16), LON, scatter_dimension=1, tiled=True
        ).astype(jnp.float32),
    )
    stacked = (
        jnp.stack([query_grad, key_grad, value_grad])
        .astype(jnp.bfloat16)
        .reshape(3, token_count, local_width)
    )
    first_grad = jnp.einsum(
        "kte,kde->td", stacked, input_weight, preferred_element_type=jnp.float32
    )
    grad_input = jnp.einsum("td,kte->kde", first_low, stacked, preferred_element_type=jnp.float32)
    first_in = head_share(first_grad)
    _, first_back = jax.vjp(layer_norm, start_sum, gain_one, shift_one)
    part_low, grad_gain_one, grad_shift_one = first_back(first_in)
    start_grad = middle_grad + part_low
    grad_lead = jnp.stack(
        [jnp.sum(start_grad * lead_rows[:, None], axis=0), jnp.sum(start_grad, axis=0)]
    )
    start_low = spread_rows(start_grad.astype(jnp.bfloat16))
    grad_mixer = outer_sum(mixed_low, start_low)
    mixed_grad = jnp.einsum(
        "td,ed->te", start_low, mixer_weight, preferred_element_type=jnp.float32
    ).astype(jnp.bfloat16)
    mixed_grad = mixed_grad.reshape(row_count, slot_width, head_count, HEAD_DIM)
    initial = (
        jnp.zeros(full_patch.shape, jnp.float32),
        jnp.zeros(full_variable.shape, jnp.float32),
        jnp.zeros(head_query.shape, jnp.float32),
        jnp.zeros(pair_weight.shape, jnp.float32),
    )
    mixer_step = partial(
        mixer_back,
        full_patch=full_patch,
        full_variable=full_variable,
        pair_weight=pair_weight,
        head_query=head_query,
    )
    (grad_patch, grad_variable, grad_query, grad_pair), slot_grads = lax.scan(
        mixer_step, initial, (patches, mixed_grad)
    )
    slot_total = head_total(slot_grads).reshape(row_count, slot_width, var_count, 2, 2)
    table_grads = jnp.einsum(
        "rjsa,rjvpx->svapjx", chosen.astype(jnp.float32), slot_total, precision=highest
    )
    side_grads = jnp.pad(
        table_grads[:, :, :, 0], ((0, 0), (0, 0), (0, 1), (0, 0), (0, 0))
    ) + jnp.pad(table_grads[:, :, :, 1], ((0, 0), (0, 0), (1, 0), (0, 0), (0, 0)))
    west_grad = side_grads[0].reshape(var_count, lat_count, 2 * slot_width)
    east_grad = side_grads[1].reshape(var_count, lat_count, 2 * slot_width)
    padded_grad = jnp.pad(west_grad, ((0, 0), (0, 0), (0, 2))) + jnp.pad(
        east_grad, ((0, 0), (0, 0), (2, 0))
    )
    rim_values = jnp.stack([padded_grad[:, :, 0], padded_grad[:, :, -1]], axis=2)
    returned = extended(rim_values, ((LON, 2),), 1)
    pixel_grad = (
        padded_grad[:, :, 1:-1]
        + jnp.pad(returned[:, :, 0:1], ((0, 0), (0, 0), (0, 2 * slot_width - 1)))
        + jnp.pad(returned[:, :, 3:4], ((0, 0), (0, 0), (2 * slot_width - 1, 0)))
    )
    sector_out = (
        lax.psum_scatter(
            grad_query.astype(jnp.bfloat16), LON, scatter_dimension=1, tiled=True
        ).astype(jnp.float32),
        lax.psum_scatter(
            grad_pair[:, :local_width].astype(jnp.bfloat16), LON, scatter_dimension=0, tiled=True
        ).astype(jnp.float32),
        lax.psum_scatter(
            grad_pair[:, local_width:].astype(jnp.bfloat16), LON, scatter_dimension=0, tiled=True
        ).astype(jnp.float32),
        lax.psum_scatter(
            grad_mixer.astype(jnp.bfloat16), LON, scatter_dimension=1, tiled=True
        ).astype(jnp.float32),
        lax.psum_scatter(
            grad_input.astype(jnp.bfloat16), LON, scatter_dimension=1, tiled=True
        ).astype(jnp.float32),
        lax.psum_scatter(
            grad_proj.astype(jnp.bfloat16), LON, scatter_dimension=1, tiled=True
        ).astype(jnp.float32),
        lax.psum_scatter(
            grad_up.astype(jnp.bfloat16), LON, scatter_dimension=0, tiled=True
        ).astype(jnp.float32),
        lax.psum_scatter(
            grad_up_bias.astype(jnp.bfloat16), LON, scatter_dimension=1, tiled=True
        ).astype(jnp.float32),
        lax.psum_scatter(
            grad_down.astype(jnp.bfloat16), LON, scatter_dimension=1, tiled=True
        ).astype(jnp.float32),
        lax.psum_scatter(
            grad_final_weight.astype(jnp.bfloat16), LON, scatter_dimension=0, tiled=True
        ).astype(jnp.float32),
    )
    shared_out = (
        lax.psum_scatter(grad_patch, (LON, HEAD), scatter_dimension=2, tiled=True),
        lax.psum_scatter(grad_variable, (LON, HEAD), scatter_dimension=1, tiled=True),
        lax.psum_scatter(grad_lead, (LON, HEAD), scatter_dimension=1, tiled=True),
        lax.psum_scatter(grad_gain_one, (LON, HEAD), scatter_dimension=0, tiled=True),
        lax.psum_scatter(grad_shift_one, (LON, HEAD), scatter_dimension=0, tiled=True),
        lax.psum_scatter(grad_gain_two, (LON, HEAD), scatter_dimension=0, tiled=True),
        lax.psum_scatter(grad_shift_two, (LON, HEAD), scatter_dimension=0, tiled=True),
    )
    return (
        predicted,
        pixel_grad,
        shared_out[0],
        shared_out[1],
        sector_out[0],
        sector_out[1],
        sector_out[2],
        sector_out[3],
        shared_out[2],
        shared_out[3],
        shared_out[4],
        sector_out[4],
        sector_out[5],
        shared_out[5],
        shared_out[6],
        sector_out[6],
        sector_out[7],
        sector_out[8],
        sector_out[9],
    )


MESH = pl.DeviceIdType.MESH
BOTH = (LON, HEAD)
LON_SIZE = 16
HEAD_SIZE = 2
CHUNK = 256
LATE_PAIRS = 1
low = jnp.bfloat16
wide = jnp.float32


def planned(mesh):
    return mesh.shape[LON] == LON_SIZE and mesh.shape[HEAD] == HEAD_SIZE


def dot(left, right, left_dim=1, right_dim=0):
    return lax.dot_general(
        left, right, (((left_dim,), (right_dim,)), ((), ())), preferred_element_type=wide
    )


def position():
    lon = lax.axis_index(LON)
    x = lax.axis_index(HEAD)
    z = lax.div(lon, 4)
    y = lax.rem(lax.div(lon, 2), 2)
    c = lax.rem(lon, 2)
    return x, z, y, c


def partners(x, z, y, c):
    here = z * 4 + y * 2 + c
    across = {
        "x": (here, 1 - x),
        "y": (z * 4 + (1 - y) * 2 + c, x),
        "c": (z * 4 + y * 2 + 1 - c, x),
    }
    line = [(lax.rem(z + step, 4) * 4 + y * 2 + c, x) for step in (1, 2, 3)]
    return across, line


def sector_of(z, y, c, x, part, side):
    return (y * 2 + c) * 4 + x * 2 + part, side


def block_of(z, y, row):
    return row * 4 + z, y


def meet(peers, others=(), own=None):
    barrier = pltpu.get_barrier_semaphore()
    for device in peers:
        pl.semaphore_signal(barrier, inc=1, device_id=device, device_id_type=MESH)
    for device in others:

        @pl.when(jnp.logical_not(same(device, own)))
        def _():
            pl.semaphore_signal(barrier, inc=1, device_id=device, device_id_type=MESH)

    expected = len(peers)
    for device in others:
        expected = expected + 1 - same(device, own).astype(jnp.int32)
    pl.semaphore_wait(barrier, expected)


def same(device, own):
    return jnp.logical_and(device[0] == own[0], device[1] == own[1])


def post(source, target, send_sem, recv_sem, device, own):
    here = same(device, own)

    @pl.when(here)
    def _():
        pltpu.make_async_copy(source, target, recv_sem).start()

    @pl.when(jnp.logical_not(here))
    def _():
        remote(source, target, send_sem, recv_sem, device).start()


def settle(source, target, send_sem, recv_sem, device, own):
    @pl.when(jnp.logical_not(same(device, own)))
    def _():
        remote(source, target, send_sem, recv_sem, device).wait_send()


def remote(source, target, send_sem, recv_sem, device):
    return pltpu.make_async_remote_copy(
        src_ref=source,
        dst_ref=target,
        send_sem=send_sem,
        recv_sem=recv_sem,
        device_id=device,
        device_id_type=MESH,
    )


def gatherer(views, sems):
    own_sem, line_send, line_recv, hop_send, hop_recv = sems
    x, z, y, c = position()
    across, line = partners(x, z, y, c)

    def keep(number):
        source, target, span, _ = views(number)
        return pltpu.make_async_copy(source, target.at[x, z, y, c, span], own_sem.at[number])

    def along(number, d):
        source, target, span, _ = views(number)
        return remote(
            source,
            target.at[x, z, y, c, span],
            line_send.at[number, d],
            line_recv.at[number, d],
            line[d],
        )

    def hop(number, k):
        _, target, span, color = views(number)
        if k == 0:
            part, axis = target.at[x, :, y, c, span], "yx"[color]
        elif k == 1 and color == 0:
            part, axis = target.at[x, :, :, c, span], "x"
        elif k == 1:
            part, axis = target.at[:, :, y, c, span], "y"
        else:
            part, axis = target.at[:, :, :, c, span], "c"
        return remote(
            part, part, hop_send.at[number, k], hop_recv.at[number, k], across[axis]
        )

    def begin(number):
        keep(number).start()
        for d in range(3):
            along(number, d).start()

    def spread(number):
        keep(number).wait()
        for d in range(3):
            along(number, d).wait_recv()
        hop(number, 0).start()

    def widen(number):
        hop(number, 0).wait_recv()
        hop(number, 1).start()

    def pair_up(number):
        hop(number, 1).wait_recv()
        hop(number, 2).start()

    def close(number):
        hop(number, 2).wait_recv()

    def finish(number):
        for k in range(3):
            along(number, k).wait_send()
            hop(number, k).wait_send()

    return (begin, spread, widen, pair_up, close), finish


def reduce_kernel(chunks, count, *refs):
    ins, refs = refs[:count], refs[count:]
    value_in, key_weight, value_weight, input_weight, back_weight, refs = refs[:5] + (refs[5:],)
    lat_ref, shift_ref, refs = refs[:2] + (refs[2:],)
    patch_ref, prob_ref, score_table, value_table, key_table, mixed_ref, refs = refs[:6] + (
        refs[6:],
    )
    full_ref, query_ref, second_ref, rest_ref, bias_ref, refs = refs[:5] + (refs[5:],)
    stacked_ref, low_ref, start_ref, middle_ref, vector_ref, lead_ref, refs = refs[:6] + (refs[6:],)
    out, value_out, pixel_out, refs = refs[:3] + (refs[3:],)
    buffers, sems, refs = refs[:6], refs[6:13], refs[13:]
    grad_out, field, edge, west_edge, east_edge, refs = refs[:5] + (refs[5:],)
    value_send, value_recv, grad_send, grad_recv, edge_send, edge_recv, refs = refs[:6] + (
        refs[6:],
    )
    grad_in, pooled_ref, count_ref, patch_grad, weight_a, weight_b, key_low, query_grad = refs[:8]
    input_ref, mixer_ref, values_ref, tail_ref, load_sem, first_ref, mixed_grad, turned, total_ref = (
        refs[8:]
    )
    ins = ins + (input_ref, mixer_ref, values_ref, tail_ref)
    x, z, y, c = position()
    across, line = partners(x, z, y, c)
    lon = z * 4 + y * 2 + c
    own = (lon, x)
    east, west = (lax.rem(lon + 1, 16), x), (lax.rem(lon + 15, 16), x)
    sources = [block_of(z, y, row) for row in range(4)]
    meet(list(across.values()) + line + [east, west], sources, own)
    letters = []
    for part in range(2):
        for side in range(2):
            device = sector_of(z, y, c, x, part, side)
            at = 2 * part + side
            letters.append(
                (grad_in.at[part], grad_out.at[z], grad_send.at[at], grad_recv.at[z])
                + (device, own)
            )
            letters.append(
                (value_in.at[side, part], value_out.at[z], value_send.at[at], value_recv.at[z])
                + (device, own)
            )
    for letter in letters[1::2]:
        post(*letter)
    total = len(chunks)
    weights = (weight_a, weight_b)
    queue = [input_weight.at[0], input_weight.at[1], input_weight.at[2], back_weight]
    queue += [key_weight, value_weight]

    def load(number):
        return pltpu.make_async_copy(queue[number], weights[number % 2], load_sem.at[number % 2])

    load(0).start()
    load(1).start()
    half_width = weight_a.shape[-1]

    def input_grads(kind):
        if kind == 0:
            turned[...] = low_ref[...].T
            total_ref[...] = jnp.zeros_like(total_ref)
        load(kind).wait()
        pairs = half_width // stacked_ref.shape[-1]
        for side in range(2):
            piece = jnp.concatenate(
                [stacked_ref[side * pairs + pair, kind] for pair in range(pairs)], axis=1
            )
            total_ref[...] += dot(piece, weights[kind % 2][side], 1, 1)
            grads = dot(turned[...], piece).astype(low)
            input_ref[2 * kind + side] = grads.reshape(input_ref.shape[1:])
        load(kind + 2).start()

    def start_grads():
        part, grad_gain, grad_shift = norm_back(start_ref[...], vector_ref[2:3], total_ref[...])
        result = middle_ref[...] + part
        first_ref[0:1] = jnp.sum(result * lead_ref[...], axis=0, keepdims=True)
        first_ref[1:2] = jnp.sum(result, axis=0, keepdims=True)
        first_ref[2:3] = grad_gain
        first_ref[3:4] = grad_shift
        result_low = result.astype(low)
        turned[...] = result_low.T
        load(3).wait()
        for side in range(2):
            span = slice(side * half_width, (side + 1) * half_width)
            grads = dot(turned[...], mixed_ref[span, :], 1, 1).astype(low)
            mixer_ref[side] = grads.reshape(mixer_ref.shape[1:])
            mixed_grad[span, :] = dot(result_low, weight_b[side]).astype(low).T
        load(5).start()
    head_total, var_total, tokens = prob_ref.shape
    padded = patch_ref.shape[0]
    scale = HEAD_DIM ** (-0.5)

    def halves_of(values):
        upper = values.astype(low)
        return upper, (values - upper.astype(wide)).astype(low)

    def heads(first):
        mask = diagonal(var_total, padded)
        if first == 0:
            patch_grad[...] = jnp.zeros_like(patch_grad)
            query_grad[...] = jnp.zeros_like(query_grad)

        def head_step(h, carry):
            span = pl.ds(pl.multiple_of(h * HEAD_DIM, HEAD_DIM), HEAD_DIM)
            grads = mixed_grad[span, :]
            prob = prob_ref[h]
            back = dot(value_table[span, :], grads, 0, 0)
            pieces = [
                patch_ref[k * var_total : (k + 1) * var_total, :].astype(wide) for k in range(5)
            ]
            backs = [back[k * var_total : (k + 1) * var_total, :] for k in range(5)]
            prob_grad = pieces[0] * backs[0]
            for k in range(1, 5):
                prob_grad = prob_grad + pieces[k] * backs[k]
            mean = jnp.sum(prob * prob_grad, axis=0, keepdims=True)
            upper, lower = halves_of(prob * (prob_grad - mean))
            spread = jnp.where(mask, score_table[pl.ds(h, 1), :], 0.0).astype(low)
            patch_grad[...] += dot(spread, upper, 0, 0)
            for k in range(4):
                patch_grad[k * var_total : (k + 1) * var_total, :] += prob * backs[k]
            patch = patch_ref[...]
            counts = dot(upper, patch, 1, 1) + dot(lower, patch, 1, 1)
            counts = jnp.sum(jnp.where(mask, counts, 0.0), axis=0, keepdims=True) * scale
            count_ref[pl.ds(h, 1), :] = counts
            table = key_table[span, :].astype(low)
            upper, lower = halves_of(counts)
            query_grad[pl.ds(h, 1), :HEAD_DIM] = dot(upper, table, 1, 1) + dot(lower, table, 1, 1)
            pooled = jnp.concatenate(
                [(prob * piece).astype(low) for piece in pieces]
                + [jnp.zeros((padded - 5 * var_total, tokens), low)],
                axis=0,
            )
            pooled_ref[span, :] = dot(grads, pooled, 1, 1).astype(low)
            return carry

        lax.fori_loop(first, first + head_total // 4, head_step, 0)

    def send_cut():
        taps = 4 * var_total
        for part in range(2):
            grad_in[part] = patch_grad[:taps, part * 128 : (part + 1) * 128].astype(low)
        for letter in letters[0::2]:
            post(*letter)

    def value_grads():
        rows = full_ref.shape[0] // 4
        for part in range(4):
            piece = dot(full_ref[part * rows : (part + 1) * rows, :], pooled_ref[...], 1, 1)
            values_ref[part] = piece.astype(low).reshape(values_ref.shape[1:])

    def tail_grads():
        load(4).wait()
        load(5).wait()
        wide_query = jnp.concatenate([query_ref[...]] * (head_total * HEAD_DIM // 128), axis=1)
        head = lax.div(lax.broadcasted_iota(jnp.int32, wide_query.shape, 1), HEAD_DIM)
        row = lax.broadcasted_iota(jnp.int32, wide_query.shape, 0)
        wide_query = jnp.where(head == row, wide_query, 0.0).astype(low)
        count_parts = halves_of(count_ref[...])
        key_low[...] = sum(dot(wide_query, part, 0, 0) for part in count_parts).astype(low)
        spots = lax.broadcasted_iota(jnp.int32, (8, padded), 1) - 5 * var_total
        kinds = lax.broadcasted_iota(jnp.int32, (8, padded), 0)
        vectors = jnp.concatenate(
            [first_ref[...], second_ref[...], jnp.zeros((2, first_ref.shape[1]), wide)], axis=0
        )
        result = dot(vectors.astype(low), jnp.where(spots == kinds, 1.0, 0.0).astype(low), 0, 0)
        for side in range(2):
            span = slice(side * half_width, (side + 1) * half_width)
            result = result + dot(weight_a[side], key_low[span, :])
            result = result + dot(weight_b[side], pooled_ref[span, :])
        result = result.astype(low)
        sector = tail_ref.shape[-2] // 2
        for place in range(16):
            at = (place // 4, place // 2 % 2, place % 2)
            for side in range(2):
                first = (2 * place + side) * sector
                for half in range(2):
                    tail_ref[
                        (side,) + at + (slice(half * sector, (half + 1) * sector), slice(0, 128))
                    ] = result[first : first + sector, half * 128 : (half + 1) * 128]

    def rest_grads():
        used = rest_ref.shape[2] - 32
        head_half = head_total // 2
        model = full_ref.shape[0]
        count_parts = halves_of(count_ref[...])
        head = lax.broadcasted_iota(jnp.int32, (head_total, 128), 0)
        lane = lax.broadcasted_iota(jnp.int32, (head_total, 128), 1)
        rows = lax.broadcasted_iota(jnp.int32, (model, head_total), 0)
        columns = lax.broadcasted_iota(jnp.int32, (model, head_total), 1)
        inner = lax.rem(rows, model // 16)
        sectors = lax.div(lax.broadcasted_iota(jnp.int32, (model, 128), 0), model // 16)
        lanes_at = lax.broadcasted_iota(jnp.int32, (model, 128), 1)
        source_lane = lax.broadcasted_iota(jnp.int32, (128, 128), 0)
        target_lane = lax.broadcasted_iota(jnp.int32, (128, 128), 1)
        query_at = used + head_half + 4
        move = jnp.where(target_lane == query_at + lax.rem(source_lane, 4), 1.0, 0.0).astype(low)
        for side in range(2):
            spot = used + head - head_half * side
            inside = lax.div(head, head_half) == side
            target = jnp.where(jnp.logical_and(inside, lane == spot), 1.0, 0.0).astype(low)
            sums = sum(dot(part, target, 0, 0) for part in count_parts)
            result = rest_ref[side].astype(wide) + bias_ref[side].astype(wide)
            for part in halves_of(sums):
                result = result + dot(full_ref[...], part)
            chosen = jnp.logical_and(inner < head_half, columns == inner + head_half * side)
            spread = dot(jnp.where(chosen, 1.0, 0.0).astype(low), query_grad[...].astype(low))
            spread = jnp.where(lax.div(lanes_at, 4) == sectors, spread, 0.0).astype(low)
            result = result + dot(spread, move)
            tail_ref[side, :, :, :, :, 128:] = result.astype(low).reshape(
                tail_ref.shape[1:-1] + (128,)
            )

    lat_count, var_count, lanes = field.shape
    half = lanes // 2
    column_count = pixel_out.shape[2]

    def paste(row):
        pltpu.make_async_copy(grad_in.at[0], grad_out.at[row], grad_recv.at[row]).wait()
        lat = lat_ref[row : row + 1, :]
        going_west = shift_ref[row : row + 1, :] < 0
        lat_both = jnp.concatenate([lat, lat], axis=1)
        both = []
        for py in range(2):
            k = 2 * py
            grads = jnp.concatenate(
                [
                    grad_out[row, k * var_count : (k + 1) * var_count, :].astype(wide),
                    grad_out[row, (k + 1) * var_count : (k + 2) * var_count, :].astype(wide),
                ],
                axis=1,
            )
            left = jnp.where(going_west, grads, 0.0)
            both.append(jnp.concatenate([left, grads - left], axis=1))

        def body(b, carry):
            piece = jnp.where(lat_both == b, both[0], 0.0) + jnp.where(
                lat_both == b - 1, both[1], 0.0
            )
            if row == 0:
                field[b] = piece
            else:
                field[b] += piece
            return carry

        lax.fori_loop(0, lat_count, body, 0)

    def thirds(values):
        one = values.astype(low)
        rest = values - one.astype(wide)
        two = rest.astype(low)
        return one, two, (rest - two.astype(wide)).astype(low)

    def edges():
        kind = lax.broadcasted_iota(jnp.int32, (8, lanes), 0)
        wanted = columns_of((8, lanes), 1, half)
        pick = jnp.where(
            jnp.logical_or(
                jnp.logical_and(kind == 0, wanted == -1),
                jnp.logical_and(kind == 1, wanted == column_count),
            ),
            1.0,
            0.0,
        ).astype(low)
        flat = field[...].reshape(lat_count * var_count, lanes)
        one, two, three = thirds(flat)
        edge[...] = dot(pick, one, 1, 1) + dot(pick, two, 1, 1) + dot(pick, three, 1, 1)
        remote(edge, west_edge, edge_send.at[0], edge_recv.at[0], east).start()
        remote(edge, east_edge, edge_send.at[1], edge_recv.at[1], west).start()

    def pixels():
        remote(edge, west_edge, edge_send.at[0], edge_recv.at[0], east).wait()
        remote(edge, east_edge, edge_send.at[1], edge_recv.at[1], west).wait()
        wanted = columns_of((lanes, column_count), 0, half)
        column = lax.broadcasted_iota(jnp.int32, (lanes, column_count), 1)
        place = jnp.where(wanted == column, 1.0, 0.0).astype(low)
        kind = lax.broadcasted_iota(jnp.int32, (8, column_count), 0)
        column = lax.broadcasted_iota(jnp.int32, (8, column_count), 1)
        from_west = jnp.logical_and(kind == 1, column == 0)
        from_east = jnp.logical_and(kind == 0, column == column_count - 1)
        west_place = jnp.where(from_west, 1.0, 0.0).astype(low)
        east_place = jnp.where(from_east, 1.0, 0.0).astype(low)
        borders = None
        for values, target in ((west_edge[...], west_place), (east_edge[...], east_place)):
            for part in thirds(values):
                piece = dot(part, target, 0, 0)
                borders = piece if borders is None else borders + piece
        pixel_out[...] = borders.reshape(pixel_out.shape)

        def body(b, carry):
            result = pixel_out[b]
            for part in thirds(field[b]):
                result = result + dot(part, place)
            pixel_out[b] = result
            return carry

        lax.fori_loop(0, lat_count, body, 0)

    quarter = head_total // 4
    extra = {kind: partial(input_grads, kind) for kind in range(3)}
    extra[3] = start_grads
    extra.update({4 + step: partial(heads, step * quarter) for step in range(4)})
    extra.update({8: lambda: (send_cut(), value_grads()), 9: tail_grads, 10: rest_grads})
    extra.update({12 + row: partial(paste, row) for row in range(3)})
    extra.update({15: lambda: (paste(3), edges()), 18: pixels})

    def source_of(pair, color, side, core):
        index, lead, offset = chunks[2 * pair + color][side]
        source = ins[index] if lead is None else ins[index].at[lead]
        return source.at[:, :, core, :, pl.ds(offset, CHUNK)]

    begin, stage_core, stage_first, stage_second, stage_third, finish = reducer(
        source_of, buffers, sems, out
    )
    plan = ((0, begin), (2, stage_core), (4, stage_first), (6, stage_second), (8, stage_third))
    for step in range(total + 8):
        for back, stage in plan:
            if 0 <= step - back < total:
                stage((step - back) // 2, (step - back) % 2)
        if step in extra:
            extra[step]()
    for k in range(total):
        finish(k // 2, k % 2)
    for letter in letters:
        settle(*letter)
    for row in range(4):
        pltpu.make_async_copy(value_in.at[0, 0], value_out.at[row], value_recv.at[row]).wait()


def reduce_all(feed_grads, item, values, weights, lat_lanes, shift_lanes, mixer, rest, block, lat_count, number):
    chunks = []
    model, half = item.shape[-2:]
    views = [
        part.reshape((-1, 4, 2, 2, model // 16, part.shape[-1])) for part in (feed_grads, item)
    ]
    kinds = weights[2].shape[0]
    columns = feed_grads.shape[-1]
    for offset in range(columns - 2 * LATE_PAIRS * CHUNK, columns, CHUNK):
        chunks.append(((0, 2, offset), (0, 3, offset)))
    for index, leads in ((1, 1), (2, kinds), (3, 1)):
        for first in range(0, 2 * leads, 2):
            for offset in range(0, half, CHUNK):
                chunks.append(((index, first, offset), (index, first + 1, offset)))
    count = len(views)
    for offset in range(0, half, CHUNK):
        chunks.append(((4, None, offset), (4, None, half + offset)))
    chunks.append(((5, 0, 0), (5, 1, 0)))
    total = len(chunks)
    rows = views[0].shape[-2]
    probs = mixer[1]
    head_count, var_count, tokens = probs.shape
    padded = mixer[0].shape[0]
    lanes = 2 * lat_lanes.shape[1]
    columns = lat_lanes.shape[1]
    cut = (4, 4 * var_count, 128)
    vmem = pl.BlockSpec(memory_space=pltpu.VMEM)
    hbm = pl.BlockSpec(memory_space=pl.ANY)
    sem = pltpu.SemaphoreType.DMA
    return pl.pallas_call(
        partial(reduce_kernel, chunks, count),
        out_shape=[
            jax.ShapeDtypeStruct((rows, total * CHUNK), wide),
            jax.ShapeDtypeStruct((4,) + values.shape[2:], values.dtype),
            jax.ShapeDtypeStruct((lat_count, var_count, columns), wide),
        ],
        in_specs=[hbm] * (count + 5) + [vmem] * (2 + len(mixer) + len(rest) + len(block)),
        out_specs=[vmem, hbm, vmem],
        scratch_shapes=reducer_scratch(total, rows)
        + [
            pltpu.VMEM(cut, low),
            pltpu.VMEM((lat_count, var_count, lanes), wide),
            pltpu.VMEM((8, lat_count * var_count), wide),
            pltpu.VMEM((8, lat_count * var_count), wide),
            pltpu.VMEM((8, lat_count * var_count), wide),
            sem((4,)),
            sem((4,)),
            sem((4,)),
            sem((4,)),
            sem((2,)),
            sem((2,)),
            pltpu.VMEM((2,) + cut[1:], low),
            pltpu.VMEM((model, padded), low),
            pltpu.VMEM((head_count, padded), wide),
            pltpu.VMEM((padded, tokens), wide),
            pltpu.VMEM(weights[0].shape, low),
            pltpu.VMEM(weights[0].shape, low),
            pltpu.VMEM((model, padded), low),
            pltpu.VMEM((head_count, 128), wide),
            pltpu.VMEM((2 * kinds, 4, 2, 2, rows, half), low),
            pltpu.VMEM((2, 4, 2, 2, rows, half), low),
            pltpu.VMEM((4, 2, 2, rows, 2 * half), low),
            pltpu.VMEM((2, 4, 2, 2, rows, CHUNK), low),
            sem((2,)),
            pltpu.VMEM((4, model), wide),
            pltpu.VMEM((model, tokens), low),
            pltpu.VMEM((model, tokens), low),
            pltpu.VMEM((tokens, model), wide),
        ],
        compiler_params=pltpu.CompilerParams(
            collective_id=number, has_side_effects=True, vmem_limit_bytes=63 * 2**20
        ),
    )(*views, values, *weights, lat_lanes, shift_lanes, *mixer, *rest, *block)


def diagonal(var_count, columns):
    column = lax.broadcasted_iota(jnp.int32, (var_count, columns), 1)
    row = lax.broadcasted_iota(jnp.int32, (var_count, columns), 0)
    return (lax.rem(column, var_count) == row) & (column < 5 * var_count)


def head_lanes(values, h):
    lane = lax.broadcasted_iota(jnp.int32, values.shape, values.ndim - 1)
    inside = lane < HEAD_DIM if h == 0 else lane >= HEAD_DIM
    return jnp.where(inside, values, jnp.zeros_like(values))


def plane_device(z, index):
    return z * 4 + lax.div(index, 2), lax.rem(index, 2)


def plane_meet(x, z, y, c):
    barrier = pltpu.get_barrier_semaphore()
    for flip in range(1, 8):
        there_y = 1 - y if flip & 4 else y
        there_c = 1 - c if flip & 2 else c
        there_x = 1 - x if flip & 1 else x
        device = (z * 4 + there_y * 2 + there_c, there_x)
        pl.semaphore_signal(barrier, inc=1, device_id=device, device_id_type=MESH)
    return barrier


def joined(left, right):
    return (left.astype(wide) + right.astype(wide)).astype(low)


def reducer(source_of, buffers, sems, out):
    mine, other, first_a, first_b, second, third = buffers
    own_sem, core_send, core_recv, hop_send, hop_recv, line_send, line_recv = sems
    x, z, y, c = position()
    across, line = partners(x, z, y, c)

    def keeps(pair, color):
        k = 2 * pair + color
        return [
            pltpu.make_async_copy(
                source_of(pair, color, side, c), mine.at[2 * k + side], own_sem.at[k, side]
            )
            for side in range(2)
        ]

    def swaps(pair, color):
        k = 2 * pair + color
        return [
            remote(
                source_of(pair, color, side, 1 - c),
                other.at[2 * k + side],
                core_send.at[k, side],
                core_recv.at[k, side],
                across["c"],
            )
            for side in range(2)
        ]

    def hop_one(pair, color):
        k = 2 * pair + color
        if color == 0:
            source, target, axis = mine.at[2 * k + 1 - x], first_a.at[pair], "x"
        else:
            source = mine.at[pl.ds(2 * k, 2), :, 1 - y]
            target, axis = first_b.at[pair], "y"
        return remote(source, target, hop_send.at[k, 0], hop_recv.at[k, 0], across[axis])

    def hop_two(pair, color):
        k = 2 * pair + color
        if color == 0:
            source, axis = mine.at[2 * k + x, :, 1 - y], "y"
        else:
            source, axis = mine.at[2 * k + 1 - x, :, y], "x"
        return remote(source, second.at[k], hop_send.at[k, 1], hop_recv.at[k, 1], across[axis])

    def along(pair, color):
        k = 2 * pair + color
        return [
            remote(
                mine.at[2 * k + x, lax.rem(z + d + 1, 4), y],
                third.at[k, d],
                line_send.at[k, d],
                line_recv.at[k, d],
                line[d],
            )
            for d in range(3)
        ]

    def begin(pair, color):
        for copy in swaps(pair, color) + keeps(pair, color):
            copy.start()

    def stage_core(pair, color):
        k = 2 * pair + color
        for copy in keeps(pair, color):
            copy.wait()
        for copy in swaps(pair, color):
            copy.wait_recv()

        def body(step, carry):
            side, row = lax.div(step, 4), lax.rem(step, 4)
            for part in range(2):
                mine[2 * k + side, row, part] = joined(
                    mine[2 * k + side, row, part], other[2 * k + side, row, part]
                )
            return carry

        lax.fori_loop(0, 8, body, 0)
        hop_one(pair, color).start()

    def stage_first(pair, color):
        k = 2 * pair + color
        hop_one(pair, color).wait_recv()

        def body(row, carry):
            for part in range(2):
                if color == 0:
                    mine[2 * k + x, row, part] = joined(
                        mine[2 * k + x, row, part], first_a[pair, row, part]
                    )
                else:
                    mine[2 * k + part, row, y] = joined(
                        mine[2 * k + part, row, y], first_b[pair, part, row]
                    )
            return carry

        lax.fori_loop(0, 4, body, 0)
        hop_two(pair, color).start()

    def stage_second(pair, color):
        k = 2 * pair + color
        hop_two(pair, color).wait_recv()

        def body(row, carry):
            mine[2 * k + x, row, y] = joined(mine[2 * k + x, row, y], second[k, row])
            return carry

        lax.fori_loop(0, 4, body, 0)
        for copy in along(pair, color):
            copy.start()

    def stage_third(pair, color):
        k = 2 * pair + color
        for copy in along(pair, color):
            copy.wait_recv()
        result = mine[2 * k + x, z, y].astype(wide)
        for d in range(3):
            result = result + third[k, d].astype(wide)
        start = k * CHUNK
        if not isinstance(k, int):
            start = pl.multiple_of(start, CHUNK)
        out[:, pl.ds(start, CHUNK)] = result

    def finish(pair, color):
        hop_one(pair, color).wait_send()
        hop_two(pair, color).wait_send()
        for copy in swaps(pair, color) + along(pair, color):
            copy.wait_send()

    return begin, stage_core, stage_first, stage_second, stage_third, finish


def reducer_scratch(total, rows):
    sem = pltpu.SemaphoreType.DMA
    pairs = (total + 1) // 2
    return [
        pltpu.VMEM((2 * total, 4, 2, rows, CHUNK), low),
        pltpu.VMEM((2 * total, 4, 2, rows, CHUNK), low),
        pltpu.VMEM((pairs, 4, 2, rows, CHUNK), low),
        pltpu.VMEM((pairs, 2, 4, rows, CHUNK), low),
        pltpu.VMEM((total, 4, rows, CHUNK), low),
        pltpu.VMEM((total, 3, rows, CHUNK), low),
    ] + [
        sem((total, 2)),
        sem((total, 2)),
        sem((total, 2)),
        sem((total, 2)),
        sem((total, 2)),
        sem((total, 3)),
        sem((total, 3)),
    ]


def attend_back_kernel(
    joint,
    tag_ref,
    crop_ref,
    out_ref,
    total_ref,
    source,
    feed_ref,
    stacked,
    sums,
    grads,
    result,
    key_acc,
    value_acc,
    *rest
):
    buffers, sems = rest[:6], rest[6:13]
    in_own, in_send, in_recv, back_own, back_send, back_recv = rest[13:]
    x, z, y, c = position()
    across, line = partners(x, z, y, c)
    me = y * 4 + c * 2 + x
    peers, kinds, share, lanes = joint.shape
    slots = peers * share
    scale = HEAD_DIM ** (-0.5)
    each = feed_ref.shape[-1] // CHUNK

    def source_of(pair, color, side, core):
        k = 2 * pair + color
        offset = pl.multiple_of(lax.rem(k, each) * CHUNK, CHUNK)
        return feed_ref.at[lax.div(k, each), side, :, :, core, :, pl.ds(offset, CHUNK)]

    begin, stage_core, stage_first, stage_second, stage_third, finish = reducer(
        source_of, buffers, sems, sums
    )
    keep = pltpu.make_async_copy(source.at[me], grads.at[me], in_own)
    keep.start()
    barrier = plane_meet(x, z, y, c)
    for device in line:
        pl.semaphore_signal(barrier, inc=1, device_id=device, device_id_type=MESH)
    pl.semaphore_wait(barrier, peers - 1 + len(line))

    def inward(there):
        return remote(
            source.at[there],
            grads.at[me],
            in_send.at[there],
            in_recv.at[me],
            plane_device(z, there),
        )

    def outward(there, part):
        span = pl.ds(0, 1) if part == 0 else pl.ds(1, 2)
        return remote(
            result.at[there, span],
            stacked.at[me, span],
            back_send.at[there, part],
            back_recv.at[me, part],
            plane_device(z, there),
        )

    for step in range(1, peers):
        inward(lax.rem(me + step, peers)).start()
    key_acc[...] = jnp.zeros_like(key_acc)
    value_acc[...] = jnp.zeros_like(value_acc)
    pairs = feed_ref.shape[0] * each // 2 - LATE_PAIRS

    def attention(index):
        span = pl.ds(pl.multiple_of(index * share, share), share)
        queries = joint[index, 0]
        keys = joint[:, 1].reshape(slots, lanes)
        values = joint[:, 2].reshape(slots, lanes)
        grad = grads[index]
        product = grad.astype(wide) * out_ref[span, :]
        allowed = crop_ref[span, :] == tag_ref[0:1, :]
        query_grad = None
        for h in range(2):
            query_part, grad_part = head_lanes(queries, h), head_lanes(grad, h)
            scores = jnp.where(allowed, dot(query_part, keys, 1, 1), masked_score)
            weights = jnp.exp(scores - total_ref[h, span, :])
            weight_grads = dot(grad_part, values, 1, 1)
            delta = jnp.sum(head_lanes(product, h), axis=1, keepdims=True)
            score_grads = (weights * (weight_grads - delta)).astype(low)
            weights = weights.astype(low)
            value_acc[...] += dot(grad_part, weights, 0, 0)
            key_acc[...] += dot(query_part, score_grads, 0, 0)
            part = head_lanes(dot(score_grads, keys), h)
            query_grad = part if query_grad is None else query_grad + part
        result[index, 0] = (query_grad * scale).astype(low)

    def step_body(step, carry):
        @pl.when(step < pairs)
        def _():
            begin(step, 0)
            begin(step, 1)

        for back, stage in ((1, stage_core), (2, stage_first), (3, stage_second), (4, stage_third)):

            @pl.when(jnp.logical_and(step >= back, step < pairs + back))
            def _():
                stage(step - back, 0)
                stage(step - back, 1)

        @pl.when(step < peers)
        def _():
            index = lax.rem(me + step, peers)

            @pl.when(step == 0)
            def _():
                keep.wait()

            @pl.when(step > 0)
            def _():
                pltpu.make_async_copy(
                    grads.at[index], grads.at[index], in_recv.at[index]
                ).wait()

            attention(index)

            @pl.when(step > 0)
            def _():
                outward(index, 0).start()

        @pl.when(step == peers - 1)
        def _():
            for index in range(peers):
                span = slice(index * share, (index + 1) * share)
                result[index, 1] = key_acc[:, span].T.astype(low)
                result[index, 2] = value_acc[:, span].T.astype(low)
            for other in range(1, peers):
                outward(lax.rem(me + other, peers), 1).start()
            pltpu.make_async_copy(result.at[me], stacked.at[me], back_own).start()

        return carry

    lax.fori_loop(0, pairs + 4, step_body, 0)

    def finish_body(pair, carry):
        finish(pair, 0)
        finish(pair, 1)
        return carry

    lax.fori_loop(0, pairs, finish_body, 0)
    for step in range(1, peers):
        there = lax.rem(me + step, peers)
        inward(there).wait_send()
        for part in range(2):
            outward(there, part).wait_send()
            span = pl.ds(0, 1) if part == 0 else pl.ds(1, 2)
            pltpu.make_async_copy(
                result.at[there, span], stacked.at[there, span], back_recv.at[there, part]
            ).wait()
    pltpu.make_async_copy(result.at[me], stacked.at[me], back_own).wait()


def attend_back(joint, tags, crops, outputs, totals, source, feed_grads, number):
    peers, kinds, share, lanes = joint.shape
    slots = peers * share
    sides, halves, rows, columns = feed_grads.shape
    total = sides * columns // CHUNK - 2 * LATE_PAIRS
    sem = pltpu.SemaphoreType.DMA
    vmem = pl.BlockSpec(memory_space=pltpu.VMEM)
    hbm = pl.BlockSpec(memory_space=pl.ANY)
    return pl.pallas_call(
        attend_back_kernel,
        out_shape=[
            jax.ShapeDtypeStruct(joint.shape, low),
            jax.ShapeDtypeStruct((rows // 16, total * CHUNK), wide),
        ],
        in_specs=[vmem] * 5 + [hbm] * 2,
        out_specs=[hbm, vmem],
        scratch_shapes=[
            pltpu.VMEM((peers, share, lanes), low),
            pltpu.VMEM(joint.shape, low),
            pltpu.VMEM((lanes, slots), wide),
            pltpu.VMEM((lanes, slots), wide),
        ]
        + reducer_scratch(total, rows // 16)
        + [
            sem,
            sem((peers,)),
            sem((peers,)),
            sem,
            sem((peers, 2)),
            sem((peers, 2)),
        ],
        compiler_params=pltpu.CompilerParams(
            collective_id=number, has_side_effects=True, vmem_limit_bytes=60 * 2**20
        ),
    )(
        joint,
        tags,
        crops,
        outputs,
        totals,
        source,
        feed_grads.reshape(sides, halves, 4, 2, 2, rows // 16, columns),
    )


def whole(array):
    rank = len(array.shape)
    return pl.BlockSpec(array.shape, lambda *_: (0,) * rank)


def norm_parts(values):
    center = values - jnp.mean(values, axis=-1, keepdims=True)
    inverse = lax.rsqrt(jnp.mean(center * center, axis=-1, keepdims=True) + epsilon)
    return center * inverse, inverse


def norm_back(values, gain, grads):
    normed, inverse = norm_parts(values)
    scaled = grads * gain
    inner = (
        scaled
        - jnp.mean(scaled, axis=-1, keepdims=True)
        - normed * jnp.mean(scaled * normed, axis=-1, keepdims=True)
    )
    return (
        inner * inverse,
        jnp.sum(grads * normed, axis=0, keepdims=True),
        jnp.sum(grads, axis=0, keepdims=True),
    )


def columns_of(shape, axis, half):
    spot = lax.broadcasted_iota(jnp.int32, shape, axis)
    side, spot = lax.div(spot, half), lax.rem(spot, half)
    slots = half // 2
    return 2 * lax.rem(spot, slots) + 2 * side + lax.div(spot, slots) - 1


def front_kernel(items, *refs):
    arrays, refs = refs[:8], refs[8:]
    grad_in, hour_ref, pixel_ref, lat_ref, shift_ref, refs = refs[:5] + (refs[5:],)
    outs, grad_out, received, refs = refs[:8], refs[8], refs[9], refs[10:]
    joint, wide_ref, total_ref, tag_ref, crop_ref, refs = refs[:5] + (refs[5:],)
    patch_ref, prob_ref, mixed_ref, value_table, key_table, score_table, refs = refs[:6] + (
        refs[6:],
    )
    full_ref, vector_ref, query_ref, start_ref, low_ref, lead_ref, keep_ref, refs = refs[:7] + (
        refs[7:],
    )
    cut_ref, misc_ref, small_ref, weight_a, weight_b, projected, sending, turned, refs = refs[
        :8
    ] + (refs[8:],)
    gather_sems, refs = refs[:5], refs[5:]
    post_send, post_recv, load_sem, own_sem, send_sem, recv_sem, out_own, refs = refs[:7] + (
        refs[7:],
    )
    out_send, out_recv, cut_in, cut_rows, field, edge, west_edge, east_edge, edge_send, edge_recv = refs
    x, z, y, c = position()
    across, line = partners(x, z, y, c)
    lon = z * 4 + y * 2 + c
    own = (lon, x)
    east, west = (lax.rem(lon + 1, 16), x), (lax.rem(lon + 15, 16), x)
    me = y * 4 + c * 2 + x
    peers, kinds, share, lanes = joint.shape
    slots = peers * share
    head_count, var_count, tokens = prob_ref.shape
    padded = patch_ref.shape[0]
    taps = 4 * var_count
    halves = 2
    half_width = weight_a.shape[-1]

    everyone = [across["x"], across["y"], across["c"]] + line
    for flip in (3, 5, 6, 7):
        there_y = 1 - y if flip & 4 else y
        there_c = 1 - c if flip & 2 else c
        there_x = 1 - x if flip & 1 else x
        everyone.append((z * 4 + there_y * 2 + there_c, there_x))
    sources = [sector_of(z, y, c, x, part, side) for part in range(2) for side in range(2)]
    meet(everyone + [east, west], sources, own)
    letters = []
    for part in range(2):
        row = 2 * x + part
        letters.append(
            (cut_in.at[part], cut_ref.at[c], post_send.at[part], post_recv.at[c])
            + (block_of(z, y, row), own)
        )
    for row in range(4):
        letters.append(
            (grad_in.at[row], grad_out.at[x, c], post_send.at[2 + row])
            + (post_recv.at[2 + 2 * x + c], block_of(z, y, row), own)
        )
    for letter in letters[2:]:
        post(*letter)
    var_total, lat_count, column_count = pixel_ref.shape
    half = lat_ref.shape[1]

    def edge_copies():
        return [
            remote(edge, west_edge, edge_send.at[0], edge_recv.at[0], east),
            remote(edge, east_edge, edge_send.at[1], edge_recv.at[1], west),
        ]

    def send_edges():
        kind = lax.broadcasted_iota(jnp.int32, (16, column_count), 0)
        column = lax.broadcasted_iota(jnp.int32, (16, column_count), 1)
        pick = jnp.where(column == kind * (column_count - 1), 1.0, 0.0).astype(low)
        flat = pixel_ref[...].reshape(var_total * lat_count, column_count)
        edge[...] = dot(pick, flat, 1, 1).astype(low)
        for copy in edge_copies():
            copy.start()

    def make_field():
        for copy in edge_copies():
            copy.wait()
        wanted = columns_of((column_count, 2 * half), 1, half)
        column = lax.broadcasted_iota(jnp.int32, (column_count, 2 * half), 0)
        select = jnp.where(wanted == column, 1.0, 0.0).astype(low)
        kind = lax.broadcasted_iota(jnp.int32, (16, 2 * half), 0)
        wanted = columns_of((16, 2 * half), 1, half)
        from_west = jnp.logical_and(kind == 1, wanted == -1)
        from_east = jnp.logical_and(kind == 0, wanted == column_count)
        flat = pixel_ref[...].reshape(var_total * lat_count, column_count)
        result = dot(flat, select)
        for values, place in ((west_edge, from_west), (east_edge, from_east)):
            result = result + dot(values[...], jnp.where(place, 1.0, 0.0).astype(low), 0, 0)
        field[...] = result.astype(low).reshape(field.shape)

    def cut_row(part):
        lat = jnp.where(x == 0, lat_ref[part : part + 1, :], lat_ref[part + 2 : part + 3, :])
        shift = jnp.where(x == 0, shift_ref[part : part + 1, :], shift_ref[part + 2 : part + 3, :])
        row = lax.broadcasted_iota(jnp.int32, (lat_count, half), 0)
        slots = half // 2

        def body(v, carry):
            values = field[v].astype(wide)
            chosen = jnp.where(shift < 0, values[:, :half], values[:, half:])
            for py in range(2):
                taken = jnp.sum(jnp.where(row == lat + py, chosen, 0.0), axis=0, keepdims=True)
                for px in range(2):
                    spot = pl.ds((2 * py + px) * var_total + v, 1)
                    cut_rows[part, spot, :] = taken[:, px * slots : (px + 1) * slots]
            return carry

        lax.fori_loop(0, var_total, body, 0)

    def send_cut():
        cut_in[...] = cut_rows[...].astype(low)
        for letter in letters[:2]:
            post(*letter)

    def views(number):
        index, lead, first, rows, color = items[number]
        source, target = arrays[index], outs[index]
        if lead is not None:
            source, target = source.at[lead], target.at[lead]
        return source.at[pl.ds(first, rows)], target, pl.ds(first, rows), color

    stages, finish = gatherer(views, gather_sems)

    def load(source, target, spot):
        return pltpu.make_async_copy(source, target, load_sem.at[spot])

    def ask_small():
        load(outs[0], misc_ref, 0).start()
        load(outs[1], small_ref, 1).start()
        load(outs[2], weight_a, 2).start()
        load(outs[3], weight_b, 3).start()

    def read_small():
        load(outs[0], misc_ref, 0).wait()
        load(outs[1], small_ref, 1).wait()
        sector = small_ref.shape[4] // 2
        for lon in range(16):
            at = (lon // 4, lon // 2 % 2, lon % 2)
            for side in range(2):
                rows = slice((2 * lon + side) * sector, (2 * lon + side + 1) * sector)
                for half in range(2):
                    full_ref[rows, half * 128 : (half + 1) * 128] = small_ref[
                        (side,) + at + (slice(half * sector, (half + 1) * sector),)
                    ]
        upper = full_ref[:, 128:]
        vector_ref[...] = upper.astype(wide).T[taps + var_count - 128 : taps + var_count - 120]
        lane = lax.broadcasted_iota(jnp.int32, upper.shape, 1)
        full_ref[:, 128:] = jnp.where(lane < taps + var_count - 128, upper.astype(wide), 0.0).astype(
            low
        )
        kind = lax.broadcasted_iota(jnp.int32, (16, 128), 0)
        across_rows = lax.broadcasted_iota(jnp.int32, (128, 128), 0)
        across_lanes = lax.broadcasted_iota(jnp.int32, (128, 128), 1)
        queries = [None, None]
        for lon in range(16):
            at = (lon // 4, lon // 2 % 2, lon % 2)
            span = slice(lon * 128, (lon + 1) * 128)
            block = misc_ref[(0,) + at + (slice(0, 16),)].astype(wide)
            tag = jnp.sum(jnp.where(kind == z, block, 0.0), axis=0, keepdims=True)
            crop = jnp.sum(jnp.where(kind == 4 + z, block, 0.0), axis=0, keepdims=True)
            tag_ref[0:1, span] = tag
            for row, target in ((crop, crop_ref), (tag, turned)):
                target[span, :] = jnp.sum(
                    jnp.where(across_rows == across_lanes, row, 0.0), axis=1, keepdims=True
                )
            for side in range(2):
                block = misc_ref[(side,) + at + (slice(0, 16),)].astype(wide)[8:16]
                queries[side] = block if lon == 0 else queries[side] + block
        query_ref[...] = jnp.concatenate(queries, axis=0)
        mine = pl.ds(pl.multiple_of(me * share, share), share)
        keep_ref[...] = jnp.where(turned[mine, :] >= 0.0, 1.0, 0.0)
        crops = crop_ref[mine, :]
        hours = jnp.zeros((tokens, 1), wide)
        for k in range(8):
            hours = hours + jnp.where(crops == float(k), hour_ref[0:1, k : k + 1], 0.0)
        lead_ref[...] = hours
        for part in range(2):
            pltpu.make_async_copy(cut_in.at[part], cut_ref.at[part], post_recv.at[part]).wait()
            patch_ref[:taps, part * 128 : (part + 1) * 128] = cut_ref[part]
        patch_ref[taps : taps + var_count, :] = jnp.ones((var_count, tokens), low)
        patch_ref[taps + var_count :, :] = jnp.zeros((padded - taps - var_count, tokens), low)

    def tables(weight, spot, table):
        load(outs[spot], weight, spot).wait()
        for side in range(halves):
            product = dot(weight[side].reshape(-1, half_width), full_ref[...], 0, 0)
            table[side * half_width : (side + 1) * half_width, :] = product.astype(table.dtype)

    def score():
        tables(weight_a, 2, key_table)
        wide_query = jnp.concatenate([query_ref[...]] * (head_count * HEAD_DIM // 128), axis=1)
        head = lax.div(lax.broadcasted_iota(jnp.int32, wide_query.shape, 1), HEAD_DIM)
        row = lax.broadcasted_iota(jnp.int32, wide_query.shape, 0)
        wide_query = jnp.where(head == row, wide_query, 0.0).astype(low)
        rest, result = key_table[...], None
        for _ in range(3):
            part = rest.astype(low)
            rest = rest - part.astype(wide)
            piece = dot(wide_query, part)
            result = piece if result is None else result + piece
        score_table[...] = result * HEAD_DIM ** (-0.5)

    def ask_back():
        load(outs[4], weight_a, 2).start()

    def heads(first):
        mask = diagonal(var_count, padded)

        def head_step(h, carry):
            spread = jnp.where(mask, score_table[pl.ds(h, 1), :], 0.0)
            upper = spread.astype(low)
            lower = (spread - upper.astype(wide)).astype(low)
            patch = patch_ref[...]
            scores = dot(upper, patch) + dot(lower, patch)
            raised = jnp.exp(scores - jnp.max(scores, axis=0, keepdims=True))
            prob = raised / jnp.sum(raised, axis=0, keepdims=True)
            prob_ref[h] = prob
            pooled = jnp.concatenate(
                [
                    (prob * patch_ref[k * var_count : (k + 1) * var_count, :].astype(wide)).astype(
                        low
                    )
                    for k in range(5)
                ]
                + [jnp.zeros((padded - 5 * var_count, tokens), low)],
                axis=0,
            )
            start = pl.multiple_of(h * HEAD_DIM, HEAD_DIM)
            mixed_ref[pl.ds(start, HEAD_DIM), :] = dot(
                value_table[pl.ds(start, HEAD_DIM), :], pooled
            ).astype(low)
            return carry

        lax.fori_loop(first, first + 4, head_step, 0)

    def begin_block():
        load(outs[4], weight_a, 2).wait()
        total = lead_ref[...] * vector_ref[0:1] + vector_ref[1:2]
        mixed = mixed_ref[...].T
        for side in range(halves):
            total = total + dot(
                mixed[:, side * half_width : (side + 1) * half_width],
                weight_a[side].reshape(-1, half_width),
                1,
                1,
            )
        start_ref[...] = total
        normed, _ = norm_parts(total)
        low_ref[...] = (normed * vector_ref[2:3] + vector_ref[3:4]).astype(low)

    def ask_input(kind):
        target = weight_b if kind % 2 == 0 else weight_a
        load(outs[5].at[kind], target, 3 - kind % 2).start()

    def project(kind):
        target = weight_b if kind % 2 == 0 else weight_a
        load(outs[5].at[kind], target, 3 - kind % 2).wait()
        pairs = half_width // lanes
        for side in range(halves):
            result = dot(low_ref[...], target[side].reshape(-1, half_width)).astype(low)
            if kind == 0:
                result = result * low(HEAD_DIM ** (-0.5))
            for pair in range(pairs):
                projected[side * pairs + pair, kind] = result[
                    :, pair * lanes : (pair + 1) * lanes
                ]

    def inward(step):
        there = lax.rem(me + step, peers)
        return remote(
            projected.at[there],
            joint.at[me],
            send_sem.at[there],
            recv_sem.at[me],
            plane_device(z, there),
        )

    def outward(index):
        return remote(
            sending.at[index],
            received.at[me],
            out_send.at[index],
            out_recv.at[me],
            plane_device(z, index),
        )

    def send_heads():
        pltpu.make_async_copy(projected.at[me], joint.at[me], own_sem).start()
        for step in range(1, peers):
            inward(step).start()

    def take_heads():
        pltpu.make_async_copy(projected.at[me], joint.at[me], own_sem).wait()
        for step in range(1, peers):
            there = lax.rem(me + step, peers)
            pltpu.make_async_copy(joint.at[there], joint.at[there], recv_sem.at[there]).wait()

    def attention(first, count):
        def block(step, carry):
            index = lax.rem(me + 1 + step, peers)
            span = pl.ds(pl.multiple_of(index * share, share), share)
            queries = joint[index, 0]
            keys = joint[:, 1].reshape(slots, lanes)
            values = joint[:, 2].reshape(slots, lanes)
            allowed = crop_ref[span, :] == tag_ref[0:1, :]
            result = None
            for h in range(2):
                scores = dot(head_lanes(queries, h), keys, 1, 1)
                scores = jnp.where(allowed, scores, masked_score)
                largest = jnp.max(scores, axis=1, keepdims=True)
                weights = jnp.exp(scores - largest)
                total = jnp.sum(weights, axis=1, keepdims=True)
                weights = (weights * (1.0 / total)).astype(low)
                part = head_lanes(dot(weights, values), h)
                result = part if result is None else result + part
                total_ref[h, span, :] = largest + jnp.log(total)
            wide_ref[span, :] = result
            sending[index] = result.astype(low)

            @pl.when(step < peers - 1)
            def _():
                outward(index).start()

            return carry

        lax.fori_loop(first, first + count, block, 0)

    ready = {}
    for number, item in enumerate(items):
        ready[item[:2]] = number + 8
    at = ready[(3, None)]
    extra = {0: [send_edges], 3: [make_field], 4: [partial(cut_row, 0)], 5: [partial(cut_row, 1)]}
    extra.update({6: [send_cut], at: [ask_small, read_small], at + 1: [score]})
    extra[at + 2] = [lambda: tables(weight_b, 3, value_table), ask_back]
    for quarter in range(4):
        extra.setdefault(at + 3 + quarter // 2, []).append(partial(heads, 4 * quarter))
    at = max(at + 5, ready[(5, 2)])
    extra.setdefault(at, []).extend([partial(ask_input, 0), begin_block, partial(ask_input, 1)])
    extra[at + 1] = [partial(project, 0), partial(ask_input, 2), partial(project, 1)]
    extra[at + 2] = [partial(project, 2), send_heads]
    at += 5
    extra[at] = [take_heads]
    for step in range(4):
        extra.setdefault(at + step, []).append(partial(attention, 2 * step, 2))
    total = len(items)
    for step in range(max(total + 8, max(extra) + 1)):
        for back, stage in enumerate(stages):
            if 0 <= step - 2 * back < total:
                stage(step - 2 * back)
        for work in extra.get(step, []):
            work()
    last = pltpu.make_async_copy(sending.at[me], received.at[me], out_own)
    last.start()
    for number in range(total):
        finish(number)
    for letter in letters:
        settle(*letter)
    for side in range(2):
        for part in range(2):
            pltpu.make_async_copy(
                grad_in.at[0], grad_out.at[side, part], post_recv.at[2 + 2 * side + part]
            ).wait()
    for step in range(1, peers):
        there = lax.rem(me + step, peers)
        inward(step).wait_send()
        outward(there).wait_send()
        pltpu.make_async_copy(sending.at[there], received.at[there], out_recv.at[there]).wait()
    last.wait()


def front(arrays, grads, hours, pixels, lat_lanes, shift_lanes, head_count, number):
    items = []
    for index, array in enumerate(arrays):
        for lead in range(array.shape[0]) if array.ndim == 3 else (None,):
            rows = array.shape[-2]
            if rows % 64:
                items.append((index, lead, 0, rows, 0))
                continue
            for color in range(2):
                items.append((index, lead, color * rows // 2, rows // 2, color))
    width = arrays[2].shape[1]
    model = 2 * width
    var_count, lat_count = pixels.shape[:2]
    tokens = lat_lanes.shape[1]
    cut_shape = (2, 4 * var_count, tokens // 2)
    padded = 2 * arrays[1].shape[1]
    slots = 8 * tokens
    sem = pltpu.SemaphoreType.DMA
    vmem = pl.BlockSpec(memory_space=pltpu.VMEM)
    hbm = pl.BlockSpec(memory_space=pl.ANY)
    block = (2, 4, 2, 2)

    def all_of(array):
        return array.shape[:-2] + block + array.shape[-2:]

    low_outs = [all_of(a) for a in arrays] + [(2, 2) + grads.shape[1:], (8, tokens, 128)]
    vmem_outs = [
        ((8, 3, tokens, 128), low),
        ((slots, 128), wide),
        ((2, slots, 1), wide),
        ((8, slots), wide),
        ((slots, 1), wide),
        ((padded, tokens), low),
        ((head_count, var_count, tokens), wide),
        ((model, tokens), low),
        ((model, padded), low),
        ((model, padded), wide),
        ((head_count, padded), wide),
        ((model, padded), low),
        ((8, model), wide),
        ((head_count, 128), wide),
        ((tokens, model), wide),
        ((tokens, model), low),
        ((tokens, 1), wide),
        ((tokens, 1), wide),
    ]
    result = pl.pallas_call(
        partial(front_kernel, items),
        out_shape=[jax.ShapeDtypeStruct(shape, low) for shape in low_outs]
        + [jax.ShapeDtypeStruct(shape, dtype) for shape, dtype in vmem_outs],
        in_specs=[hbm] * (len(arrays) + 1) + [vmem] * 4,
        out_specs=[hbm] * len(low_outs) + [vmem] * len(vmem_outs),
        scratch_shapes=[
            pltpu.VMEM(cut_shape, low),
            pltpu.VMEM(all_of(arrays[0]), low),
            pltpu.VMEM(all_of(arrays[1]), low),
            pltpu.VMEM(all_of(arrays[2]), low),
            pltpu.VMEM(all_of(arrays[2]), low),
            pltpu.VMEM((8, 3, tokens, 128), low),
            pltpu.VMEM((8, tokens, 128), low),
            pltpu.VMEM((slots, 1), wide),
            sem((len(items),)),
        ]
        + [sem((len(items), 3))] * 4
        + [sem((6,)), sem((6,)), sem((4,)), sem, sem((8,)), sem((8,)), sem, sem((8,)), sem((8,))]
        + [
            pltpu.VMEM(cut_shape, low),
            pltpu.VMEM(cut_shape, wide),
            pltpu.VMEM((var_count, lat_count, 2 * tokens), low),
            pltpu.VMEM((16, var_count * lat_count), low),
            pltpu.VMEM((16, var_count * lat_count), low),
            pltpu.VMEM((16, var_count * lat_count), low),
            sem((2,)),
            sem((2,)),
        ],
        compiler_params=pltpu.CompilerParams(
            collective_id=number, has_side_effects=True, vmem_limit_bytes=58 * 2**20
        ),
    )(*arrays, grads, hours, pixels, lat_lanes, shift_lanes)
    count = len(arrays)
    gathered = [
        g.reshape(a.shape[:-2] + (2, 16 * a.shape[-2], a.shape[-1]))
        for g, a in zip(result, arrays)
    ]
    return gathered, result[count:]


def feed_kernel(
    attended_ref,
    proj_ref,
    start_ref,
    vector_ref,
    up_ref,
    down_ref,
    bias_ref,
    final_ref,
    masked_ref,
    keep_ref,
    predicted_ref,
    middle_grad_ref,
    unit_ref,
    grad_feed_ref,
    grad_proj_ref,
    grad_final_ref,
    grad_bias_ref,
    grad_vector_ref,
    flat,
    middle,
    second,
    second_turned,
    active,
    slope,
    total,
    grad_low,
    grad_turned,
    grad_final,
):
    step = pl.program_id(0)
    count = active.shape[0]
    row_count, units, share, lanes = attended_ref.shape
    _, halves, _, half_width = proj_ref.shape
    tokens = row_count * share

    @pl.when(step == 0)
    def _():
        for unit in range(units):
            flat[:, unit * lanes : (unit + 1) * lanes] = attended_ref[:, unit].reshape(
                tokens, lanes
            )
        result = start_ref[...]
        for side in range(halves):
            result = result + dot(
                flat[:, side * half_width : (side + 1) * half_width], proj_ref[0, side], 1, 1
            )
        middle[...] = result
        normed, _ = norm_parts(result)
        normed = (normed * vector_ref[4:5] + vector_ref[5:6]).astype(low)
        second[...] = normed
        second_turned[...] = normed.T
        total[...] = result

    @pl.when(step < count)
    def _():
        hidden = dot(second[...], up_ref[0, 0]) + bias_ref[...]
        share_of = 0.5 * (1.0 + lax.erf(hidden * (0.5**0.5)))
        fired = (hidden * share_of).astype(low)
        active[step] = fired
        slope[step] = share_of + hidden * jnp.exp(-0.5 * hidden * hidden) * (
            0.5 / 1.2533141373155003
        )
        total[...] += dot(fired, down_ref[0, 0], 1, 1)

    @pl.when(step == count - 1)
    def _():
        final_low = total[...].astype(low)
        final_turned = final_low.T
        grads = None
        for side in range(halves):
            predicted_ref[side] = (dot(final_low, final_ref[side]) * keep_ref[...]).astype(low)
            part = dot(masked_ref[side], final_ref[side], 1, 1)
            grads = part if grads is None else grads + part
            grad_final_ref[side] = dot(final_turned, masked_ref[side]).astype(low)
        grad_final[...] = grads
        grad_low[...] = grads.astype(low)
        grad_turned[...] = grads.astype(low).T
        total[...] = jnp.zeros_like(total)

    @pl.when(step >= count)
    def _():
        block = step - count
        hidden_grad = dot(grad_low[...], down_ref[0, 0]) * slope[block]
        hidden_low = hidden_grad.astype(low)
        grad_bias_ref[...] = jnp.sum(hidden_low.astype(wide), axis=0, keepdims=True)
        total[...] += dot(hidden_low, up_ref[0, 0], 1, 1)
        grad_feed_ref[0, 0] = dot(second_turned[...], hidden_low).astype(low)
        grad_feed_ref[1, 0] = dot(grad_turned[...], active[block]).astype(low)

    @pl.when(step == 2 * count - 1)
    def _():
        part, grad_gain, grad_shift = norm_back(middle[...], vector_ref[4:5], total[...])
        result = grad_final[...] + part
        middle_grad_ref[...] = result
        grad_vector_ref[0:1] = grad_gain
        grad_vector_ref[1:2] = grad_shift
        result_low = result.astype(low)
        result_turned = result_low.T
        pairs = half_width // lanes
        for side in range(halves):
            span = slice(side * half_width, (side + 1) * half_width)
            grad_proj_ref[side] = dot(result_turned, flat[:, span]).astype(low)
            out = dot(result_low, proj_ref[0, side]).astype(low)
            for pair in range(pairs):
                unit_ref[:, side * pairs + pair] = out[
                    :, pair * lanes : (pair + 1) * lanes
                ].reshape(row_count, share, lanes)


def feed(attended, start, vectors, late, up_bias, final_weight, masked, keep):
    blocks, halves, model, block = late.shape
    half_width = block
    each = blocks // 2
    full = each * block
    tokens = start.shape[0]
    count = halves * each

    def block_of_kind(kind):
        def block_at(i):
            j = lax.rem(i, count)
            return (kind * each + lax.rem(j, each), lax.div(j, each), 0, 0)

        return pl.BlockSpec((1, 1, model, block), block_at)

    def late_block(i):
        j = lax.max(i - count, 0)
        return (0, lax.div(j, each), 0, lax.rem(j, each))

    def fixed(shape, dtype):
        rank = len(shape)
        return jax.ShapeDtypeStruct(shape, dtype), pl.BlockSpec(shape, lambda i: (0,) * rank)

    outs = [
        fixed((halves, tokens, 128), low),
        fixed((tokens, model), wide),
        fixed(attended.shape, low),
        (
            jax.ShapeDtypeStruct((2, halves, model, full), low),
            pl.BlockSpec((2, 1, model, block), late_block),
        ),
        fixed((halves, model, half_width), low),
        fixed((halves, model, 128), low),
        (
            jax.ShapeDtypeStruct((1, halves * full), wide),
            pl.BlockSpec((1, block), lambda i: (0, lax.max(i - count, 0))),
        ),
        fixed((2, model), wide),
    ]
    return pl.pallas_call(
        feed_kernel,
        grid=(2 * count,),
        out_shape=[shape for shape, _ in outs],
        in_specs=[
            whole(attended),
            pl.BlockSpec((1, halves, model, block), lambda i: (blocks - 1, 0, 0, 0)),
            whole(start),
            whole(vectors),
            block_of_kind(0),
            block_of_kind(1),
            pl.BlockSpec((1, block), lambda i: (0, lax.rem(i, count))),
            whole(final_weight),
            whole(masked),
            whole(keep),
        ],
        out_specs=[spec for _, spec in outs],
        scratch_shapes=[
            pltpu.VMEM((tokens, model), low),
            pltpu.VMEM((tokens, model), wide),
            pltpu.VMEM((tokens, model), low),
            pltpu.VMEM((model, tokens), low),
            pltpu.VMEM((count, tokens, block), low),
            pltpu.VMEM((count, tokens, block), wide),
            pltpu.VMEM((tokens, model), wide),
            pltpu.VMEM((tokens, model), low),
            pltpu.VMEM((model, tokens), low),
            pltpu.VMEM((tokens, model), wide),
        ],
        compiler_params=pltpu.CompilerParams(vmem_limit_bytes=56 * 2**20),
    )(attended, late, start, vectors, late, late, up_bias, final_weight, masked, keep)


def einsum(spec, left, right):
    return jnp.einsum(spec, left, right, preferred_element_type=wide)


def fast_local(
    pixels,
    crop_starts,
    crop_shifts,
    slot_crops,
    occupied,
    lead_hours,
    patch_weight,
    variable_embed,
    mixer_query,
    mixer_keys,
    mixer_values,
    mixer_output,
    lead_embed,
    first_gain,
    first_bias,
    attention_in,
    attention_out,
    second_gain,
    second_bias,
    expand_weight,
    expand_bias,
    reduce_weight,
    output_weight,
    cotangent,
):
    lon, head = lax.axis_index(LON), lax.axis_index(HEAD)
    row_count, slot_width = slot_crops.shape
    share = slot_width // HEAD_SIZE
    tokens = row_count * share
    var_count, lat_count, column_count = pixels.shape
    head_half, query_width = mixer_query.shape
    head_count = HEAD_SIZE * head_half
    half_width = head_half * HEAD_DIM
    out_half = output_weight.shape[1]
    slice_width = patch_weight.shape[2]
    model = slice_width * LON_SIZE * HEAD_SIZE
    block_rows = model // LON_SIZE
    taps = 4 * var_count
    pairs = half_width // 128
    scale = HEAD_DIM ** (-0.5)

    lat_lanes = jnp.tile(crop_lookup(crop_starts, slot_crops), (1, 2))
    shift_lanes = jnp.tile(crop_lookup(crop_shifts, slot_crops), (1, 2))
    masked = cotangent * occupied[:, :, None].astype(low)
    masked = jnp.pad(masked, ((0, 0), (0, 0), (0, 128 - out_half)))
    late = jnp.concatenate(
        [
            jnp.transpose(part.reshape(block_rows, -1, half_width), (1, 0, 2))
            for part in (expand_weight, reduce_weight.T, attention_out.T)
        ]
    )
    padded = 256
    small = jnp.concatenate(
        [
            jnp.transpose(patch_weight, (1, 0, 2)).reshape(taps, slice_width),
            variable_embed,
            jnp.concatenate(
                [
                    lead_embed.reshape(-1),
                    first_gain,
                    first_bias,
                    second_gain,
                    second_bias,
                    jnp.zeros(((padded - taps - var_count - 6) * slice_width,), low),
                ]
            ).reshape(-1, slice_width),
        ]
    ).T
    small = jnp.concatenate([small[:, :128], small[:, 128:]])
    tags = jnp.where(occupied == 1, slot_crops, -1).astype(low)
    lane = jnp.arange(128) % (LON_SIZE * query_width) // query_width
    spread = jnp.tile(jnp.concatenate([mixer_query, expand_bias]), (1, 128 // query_width))
    spread = jnp.where(lane == lon, spread, 0)
    misc = jnp.concatenate([tags, slot_crops.astype(low), spread])
    out_block = jnp.pad(output_weight, ((0, 0), (0, 128 - out_half)))
    my_row = lax.div(lon, LON_SIZE // row_count)
    hours = lax.dynamic_index_in_dim(lead_hours, my_row, 0).astype(wide) / 100.0
    hours = jnp.pad(hours, ((0, 0), (0, 128 - hours.shape[1])))
    gathered, made = front(
        [
            misc,
            small,
            mixer_keys,
            mixer_values,
            mixer_output.T,
            attention_in,
            out_block,
            late,
        ],
        masked,
        hours,
        pixels,
        lat_lanes,
        shift_lanes,
        head_count,
        1,
    )
    misc_all, _, key_weight, value_weight, mixer_weight, input_weight, final_weight, late = gathered
    masked, attended, joint, attended_wide, totals, tag_row, crop_column = made[:7]
    patches, probs, mixed, value_table, key_table, score_table = made[7:13]
    patch_full, vectors, query, start_sum, first_low, lead_column, keep_mask = made[13:]
    masked = masked.reshape(HEAD_SIZE, tokens, 128)
    attended = attended[None]
    query_wide, query = query, query[:, :HEAD_DIM]
    bias_rows = expand_bias.shape[0]
    up_bias = misc_all.reshape(HEAD_SIZE, LON_SIZE, -1, 128)[:, :, 2 * row_count + head_half :]
    up_bias = jnp.sum(up_bias[..., : LON_SIZE * query_width].astype(wide), axis=1)
    units = HEAD_SIZE * pairs
    (
        predicted,
        middle_grad,
        out_grads,
        grad_feed,
        grad_proj,
        grad_out,
        grad_up_bias,
        second_vectors,
    ) = feed(
        attended,
        start_sum,
        vectors,
        late,
        up_bias.reshape(1, -1),
        final_weight,
        masked,
        keep_mask,
    )
    stacked, feed_sums = attend_back(
        joint,
        tag_row,
        crop_column,
        attended_wide,
        totals,
        out_grads.reshape(units, tokens, 128),
        grad_feed,
        4,
    )
    bias_cols = expand_bias.shape[1]
    bias_block = jnp.transpose(
        grad_up_bias.reshape(HEAD_SIZE, bias_rows, LON_SIZE, bias_cols), (0, 2, 1, 3)
    )
    bias_at = out_half + head_half
    bias_block = jnp.pad(
        bias_block,
        (
            (0, 0),
            (0, 0),
            (0, block_rows - bias_rows),
            (bias_at, 128 - bias_at - bias_cols),
        ),
    ).reshape(HEAD_SIZE, model, 128)
    spot = taps + var_count
    sums, predicted, pixel_grad = reduce_all(
        grad_feed,
        grad_proj,
        predicted.reshape(HEAD_SIZE, 2, slot_width, 128),
        (key_weight, value_weight, input_weight, mixer_weight),
        lat_lanes,
        shift_lanes,
        (patches, probs, score_table, value_table, key_table, mixed),
        (patch_full, query_wide, second_vectors, grad_out, bias_block.astype(low)),
        (stacked, first_low, start_sum, middle_grad, vectors, lead_column),
        lat_count,
        2,
    )
    predicted = predicted[:, :, :out_half]
    full_half = expand_weight.shape[1]
    place = [0]

    def take(width):
        begin = place[0]
        place[0] = begin + width
        return sums[:, begin : begin + width]

    out_up = feed_sums[:, :full_half]
    out_down = jnp.concatenate([feed_sums[:, full_half:], take(2 * LATE_PAIRS * CHUNK)], axis=1).T
    out_proj = take(half_width).T
    out_input = jnp.stack([take(half_width) for _ in range(3)])
    out_mixer = take(half_width).T
    out_values = take(half_width)
    tail_small = take(128)
    tail_rest = take(128)
    tail_small = jnp.concatenate([tail_small[:slice_width], tail_small[slice_width:]], axis=1).T
    out_patch = jnp.transpose(tail_small[:taps].reshape(4, var_count, slice_width), (1, 0, 2))
    out_variable = tail_small[taps:spot]
    out_lead = tail_small[spot : spot + 2]
    out_final = tail_rest[:, :out_half]
    at = out_half
    my_heads = tail_rest[:, at : at + head_half]
    at += head_half
    out_bias = tail_rest[:bias_rows, at : at + bias_cols]
    at += bias_cols
    out_query = tail_rest[:head_half, at : at + query_width]
    my_query = block_slice(query, head, head_half, 0)
    out_keys = (my_heads[:, :, None] * my_query[None]).reshape(block_rows, half_width)

    pixel_grad = jnp.transpose(pixel_grad, (1, 0, 2))
    return (
        predicted,
        pixel_grad,
        out_patch,
        out_variable,
        out_query,
        out_keys,
        out_values,
        out_mixer,
        out_lead,
        tail_small[spot + 2],
        tail_small[spot + 3],
        out_input,
        out_proj,
        tail_small[spot + 4],
        tail_small[spot + 5],
        out_up,
        out_bias,
        out_down,
        out_final,
    )


def solution(mesh):
    body = fast_local if planned(mesh) else local
    placed = (
        P(None, None, LON),
        P(),
        P(),
        P(None, LON),
        P(None, LON),
        P(),
        P(None, None, (LON, HEAD)),
        P(None, (LON, HEAD)),
        P(HEAD, LON),
        P(LON, HEAD),
        P(LON, HEAD),
        P(HEAD, LON),
        P(None, (LON, HEAD)),
        P((LON, HEAD)),
        P((LON, HEAD)),
        P(None, LON, HEAD),
        P(HEAD, LON),
        P((LON, HEAD)),
        P((LON, HEAD)),
        P(LON, HEAD),
        P(HEAD, LON),
        P(HEAD, LON),
        P(LON, HEAD),
        P(None, LON, HEAD),
    )
    return jax.shard_map(
        body,
        mesh=mesh,
        in_specs=placed,
        out_specs=(
            P(None, LON, HEAD),
            P(None, None, LON),
            P(None, None, (LON, HEAD)),
            P(None, (LON, HEAD)),
            P(HEAD, LON),
            P(LON, HEAD),
            P(LON, HEAD),
            P(HEAD, LON),
            P(None, (LON, HEAD)),
            P((LON, HEAD)),
            P((LON, HEAD)),
            P(None, LON, HEAD),
            P(HEAD, LON),
            P((LON, HEAD)),
            P((LON, HEAD)),
            P(LON, HEAD),
            P(HEAD, LON),
            P(HEAD, LON),
            P(LON, HEAD),
        ),
        check_vma=False,
    )
```
